32 devices in a mesh: dp: 8 (over z, x), sp: 4 (over y, core).
Axes of the slice: x: 2, y: 2, z: 4, core: 2. Of those that a mesh axis runs over, the one named last changes fastest.
Arguments:
- tokens: bfloat16 [8, 4096, 256], P('dp', 'sp'), may hold values from -12 to 12, as said below
- ln1_gain: bfloat16 [256], replicated, may hold values from 0.25 to 1.75
- ffn1_in: bfloat16 [256, 1024], replicated, may hold values from -0.375 to 0.375
- ffn1_out: bfloat16 [1024, 256], replicated, may hold values from -0.1875 to 0.1875
- ln2_gain: bfloat16 [256], replicated, may hold values from 0.25 to 1.75
- w_qkv: bfloat16 [256, 768], replicated, may hold values from -0.375 to 0.375
- w_out: bfloat16 [256, 256], replicated, may hold values from -1.5 to 1.5
- ln3_gain: bfloat16 [256], replicated, may hold values from 0.25 to 1.75
- w_point1: bfloat16 [256, 512], replicated, may hold values from -0.375 to 0.375
- depthwise: bfloat16 [32, 256], replicated, may hold values from -1 to 1
- bn_gain: bfloat16 [256], replicated, may hold values from 0.25 to 1.75
- bn_bias: bfloat16 [256], replicated, may hold values from -3 to 3
- w_point2: bfloat16 [256, 256], replicated, may hold values from -0.375 to 0.375
- ln4_gain: bfloat16 [256], replicated, may hold values from 0.25 to 1.75
- ffn2_in: bfloat16 [256, 1024], replicated, may hold values from -0.375 to 0.375
- ffn2_out: bfloat16 [1024, 256], replicated, may hold values from -0.1875 to 0.1875
- ln5_gain: bfloat16 [256], replicated, may hold values from 0.25 to 1.75
- lengths: int32 [8, 4], P('dp'), may hold values from 128 to 3328, as said below
- cotangent: bfloat16 [8, 4096, 256], P('dp', 'sp'), may hold values from -6 to 6
Outputs:
- output: bfloat16 [8, 4096, 256], P('dp', 'sp')
- input_grad: bfloat16 [8, 4096, 256], P('dp', 'sp')
- grad_ln1_gain: float32 [256], replicated
- grad_ffn1_in: float32 [256, 1024], replicated
- grad_ffn1_out: float32 [1024, 256], replicated
- grad_ln2_gain: float32 [256], replicated
- grad_w_qkv: float32 [256, 768], replicated
- grad_w_out: float32 [256, 256], replicated
- grad_ln3_gain: float32 [256], replicated
- grad_w_point1: float32 [256, 512], replicated
- grad_depthwise: float32 [32, 256], replicated
- grad_bn_gain: float32 [256], replicated
- grad_bn_bias: float32 [256], replicated
- grad_w_point2: float32 [256, 256], replicated
- grad_ln4_gain: float32 [256], replicated
- grad_ffn2_in: float32 [256, 1024], replicated
- grad_ffn2_out: float32 [1024, 256], replicated
- grad_ln5_gain: float32 [256], replicated
The draws below stay inside these ranges and needn't reach their ends.
Inputs may be any that keep to these rules, and one draw needn't show every extreme that they name: `lengths`: one item of each sequence, at a place drawn from the seed, has exactly (3) * 1024 + 1024 // 4 frames; the others have 1024 // 8 to 256. Frames after the last item are padding. `tokens`: frames have features of order one, with a part in common along one direction.
All inputs are finite; a program needn't handle non-finite values.
Results may differ from the reference program's by a relative error of at most 0.025.
Values may be sent and summed in bfloat16 or wider, within the bound.
A program may use at most 192 MiB of HBM per device.

```python
import jax
import jax.numpy as jnp
from jax import lax

D = 256
FF = 1024
HEADS = 4
KERNEL = 32
ITEMS = 4
FRAMES = 1024
SEQS = 8
LENGTH = 4096


def draw_tokens(key, part):
    key = jax.random.fold_in(key, 11)
    noise_key, direction_key = jax.random.split(key, 2)
    direction = jax.random.normal(direction_key, (D,), jnp.float32)
    rising = 0.5 + jnp.arange(SEQS, dtype=jnp.float32) / max(SEQS - 1, 1)
    noise = jax.random.normal(noise_key, (SEQS, LENGTH, D), jnp.float32)
    level = rising[:, None, None] * jnp.ones((1, LENGTH, 1), jnp.float32)
    return jnp.clip(noise + level * direction[None, None, :], -12.0, 12.0).astype(jnp.bfloat16)


def draw_lengths(key, part):
    key = jax.random.fold_in(key, 23)
    short_key, place_key = jax.random.split(key, 2)
    others = jax.random.randint(short_key, (SEQS, ITEMS - 1), FRAMES // 8, FRAMES // 4 + 1, dtype=jnp.int32)
    place = jax.random.randint(place_key, (SEQS, 1), 0, ITEMS, dtype=jnp.int32)
    slots = jnp.arange(ITEMS, dtype=jnp.int32)[None, :]
    source = jnp.clip(jnp.where(slots < place, slots, slots - 1), 0, ITEMS - 2)
    picked = jnp.take_along_axis(others, jnp.broadcast_to(source, (SEQS, ITEMS)), axis=1)
    longest = LENGTH - FRAMES + FRAMES // 4
    return jnp.where(slots == place, longest, picked).astype(jnp.int32)


def block_levels(stream_key, shape, cuts, low, top_value):
    loudness = 1.0
    for dim, blocks in cuts:
        draws = jax.random.uniform(jax.random.fold_in(jax.random.fold_in(stream_key, 6), dim), (blocks,), jnp.float32, low / len(cuts), top_value / len(cuts))
        loudness = loudness * jnp.repeat(jnp.exp(draws), shape[dim] // blocks).reshape((-1,) + (1,) * (len(shape) - 1 - dim))
    return loudness


def scatter_about(rng, extent, scale, most, shards=(), held_as=jnp.bfloat16):
    array = jax.random.normal(rng, extent, jnp.float32) * scale
    if len(shards) > 0:
        array = block_levels(rng, extent, shards, -0.22, 0.18) * array
    return jnp.clip(array, min=-most, max=most).astype(held_as)


def setup_inputs(seed: int = 0) -> dict:
    key_list = jax.random.split(jax.random.key(seed), 20)
    tokens = draw_tokens(jax.random.fold_in(key_list[19], 71), 0)
    ln1_gain = jnp.clip(1.0 + 0.15 * jax.random.normal(key_list[1], (D,), jnp.float32), 0.25, 1.75).astype(jnp.bfloat16)
    ffn1_in = scatter_about(key_list[2], (D, FF), D ** -0.5, 0.375)
    ffn1_out = scatter_about(key_list[3], (FF, D), FF ** -0.5, 0.1875)
    ln2_gain = jnp.clip(1.0 + 0.15 * jax.random.normal(key_list[4], (D,), jnp.float32), 0.25, 1.75).astype(jnp.bfloat16)
    w_qkv = scatter_about(key_list[5], (D, 3 * D), D ** -0.5, 0.375)
    w_out = scatter_about(key_list[6], (D, D), (D // 16) ** -0.5, 1.5)
    ln3_gain = jnp.clip(1.0 + 0.15 * jax.random.normal(key_list[7], (D,), jnp.float32), 0.25, 1.75).astype(jnp.bfloat16)
    w_point1 = scatter_about(key_list[8], (D, 2 * D), D ** -0.5, 0.375)
    depthwise = scatter_about(key_list[9], (KERNEL, D), KERNEL ** -0.5, 1.0)
    bn_gain = jnp.clip(1.0 + 0.15 * jax.random.normal(key_list[10], (D,), jnp.float32), 0.25, 1.75).astype(jnp.bfloat16)
    bn_bias = scatter_about(key_list[11], (D,), 0.5, 3.0)
    w_point2 = scatter_about(key_list[12], (D, D), D ** -0.5, 0.375)
    ln4_gain = jnp.clip(1.0 + 0.15 * jax.random.normal(key_list[13], (D,), jnp.float32), 0.25, 1.75).astype(jnp.bfloat16)
    ffn2_in = scatter_about(key_list[14], (D, FF), D ** -0.5, 0.375)
    ffn2_out = scatter_about(key_list[15], (FF, D), FF ** -0.5, 0.1875)
    ln5_gain = jnp.clip(1.0 + 0.15 * jax.random.normal(key_list[16], (D,), jnp.float32), 0.25, 1.75).astype(jnp.bfloat16)
    lengths = draw_lengths(jax.random.fold_in(key_list[19], 71), 0)
    cotangent = scatter_about(key_list[18], (SEQS, LENGTH, D), 1.0, 6.0, ((0, 8), (1, 4)))
    return dict(tokens=tokens, ln1_gain=ln1_gain, ffn1_in=ffn1_in, ffn1_out=ffn1_out, ln2_gain=ln2_gain, w_qkv=w_qkv, w_out=w_out, ln3_gain=ln3_gain, w_point1=w_point1, depthwise=depthwise, bn_gain=bn_gain, bn_bias=bn_bias, w_point2=w_point2, ln4_gain=ln4_gain, ffn2_in=ffn2_in, ffn2_out=ffn2_out, ln5_gain=ln5_gain, lengths=lengths, cotangent=cotangent)


EPS = 1e-05
BIG = -1e+30
HIGH = lax.Precision.HIGHEST

@jax.custom_vjp
def low(v):
    return lax.optimization_barrier(v.astype(jnp.bfloat16)).astype(jnp.float32)

@jax.custom_vjp
def low_back(v):
    return v

def low_keep(v):
    return (low(v), None)

def low_pass(kept, grad):
    return (grad,)

def back_keep(v):
    return (v, None)

def back_low(kept, grad):
    return (low(grad),)
low.defvjp(low_keep, low_pass)
low_back.defvjp(back_keep, back_low)

def matmul(left, right):
    return jnp.dot(left, right, precision=HIGH, preferred_element_type=jnp.float32)

def layer_norm(rows, gain):
    centre = rows - lax.optimization_barrier(jnp.mean(rows, axis=-1, keepdims=True))
    spread = lax.optimization_barrier(jnp.mean(centre * centre, axis=-1, keepdims=True))
    return centre * lax.rsqrt(spread + EPS) * gain

def segment_of(index, item_ends):
    return lax.optimization_barrier(jnp.sum((index[:, None] >= item_ends[None, :]).astype(jnp.int32), axis=1))

def position_of(index, segment, starts, whole_total):
    begins = jnp.concatenate([starts, whole_total[None]])
    labels = jnp.arange(begins.shape[0], dtype=jnp.int32)
    picked = lax.optimization_barrier(jnp.sum(jnp.where(segment[:, None] == labels[None, :], begins[None, :], 0), axis=1))
    return (index - picked).astype(jnp.float32)

def rotate(rows, position, head_dim, sign):
    count = rows.shape[0]
    split = rows.reshape(count, rows.shape[1] // head_dim, head_dim)
    half = head_dim // 2
    freq = 10000.0 ** (-(jnp.arange(half, dtype=jnp.float32) / half))
    angle = position[:, None, None] * freq[None, None, :]
    cosine = jnp.cos(angle)
    sine = jnp.sin(angle)
    first_half = split[..., :half]
    second_half = split[..., half:]
    turned = jnp.concatenate([first_half * cosine - sign * second_half * sine, sign * first_half * sine + second_half * cosine], axis=-1)
    return turned.reshape(count, rows.shape[1])

def gated_unit(joined):
    half = joined.shape[1] // 2
    return joined[:, :half] * jax.nn.sigmoid(joined[:, half:])

def feed_forward(rows, gain, w_in, w_out):
    normed = low(layer_norm(rows, gain))
    hidden = low_back(matmul(normed, w_in))
    activated = low(jax.nn.silu(hidden))
    return rows + 0.5 * low_back(matmul(activated, w_out))

def attention(rows, gain, w_qkv, w_out, segment, position):
    length = rows.shape[0]
    width = rows.shape[1]
    head_dim = width // HEADS
    normed = low(layer_norm(rows, gain))
    joined = low_back(matmul(normed, w_qkv))
    queries = low(rotate(joined[:, :width], position, head_dim, 1.0)).reshape(length, HEADS, head_dim)
    key_rows = low(rotate(joined[:, width:2 * width], position, head_dim, 1.0)).reshape(length, HEADS, head_dim)
    value_rows = low(joined[:, 2 * width:]).reshape(length, HEADS, head_dim)
    block_rows = min(512, length)
    score_scale = head_dim ** (-0.5)

    def score_block(inputs):
        query_block, segment_block = inputs
        scores = low_back(jnp.einsum('bhd,khd->hbk', query_block, key_rows, precision=HIGH) * score_scale)
        scores = jnp.where((segment_block[:, None] == segment[None, :])[None], scores, BIG)
        row_max = lax.optimization_barrier(jnp.max(scores, axis=-1, keepdims=True))
        powers = jnp.exp(scores - row_max)
        probs = low(powers / lax.optimization_barrier(jnp.sum(powers, axis=-1, keepdims=True)))
        return jnp.einsum('hbk,khd->bhd', probs, value_rows, precision=HIGH)
    context = lax.map(jax.checkpoint(score_block), (queries.reshape(length // block_rows, block_rows, HEADS, head_dim), segment.reshape(length // block_rows, block_rows)))
    context = low(low_back(context.reshape(length, width)))
    return rows + low_back(matmul(context, w_out))

def conv_front(rows, gain, w_point1, kernel, segment):
    length = rows.shape[0]
    tap_count = kernel.shape[0]
    half_taps = tap_count // 2
    normed = low(layer_norm(rows, gain))
    gated_rows = low(gated_unit(low_back(matmul(normed, w_point1))))
    padded = jnp.pad(gated_rows, ((half_taps, half_taps), (0, 0)))
    padded_segment = jnp.pad(segment, (half_taps, half_taps), constant_values=-1)
    summed = jnp.zeros_like(gated_rows)
    for tap_index in range(tap_count):
        same_item = (padded_segment[tap_index:tap_index + length] == segment).astype(jnp.float32)[:, None]
        summed = summed + kernel[tap_index][None, :] * padded[tap_index:tap_index + length] * same_item
    return summed

def conv_rest(rows, conv_out, bn_mean, inv_std, bn_gain, bn_bias, w_point2):
    normed = (conv_out - bn_mean) * inv_std
    activated = low(jax.nn.silu(normed * bn_gain + bn_bias))
    return rows + low_back(matmul(activated, w_point2))

def reference(tokens, ln1_gain, ffn1_in, ffn1_out, ln2_gain, w_qkv, w_out, ln3_gain, w_point1, depthwise, bn_gain, bn_bias, w_point2, ln4_gain, ffn2_in, ffn2_out, ln5_gain, lengths, cotangent):
    whole_index = jnp.arange(LENGTH, dtype=jnp.int32)
    item_ends = jnp.cumsum(lengths, axis=1).astype(jnp.int32)
    starts = (item_ends - lengths).astype(jnp.int32)
    segments = jax.vmap(lambda ends_row: segment_of(whole_index, ends_row))(item_ends)
    positions = jax.vmap(lambda ends_row, starts_row, seg_row: position_of(whole_index, seg_row, starts_row, ends_row[-1]))(item_ends, starts, segments)

    def forward(rows, gain_one, in_one, out_one, gain_two, qkv_weight, out_weight, gain_three, point_one, kernel, norm_gain, norm_bias, point_two, gain_four, in_two, out_two, gain_five):

        def section_first(inputs):
            seq_rows, seq_segment, seq_position = inputs
            after_ffn = feed_forward(seq_rows, gain_one, in_one, out_one)
            after_attn = attention(after_ffn, gain_two, qkv_weight, out_weight, seq_segment, seq_position)
            return (after_attn, conv_front(after_attn, gain_three, point_one, kernel, seq_segment))
        middles, convs = lax.map(jax.checkpoint(section_first), (rows, segments, positions))
        valid_rows = (segments < ITEMS).astype(jnp.float32)[..., None]
        frame_count = jnp.sum(valid_rows)
        bn_mean = lax.optimization_barrier(jnp.sum(valid_rows * convs, axis=(0, 1))) / frame_count
        centered = convs - bn_mean
        inv_std = lax.rsqrt(lax.optimization_barrier(jnp.sum(valid_rows * centered * centered, axis=(0, 1))) / frame_count + EPS)

        def section_second(inputs):
            seq_rows, seq_conv = inputs
            after_conv = conv_rest(seq_rows, seq_conv, bn_mean, inv_std, norm_gain, norm_bias, point_two)
            after_ffn = feed_forward(after_conv, gain_four, in_two, out_two)
            return layer_norm(after_ffn, gain_five)
        return lax.map(jax.checkpoint(section_second), (middles, convs))
    primals = (tokens.astype(jnp.float32), ln1_gain.astype(jnp.float32), ffn1_in.astype(jnp.float32), ffn1_out.astype(jnp.float32), ln2_gain.astype(jnp.float32), w_qkv.astype(jnp.float32), w_out.astype(jnp.float32), ln3_gain.astype(jnp.float32), w_point1.astype(jnp.float32), depthwise.astype(jnp.float32), bn_gain.astype(jnp.float32), bn_bias.astype(jnp.float32), w_point2.astype(jnp.float32), ln4_gain.astype(jnp.float32), ffn2_in.astype(jnp.float32), ffn2_out.astype(jnp.float32), ln5_gain.astype(jnp.float32))
    result, pullback = jax.vjp(forward, *primals)
    grads = pullback(cotangent.astype(jnp.float32))
    return (result.astype(jnp.bfloat16), grads[0].astype(jnp.bfloat16), grads[1], grads[2], grads[3], grads[4], grads[5], grads[6], grads[7], grads[8], grads[9], grads[10], grads[11], grads[12], grads[13], grads[14], grads[15], grads[16])
```

```python
import functools

import jax
import jax.numpy as jnp
import numpy as np
from jax import lax
from jax.experimental import pallas as pl
from jax.experimental.pallas import tpu as pltpu
from jax.sharding import PartitionSpec as P

HEADS = 4
EPS = 1e-05
NEG = -1e30
LN2 = float(np.log(2.0))
F32 = jnp.float32
BF16 = jnp.bfloat16
I32 = jnp.int32
MESH = pl.DeviceIdType.MESH
VMEM = pl.BlockSpec(memory_space=pltpu.VMEM)
SMEM = pl.BlockSpec(memory_space=pltpu.SMEM)
DMA = pltpu.SemaphoreType.DMA
VMEM_LIMIT = 56 * 2**20


def dg(left, right, left_dim, right_dim):
    return lax.dot_general(
        left, right, (((left_dim,), (right_dim,)), ((), ())), preferred_element_type=F32
    )


def rows_at(index, count):
    return pl.ds(pl.multiple_of(index * count, count), count)


def greet(devices):
    barrier = pltpu.get_barrier_semaphore()
    for device in devices:
        pl.semaphore_signal(barrier, inc=1, device_id=device, device_id_type=MESH)
    pl.semaphore_wait(barrier, len(devices))


def sp_peers(count):
    dp, sp = lax.axis_index("dp"), lax.axis_index("sp")
    return [(dp, lax.rem(sp + step, count)) for step in range(1, count)]


def ends_of(len_ref, items):
    ends, total = [], 0
    for item in range(items):
        total = total + len_ref[0, item]
        ends.append(total)
    return ends


def segment_row(first, count, ends):
    frame = first + lax.broadcasted_iota(I32, (1, count), 1)
    segment = jnp.zeros((1, count), I32)
    for end in ends:
        segment = segment + (frame >= end).astype(I32)
    return segment


def position_row(first, count, ends):
    frame = first + lax.broadcasted_iota(I32, (1, count), 1)
    start = jnp.zeros((1, count), I32)
    for end in ends:
        start = jnp.where(frame >= end, end, start)
    return (frame - start).astype(F32)


def block_bounds(first, count, ends, length):
    low, high = 0, length
    for end in ends:
        low = jnp.where(first >= end, end, low)
    for end in reversed(ends):
        high = jnp.where(first + count - 1 < end, end, high)
    return low, high


def onehot_rows(segment, items, other, same):
    row = lax.broadcasted_iota(I32, (16, segment.shape[1]), 0)
    return jnp.where(row <= items, jnp.where(row == segment, same, other), 0.0)


def norm_parts(rows):
    centre = rows - jnp.mean(rows, axis=-1, keepdims=True)
    inv = lax.rsqrt(jnp.mean(centre * centre, axis=-1, keepdims=True) + EPS)
    return centre * inv, inv


def norm_back(grad, hat, inv, gain):
    scaled = grad * gain
    first = jnp.mean(scaled, axis=-1, keepdims=True)
    second = jnp.mean(scaled * hat, axis=-1, keepdims=True)
    return inv * (scaled - first - hat * second)


def sigmoid(x):
    return 1.0 / (1.0 + jnp.exp(-x))


def sine_cosine(position, freq_hi, freq_lo):
    turns = position * freq_hi
    turns = turns - jnp.round(turns) + position * freq_lo
    turns = turns - jnp.round(turns)
    x = turns * float(np.pi)
    x2 = x * x
    s = x * (1 + x2 * (-1 / 6 + x2 * (1 / 120 + x2 * (-1 / 5040 + x2 * (1 / 362880 - x2 / 39916800)))))
    c = 1 + x2 * (-1 / 2 + x2 * (1 / 24 + x2 * (-1 / 720 + x2 * (1 / 40320 + x2 * (-1 / 3628800 + x2 / 479001600)))))
    return 2 * s * c, 1 - 2 * s * s


def front_kernel(
    sp, items, chunk, len_ref, tok, gain1, w_in, w_out, gain2, w_qkv, freq,
    x1_ref, n2_ref, trig, heads, parts, send, recv, local,
):
    me = lax.axis_index("sp")
    frames = tok.shape[0]
    width = heads.shape[1]
    half = trig.shape[0] // 2
    peers = sp_peers(sp)
    greet(peers)
    ends = ends_of(len_ref, items)
    scale = float(np.log2(np.e)) * (2 * half) ** -0.5

    def copies(c):
        cols = rows_at(c, chunk)
        out = [
            pltpu.make_async_remote_copy(
                src_ref=parts.at[peer[1], :, cols],
                dst_ref=heads.at[me, :, cols],
                send_sem=send.at[i, c],
                recv_sem=recv.at[i, c],
                device_id=peer,
                device_id_type=MESH,
            )
            for i, peer in enumerate(peers)
        ]
        own = pltpu.make_async_copy(parts.at[me, :, cols], heads.at[me, :, cols], local.at[c])
        return out, own

    def step(c, carry):
        rows = rows_at(c, chunk)
        x = tok[rows, :].astype(F32)
        hat, _ = norm_parts(x)
        n1 = (hat * gain1[...].astype(F32)).astype(BF16)
        a = dg(n1, w_in[...], 1, 0)
        s = (a * sigmoid(a)).astype(BF16)
        x1 = x + 0.5 * dg(s, w_out[...], 1, 0)
        x1_ref[rows, :] = x1
        hat, _ = norm_parts(x1)
        n2 = (hat * gain2[...].astype(F32)).astype(BF16)
        n2_ref[rows, :] = n2
        joined = dg(w_qkv[...], n2, 1, 1)
        sine, cosine = sine_cosine(
            position_row(me * frames + c * chunk, chunk, ends), freq[:, 0:1], freq[:, 1:2]
        )
        trig[0:half, rows] = sine
        trig[half:, rows] = cosine
        for head in range(sp):
            base = head * width
            for part, factor in ((0, scale), (1, 1.0)):
                low = base + part * 2 * half
                first, second = joined[low : low + half], joined[low + half : low + 2 * half]
                parts[head, part * 2 * half : part * 2 * half + half, rows] = (
                    (first * cosine - second * sine) * factor
                ).astype(BF16)
                parts[head, part * 2 * half + half : (part + 1) * 2 * half, rows] = (
                    (first * sine + second * cosine) * factor
                ).astype(BF16)
            parts[head, 4 * half : 6 * half, rows] = joined[base + 4 * half : base + 6 * half].astype(BF16)
        out, own = copies(c)
        for copy in out:
            copy.start()
        own.start()
        return carry

    lax.fori_loop(0, frames // chunk, step, 0)

    def finish(c, carry):
        out, own = copies(c)
        for copy in out:
            copy.wait()
        own.wait()
        return carry

    lax.fori_loop(0, frames // chunk, finish, 0)


def front(lengths, tok, gain1, w_in, w_out, gain2, w_qkv, freq, sp):
    frames, width = tok.shape
    chunk = min(256, frames)
    count = frames // chunk
    head_width = w_qkv.shape[0] // sp
    half = freq.shape[0]
    return pl.pallas_call(
        functools.partial(front_kernel, sp, lengths.shape[1], chunk),
        out_shape=[
            jax.ShapeDtypeStruct((frames, width), F32),
            jax.ShapeDtypeStruct((frames, width), BF16),
            jax.ShapeDtypeStruct((2 * half, frames), F32),
            jax.ShapeDtypeStruct((sp, head_width, frames), BF16),
        ],
        in_specs=[SMEM] + [VMEM] * 7,
        out_specs=[VMEM] * 4,
        scratch_shapes=[
            pltpu.VMEM((sp, head_width, frames), BF16),
            DMA((sp - 1, count)),
            DMA((sp - 1, count)),
            DMA((count,)),
        ],
        compiler_params=pltpu.CompilerParams(
            collective_id=0, has_side_effects=True, vmem_limit_bytes=VMEM_LIMIT
        ),
        name="front",
    )(lengths, tok, gain1, w_in, w_out, gain2, w_qkv, freq)


def fwd_kernel(items,bq,bk,nsub,len_ref,x_ref,ctx_ref,o_ref,lse_ref,qa,ka,va):
    srcs,rows,fr=x_ref.shape; hd=rows//3; L=srcs*fr
    ends=ends_of(len_ref,items)
    for s in range(srcs):
        cols=pl.ds(s*fr,fr)
        seg=segment_row(s*fr,fr,ends)
        qa[0:hd,cols]=x_ref[s,0:hd,:]
        qa[hd:hd+16,cols]=onehot_rows(seg,items,0.0,1.0).astype(BF16)
        qa[hd+16:2*hd,cols]=jnp.zeros((hd-16,fr),BF16)
        kT=jnp.concatenate([x_ref[s,hd:2*hd,:],onehot_rows(seg,items,NEG,0.0).astype(BF16),jnp.zeros((hd-16,fr),BF16)],axis=0)
        ka[cols,:]=kT.T
        va[0:hd,cols]=x_ref[s,2*hd:3*hd,:]
        one=lax.broadcasted_iota(I32,(16,fr),0)==0
        va[hd:hd+16,cols]=jnp.where(one,1.0,0.0).astype(BF16)
    per=fr//bq
    def qbody(i,c):
        q0=i*bq
        q=qa[:,pl.ds(pl.multiple_of(q0,bq),bq)]
        lo,hi=block_bounds(q0,bq,ends,L)
        def kbody(j,car):
            m,acc=car
            w=bk//nsub
            ks=[pl.ds(pl.multiple_of(j*bk+u*w,w),w) for u in range(nsub)]
            ss=[dg(ka[k,:],q,1,0) for k in ks]
            mn=m
            for s in ss: mn=jnp.maximum(mn,jnp.max(s,axis=0,keepdims=True))
            acc=acc*jnp.exp2(m-mn)
            for s,k in zip(ss,ks):
                p=jnp.exp2(s-mn).astype(BF16)
                acc=acc+dg(va[:,k],p,1,0)
            return mn,acc
        m,acc=lax.fori_loop(lo//bk,(hi+bk-1)//bk,kbody,(jnp.full((1,bq),NEG,F32),jnp.zeros((hd+16,bq),F32)))
        l=acc[hd:hd+1,:]
        o=acc[0:hd,:]/l
        d=i//per; qc=pl.ds(pl.multiple_of((i%per)*bq,bq),bq)
        ctx_ref[d,:,qc]=o.astype(BF16)
        o_ref[d,:,qc]=o
        lse_ref[:,pl.ds(pl.multiple_of(q0,bq),bq)]=m+jnp.log2(l)
        return c
    lax.fori_loop(0,L//bq,qbody,0)
def attend(x,lengths,bq=1024,bk=1024,nsub=4):
    srcs,rows,fr=x.shape; hd=rows//3; L=srcs*fr
    return pl.pallas_call(functools.partial(fwd_kernel,lengths.shape[1],min(bq,fr),min(bk,fr),nsub),
      out_shape=[jax.ShapeDtypeStruct((srcs,hd,fr),BF16),jax.ShapeDtypeStruct((srcs,hd,fr),F32),jax.ShapeDtypeStruct((1,L),F32)],
      in_specs=[SMEM,VMEM],out_specs=[VMEM]*3,
      scratch_shapes=[pltpu.VMEM((2*hd,L),BF16),pltpu.VMEM((L,2*hd),BF16),pltpu.VMEM((hd+16,L),BF16)],
      compiler_params=pltpu.CompilerParams(vmem_limit_bytes=VMEM_LIMIT),name="attend")(lengths,x)

def split3(v):
    a=v.astype(BF16); r=v-a.astype(F32); b=r.astype(BF16); c=(r-b.astype(F32)).astype(BF16)
    return a,b,c
def bwd_kernel(items,bq,bk,len_ref,x_ref,o_ref,lse_ref,do_ref,g_ref,qa,ka,da,va,dq,dk,dv):
    srcs,rows,fr=x_ref.shape; hd=rows//3; L=srcs*fr
    ends=ends_of(len_ref,items)
    row16=lax.broadcasted_iota(I32,(16,fr),0)
    pad=jnp.zeros((hd-32,fr),BF16)
    def stack3(v):
        a,b,c=[u.astype(F32) for u in split3(v)]
        return jnp.where(row16==0,a,jnp.where(row16==1,b,jnp.where(row16==2,c,0.0))).astype(BF16)
    ones3=jnp.where(row16<3,1.0,0.0).astype(BF16)
    for s in range(srcs):
        cols=pl.ds(s*fr,fr)
        seg=segment_row(s*fr,fr,ends)
        qT=jnp.concatenate([x_ref[s,0:hd,:],onehot_rows(seg,items,0.0,1.0).astype(BF16),stack3(-lse_ref[:,cols]),pad],axis=0)
        qa[cols,:]=qT.T
        ka[0:hd,cols]=x_ref[s,hd:2*hd,:]
        ka[hd:hd+16,cols]=onehot_rows(seg,items,NEG,0.0).astype(BF16)
        ka[hd+16:hd+32,cols]=ones3
        ka[hd+32:2*hd,cols]=pad
        do=do_ref[s]
        D=jnp.sum(do.astype(F32)*o_ref[s],axis=0,keepdims=True)
        dT=jnp.concatenate([do,stack3(-D),pad,jnp.zeros((16,fr),BF16)],axis=0)
        da[cols,:]=dT.T
        va[0:hd,cols]=x_ref[s,2*hd:3*hd,:]
        va[hd:hd+16,cols]=ones3
        va[hd+16:2*hd,cols]=jnp.zeros((hd-16,fr),BF16)
    dq[...]=jnp.zeros_like(dq)
    per=fr//bk; perq=fr//bq
    def kbody(j,c):
        k0=j*bk
        ks=pl.ds(pl.multiple_of(k0,bk),bk)
        lo,hi=block_bounds(k0,bk,ends,L)
        d=j//per; kc=pl.ds(pl.multiple_of((j%per)*bk,bk),bk)
        dk[...]=jnp.zeros_like(dk); dv[...]=jnp.zeros_like(dv)
        def qbody(i,car):
            qs=pl.ds(pl.multiple_of(i*bq,bq),bq)
            e=i//perq; qc=pl.ds(pl.multiple_of((i%perq)*bq,bq),bq)
            p=jnp.exp2(dg(qa[qs,:],ka[:,ks],1,0))
            dp=dg(da[qs,:],va[:,ks],1,0)
            ds=(p*dp).astype(BF16)
            pb=p.astype(BF16)
            dv[...]+=dg(do_ref[e,:,qc],pb,1,0)
            dk[...]+=dg(x_ref[e,0:hd,qc],ds,1,0)
            dq[:,qs]+=dg(ka[0:hd,ks],ds,1,1)
            return car
        lax.fori_loop(lo//bq,(hi+bq-1)//bq,qbody,0)
        g_ref[d,hd:2*hd,kc]=(dk[...]*float(np.log(2.0))).astype(BF16)
        g_ref[d,2*hd:3*hd,kc]=dv[...].astype(BF16)
        return c
    lax.fori_loop(0,L//bk,kbody,0)
    for s in range(srcs):
        g_ref[s,0:hd,:]=(dq[:,pl.ds(s*fr,fr)]*(hd**-0.5)).astype(BF16)
def attend_back(x,lengths,o,lse,do,bq=1024,bk=1024):
    srcs,rows,fr=x.shape; hd=rows//3; L=srcs*fr
    bq=min(bq,fr); bk=min(bk,fr)
    return pl.pallas_call(functools.partial(bwd_kernel,lengths.shape[1],bq,bk),
      out_shape=jax.ShapeDtypeStruct(x.shape,BF16),
      in_specs=[SMEM]+[VMEM]*4,out_specs=VMEM,
      scratch_shapes=[pltpu.VMEM((L,2*hd),BF16),pltpu.VMEM((2*hd,L),BF16),pltpu.VMEM((L,2*hd),BF16),pltpu.VMEM((2*hd,L),BF16),
        pltpu.VMEM((hd,L),F32),pltpu.VMEM((hd,bk),F32),pltpu.VMEM((hd,bk),F32)],
      compiler_params=pltpu.CompilerParams(vmem_limit_bytes=VMEM_LIMIT),name="attend_back")(lengths,x,o,lse,do)


def exchange_kernel(sp, parts, heads, send, recv, local):
    me = lax.axis_index("sp")
    peers = sp_peers(sp)
    greet(peers)
    copies = [
        pltpu.make_async_remote_copy(
            src_ref=parts.at[peer[1]],
            dst_ref=heads.at[me],
            send_sem=send.at[i],
            recv_sem=recv.at[i],
            device_id=peer,
            device_id_type=MESH,
        )
        for i, peer in enumerate(peers)
    ]
    for copy in copies:
        copy.start()
    own = pltpu.make_async_copy(parts.at[me], heads.at[me], local)
    own.start()
    own.wait()
    for copy in copies:
        copy.wait()


def exchange(parts, call):
    sp = parts.shape[0]
    anywhere = pl.BlockSpec(memory_space=pl.ANY)
    return pl.pallas_call(
        functools.partial(exchange_kernel, sp),
        out_shape=jax.ShapeDtypeStruct(parts.shape, parts.dtype),
        in_specs=[anywhere],
        out_specs=anywhere,
        scratch_shapes=[DMA((sp - 1,)), DMA((sp - 1,)), DMA],
        compiler_params=pltpu.CompilerParams(collective_id=call, has_side_effects=True),
        name="exchange",
    )(parts)


def gather_kernel(sp, dp, x_ref, all_ref, send, recv):
    me_d, me_s = lax.axis_index("dp"), lax.axis_index("sp")
    total = sp * dp
    me = me_d * sp + me_s
    peers = []
    for step in range(1, total):
        peer = lax.rem(me + step, total)
        peers.append((peer // sp, lax.rem(peer, sp)))
    greet(peers)
    copies = [
        pltpu.make_async_remote_copy(
            src_ref=x_ref,
            dst_ref=all_ref.at[i + 1],
            send_sem=send.at[i],
            recv_sem=recv.at[i],
            device_id=peer,
            device_id_type=MESH,
        )
        for i, peer in enumerate(peers)
    ]
    for copy in copies:
        copy.start()
    all_ref[0] = x_ref[...]
    for copy in copies:
        copy.wait()


def gather_all(x, sp, dp, call):
    total = sp * dp
    return pl.pallas_call(
        functools.partial(gather_kernel, sp, dp),
        out_shape=jax.ShapeDtypeStruct((total,) + x.shape, x.dtype),
        in_specs=[VMEM],
        out_specs=VMEM,
        scratch_shapes=[DMA((total - 1,)), DMA((total - 1,))],
        compiler_params=pltpu.CompilerParams(collective_id=call, has_side_effects=True),
        name="gather_all",
    )(x)


def with_halo(block, width):
    count = lax.axis_size("sp")
    forward = [(i, i + 1) for i in range(count - 1)]
    backward = [(target, source) for source, target in forward]
    low = lax.ppermute(block[-width:], "sp", forward)
    high = lax.ppermute(block[:width], "sp", backward)
    return jnp.concatenate([low, block, high], axis=0)


def layer_norm(rows, gain):
    centre = rows - jnp.mean(rows, axis=-1, keepdims=True)
    spread = jnp.mean(centre * centre, axis=-1, keepdims=True)
    return centre * lax.rsqrt(spread + EPS) * gain


def segment_of(index, item_ends):
    return jnp.sum((index[:, None] >= item_ends[None, :]).astype(jnp.int32), axis=1)


def gated_unit(joined):
    half = joined.shape[1] // 2
    return joined[:, :half] * jax.nn.sigmoid(joined[:, half:])


def feed_forward(rows, gain, w_in, w_out):
    normed, back = jax.vjp(layer_norm, rows, gain)
    normed_low = normed.astype(BF16)
    hidden = dg(normed_low, w_in, 1, 0)
    activated, act_back = jax.vjp(jax.nn.silu, hidden)
    act_low = activated.astype(BF16)
    return rows + 0.5 * dg(act_low, w_out, 1, 0), (back, normed_low, act_low, act_back)


def feed_back(grad_rows, kept, w_in, w_out):
    back, normed_low, act_low, act_back = kept
    grad_branch = (0.5 * grad_rows).astype(BF16)
    grad_w_out = dg(act_low, grad_branch, 0, 0)
    grad_act = dg(grad_branch, w_out, 1, 1)
    grad_hidden = act_back(grad_act)[0].astype(BF16)
    grad_w_in = dg(normed_low, grad_hidden, 0, 0)
    grad_normed = dg(grad_hidden, w_in, 1, 1)
    grad_input, grad_gain = back(grad_normed)
    return grad_rows + grad_input, grad_gain, grad_w_in, grad_w_out


def on_device(
    tokens, ln1_gain, ffn1_in, ffn1_out, ln2_gain, w_qkv, w_out, ln3_gain, w_point1, depthwise,
    bn_gain, bn_bias, w_point2, ln4_gain, ffn2_in, ffn2_out, ln5_gain, lengths, cotangent,
):
    frames, width = tokens.shape[1:]
    sp, dp = lax.axis_size("sp"), lax.axis_size("dp")
    assert HEADS == sp
    head_dim = width // HEADS
    half = head_dim // 2
    items = lengths.shape[1]
    taps = depthwise.shape[0]
    reach = taps // 2
    offset = lax.axis_index("sp") * frames
    item_ends = jnp.cumsum(lengths[0])
    local_segment = segment_of(offset + jnp.arange(frames, dtype=I32), item_ends)
    rim_segment = segment_of(offset - reach + jnp.arange(frames + 2 * reach, dtype=I32), item_ends)
    valid_rows = (local_segment < items).astype(F32)[:, None]
    tap_masks = [
        (rim_segment[j : j + frames] == local_segment).astype(F32)[:, None] for j in range(taps + 1)
    ]
    gain_one, gain_two, gain_three, gain_four, gain_five = (
        g.astype(F32) for g in (ln1_gain, ln2_gain, ln3_gain, ln4_gain, ln5_gain)
    )
    norm_gain, norm_bias, kernel = (g.astype(F32) for g in (bn_gain, bn_bias, depthwise))
    turns = 10000.0 ** (-np.arange(half, dtype=np.float64) / half) / (2 * np.pi)
    high = np.round(turns * 4096.0) / 4096.0
    freq = jnp.asarray(np.stack([high, turns - high], axis=1), F32)
    qkv_rows = w_qkv.T.reshape(3, HEADS, head_dim, width).transpose(1, 0, 2, 3).reshape(3 * width, width)

    after_first, attn_low, trig, heads = front(
        lengths, tokens[0], ln1_gain[None], ffn1_in, ffn1_out, ln2_gain[None], qkv_rows, freq, sp
    )
    context, raw_context, log_sums = attend(heads, lengths)
    context = exchange(context, 1).reshape(width, frames)
    after_attn = after_first + dg(context, w_out, 0, 0)
    conv_normed, conv_norm_back = jax.vjp(layer_norm, after_attn, gain_three)
    conv_low = conv_normed.astype(BF16)
    point_out = dg(conv_low, w_point1, 1, 0)
    gated_rows, gated_back = jax.vjp(gated_unit, point_out)
    rim_gated = with_halo(gated_rows.astype(BF16), reach).astype(F32)
    conv_out = jnp.zeros((frames, width), F32)
    for tap in range(taps):
        conv_out = conv_out + kernel[tap][None, :] * rim_gated[tap : tap + frames] * tap_masks[tap]
    own_count = jnp.sum(valid_rows)
    own_mean = jnp.sum(valid_rows * conv_out, axis=0) / jnp.maximum(own_count, 1.0)
    own_spread = jnp.sum(valid_rows * (conv_out - own_mean) ** 2, axis=0)
    rows = jnp.stack([own_mean, own_spread, jnp.broadcast_to(own_count, (width,))])
    every = gather_all(jnp.concatenate([rows, jnp.zeros((5, width), F32)]), sp, dp, 2)
    counts = every[:, 2]
    frame_count = jnp.sum(counts, axis=0)
    bn_mean = jnp.sum(counts * every[:, 0], axis=0) / frame_count
    variance = (
        jnp.sum(every[:, 1], axis=0) + jnp.sum(counts * (every[:, 0] - bn_mean) ** 2, axis=0)
    ) / frame_count
    centered = conv_out - bn_mean
    inv_std = lax.rsqrt(variance + EPS)
    normed = centered * inv_std
    swished, swish_back = jax.vjp(jax.nn.silu, normed * norm_gain + norm_bias)
    swish_low = swished.astype(BF16)
    after_conv = after_attn + dg(swish_low, w_point2, 1, 0)
    after_second, second_kept = feed_forward(after_conv, gain_four, ffn2_in, ffn2_out)
    output, final_back = jax.vjp(layer_norm, after_second, gain_five)
    grad_second, grad_gain_five = final_back(cotangent[0].astype(F32))
    grad_conv_rows, grad_gain_four, grad_in_two, grad_out_two = feed_back(
        grad_second, second_kept, ffn2_in, ffn2_out
    )
    grad_branch = grad_conv_rows.astype(BF16)
    grad_point_two = dg(swish_low, grad_branch, 0, 0)
    grad_norm_out = swish_back(dg(grad_branch, w_point2, 1, 1))[0]
    sums = jnp.stack([jnp.sum(grad_norm_out, axis=0), jnp.sum(grad_norm_out * normed, axis=0)])
    every = gather_all(jnp.concatenate([sums, jnp.zeros((6, width), F32)]), sp, dp, 3)
    grad_norm_bias, grad_norm_gain = jnp.sum(every[:, 0], axis=0), jnp.sum(every[:, 1], axis=0)
    grad_variance = -0.5 * inv_std * inv_std * norm_gain * grad_norm_gain
    grad_mean = -inv_std * norm_gain * grad_norm_bias
    grad_conv = (
        grad_norm_out * norm_gain * inv_std
        + valid_rows * (2.0 * centered * grad_variance + grad_mean) / frame_count
    )
    rim_grad = with_halo(grad_conv.astype(BF16), reach).astype(F32)
    grad_gated = jnp.zeros((frames, width), F32)
    for tap in range(taps):
        mirror = 2 * reach - tap
        grad_gated = (
            grad_gated + kernel[tap][None, :] * rim_grad[mirror : mirror + frames] * tap_masks[mirror]
        )
    grad_kernel = jnp.stack(
        [jnp.sum(grad_conv * rim_gated[j : j + frames] * tap_masks[j], axis=0) for j in range(taps)]
    )
    grad_point_out = gated_back(grad_gated)[0].astype(BF16)
    grad_point_one = dg(conv_low, grad_point_out, 0, 0)
    grad_conv_input, grad_gain_three = conv_norm_back(dg(grad_point_out, w_point1, 1, 1))
    grad_attn_rows = grad_conv_rows + grad_conv_input
    grad_attn_out = grad_attn_rows.astype(BF16)
    grad_out_weight = dg(context, grad_attn_out, 1, 0)
    grad_context = dg(w_out, grad_attn_out, 1, 1).astype(BF16).reshape(sp, head_dim, frames)
    grad_heads = attend_back(heads, lengths, raw_context, log_sums, exchange(grad_context, 4))
    grad_parts = exchange(grad_heads, 5).reshape(HEADS, 3, 2, half, frames).astype(F32)
    sine, cosine = trig[:half], trig[half:]
    first, second = grad_parts[:, :2, 0], grad_parts[:, :2, 1]
    turned = jnp.stack([first * cosine + second * sine, second * cosine - first * sine], axis=2)
    grad_joined = jnp.concatenate([turned, grad_parts[:, 2:]], axis=1).astype(BF16)
    grad_joined = grad_joined.reshape(3 * width, frames)
    grad_qkv = dg(grad_joined, attn_low, 1, 0).reshape(HEADS, 3, head_dim, width)
    grad_qkv = grad_qkv.transpose(1, 0, 2, 3).reshape(3 * width, width).T
    _, attn_norm_back = jax.vjp(layer_norm, after_first, gain_two)
    grad_attn_input, grad_gain_two = attn_norm_back(dg(grad_joined, qkv_rows, 0, 0))
    _, first_kept = feed_forward(tokens[0].astype(F32), gain_one, ffn1_in, ffn1_out)
    grad_start, grad_gain_one, grad_in_one, grad_out_one = feed_back(
        grad_attn_rows + grad_attn_input, first_kept, ffn1_in, ffn1_out
    )
    summed = lax.psum(
        (
            grad_gain_one, grad_in_one, grad_out_one, grad_gain_two, grad_qkv, grad_out_weight,
            grad_gain_three, grad_point_one, grad_kernel, grad_norm_gain, grad_norm_bias,
            grad_point_two, grad_gain_four, grad_in_two, grad_out_two, grad_gain_five,
        )[:9] + (
            grad_point_two, grad_gain_four, grad_in_two, grad_out_two, grad_gain_five,
        ),
        ("dp", "sp"),
    )
    return (
        (output[None].astype(BF16), grad_start[None].astype(BF16))
        + summed[:9] + (grad_norm_gain, grad_norm_bias) + summed[9:]
    )


def solution(mesh):
    split = P("dp", "sp", None)
    return jax.shard_map(
        on_device,
        mesh=mesh,
        in_specs=(split,) + (P(),) * 16 + (P("dp", None), split),
        out_specs=(split, split) + (P(),) * 16,
        check_vma=False,
    )
```

```python
import functools

import jax
import jax.numpy as jnp
import numpy as np
from jax import lax
from jax.experimental import pallas as pl
from jax.experimental.pallas import tpu as pltpu
from jax.sharding import PartitionSpec as P

HEADS = 4
EPS = 1e-05
NEG = -1e30
LN2 = float(np.log(2.0))
F32 = jnp.float32
BF16 = jnp.bfloat16
I32 = jnp.int32
MESH = pl.DeviceIdType.MESH
VMEM = pl.BlockSpec(memory_space=pltpu.VMEM)
SMEM = pl.BlockSpec(memory_space=pltpu.SMEM)
DMA = pltpu.SemaphoreType.DMA
VMEM_LIMIT = 56 * 2**20


def dg(left, right, left_dim, right_dim):
    return lax.dot_general(
        left, right, (((left_dim,), (right_dim,)), ((), ())), preferred_element_type=F32
    )


def rows_at(index, count):
    return pl.ds(pl.multiple_of(index * count, count), count)


def greet(devices):
    barrier = pltpu.get_barrier_semaphore()
    for device in devices:
        pl.semaphore_signal(barrier, inc=1, device_id=device, device_id_type=MESH)
    pl.semaphore_wait(barrier, len(devices))


def sp_peers(count):
    dp, sp = lax.axis_index("dp"), lax.axis_index("sp")
    return [(dp, lax.rem(sp + step, count)) for step in range(1, count)]


def ends_of(len_ref, items):
    ends, total = [], 0
    for item in range(items):
        total = total + len_ref[0, item]
        ends.append(total)
    return ends


def segment_row(first, count, ends):
    frame = first + lax.broadcasted_iota(I32, (1, count), 1)
    segment = jnp.zeros((1, count), I32)
    for end in ends:
        segment = segment + (frame >= end).astype(I32)
    return segment


def position_row(first, count, ends):
    frame = first + lax.broadcasted_iota(I32, (1, count), 1)
    start = jnp.zeros((1, count), I32)
    for end in ends:
        start = jnp.where(frame >= end, end, start)
    return (frame - start).astype(F32)


def block_bounds(first, count, ends, length):
    low, high = 0, length
    for end in ends:
        low = jnp.where(first >= end, end, low)
    for end in reversed(ends):
        high = jnp.where(first + count - 1 < end, end, high)
    return low, high


def onehot_rows(segment, items, other, same):
    row = lax.broadcasted_iota(I32, (16, segment.shape[1]), 0)
    return jnp.where(row <= items, jnp.where(row == segment, same, other), 0.0)


def norm_parts(rows):
    centre = rows - jnp.mean(rows, axis=-1, keepdims=True)
    inv = lax.rsqrt(jnp.mean(centre * centre, axis=-1, keepdims=True) + EPS)
    return centre * inv, inv


def norm_back(grad, hat, inv, gain):
    scaled = grad * gain
    first = jnp.mean(scaled, axis=-1, keepdims=True)
    second = jnp.mean(scaled * hat, axis=-1, keepdims=True)
    return inv * (scaled - first - hat * second)


def sigmoid(x):
    return 1.0 / (1.0 + jnp.exp(-x))


def sine_cosine(position, freq_hi, freq_lo):
    turns = position * freq_hi
    turns = turns - jnp.round(turns) + position * freq_lo
    turns = turns - jnp.round(turns)
    x = turns * float(np.pi)
    x2 = x * x
    s = x * (1 + x2 * (-1 / 6 + x2 * (1 / 120 + x2 * (-1 / 5040 + x2 * (1 / 362880 - x2 / 39916800)))))
    c = 1 + x2 * (-1 / 2 + x2 * (1 / 24 + x2 * (-1 / 720 + x2 * (1 / 40320 + x2 * (-1 / 3628800 + x2 / 479001600)))))
    return 2 * s * c, 1 - 2 * s * s


def front_kernel(
    sp, items, chunk, len_ref, tok, gain1, w_in, w_out, gain2, w_qkv, freq,
    x1_ref, n2_ref, trig, heads, parts, send, recv, local,
):
    me = lax.axis_index("sp")
    frames = tok.shape[0]
    width = heads.shape[1]
    half = trig.shape[0] // 2
    peers = sp_peers(sp)
    greet(peers)
    ends = ends_of(len_ref, items)
    scale = float(np.log2(np.e)) * (2 * half) ** -0.5

    def copies(c):
        cols = rows_at(c, chunk)
        out = [
            pltpu.make_async_remote_copy(
                src_ref=parts.at[peer[1], :, cols],
                dst_ref=heads.at[me, :, cols],
                send_sem=send.at[i, c],
                recv_sem=recv.at[i, c],
                device_id=peer,
                device_id_type=MESH,
            )
            for i, peer in enumerate(peers)
        ]
        own = pltpu.make_async_copy(parts.at[me, :, cols], heads.at[me, :, cols], local.at[c])
        return out, own

    def step(c, carry):
        rows = rows_at(c, chunk)
        x = tok[rows, :].astype(F32)
        hat, _ = norm_parts(x)
        n1 = (hat * gain1[...].astype(F32)).astype(BF16)
        a = dg(n1, w_in[...], 1, 0)
        s = (a * sigmoid(a)).astype(BF16)
        x1 = x + 0.5 * dg(s, w_out[...], 1, 0)
        x1_ref[rows, :] = x1
        hat, _ = norm_parts(x1)
        n2 = (hat * gain2[...].astype(F32)).astype(BF16)
        n2_ref[rows, :] = n2
        joined = dg(w_qkv[...], n2, 1, 1)
        sine, cosine = sine_cosine(
            position_row(me * frames + c * chunk, chunk, ends), freq[:, 0:1], freq[:, 1:2]
        )
        trig[0:half, rows] = sine
        trig[half:, rows] = cosine
        for head in range(sp):
            base = head * width
            for part, factor in ((0, scale), (1, 1.0)):
                low = base + part * 2 * half
                first, second = joined[low : low + half], joined[low + half : low + 2 * half]
                parts[head, part * 2 * half : part * 2 * half + half, rows] = (
                    (first * cosine - second * sine) * factor
                ).astype(BF16)
                parts[head, part * 2 * half + half : (part + 1) * 2 * half, rows] = (
                    (first * sine + second * cosine) * factor
                ).astype(BF16)
            parts[head, 4 * half : 6 * half, rows] = joined[base + 4 * half : base + 6 * half].astype(BF16)
        out, own = copies(c)
        for copy in out:
            copy.start()
        own.start()
        return carry

    lax.fori_loop(0, frames // chunk, step, 0)

    def finish(c, carry):
        out, own = copies(c)
        for copy in out:
            copy.wait()
        own.wait()
        return carry

    lax.fori_loop(0, frames // chunk, finish, 0)


def front(lengths, tok, gain1, w_in, w_out, gain2, w_qkv, freq, sp):
    frames, width = tok.shape
    chunk = min(256, frames)
    count = frames // chunk
    head_width = w_qkv.shape[0] // sp
    half = freq.shape[0]
    return pl.pallas_call(
        functools.partial(front_kernel, sp, lengths.shape[1], chunk),
        out_shape=[
            jax.ShapeDtypeStruct((frames, width), F32),
            jax.ShapeDtypeStruct((frames, width), BF16),
            jax.ShapeDtypeStruct((2 * half, frames), F32),
            jax.ShapeDtypeStruct((sp, head_width, frames), BF16),
        ],
        in_specs=[SMEM] + [VMEM] * 7,
        out_specs=[VMEM] * 4,
        scratch_shapes=[
            pltpu.VMEM((sp, head_width, frames), BF16),
            DMA((sp - 1, count)),
            DMA((sp - 1, count)),
            DMA((count,)),
        ],
        compiler_params=pltpu.CompilerParams(
            collective_id=0, has_side_effects=True, vmem_limit_bytes=VMEM_LIMIT
        ),
        name="front",
    )(lengths, tok, gain1, w_in, w_out, gain2, w_qkv, freq)


def fwd_kernel(items,bq,bk,nsub,len_ref,x_ref,ctx_ref,o_ref,lse_ref,qa,ka,va):
    srcs,rows,fr=x_ref.shape; hd=rows//3; L=srcs*fr
    ends=ends_of(len_ref,items)
    for s in range(srcs):
        cols=pl.ds(s*fr,fr)
        seg=segment_row(s*fr,fr,ends)
        qa[0:hd,cols]=x_ref[s,0:hd,:]
        qa[hd:hd+16,cols]=onehot_rows(seg,items,0.0,1.0).astype(BF16)
        qa[hd+16:2*hd,cols]=jnp.zeros((hd-16,fr),BF16)
        kT=jnp.concatenate([x_ref[s,hd:2*hd,:],onehot_rows(seg,items,NEG,0.0).astype(BF16),jnp.zeros((hd-16,fr),BF16)],axis=0)
        ka[cols,:]=kT.T
        va[0:hd,cols]=x_ref[s,2*hd:3*hd,:]
        one=lax.broadcasted_iota(I32,(16,fr),0)==0
        va[hd:hd+16,cols]=jnp.where(one,1.0,0.0).astype(BF16)
    per=fr//bq
    def qbody(i,c):
        q0=i*bq
        q=qa[:,pl.ds(pl.multiple_of(q0,bq),bq)]
        lo,hi=block_bounds(q0,bq,ends,L)
        def kbody(j,car):
            m,acc=car
            w=bk//nsub
            ks=[pl.ds(pl.multiple_of(j*bk+u*w,w),w) for u in range(nsub)]
            ss=[dg(ka[k,:],q,1,0) for k in ks]
            mn=m
            for s in ss: mn=jnp.maximum(mn,jnp.max(s,axis=0,keepdims=True))
            acc=acc*jnp.exp2(m-mn)
            for s,k in zip(ss,ks):
                p=jnp.exp2(s-mn).astype(BF16)
                acc=acc+dg(va[:,k],p,1,0)
            return mn,acc
        m,acc=lax.fori_loop(lo//bk,(hi+bk-1)//bk,kbody,(jnp.full((1,bq),NEG,F32),jnp.zeros((hd+16,bq),F32)))
        l=acc[hd:hd+1,:]
        o=acc[0:hd,:]/l
        d=i//per; qc=pl.ds(pl.multiple_of((i%per)*bq,bq),bq)
        ctx_ref[d,:,qc]=o.astype(BF16)
        o_ref[d,:,qc]=o
        lse_ref[:,pl.ds(pl.multiple_of(q0,bq),bq)]=m+jnp.log2(l)
        return c
    lax.fori_loop(0,L//bq,qbody,0)
def attend(x,lengths,bq=1024,bk=1024,nsub=4):
    srcs,rows,fr=x.shape; hd=rows//3; L=srcs*fr
    return pl.pallas_call(functools.partial(fwd_kernel,lengths.shape[1],min(bq,fr),min(bk,fr),nsub),
      out_shape=[jax.ShapeDtypeStruct((srcs,hd,fr),BF16),jax.ShapeDtypeStruct((srcs,hd,fr),F32),jax.ShapeDtypeStruct((1,L),F32)],
      in_specs=[SMEM,VMEM],out_specs=[VMEM]*3,
      scratch_shapes=[pltpu.VMEM((2*hd,L),BF16),pltpu.VMEM((L,2*hd),BF16),pltpu.VMEM((hd+16,L),BF16)],
      compiler_params=pltpu.CompilerParams(vmem_limit_bytes=VMEM_LIMIT),name="attend")(lengths,x)

def split3(v):
    a=v.astype(BF16); r=v-a.astype(F32); b=r.astype(BF16); c=(r-b.astype(F32)).astype(BF16)
    return a,b,c
def bwd_kernel(items,bq,bk,len_ref,x_ref,o_ref,lse_ref,do_ref,g_ref,qa,ka,da,va,dq,dk,dv):
    srcs,rows,fr=x_ref.shape; hd=rows//3; L=srcs*fr
    ends=ends_of(len_ref,items)
    row16=lax.broadcasted_iota(I32,(16,fr),0)
    pad=jnp.zeros((hd-32,fr),BF16)
    def stack3(v):
        a,b,c=[u.astype(F32) for u in split3(v)]
        return jnp.where(row16==0,a,jnp.where(row16==1,b,jnp.where(row16==2,c,0.0))).astype(BF16)
    ones3=jnp.where(row16<3,1.0,0.0).astype(BF16)
    for s in range(srcs):
        cols=pl.ds(s*fr,fr)
        seg=segment_row(s*fr,fr,ends)
        qT=jnp.concatenate([x_ref[s,0:hd,:],onehot_rows(seg,items,0.0,1.0).astype(BF16),stack3(-lse_ref[:,cols]),pad],axis=0)
        qa[cols,:]=qT.T
        ka[0:hd,cols]=x_ref[s,hd:2*hd,:]
        ka[hd:hd+16,cols]=onehot_rows(seg,items,NEG,0.0).astype(BF16)
        ka[hd+16:hd+32,cols]=ones3
        ka[hd+32:2*hd,cols]=pad
        do=do_ref[s]
        D=jnp.sum(do.astype(F32)*o_ref[s],axis=0,keepdims=True)
        dT=jnp.concatenate([do,stack3(-D),pad,jnp.zeros((16,fr),BF16)],axis=0)
        da[cols,:]=dT.T
        va[0:hd,cols]=x_ref[s,2*hd:3*hd,:]
        va[hd:hd+16,cols]=ones3
        va[hd+16:2*hd,cols]=jnp.zeros((hd-16,fr),BF16)
    dq[...]=jnp.zeros_like(dq)
    per=fr//bk; perq=fr//bq
    def kbody(j,c):
        k0=j*bk
        ks=pl.ds(pl.multiple_of(k0,bk),bk)
        lo,hi=block_bounds(k0,bk,ends,L)
        d=j//per; kc=pl.ds(pl.multiple_of((j%per)*bk,bk),bk)
        dk[...]=jnp.zeros_like(dk); dv[...]=jnp.zeros_like(dv)
        def qbody(i,car):
            qs=pl.ds(pl.multiple_of(i*bq,bq),bq)
            e=i//perq; qc=pl.ds(pl.multiple_of((i%perq)*bq,bq),bq)
            p=jnp.exp2(dg(qa[qs,:],ka[:,ks],1,0))
            dp=dg(da[qs,:],va[:,ks],1,0)
            ds=(p*dp).astype(BF16)
            pb=p.astype(BF16)
            dv[...]+=dg(do_ref[e,:,qc],pb,1,0)
            dk[...]+=dg(x_ref[e,0:hd,qc],ds,1,0)
            dq[:,qs]+=dg(ka[0:hd,ks],ds,1,1)
            return car
        lax.fori_loop(lo//bq,(hi+bq-1)//bq,qbody,0)
        g_ref[d,hd:2*hd,kc]=(dk[...]*float(np.log(2.0))).astype(BF16)
        g_ref[d,2*hd:3*hd,kc]=dv[...].astype(BF16)
        return c
    lax.fori_loop(0,L//bk,kbody,0)
    for s in range(srcs):
        g_ref[s,0:hd,:]=(dq[:,pl.ds(s*fr,fr)]*(hd**-0.5)).astype(BF16)
def attend_back(x,lengths,o,lse,do,bq=1024,bk=1024):
    srcs,rows,fr=x.shape; hd=rows//3; L=srcs*fr
    bq=min(bq,fr); bk=min(bk,fr)
    return pl.pallas_call(functools.partial(bwd_kernel,lengths.shape[1],bq,bk),
      out_shape=jax.ShapeDtypeStruct(x.shape,BF16),
      in_specs=[SMEM]+[VMEM]*4,out_specs=VMEM,
      scratch_shapes=[pltpu.VMEM((L,2*hd),BF16),pltpu.VMEM((2*hd,L),BF16),pltpu.VMEM((L,2*hd),BF16),pltpu.VMEM((2*hd,L),BF16),
        pltpu.VMEM((hd,L),F32),pltpu.VMEM((hd,bk),F32),pltpu.VMEM((hd,bk),F32)],
      compiler_params=pltpu.CompilerParams(vmem_limit_bytes=VMEM_LIMIT),name="attend_back")(lengths,x,o,lse,do)


def axis_bits():
    bits = []
    for axis in ("sp", "dp"):
        step = 1
        while step < lax.axis_size(axis):
            bits.append((axis, step))
            step *= 2
        assert step == lax.axis_size(axis)
    return bits


def swap_partner(axis, step):
    place = {name: lax.axis_index(name) for name in ("dp", "sp")}
    bit = lax.rem(place[axis] // step, 2)
    place[axis] = place[axis] + step - 2 * step * bit
    return (place["dp"], place["sp"]), bit


def orders(bits):
    sp_bits = [b for b in bits if b[0] == "sp"]
    dp_bits = [b for b in bits if b[0] == "dp"]
    first, far = sp_bits[:1], sp_bits[1:]
    return {
        "x_first": first + dp_bits[:1] + far + dp_bits[1:],
        "y_first": first + far + dp_bits,
        "y_last": first + dp_bits + far,
        "z_first": first + dp_bits[1:] + dp_bits[:1] + far,
        "z_mid": first + far + dp_bits[1:] + dp_bits[:1],
    }


def exchange_plan(rows, steps, offset):
    sizes, size = [], rows
    for _ in range(steps):
        halves = size % 32 == 0
        size = size // 2 if halves else size
        sizes.append((halves, size, offset))
        offset += size
    return sizes, offset, size


class Reduction:
    def __init__(self, base, rows, staged, order, acc, stage, land, full, send, recv, source=None):
        self.base, self.rows, self.order = base, rows, order
        self.acc, self.stage, self.land, self.full = acc, stage, land, full
        self.send, self.recv = send, recv
        self.source = acc if source is None else source
        self.low = base
        self.sizes, _, self.own = exchange_plan(rows, len(order), staged)

    def at(self, low, size):
        return pl.ds(pl.multiple_of(low, 16), size)

    def copy(self, step, src, dst):
        partner, _ = swap_partner(*self.order[step[1]])
        index = step[0] * len(self.order) + step[1]
        return pltpu.make_async_remote_copy(
            src_ref=src,
            dst_ref=dst,
            send_sem=self.send.at[index],
            recv_sem=self.recv.at[index],
            device_id=partner,
            device_id_type=MESH,
        )

    def sum_copy(self, k):
        _, moved, offset = self.sizes[k]
        where = pl.ds(offset, moved)
        return self.copy((0, k), self.stage.at[where, :], self.land.at[where, :])

    def sum_send(self, k):
        halves, moved, offset = self.sizes[k]
        _, bit = swap_partner(*self.order[k])
        away = self.low + (1 - bit) * moved if halves else self.low
        source = self.source if k == 0 else self.acc
        self.stage[offset : offset + moved, :] = source[self.at(away, moved), :].astype(BF16)
        self.sum_copy(k).start()

    def sum_recv(self, k):
        halves, moved, offset = self.sizes[k]
        _, bit = swap_partner(*self.order[k])
        self.sum_copy(k).wait()
        other = self.land[offset : offset + moved, :].astype(F32)
        if halves:
            self.low = self.low + bit * moved
            source = self.source if k == 0 else self.acc
            mine = source[self.at(self.low, moved), :]
        else:
            mine = self.stage[offset : offset + moved, :].astype(F32)
        self.acc[self.at(self.low, moved), :] = mine + other

    def close(self):
        where = self.at(self.low, self.own)
        self.full[where, :] = self.acc[where, :].astype(BF16)

    def share_copy(self, k):
        where = self.at(self.low, self.sizes[k][1])
        return self.copy((1, k), self.full.at[where, :], self.full.at[where, :])

    def share_send(self, k):
        if self.sizes[k][0]:
            self.share_copy(k).start()

    def share_recv(self, k):
        halves, moved, _ = self.sizes[k]
        if halves:
            self.share_copy(k).wait()
            _, bit = swap_partner(*self.order[k])
            self.low = self.low - bit * moved


def run_sum(streams, steps):
    for k in steps:
        for stream in streams:
            if k > 0:
                stream.sum_recv(k - 1)
            stream.sum_send(k)


def run_share(streams, count):
    for stream in streams:
        stream.sum_recv(count - 1)
        stream.close()
        stream.share_send(count - 1)
    for k in reversed(range(count)):
        for stream in streams:
            stream.share_recv(k)
            if k > 0:
                stream.share_send(k - 1)


def back_kernel(
    sp, chunk, parts, trig, tok, x1_ref, n2_ref, grad_x2, gain1, gain2, w_in, w_out, w_qkv, mid, small,
    grad_ref, full, heads, joined, n1_keep, branch, act, hidden, gains, acc, stage, land,
    send, recv, local, sum_send, sum_recv,
):
    me = lax.axis_index("sp")
    frames, width = tok.shape
    wide = w_in.shape[1]
    head_width = parts.shape[1]
    half = trig.shape[0] // 2
    count = frames // chunk
    peers = sp_peers(sp)
    bits = axis_bits()
    partners = [swap_partner(*bit)[0] for bit in bits if bit[0] == "dp"]
    greet(peers + partners)

    def copies(c):
        cols = rows_at(c, chunk)
        out = [
            pltpu.make_async_remote_copy(
                src_ref=parts.at[peer[1], :, cols],
                dst_ref=heads.at[me, :, cols],
                send_sem=send.at[i, c],
                recv_sem=recv.at[i, c],
                device_id=peer,
                device_id_type=MESH,
            )
            for i, peer in enumerate(peers)
        ]
        return out, pltpu.make_async_copy(parts.at[me, :, cols], heads.at[me, :, cols], local.at[c])

    def begin(c, carry):
        out, own = copies(c)
        for copy in out:
            copy.start()
        own.start()
        return carry

    lax.fori_loop(0, count, begin, 0)

    order = orders(bits)
    unit = 4 * width
    plan = [
        (0, 2 * unit, "y_last", mid),
        (2 * unit, unit, "z_first", mid),
        (3 * unit, unit, "z_first", None),
        (4 * unit, unit, "x_first", None),
        (5 * unit, unit, "y_first", None),
    ]
    steps = len(bits)
    streams, staged = [], 0
    for i, (base, rows, name, source) in enumerate(plan):
        streams.append(
            Reduction(
                base, rows, staged, order[name], acc, stage, land, full, sum_send.at[i], sum_recv.at[i], source
            )
        )
        staged = exchange_plan(rows, steps, staged)[1]
    run_sum(streams[:2], range(steps))
    gains[...] = jnp.zeros_like(gains)

    def step(c, carry):
        rows = rows_at(c, chunk)
        out, own = copies(c)
        for copy in out:
            copy.wait()
        own.wait()
        sine, cosine = trig[0:half, rows], trig[half:, rows]
        for head in range(sp):
            base = head * head_width
            for part in range(2):
                low = part * 2 * half
                first = heads[head, low : low + half, rows].astype(F32)
                second = heads[head, low + half : low + 2 * half, rows].astype(F32)
                low = base + low
                joined[low : low + half, rows] = (first * cosine + second * sine).astype(BF16)
                joined[low + half : low + 2 * half, rows] = (second * cosine - first * sine).astype(BF16)
            joined[base + 4 * half : base + 6 * half, rows] = heads[head, 4 * half : 6 * half, rows]
        grad = dg(joined[:, rows], w_qkv[...], 0, 0)
        hat, inv = norm_parts(x1_ref[rows, :])
        gains[1:2, :] += jnp.sum(grad * hat, axis=0, keepdims=True)
        grad_x1 = grad_x2[rows, :] + norm_back(grad, hat, inv, gain2[...].astype(F32))
        low_grad = (0.5 * grad_x1).astype(BF16)
        branch[rows, :] = low_grad
        hat, inv = norm_parts(tok[rows, :].astype(F32))
        gain = gain1[...].astype(F32)
        n1 = (hat * gain).astype(BF16)
        n1_keep[rows, :] = n1
        a = dg(n1, w_in[...], 1, 0)
        sig = sigmoid(a)
        act[rows, :] = (a * sig).astype(BF16)
        grad = dg(low_grad, w_out[...], 1, 1)
        low_hidden = (grad * (sig * (1.0 + a * (1.0 - sig)))).astype(BF16)
        hidden[rows, :] = low_hidden
        grad = dg(low_hidden, w_in[...], 1, 1)
        gains[0:1, :] += jnp.sum(grad * hat, axis=0, keepdims=True)
        grad_ref[rows, :] = (grad_x1 + norm_back(grad, hat, inv, gain)).astype(BF16)
        return carry

    lax.fori_loop(0, count, step, 0)
    run_share(streams[:2], steps)
    base = 3 * unit
    acc[base : base + 3 * width, :] = dg(joined[...], n2_ref[...], 1, 0)
    base = base + 3 * width
    acc[base : base + 8, :] = small[0:8, :] + gains[...]
    acc[base + 8 : base + 64, :] = small[8:64, :]
    acc[base + 64 : 4 * unit, :] = jnp.zeros((width - 64, width), F32)
    streams[2].sum_send(0)
    for j in range(wide // width):
        base = 4 * unit + j * width
        acc[base : base + width, :] = dg(act[:, j * width : (j + 1) * width], branch[...], 0, 0)
    streams[3].sum_send(0)
    for j in range(wide // width):
        base = 5 * unit + j * width
        acc[base : base + width, :] = dg(n1_keep[...], hidden[:, j * width : (j + 1) * width], 0, 0)
    streams[4].sum_send(0)
    run_sum(streams[2:], range(1, steps))
    run_share(streams[2:], steps)


def back(parts, trig, tok, x1, n2, grad_x2, gain1, gain2, w_in, w_out, w_qkv, mid, small):
    frames, width = tok.shape
    sp = parts.shape[0]
    chunk = min(256, frames)
    count = frames // chunk
    wide = w_in.shape[1]
    rows = 6 * 4 * width
    steps = len(axis_bits())
    staged = exchange_plan(8 * width, steps, 0)[1] + 4 * exchange_plan(4 * width, steps, 0)[1]
    return pl.pallas_call(
        functools.partial(back_kernel, sp, chunk),
        out_shape=[
            jax.ShapeDtypeStruct((frames, width), BF16),
            jax.ShapeDtypeStruct((rows, width), BF16),
        ],
        in_specs=[pl.BlockSpec(memory_space=pl.ANY)] + [VMEM] * 12,
        out_specs=[VMEM] * 2,
        scratch_shapes=[
            pltpu.VMEM(parts.shape, BF16),
            pltpu.VMEM((3 * width, frames), BF16),
            pltpu.VMEM((frames, width), BF16),
            pltpu.VMEM((frames, width), BF16),
            pltpu.VMEM((frames, wide), BF16),
            pltpu.VMEM((frames, wide), BF16),
            pltpu.VMEM((8, width), F32),
            pltpu.VMEM((rows, width), F32),
            pltpu.VMEM((staged, width), BF16),
            pltpu.VMEM((staged, width), BF16),
            DMA((sp - 1, count)),
            DMA((sp - 1, count)),
            DMA((count,)),
            DMA((5, 2 * steps)),
            DMA((5, 2 * steps)),
        ],
        compiler_params=pltpu.CompilerParams(
            collective_id=6, has_side_effects=True, vmem_limit_bytes=VMEM_LIMIT
        ),
        name="back",
    )(parts, trig, tok, x1, n2, grad_x2, gain1, gain2, w_in, w_out, w_qkv, mid, small)


def unpack_kernel(full, in_two, out_two, point_one, point_two, out_weight, qkv, in_one, out_one, small):
    width = full.shape[1]

    def block(base):
        return full[base : base + width, :].astype(F32)

    unit = 4 * width
    for j in range(4):
        cols = slice(j * width, (j + 1) * width)
        in_two[:, cols] = block(j * width)
        out_two[cols, :] = block(unit + j * width)
        out_one[cols, :] = block(4 * unit + j * width)
        in_one[:, cols] = block(5 * unit + j * width)
    base = 2 * unit
    for j in range(2):
        point_one[:, j * width : (j + 1) * width] = block(base + j * width)
    point_two[...] = block(base + 2 * width)
    out_weight[...] = block(base + 3 * width)
    base = 3 * unit
    head_dim = width // HEADS
    for part in range(3):
        rows = [
            full[base + (3 * head + part) * head_dim : base + (3 * head + part + 1) * head_dim, :]
            for head in range(HEADS)
        ]
        qkv[:, part * width : (part + 1) * width] = jnp.concatenate(rows, axis=0).astype(F32).T
    small[...] = full[base + 3 * width : base + 3 * width + 64, :].astype(F32)


def unpack(full):
    width = full.shape[1]
    shapes = [
        (width, 4 * width), (4 * width, width), (width, 2 * width), (width, width), (width, width),
        (width, 3 * width), (width, 4 * width), (4 * width, width), (64, width),
    ]
    return pl.pallas_call(
        unpack_kernel,
        out_shape=[jax.ShapeDtypeStruct(shape, F32) for shape in shapes],
        in_specs=[VMEM],
        out_specs=[VMEM] * len(shapes),
        compiler_params=pltpu.CompilerParams(vmem_limit_bytes=VMEM_LIMIT),
        name="unpack",
    )(full)


def exchange_kernel(sp, parts, heads, send, recv, local):
    me = lax.axis_index("sp")
    peers = sp_peers(sp)
    greet(peers)
    copies = [
        pltpu.make_async_remote_copy(
            src_ref=parts.at[peer[1]],
            dst_ref=heads.at[me],
            send_sem=send.at[i],
            recv_sem=recv.at[i],
            device_id=peer,
            device_id_type=MESH,
        )
        for i, peer in enumerate(peers)
    ]
    for copy in copies:
        copy.start()
    own = pltpu.make_async_copy(parts.at[me], heads.at[me], local)
    own.start()
    own.wait()
    for copy in copies:
        copy.wait()


def exchange(parts, call):
    sp = parts.shape[0]
    anywhere = pl.BlockSpec(memory_space=pl.ANY)
    return pl.pallas_call(
        functools.partial(exchange_kernel, sp),
        out_shape=jax.ShapeDtypeStruct(parts.shape, parts.dtype),
        in_specs=[anywhere],
        out_specs=anywhere,
        scratch_shapes=[DMA((sp - 1,)), DMA((sp - 1,)), DMA],
        compiler_params=pltpu.CompilerParams(collective_id=call, has_side_effects=True),
        name="exchange",
    )(parts)


def gather_kernel(sp, dp, x_ref, all_ref, send, recv):
    me_d, me_s = lax.axis_index("dp"), lax.axis_index("sp")
    total = sp * dp
    me = me_d * sp + me_s
    peers = []
    for step in range(1, total):
        peer = lax.rem(me + step, total)
        peers.append((peer // sp, lax.rem(peer, sp)))
    greet(peers)
    copies = [
        pltpu.make_async_remote_copy(
            src_ref=x_ref,
            dst_ref=all_ref.at[i + 1],
            send_sem=send.at[i],
            recv_sem=recv.at[i],
            device_id=peer,
            device_id_type=MESH,
        )
        for i, peer in enumerate(peers)
    ]
    for copy in copies:
        copy.start()
    all_ref[0] = x_ref[...]
    for copy in copies:
        copy.wait()


def gather_all(x, sp, dp, call):
    total = sp * dp
    return pl.pallas_call(
        functools.partial(gather_kernel, sp, dp),
        out_shape=jax.ShapeDtypeStruct((total,) + x.shape, x.dtype),
        in_specs=[VMEM],
        out_specs=VMEM,
        scratch_shapes=[DMA((total - 1,)), DMA((total - 1,))],
        compiler_params=pltpu.CompilerParams(collective_id=call, has_side_effects=True),
        name="gather_all",
    )(x)


def with_halo(block, width):
    count = lax.axis_size("sp")
    forward = [(i, i + 1) for i in range(count - 1)]
    backward = [(target, source) for source, target in forward]
    low = lax.ppermute(block[-width:], "sp", forward)
    high = lax.ppermute(block[:width], "sp", backward)
    return jnp.concatenate([low, block, high], axis=0)


def layer_norm(rows, gain):
    centre = rows - jnp.mean(rows, axis=-1, keepdims=True)
    spread = jnp.mean(centre * centre, axis=-1, keepdims=True)
    return centre * lax.rsqrt(spread + EPS) * gain


def segment_of(index, item_ends):
    return jnp.sum((index[:, None] >= item_ends[None, :]).astype(jnp.int32), axis=1)


def gated_unit(joined):
    half = joined.shape[1] // 2
    return joined[:, :half] * jax.nn.sigmoid(joined[:, half:])


def feed_forward(rows, gain, w_in, w_out):
    normed, back = jax.vjp(layer_norm, rows, gain)
    normed_low = normed.astype(BF16)
    hidden = dg(normed_low, w_in, 1, 0)
    activated, act_back = jax.vjp(jax.nn.silu, hidden)
    act_low = activated.astype(BF16)
    return rows + 0.5 * dg(act_low, w_out, 1, 0), (back, normed_low, act_low, act_back)


def feed_back(grad_rows, kept, w_in, w_out):
    back, normed_low, act_low, act_back = kept
    grad_branch = (0.5 * grad_rows).astype(BF16)
    grad_w_out = dg(act_low, grad_branch, 0, 0)
    grad_act = dg(grad_branch, w_out, 1, 1)
    grad_hidden = act_back(grad_act)[0].astype(BF16)
    grad_w_in = dg(normed_low, grad_hidden, 0, 0)
    grad_normed = dg(grad_hidden, w_in, 1, 1)
    grad_input, grad_gain = back(grad_normed)
    return grad_rows + grad_input, grad_gain, grad_w_in, grad_w_out


def on_device(
    tokens, ln1_gain, ffn1_in, ffn1_out, ln2_gain, w_qkv, w_out, ln3_gain, w_point1, depthwise,
    bn_gain, bn_bias, w_point2, ln4_gain, ffn2_in, ffn2_out, ln5_gain, lengths, cotangent,
):
    frames, width = tokens.shape[1:]
    sp, dp = lax.axis_size("sp"), lax.axis_size("dp")
    assert HEADS == sp
    head_dim = width // HEADS
    half = head_dim // 2
    items = lengths.shape[1]
    taps = depthwise.shape[0]
    reach = taps // 2
    offset = lax.axis_index("sp") * frames
    item_ends = jnp.cumsum(lengths[0])
    local_segment = segment_of(offset + jnp.arange(frames, dtype=I32), item_ends)
    rim_segment = segment_of(offset - reach + jnp.arange(frames + 2 * reach, dtype=I32), item_ends)
    valid_rows = (local_segment < items).astype(F32)[:, None]
    tap_masks = [
        (rim_segment[j : j + frames] == local_segment).astype(F32)[:, None] for j in range(taps + 1)
    ]
    gain_one, gain_two, gain_three, gain_four, gain_five = (
        g.astype(F32) for g in (ln1_gain, ln2_gain, ln3_gain, ln4_gain, ln5_gain)
    )
    norm_gain, norm_bias, kernel = (g.astype(F32) for g in (bn_gain, bn_bias, depthwise))
    turns = 10000.0 ** (-np.arange(half, dtype=np.float64) / half) / (2 * np.pi)
    high = np.round(turns * 4096.0) / 4096.0
    freq = jnp.asarray(np.stack([high, turns - high], axis=1), F32)
    qkv_rows = w_qkv.T.reshape(3, HEADS, head_dim, width).transpose(1, 0, 2, 3).reshape(3 * width, width)

    after_first, attn_low, trig, heads = front(
        lengths, tokens[0], ln1_gain[None], ffn1_in, ffn1_out, ln2_gain[None], qkv_rows, freq, sp
    )
    context, raw_context, log_sums = attend(heads, lengths)
    context = exchange(context, 1).reshape(width, frames)
    after_attn = after_first + dg(context, w_out, 0, 0)
    conv_normed, conv_norm_back = jax.vjp(layer_norm, after_attn, gain_three)
    conv_low = conv_normed.astype(BF16)
    point_out = dg(conv_low, w_point1, 1, 0)
    gated_rows, gated_back = jax.vjp(gated_unit, point_out)
    rim_gated = with_halo(gated_rows.astype(BF16), reach).astype(F32)
    conv_out = jnp.zeros((frames, width), F32)
    for tap in range(taps):
        conv_out = conv_out + kernel[tap][None, :] * rim_gated[tap : tap + frames] * tap_masks[tap]
    own_count = jnp.sum(valid_rows)
    own_mean = jnp.sum(valid_rows * conv_out, axis=0) / jnp.maximum(own_count, 1.0)
    own_spread = jnp.sum(valid_rows * (conv_out - own_mean) ** 2, axis=0)
    rows = jnp.stack([own_mean, own_spread, jnp.broadcast_to(own_count, (width,))])
    every = gather_all(jnp.concatenate([rows, jnp.zeros((5, width), F32)]), sp, dp, 2)
    counts = every[:, 2]
    frame_count = jnp.sum(counts, axis=0)
    bn_mean = jnp.sum(counts * every[:, 0], axis=0) / frame_count
    variance = (
        jnp.sum(every[:, 1], axis=0) + jnp.sum(counts * (every[:, 0] - bn_mean) ** 2, axis=0)
    ) / frame_count
    centered = conv_out - bn_mean
    inv_std = lax.rsqrt(variance + EPS)
    normed = centered * inv_std
    swished, swish_back = jax.vjp(jax.nn.silu, normed * norm_gain + norm_bias)
    swish_low = swished.astype(BF16)
    after_conv = after_attn + dg(swish_low, w_point2, 1, 0)
    after_second, second_kept = feed_forward(after_conv, gain_four, ffn2_in, ffn2_out)
    output, final_back = jax.vjp(layer_norm, after_second, gain_five)
    grad_second, grad_gain_five = final_back(cotangent[0].astype(F32))
    grad_conv_rows, grad_gain_four, grad_in_two, grad_out_two = feed_back(
        grad_second, second_kept, ffn2_in, ffn2_out
    )
    grad_branch = grad_conv_rows.astype(BF16)
    grad_point_two = dg(swish_low, grad_branch, 0, 0)
    grad_norm_out = swish_back(dg(grad_branch, w_point2, 1, 1))[0]
    sums = jnp.stack([jnp.sum(grad_norm_out, axis=0), jnp.sum(grad_norm_out * normed, axis=0)])
    every = gather_all(jnp.concatenate([sums, jnp.zeros((6, width), F32)]), sp, dp, 3)
    grad_norm_bias, grad_norm_gain = jnp.sum(every[:, 0], axis=0), jnp.sum(every[:, 1], axis=0)
    grad_variance = -0.5 * inv_std * inv_std * norm_gain * grad_norm_gain
    grad_mean = -inv_std * norm_gain * grad_norm_bias
    grad_conv = (
        grad_norm_out * norm_gain * inv_std
        + valid_rows * (2.0 * centered * grad_variance + grad_mean) / frame_count
    )
    rim_grad = with_halo(grad_conv.astype(BF16), reach).astype(F32)
    grad_gated = jnp.zeros((frames, width), F32)
    for tap in range(taps):
        mirror = 2 * reach - tap
        grad_gated = (
            grad_gated + kernel[tap][None, :] * rim_grad[mirror : mirror + frames] * tap_masks[mirror]
        )
    grad_kernel = jnp.stack(
        [jnp.sum(grad_conv * rim_gated[j : j + frames] * tap_masks[j], axis=0) for j in range(taps)]
    )
    grad_point_out = gated_back(grad_gated)[0].astype(BF16)
    grad_point_one = dg(conv_low, grad_point_out, 0, 0)
    grad_conv_input, grad_gain_three = conv_norm_back(dg(grad_point_out, w_point1, 1, 1))
    grad_attn_rows = grad_conv_rows + grad_conv_input
    grad_attn_out = grad_attn_rows.astype(BF16)
    grad_out_weight = dg(context, grad_attn_out, 1, 0)
    grad_context = dg(w_out, grad_attn_out, 1, 1).astype(BF16).reshape(sp, head_dim, frames)
    grad_heads = attend_back(heads, lengths, raw_context, log_sums, exchange(grad_context, 4))
    def blocks(matrix):
        return [matrix[:, k : k + width] for k in range(0, matrix.shape[1], width)]

    mid = jnp.concatenate(
        blocks(grad_in_two) + [grad_out_two] + blocks(grad_point_one) + [grad_point_two, grad_out_weight]
    )
    zero = jnp.zeros((1, width), F32)
    small = jnp.concatenate(
        [zero, zero, grad_gain_three[None], grad_gain_four[None], grad_gain_five[None], zero, zero, zero]
        + [grad_kernel, jnp.zeros((56 - taps, width), F32)]
    )
    grad_start, full = back(
        grad_heads, trig, tokens[0], after_first, attn_low, grad_attn_rows, ln1_gain[None], ln2_gain[None],
        ffn1_in, ffn1_out, qkv_rows, mid, small,
    )
    in_two, out_two, point_one, point_two, out_weight, qkv, in_one, out_one, small = unpack(full)
    return (
        output[None].astype(BF16), grad_start[None], small[0], in_one, out_one, small[1], qkv, out_weight,
        small[2], point_one, small[8 : 8 + taps], grad_norm_gain, grad_norm_bias, point_two, small[3],
        in_two, out_two, small[4],
    )


def solution(mesh):
    split = P("dp", "sp", None)
    return jax.shard_map(
        on_device,
        mesh=mesh,
        in_specs=(split,) + (P(),) * 16 + (P("dp", None), split),
        out_specs=(split, split) + (P(),) * 16,
        check_vma=False,
    )
```

```python
import functools

import jax
import jax.numpy as jnp
import numpy as np
from jax import lax
from jax.experimental import pallas as pl
from jax.experimental.pallas import tpu as pltpu
from jax.sharding import PartitionSpec as P

HEADS = 4
EPS = 1e-05
NEG = -1e30
LN2 = float(np.log(2.0))
F32 = jnp.float32
BF16 = jnp.bfloat16
I32 = jnp.int32
MESH = pl.DeviceIdType.MESH
VMEM = pl.BlockSpec(memory_space=pltpu.VMEM)
SMEM = pl.BlockSpec(memory_space=pltpu.SMEM)
DMA = pltpu.SemaphoreType.DMA
VMEM_LIMIT = 56 * 2**20


def dg(left, right, left_dim, right_dim):
    return lax.dot_general(
        left, right, (((left_dim,), (right_dim,)), ((), ())), preferred_element_type=F32
    )


def rows_at(index, count):
    return pl.ds(pl.multiple_of(index * count, count), count)


def greet(devices):
    barrier = pltpu.get_barrier_semaphore()
    for device in devices:
        pl.semaphore_signal(barrier, inc=1, device_id=device, device_id_type=MESH)
    pl.semaphore_wait(barrier, len(devices))


def sp_peers(count):
    dp, sp = lax.axis_index("dp"), lax.axis_index("sp")
    return [(dp, lax.rem(sp + step, count)) for step in range(1, count)]


def ends_of(len_ref, items):
    ends, total = [], 0
    for item in range(items):
        total = total + len_ref[0, item]
        ends.append(total)
    return ends


def segment_row(first, count, ends):
    frame = first + lax.broadcasted_iota(I32, (1, count), 1)
    segment = jnp.zeros((1, count), I32)
    for end in ends:
        segment = segment + (frame >= end).astype(I32)
    return segment


def position_row(first, count, ends):
    frame = first + lax.broadcasted_iota(I32, (1, count), 1)
    start = jnp.zeros((1, count), I32)
    for end in ends:
        start = jnp.where(frame >= end, end, start)
    return (frame - start).astype(F32)


def block_bounds(first, count, ends, length):
    low, high = 0, length
    for end in ends:
        low = jnp.where(first >= end, end, low)
    for end in reversed(ends):
        high = jnp.where(first + count - 1 < end, end, high)
    return low, high


def onehot_rows(segment, items, other, same):
    row = lax.broadcasted_iota(I32, (16, segment.shape[1]), 0)
    return jnp.where(row <= items, jnp.where(row == segment, same, other), 0.0)


def norm_parts(rows):
    centre = rows - jnp.mean(rows, axis=-1, keepdims=True)
    inv = lax.rsqrt(jnp.mean(centre * centre, axis=-1, keepdims=True) + EPS)
    return centre * inv, inv


def norm_back(grad, hat, inv, gain):
    scaled = grad * gain
    first = jnp.mean(scaled, axis=-1, keepdims=True)
    second = jnp.mean(scaled * hat, axis=-1, keepdims=True)
    return inv * (scaled - first - hat * second)


def sigmoid(x):
    return 1.0 / (1.0 + jnp.exp(-x))


def sine_cosine(position, freq_hi, freq_lo):
    turns = position * freq_hi
    turns = turns - jnp.round(turns) + position * freq_lo
    turns = turns - jnp.round(turns)
    x = turns * float(np.pi)
    x2 = x * x
    s = x * (1 + x2 * (-1 / 6 + x2 * (1 / 120 + x2 * (-1 / 5040 + x2 * (1 / 362880 - x2 / 39916800)))))
    c = 1 + x2 * (-1 / 2 + x2 * (1 / 24 + x2 * (-1 / 720 + x2 * (1 / 40320 + x2 * (-1 / 3628800 + x2 / 479001600)))))
    return 2 * s * c, 1 - 2 * s * s


def front_kernel(
    sp, items, chunk, len_ref, tok, gain1, w_in, w_out, gain2, w_qkv, freq,
    x1_ref, n2_ref, trig, heads, parts, send, recv, local,
):
    me = lax.axis_index("sp")
    frames = tok.shape[0]
    width = heads.shape[1]
    half = trig.shape[0] // 2
    peers = sp_peers(sp)
    greet(peers)
    ends = ends_of(len_ref, items)
    scale = float(np.log2(np.e)) * (2 * half) ** -0.5

    def copies(c):
        cols = rows_at(c, chunk)
        out = [
            pltpu.make_async_remote_copy(
                src_ref=parts.at[peer[1], :, cols],
                dst_ref=heads.at[me, :, cols],
                send_sem=send.at[i, c],
                recv_sem=recv.at[i, c],
                device_id=peer,
                device_id_type=MESH,
            )
            for i, peer in enumerate(peers)
        ]
        own = pltpu.make_async_copy(parts.at[me, :, cols], heads.at[me, :, cols], local.at[c])
        return out, own

    def step(c, carry):
        rows = rows_at(c, chunk)
        x = tok[rows, :].astype(F32)
        hat, _ = norm_parts(x)
        n1 = (hat * row_of(gain1)).astype(BF16)
        a = dg(n1, w_in[...], 1, 0)
        s = (a * sigmoid(a)).astype(BF16)
        x1 = x + 0.5 * dg(s, w_out[...], 1, 0)
        x1_ref[rows, :] = x1
        hat, _ = norm_parts(x1)
        n2 = (hat * row_of(gain2)).astype(BF16)
        n2_ref[rows, :] = n2
        joined = dg(w_qkv[...], n2, 1, 1)
        sine, cosine = sine_cosine(
            position_row(me * frames + c * chunk, chunk, ends), freq[:, 0:1], freq[:, 1:2]
        )
        trig[0:half, rows] = sine
        trig[half:, rows] = cosine
        for head in range(sp):
            base = head * width
            for part, factor in ((0, scale), (1, 1.0)):
                low = base + part * 2 * half
                first, second = joined[low : low + half], joined[low + half : low + 2 * half]
                parts[head, part * 2 * half : part * 2 * half + half, rows] = (
                    (first * cosine - second * sine) * factor
                ).astype(BF16)
                parts[head, part * 2 * half + half : (part + 1) * 2 * half, rows] = (
                    (first * sine + second * cosine) * factor
                ).astype(BF16)
            parts[head, 4 * half : 6 * half, rows] = joined[base + 4 * half : base + 6 * half].astype(BF16)
        out, own = copies(c)
        for copy in out:
            copy.start()
        own.start()
        return carry

    lax.fori_loop(0, frames // chunk, step, 0)

    def finish(c, carry):
        out, own = copies(c)
        for copy in out:
            copy.wait()
        own.wait()
        return carry

    lax.fori_loop(0, frames // chunk, finish, 0)


def front(lengths, tok, gain1, w_in, w_out, gain2, w_qkv, freq, sp):
    frames, width = tok.shape
    chunk = min(256, frames)
    count = frames // chunk
    head_width = w_qkv.shape[0] // sp
    half = freq.shape[0]
    return pl.pallas_call(
        functools.partial(front_kernel, sp, lengths.shape[1], chunk),
        out_shape=[
            jax.ShapeDtypeStruct((frames, width), F32),
            jax.ShapeDtypeStruct((frames, width), BF16),
            jax.ShapeDtypeStruct((2 * half, frames), F32),
            jax.ShapeDtypeStruct((sp, head_width, frames), BF16),
        ],
        in_specs=[SMEM] + [VMEM] * 7,
        out_specs=[VMEM] * 4,
        scratch_shapes=[
            pltpu.VMEM((sp, head_width, frames), BF16),
            DMA((sp - 1, count)),
            DMA((sp - 1, count)),
            DMA((count,)),
        ],
        compiler_params=pltpu.CompilerParams(
            collective_id=0, has_side_effects=True, vmem_limit_bytes=VMEM_LIMIT
        ),
        name="front",
    )(lengths, tok, gain1, w_in, w_out, gain2, w_qkv, freq)


def fwd_kernel(items,bq,bk,nsub,len_ref,x_ref,ctx_ref,o_ref,lse_ref,qa,ka,va):
    srcs,rows,fr=x_ref.shape; hd=rows//3; L=srcs*fr
    ends=ends_of(len_ref,items)
    for s in range(srcs):
        cols=pl.ds(s*fr,fr)
        seg=segment_row(s*fr,fr,ends)
        qa[0:hd,cols]=x_ref[s,0:hd,:]
        qa[hd:hd+16,cols]=onehot_rows(seg,items,0.0,1.0).astype(BF16)
        qa[hd+16:2*hd,cols]=jnp.zeros((hd-16,fr),BF16)
        kT=jnp.concatenate([x_ref[s,hd:2*hd,:],onehot_rows(seg,items,NEG,0.0).astype(BF16),jnp.zeros((hd-16,fr),BF16)],axis=0)
        ka[cols,:]=kT.T
        va[0:hd,cols]=x_ref[s,2*hd:3*hd,:]
        one=lax.broadcasted_iota(I32,(16,fr),0)==0
        va[hd:hd+16,cols]=jnp.where(one,1.0,0.0).astype(BF16)
    per=fr//bq
    def qbody(i,c):
        q0=i*bq
        q=qa[:,pl.ds(pl.multiple_of(q0,bq),bq)]
        lo,hi=block_bounds(q0,bq,ends,L)
        def kbody(j,car):
            m,acc=car
            w=bk//nsub
            ks=[pl.ds(pl.multiple_of(j*bk+u*w,w),w) for u in range(nsub)]
            ss=[dg(ka[k,:],q,1,0) for k in ks]
            mn=m
            for s in ss: mn=jnp.maximum(mn,jnp.max(s,axis=0,keepdims=True))
            acc=acc*jnp.exp2(m-mn)
            for s,k in zip(ss,ks):
                p=jnp.exp2(s-mn).astype(BF16)
                acc=acc+dg(va[:,k],p,1,0)
            return mn,acc
        m,acc=lax.fori_loop(lo//bk,(hi+bk-1)//bk,kbody,(jnp.full((1,bq),NEG,F32),jnp.zeros((hd+16,bq),F32)))
        l=acc[hd:hd+1,:]
        o=acc[0:hd,:]/l
        d=i//per; qc=pl.ds(pl.multiple_of((i%per)*bq,bq),bq)
        ctx_ref[d,:,qc]=o.astype(BF16)
        o_ref[d,:,qc]=o
        lse_ref[:,pl.ds(pl.multiple_of(q0,bq),bq)]=m+jnp.log2(l)
        return c
    lax.fori_loop(0,L//bq,qbody,0)
def attend(x,lengths,bq=1024,bk=1024,nsub=4):
    srcs,rows,fr=x.shape; hd=rows//3; L=srcs*fr
    return pl.pallas_call(functools.partial(fwd_kernel,lengths.shape[1],min(bq,fr),min(bk,fr),nsub),
      out_shape=[jax.ShapeDtypeStruct((srcs,hd,fr),BF16),jax.ShapeDtypeStruct((srcs,hd,fr),F32),jax.ShapeDtypeStruct((1,L),F32)],
      in_specs=[SMEM,VMEM],out_specs=[VMEM]*3,
      scratch_shapes=[pltpu.VMEM((2*hd,L),BF16),pltpu.VMEM((L,2*hd),BF16),pltpu.VMEM((hd+16,L),BF16)],
      compiler_params=pltpu.CompilerParams(vmem_limit_bytes=VMEM_LIMIT),name="attend")(lengths,x)

def split3(v):
    a=v.astype(BF16); r=v-a.astype(F32); b=r.astype(BF16); c=(r-b.astype(F32)).astype(BF16)
    return a,b,c
def bwd_kernel(items,bq,bk,len_ref,x_ref,o_ref,lse_ref,do_ref,g_ref,qa,ka,da,va,dq,dk,dv):
    srcs,rows,fr=x_ref.shape; hd=rows//3; L=srcs*fr
    ends=ends_of(len_ref,items)
    row16=lax.broadcasted_iota(I32,(16,fr),0)
    pad=jnp.zeros((hd-32,fr),BF16)
    def stack3(v):
        a,b,c=[u.astype(F32) for u in split3(v)]
        return jnp.where(row16==0,a,jnp.where(row16==1,b,jnp.where(row16==2,c,0.0))).astype(BF16)
    ones3=jnp.where(row16<3,1.0,0.0).astype(BF16)
    for s in range(srcs):
        cols=pl.ds(s*fr,fr)
        seg=segment_row(s*fr,fr,ends)
        qT=jnp.concatenate([x_ref[s,0:hd,:],onehot_rows(seg,items,0.0,1.0).astype(BF16),stack3(-lse_ref[:,cols]),pad],axis=0)
        qa[cols,:]=qT.T
        ka[0:hd,cols]=x_ref[s,hd:2*hd,:]
        ka[hd:hd+16,cols]=onehot_rows(seg,items,NEG,0.0).astype(BF16)
        ka[hd+16:hd+32,cols]=ones3
        ka[hd+32:2*hd,cols]=pad
        do=do_ref[s]
        D=jnp.sum(do.astype(F32)*o_ref[s],axis=0,keepdims=True)
        dT=jnp.concatenate([do,stack3(-D),pad,jnp.zeros((16,fr),BF16)],axis=0)
        da[cols,:]=dT.T
        va[0:hd,cols]=x_ref[s,2*hd:3*hd,:]
        va[hd:hd+16,cols]=ones3
        va[hd+16:2*hd,cols]=jnp.zeros((hd-16,fr),BF16)
    dq[...]=jnp.zeros_like(dq)
    per=fr//bk; perq=fr//bq
    def kbody(j,c):
        k0=j*bk
        ks=pl.ds(pl.multiple_of(k0,bk),bk)
        lo,hi=block_bounds(k0,bk,ends,L)
        d=j//per; kc=pl.ds(pl.multiple_of((j%per)*bk,bk),bk)
        dk[...]=jnp.zeros_like(dk); dv[...]=jnp.zeros_like(dv)
        def qbody(i,car):
            qs=pl.ds(pl.multiple_of(i*bq,bq),bq)
            e=i//perq; qc=pl.ds(pl.multiple_of((i%perq)*bq,bq),bq)
            p=jnp.exp2(dg(qa[qs,:],ka[:,ks],1,0))
            dp=dg(da[qs,:],va[:,ks],1,0)
            ds=(p*dp).astype(BF16)
            pb=p.astype(BF16)
            dv[...]+=dg(do_ref[e,:,qc],pb,1,0)
            dk[...]+=dg(x_ref[e,0:hd,qc],ds,1,0)
            dq[:,qs]+=dg(ka[0:hd,ks],ds,1,1)
            return car
        lax.fori_loop(lo//bq,(hi+bq-1)//bq,qbody,0)
        g_ref[d,hd:2*hd,kc]=(dk[...]*float(np.log(2.0))).astype(BF16)
        g_ref[d,2*hd:3*hd,kc]=dv[...].astype(BF16)
        return c
    lax.fori_loop(0,L//bk,kbody,0)
    for s in range(srcs):
        g_ref[s,0:hd,:]=(dq[:,pl.ds(s*fr,fr)]*(hd**-0.5)).astype(BF16)
def attend_back(x,lengths,o,lse,do,bq=1024,bk=1024):
    srcs,rows,fr=x.shape; hd=rows//3; L=srcs*fr
    bq=min(bq,fr); bk=min(bk,fr)
    return pl.pallas_call(functools.partial(bwd_kernel,lengths.shape[1],bq,bk),
      out_shape=jax.ShapeDtypeStruct(x.shape,BF16),
      in_specs=[SMEM]+[VMEM]*4,out_specs=VMEM,
      scratch_shapes=[pltpu.VMEM((L,2*hd),BF16),pltpu.VMEM((2*hd,L),BF16),pltpu.VMEM((L,2*hd),BF16),pltpu.VMEM((2*hd,L),BF16),
        pltpu.VMEM((hd,L),F32),pltpu.VMEM((hd,bk),F32),pltpu.VMEM((hd,bk),F32)],
      compiler_params=pltpu.CompilerParams(vmem_limit_bytes=VMEM_LIMIT),name="attend_back")(lengths,x,o,lse,do)


def row_of(ref):
    return ref[...].astype(F32).reshape(1, ref.shape[0])


def halves_of(ref, rows):
    return jnp.concatenate([ref[0, rows, :], ref[1, rows, :]], axis=1)


def combine(entries):
    count = sum(e[2] for e in entries)
    safe = jnp.maximum(count, 1.0)
    mean = sum(e[2] * e[0] for e in entries) / safe
    spread = sum(e[1] + e[2] * (e[0] - mean) * (e[0] - mean) for e in entries)
    return mean, spread, count


def pick(ref):
    return ref[0:1, :], ref[1:2, :], ref[2:3, :]


def total(entries):
    return tuple(sum(e[i] for e in entries) for i in range(3))


def middle_kernel(
    sp, dp, items, taps, chunk, block, len_ref, parts, x1_ref, cot, gain3, gain4, gain5, w_out, w_point1,
    depthwise, bn_gain, bn_bias, w_point2, w_in, w_down,
    out_ref, grad_x2, heads, mid, small, bn_grads,
    ctx, x2_ref, n3_keep, point, glu, conv, low_lim, high_lim, act, hidden, n4_keep, branch, swish, branch2,
    grad_x3, grad_y, grad_conv, grad_glu, grad_point, branch3, back_parts, tap_sums, edge_out, edge_in,
    send_box, near_box, far_box, sums,
    send, recv, local, back_send, back_recv, back_local, rim_send, rim_recv, box_send, box_recv,
):
    me, me_dp = lax.axis_index("sp"), lax.axis_index("dp")
    frames, width = x1_ref.shape
    lanes = width // 2
    reach = taps // 2
    count = frames // chunk
    peers = sp_peers(sp)
    far_peers = [(lax.rem(me_dp + step, dp), me) for step in range(1, dp)]
    greeted = peers + far_peers
    barrier = pltpu.get_barrier_semaphore()
    length = sp * frames
    ends = ends_of(len_ref, items)
    first_frame = me * frames

    def limits(b, carry):
        rows = rows_at(b, chunk)
        frame = first_frame + b * chunk + lax.broadcasted_iota(I32, (chunk, lanes), 0)
        low, high = jnp.zeros_like(frame), jnp.full_like(frame, length)
        for end in ends:
            low = jnp.where(frame >= end, end, low)
        for end in reversed(ends):
            high = jnp.where(frame < end, end, high)
        low_lim[rows, :] = low - frame
        high_lim[rows, :] = high - 1 - frame
        return carry

    for ref in (glu, grad_conv):
        for h in range(2):
            ref[h, 0:reach, :] = jnp.zeros((reach, lanes), F32)
            ref[h, reach + frames :, :] = jnp.zeros((reach, lanes), F32)
    edge_in[...] = jnp.zeros_like(edge_in)
    send_box[...] = jnp.zeros_like(send_box)
    for device in greeted:
        pl.semaphore_signal(barrier, inc=1, device_id=device, device_id_type=MESH)
    lax.fori_loop(0, count, limits, 0)
    tap_sums[...] = jnp.zeros_like(tap_sums)
    sums[...] = jnp.zeros_like(sums)
    pl.semaphore_wait(barrier, len(greeted))

    def moves(c, source, target, send_sems, recv_sems, local_sems):
        cols = rows_at(c, chunk)
        out = [
            pltpu.make_async_remote_copy(
                src_ref=source.at[peer[1], :, cols],
                dst_ref=target.at[me, :, cols],
                send_sem=send_sems.at[i, c],
                recv_sem=recv_sems.at[i, c],
                device_id=peer,
                device_id_type=MESH,
            )
            for i, peer in enumerate(peers)
        ]
        return out + [pltpu.make_async_copy(source.at[me, :, cols], target.at[me, :, cols], local_sems.at[c])]

    def context_moves(c):
        return moves(c, parts, ctx, send, recv, local)

    def begin(c, carry):
        for copy in context_moves(c):
            copy.start()
        return carry

    lax.fori_loop(0, count, begin, 0)

    def open_step(c, carry):
        rows = rows_at(c, chunk)
        for copy in context_moves(c):
            copy.wait()
        context = ctx[:, :, rows].reshape(width, chunk)
        x2 = x1_ref[rows, :] + dg(context, w_out[...], 0, 0)
        x2_ref[rows, :] = x2
        hat, _ = norm_parts(x2)
        n3 = (hat * row_of(gain3)).astype(BF16)
        n3_keep[rows, :] = n3
        pair = dg(n3, w_point1[...], 1, 0)
        point[rows, :] = pair
        gated = (pair[:, :width] * sigmoid(pair[:, width:])).astype(BF16).astype(F32)
        where = pl.ds(pl.multiple_of(reach + c * chunk, 8), chunk)
        glu[0, where, :] = gated[:, :lanes]
        glu[1, where, :] = gated[:, lanes:]
        return carry

    lax.fori_loop(0, count, open_step, 0)

    def rim_copies(call, side, source, target):
        peer = (me_dp, me - 1 if side == 0 else me + 1)
        return pltpu.make_async_remote_copy(
            src_ref=source, dst_ref=target, send_sem=rim_send.at[call, side], recv_sem=rim_recv.at[call, side],
            device_id=peer, device_id_type=MESH,
        )

    def swap_rims(call, sources, targets):
        @pl.when(me > 0)
        def _():
            rim_copies(call, 0, sources[0], targets[1]).start()

        @pl.when(me < sp - 1)
        def _():
            rim_copies(call, 1, sources[1], targets[0]).start()

    def await_rims(call, sources, targets):
        @pl.when(me > 0)
        def _():
            rim_copies(call, 0, sources[0], targets[1]).wait_send()
            rim_copies(call, 1, sources[1], targets[0]).wait_recv()

        @pl.when(me < sp - 1)
        def _():
            rim_copies(call, 1, sources[1], targets[0]).wait_send()
            rim_copies(call, 0, sources[0], targets[1]).wait_recv()

    for side, rows in ((0, slice(reach, 2 * reach)), (1, slice(frames, frames + reach))):
        for h in range(2):
            edge_out[side, 0:reach, h * lanes : (h + 1) * lanes] = glu[h, rows, :]
    glu_rims = (
        [edge_out.at[0, 0:reach, :], edge_out.at[1, 0:reach, :]],
        [edge_in.at[0, 0:reach, :], edge_in.at[1, 0:reach, :]],
    )
    swap_rims(0, *glu_rims)

    zero = jnp.zeros((block, lanes), F32)

    def conv_step(b, carry):
        low, high = low_lim[rows_at(b, block), :], high_lim[rows_at(b, block), :]
        start = pl.multiple_of(b * block, block)
        result = [zero, zero]
        for tap in range(taps):
            shift = tap - reach
            inside = (low <= shift) if shift < 0 else (high >= shift)
            for h in range(2):
                view = glu.at[h, pl.ds(start, block + 2 * reach), :]
                term = jnp.where(inside, view[tap : tap + block, :], 0.0)
                result[h] = result[h] + depthwise[tap : tap + 1, h * lanes : (h + 1) * lanes].astype(F32) * term
        valid = (first_frame + start + lax.broadcasted_iota(I32, (block, lanes), 0)) < ends[-1]
        for h in range(2):
            conv[h, rows_at(b, block), :] = result[h]
            sums[0:1, h * lanes : (h + 1) * lanes] += jnp.sum(jnp.where(valid, result[h], 0.0), axis=0, keepdims=True)
        return carry

    blocks = frames // block
    lax.fori_loop(1, blocks - 1, conv_step, 0)
    await_rims(0, *glu_rims)
    for h in range(2):
        glu[h, 0:reach, :] = edge_in[0, 0:reach, h * lanes : (h + 1) * lanes]
        glu[h, reach + frames :, :] = edge_in[1, 0:reach, h * lanes : (h + 1) * lanes]
    conv_step(0, 0)
    conv_step(blocks - 1, 0)

    own_count = jnp.clip(ends[-1] - first_frame, 0, frames).astype(F32)
    own_mean = sums[0:1, :] / jnp.maximum(own_count, 1.0)
    sums[0:1, :] = jnp.zeros((1, width), F32)

    def spread_step(c, carry):
        rows = rows_at(c, chunk)
        valid = (first_frame + c * chunk + lax.broadcasted_iota(I32, (chunk, width), 0)) < ends[-1]
        apart = jnp.where(valid, halves_of(conv, rows) - own_mean, 0.0)
        sums[1:2, :] += jnp.sum(apart * apart, axis=0, keepdims=True)
        return carry

    lax.fori_loop(0, count, spread_step, 0)

    def box_copies(call, stage):
        group = peers if stage == 0 else far_peers
        target = near_box if stage == 0 else far_box
        base = 0 if stage == 0 else sp - 1
        return [
            pltpu.make_async_remote_copy(
                src_ref=send_box.at[call, stage],
                dst_ref=target.at[call, i],
                send_sem=box_send.at[call, base + i],
                recv_sem=box_recv.at[call, base + i],
                device_id=peer,
                device_id_type=MESH,
            )
            for i, peer in enumerate(group)
        ]

    def box_begin(call, stage, rows):
        for i, row in enumerate(rows):
            send_box[call, stage, i : i + 1, :] = row
        for copy in box_copies(call, stage):
            copy.start()

    def box_end(call, stage, rows, merge):
        target = near_box if stage == 0 else far_box
        copies = box_copies(call, stage)
        for copy in copies:
            copy.wait()
        return merge([rows] + [pick(target[call, i]) for i in range(len(copies))])

    stats = (own_mean, sums[1:2, :], jnp.full((1, width), 1.0, F32) * own_count)
    sums[1:2, :] = jnp.zeros((1, width), F32)
    box_begin(0, 0, stats)
    stats = box_end(0, 0, stats, combine)
    box_begin(0, 1, stats)
    mean, spread, frame_count = box_end(0, 1, stats, combine)
    inv_std = lax.rsqrt(spread / frame_count + EPS)
    norm_gain, norm_bias = row_of(bn_gain), row_of(bn_bias)

    def heart_step(c, carry):
        rows = rows_at(c, chunk)
        normed = (halves_of(conv, rows) - mean) * inv_std
        y = normed * norm_gain + norm_bias
        sig_y = sigmoid(y)
        w = (y * sig_y).astype(BF16)
        swish[rows, :] = w
        x3 = x2_ref[rows, :] + dg(w, w_point2[...], 1, 0)
        hat4, inv4 = norm_parts(x3)
        g4 = row_of(gain4)
        n4 = (hat4 * g4).astype(BF16)
        n4_keep[rows, :] = n4
        a = dg(n4, w_in[...], 1, 0)
        sig = sigmoid(a)
        s = (a * sig).astype(BF16)
        act[rows, :] = s
        x4 = x3 + 0.5 * dg(s, w_down[...], 1, 0)
        hat5, inv5 = norm_parts(x4)
        g5 = row_of(gain5)
        out_ref[rows, :] = (hat5 * g5).astype(BF16)
        top = cot[rows, :].astype(F32)
        small[4:5, :] += jnp.sum(top * hat5, axis=0, keepdims=True)
        grad_x4 = norm_back(top, hat5, inv5, g5)
        low_grad = (0.5 * grad_x4).astype(BF16)
        branch[rows, :] = low_grad
        grad = dg(low_grad, w_down[...], 1, 1)
        low_hidden = (grad * (sig * (1.0 + a * (1.0 - sig)))).astype(BF16)
        hidden[rows, :] = low_hidden
        grad = dg(low_hidden, w_in[...], 1, 1)
        small[3:4, :] += jnp.sum(grad * hat4, axis=0, keepdims=True)
        grad3 = grad_x4 + norm_back(grad, hat4, inv4, g4)
        grad_x3[rows, :] = grad3
        low_grad = grad3.astype(BF16)
        branch2[rows, :] = low_grad
        grad = dg(low_grad, w_point2[...], 1, 1) * (sig_y * (1.0 + y * (1.0 - sig_y)))
        grad_y[0, rows, :] = grad[:, :lanes]
        grad_y[1, rows, :] = grad[:, lanes:]
        sums[2:3, :] += jnp.sum(grad, axis=0, keepdims=True)
        sums[3:4, :] += jnp.sum(grad * normed, axis=0, keepdims=True)
        return carry

    small[...] = jnp.zeros_like(small)
    lax.fori_loop(0, count, heart_step, 0)

    pair = (sums[2:3, :], sums[3:4, :], jnp.zeros((1, width), F32))
    box_begin(1, 0, pair)
    for side, rows in ((0, slice(0, reach)), (1, slice(frames - reach, frames))):
        for h in range(2):
            cols = slice(h * lanes, (h + 1) * lanes)
            edge_out[side, reach : 2 * reach, cols] = grad_y[h, rows, :]
            edge_out[side, 2 * reach : 3 * reach, cols] = conv[h, rows, :]
    grad_rims = (
        [edge_out.at[0, reach : 3 * reach, :], edge_out.at[1, reach : 3 * reach, :]],
        [edge_in.at[0, reach : 3 * reach, :], edge_in.at[1, reach : 3 * reach, :]],
    )
    swap_rims(1, *grad_rims)
    unit = 4 * width
    for j in range(4):
        cols = slice(j * width, (j + 1) * width)
        mid[unit + j * width : unit + (j + 1) * width, :] = dg(act[:, cols], branch[...], 0, 0)
    pair = box_end(1, 0, pair, total)
    box_begin(1, 1, pair)
    for j in range(4):
        cols = slice(j * width, (j + 1) * width)
        mid[j * width : (j + 1) * width, :] = dg(n4_keep[...], hidden[:, cols], 0, 0)
    mid[2 * unit + 2 * width : 2 * unit + 3 * width, :] = dg(swish[...], branch2[...], 0, 0)
    await_rims(1, *grad_rims)
    bias_sum, gain_sum, _ = box_end(1, 1, pair, total)
    bn_grads[0:1, :] = gain_sum
    bn_grads[1:2, :] = bias_sum
    bn_grads[2:8, :] = jnp.zeros((6, width), F32)

    scale = norm_gain * inv_std
    slope = -inv_std * inv_std * norm_gain * gain_sum / frame_count
    shift_all = -inv_std * norm_gain * bias_sum / frame_count

    def conv_grad(grad, value, frame, h):
        cols = slice(h * lanes, (h + 1) * lanes)
        extra = (value - mean[:, cols]) * slope[:, cols] + shift_all[:, cols]
        return grad * scale[:, cols] + jnp.where(frame < ends[-1], extra, 0.0)

    def grad_conv_step(c, carry):
        rows = rows_at(c, chunk)
        frame = first_frame + c * chunk + lax.broadcasted_iota(I32, (chunk, lanes), 0)
        where = pl.ds(pl.multiple_of(reach + c * chunk, 8), chunk)
        for h in range(2):
            grad_conv[h, where, :] = conv_grad(grad_y[h, rows, :], conv[h, rows, :], frame, h)
        return carry

    lax.fori_loop(0, count, grad_conv_step, 0)
    for side, rows, begin_frame in (
        (0, slice(0, reach), first_frame - reach),
        (1, slice(reach + frames, 2 * reach + frames), first_frame + frames),
    ):
        frame = begin_frame + lax.broadcasted_iota(I32, (reach, lanes), 0)
        for h in range(2):
            cols = slice(h * lanes, (h + 1) * lanes)
            grad_conv[h, rows, :] = conv_grad(
                edge_in[side, reach : 2 * reach, cols], edge_in[side, 2 * reach : 3 * reach, cols], frame, h
            )

    def conv_back_step(b, carry):
        low, high = low_lim[rows_at(b, block), :], high_lim[rows_at(b, block), :]
        start = pl.multiple_of(b * block, block)
        result = [zero, zero]
        here = [glu[h, pl.ds(pl.multiple_of(reach + start, 8), block), :] for h in range(2)]
        for tap in range(taps):
            shift = reach - tap
            inside = (low <= shift) if shift < 0 else (high >= shift)
            at = reach + shift
            for h in range(2):
                view = grad_conv.at[h, pl.ds(start, block + 2 * reach), :]
                term = jnp.where(inside, view[at : at + block, :], 0.0)
                result[h] = result[h] + depthwise[tap : tap + 1, h * lanes : (h + 1) * lanes].astype(F32) * term
                tap_sums[tap, h] += jnp.sum((here[h] * term).reshape(block // 8, 8, lanes), axis=0)
        for h in range(2):
            grad_glu[h, rows_at(b, block), :] = result[h]
        return carry

    lax.fori_loop(0, blocks, conv_back_step, 0)

    def back_moves(c):
        return moves(c, back_parts, heads, back_send, back_recv, back_local)

    def close_step(c, carry):
        rows = rows_at(c, chunk)
        grad = halves_of(grad_glu, rows)
        value, gate = point[rows, :width], sigmoid(point[rows, width:])
        low_grad = jnp.concatenate([grad * gate, grad * value * gate * (1.0 - gate)], axis=1).astype(BF16)
        grad_point[rows, :] = low_grad
        grad = dg(low_grad, w_point1[...], 1, 1)
        hat, inv = norm_parts(x2_ref[rows, :])
        small[2:3, :] += jnp.sum(grad * hat, axis=0, keepdims=True)
        grad2 = grad_x3[rows, :] + norm_back(grad, hat, inv, row_of(gain3))
        grad_x2[rows, :] = grad2
        low_grad = grad2.astype(BF16)
        branch3[rows, :] = low_grad
        back_parts[:, :, rows] = dg(w_out[...], low_grad, 1, 1).astype(BF16).reshape(sp, width // sp, chunk)
        for copy in back_moves(c):
            copy.start()
        return carry

    lax.fori_loop(0, count, close_step, 0)
    for j in range(2):
        mid[2 * unit + j * width : 2 * unit + (j + 1) * width, :] = dg(
            n3_keep[...], grad_point[:, j * width : (j + 1) * width], 0, 0
        )
    mid[2 * unit + 3 * width : 3 * unit, :] = dg(ctx[...].reshape(width, frames), branch3[...], 1, 0)
    for tap in range(taps):
        for h in range(2):
            small[8 + tap : 9 + tap, h * lanes : (h + 1) * lanes] = jnp.sum(tap_sums[tap, h], axis=0, keepdims=True)

    def finish(c, carry):
        for copy in back_moves(c):
            copy.wait()
        return carry

    lax.fori_loop(0, count, finish, 0)


def middle(
    lengths, parts, x1, cot, gain3, gain4, gain5, w_out, w_point1, depthwise, bn_gain, bn_bias, w_point2,
    w_in, w_down, dp,
):
    frames, width = x1.shape
    sp = parts.shape[0]
    wide = w_in.shape[1]
    taps = depthwise.shape[0]
    reach = taps // 2
    chunk = min(256, frames)
    count = frames // chunk
    lanes = width // 2
    keep, low_keep = pltpu.VMEM((frames, width), F32), pltpu.VMEM((frames, width), BF16)
    split = pltpu.VMEM((2, frames, lanes), F32)
    rimmed = pltpu.VMEM((2, frames + 2 * reach, lanes), F32)
    rims = pltpu.VMEM((2, 3 * reach, width), F32)
    moves = [DMA((sp - 1, count)), DMA((sp - 1, count)), DMA((count,))]
    return pl.pallas_call(
        functools.partial(middle_kernel, sp, dp, lengths.shape[1], taps, chunk, 32),
        out_shape=[
            jax.ShapeDtypeStruct((frames, width), BF16),
            jax.ShapeDtypeStruct((frames, width), F32),
            jax.ShapeDtypeStruct(parts.shape, BF16),
            jax.ShapeDtypeStruct((12 * width, width), F32),
            jax.ShapeDtypeStruct((64, width), F32),
            jax.ShapeDtypeStruct((8, width), F32),
        ],
        in_specs=[SMEM, pl.BlockSpec(memory_space=pl.ANY)] + [VMEM] * 13,
        out_specs=[VMEM] * 6,
        scratch_shapes=[
            pltpu.VMEM(parts.shape, BF16),
            keep,
            low_keep,
            pltpu.VMEM((frames, 2 * width), F32),
            rimmed,
            split,
            pltpu.VMEM((frames, lanes), I32),
            pltpu.VMEM((frames, lanes), I32),
            pltpu.VMEM((frames, wide), BF16),
            pltpu.VMEM((frames, wide), BF16),
            low_keep,
            low_keep,
            low_keep,
            low_keep,
            keep,
            split,
            rimmed,
            split,
            pltpu.VMEM((frames, 2 * width), BF16),
            low_keep,
            pltpu.VMEM(parts.shape, BF16),
            pltpu.VMEM((taps, 2, 8, lanes), F32),
            rims,
            rims,
            pltpu.VMEM((2, 2, 8, width), F32),
            pltpu.VMEM((2, sp - 1, 8, width), F32),
            pltpu.VMEM((2, dp - 1, 8, width), F32),
            pltpu.VMEM((8, width), F32),
        ]
        + moves
        + moves
        + [DMA((2, 2)), DMA((2, 2)), DMA((2, sp + dp - 2)), DMA((2, sp + dp - 2))],
        compiler_params=pltpu.CompilerParams(
            collective_id=1, has_side_effects=True, vmem_limit_bytes=VMEM_LIMIT
        ),
        name="middle",
    )(
        lengths, parts, x1, cot, gain3, gain4, gain5, w_out, w_point1, depthwise, bn_gain, bn_bias, w_point2,
        w_in, w_down,
    )


def axis_bits():
    bits = []
    for axis in ("sp", "dp"):
        step = 1
        while step < lax.axis_size(axis):
            bits.append((axis, step))
            step *= 2
        assert step == lax.axis_size(axis)
    return bits


def swap_partner(axis, step):
    place = {name: lax.axis_index(name) for name in ("dp", "sp")}
    bit = lax.rem(place[axis] // step, 2)
    place[axis] = place[axis] + step - 2 * step * bit
    return (place["dp"], place["sp"]), bit


def orders(bits):
    sp_bits = [b for b in bits if b[0] == "sp"]
    dp_bits = [b for b in bits if b[0] == "dp"]
    first, far = sp_bits[:1], sp_bits[1:]
    return {
        "x_first": first + dp_bits[:1] + far + dp_bits[1:],
        "y_first": first + far + dp_bits,
        "y_last": first + dp_bits + far,
        "z_first": first + dp_bits[1:] + dp_bits[:1] + far,
        "z_mid": first + far + dp_bits[1:] + dp_bits[:1],
    }


def exchange_plan(rows, steps, offset):
    sizes, size = [], rows
    for _ in range(steps):
        halves = size % 32 == 0
        size = size // 2 if halves else size
        sizes.append((halves, size, offset))
        offset += size
    return sizes, offset, size


class Reduction:
    def __init__(self, base, rows, staged, order, acc, stage, land, full, send, recv, source=None):
        self.base, self.rows, self.order = base, rows, order
        self.acc, self.stage, self.land, self.full = acc, stage, land, full
        self.send, self.recv = send, recv
        self.source = acc if source is None else source
        self.low = base
        self.sizes, _, self.own = exchange_plan(rows, len(order), staged)

    def at(self, low, size):
        return pl.ds(pl.multiple_of(low, 16), size)

    def copy(self, step, src, dst):
        partner, _ = swap_partner(*self.order[step[1]])
        index = step[0] * len(self.order) + step[1]
        return pltpu.make_async_remote_copy(
            src_ref=src,
            dst_ref=dst,
            send_sem=self.send.at[index],
            recv_sem=self.recv.at[index],
            device_id=partner,
            device_id_type=MESH,
        )

    def sum_copy(self, k):
        _, moved, offset = self.sizes[k]
        where = pl.ds(offset, moved)
        return self.copy((0, k), self.stage.at[where, :], self.land.at[where, :])

    def sum_send(self, k):
        halves, moved, offset = self.sizes[k]
        _, bit = swap_partner(*self.order[k])
        away = self.low + (1 - bit) * moved if halves else self.low
        source = self.source if k == 0 else self.acc
        self.stage[offset : offset + moved, :] = source[self.at(away, moved), :].astype(BF16)
        self.sum_copy(k).start()

    def sum_recv(self, k):
        halves, moved, offset = self.sizes[k]
        _, bit = swap_partner(*self.order[k])
        self.sum_copy(k).wait()
        other = self.land[offset : offset + moved, :].astype(F32)
        if halves:
            self.low = self.low + bit * moved
            source = self.source if k == 0 else self.acc
            mine = source[self.at(self.low, moved), :]
        else:
            mine = self.stage[offset : offset + moved, :].astype(F32)
        self.acc[self.at(self.low, moved), :] = mine + other

    def close(self):
        where = self.at(self.low, self.own)
        self.full[where, :] = self.acc[where, :].astype(BF16)

    def share_copy(self, k):
        where = self.at(self.low, self.sizes[k][1])
        return self.copy((1, k), self.full.at[where, :], self.full.at[where, :])

    def share_send(self, k):
        if self.sizes[k][0]:
            self.share_copy(k).start()

    def share_recv(self, k):
        halves, moved, _ = self.sizes[k]
        if halves:
            self.share_copy(k).wait()
            _, bit = swap_partner(*self.order[k])
            self.low = self.low - bit * moved


def run_sum(streams, steps):
    for k in steps:
        for stream in streams:
            if k > 0:
                stream.sum_recv(k - 1)
            stream.sum_send(k)


def run_share(streams, count):
    for stream in streams:
        stream.sum_recv(count - 1)
        stream.close()
        stream.share_send(count - 1)
    for k in reversed(range(count)):
        for stream in streams:
            stream.share_recv(k)
            if k > 0:
                stream.share_send(k - 1)


def back_kernel(
    sp, chunk, parts, trig, tok, x1_ref, n2_ref, grad_x2, gain1, gain2, w_in, w_out, w_qkv, mid, small,
    grad_ref, full, heads, joined, n1_keep, branch, act, hidden, gains, acc, stage, land,
    send, recv, local, sum_send, sum_recv,
):
    me = lax.axis_index("sp")
    frames, width = tok.shape
    wide = w_in.shape[1]
    head_width = parts.shape[1]
    half = trig.shape[0] // 2
    count = frames // chunk
    peers = sp_peers(sp)
    bits = axis_bits()
    partners = [swap_partner(*bit)[0] for bit in bits if bit[0] == "dp"]
    greet(peers + partners)

    def copies(c):
        cols = rows_at(c, chunk)
        out = [
            pltpu.make_async_remote_copy(
                src_ref=parts.at[peer[1], :, cols],
                dst_ref=heads.at[me, :, cols],
                send_sem=send.at[i, c],
                recv_sem=recv.at[i, c],
                device_id=peer,
                device_id_type=MESH,
            )
            for i, peer in enumerate(peers)
        ]
        return out, pltpu.make_async_copy(parts.at[me, :, cols], heads.at[me, :, cols], local.at[c])

    def begin(c, carry):
        out, own = copies(c)
        for copy in out:
            copy.start()
        own.start()
        return carry

    lax.fori_loop(0, count, begin, 0)

    order = orders(bits)
    unit = 4 * width
    plan = [
        (0, 2 * unit, "y_last", mid),
        (2 * unit, unit, "z_first", mid),
        (3 * unit, unit, "z_first", None),
        (4 * unit, unit, "x_first", None),
        (5 * unit, unit, "y_first", None),
    ]
    steps = len(bits)
    streams, staged = [], 0
    for i, (base, rows, name, source) in enumerate(plan):
        streams.append(
            Reduction(
                base, rows, staged, order[name], acc, stage, land, full, sum_send.at[i], sum_recv.at[i], source
            )
        )
        staged = exchange_plan(rows, steps, staged)[1]
    run_sum(streams[:2], range(steps))
    gains[...] = jnp.zeros_like(gains)

    def step(c, carry):
        rows = rows_at(c, chunk)
        out, own = copies(c)
        for copy in out:
            copy.wait()
        own.wait()
        sine, cosine = trig[0:half, rows], trig[half:, rows]
        for head in range(sp):
            base = head * head_width
            for part in range(2):
                low = part * 2 * half
                first = heads[head, low : low + half, rows].astype(F32)
                second = heads[head, low + half : low + 2 * half, rows].astype(F32)
                low = base + low
                joined[low : low + half, rows] = (first * cosine + second * sine).astype(BF16)
                joined[low + half : low + 2 * half, rows] = (second * cosine - first * sine).astype(BF16)
            joined[base + 4 * half : base + 6 * half, rows] = heads[head, 4 * half : 6 * half, rows]
        grad = dg(joined[:, rows], w_qkv[...], 0, 0)
        hat, inv = norm_parts(x1_ref[rows, :])
        gains[1:2, :] += jnp.sum(grad * hat, axis=0, keepdims=True)
        grad_x1 = grad_x2[rows, :] + norm_back(grad, hat, inv, row_of(gain2))
        low_grad = (0.5 * grad_x1).astype(BF16)
        branch[rows, :] = low_grad
        hat, inv = norm_parts(tok[rows, :].astype(F32))
        gain = row_of(gain1)
        n1 = (hat * gain).astype(BF16)
        n1_keep[rows, :] = n1
        a = dg(n1, w_in[...], 1, 0)
        sig = sigmoid(a)
        act[rows, :] = (a * sig).astype(BF16)
        grad = dg(low_grad, w_out[...], 1, 1)
        low_hidden = (grad * (sig * (1.0 + a * (1.0 - sig)))).astype(BF16)
        hidden[rows, :] = low_hidden
        grad = dg(low_hidden, w_in[...], 1, 1)
        gains[0:1, :] += jnp.sum(grad * hat, axis=0, keepdims=True)
        grad_ref[rows, :] = (grad_x1 + norm_back(grad, hat, inv, gain)).astype(BF16)
        return carry

    lax.fori_loop(0, count, step, 0)
    run_share(streams[:2], steps)
    base = 3 * unit
    acc[base : base + 3 * width, :] = dg(joined[...], n2_ref[...], 1, 0)
    base = base + 3 * width
    acc[base : base + 8, :] = small[0:8, :] + gains[...]
    acc[base + 8 : base + 64, :] = small[8:64, :]
    acc[base + 64 : 4 * unit, :] = jnp.zeros((width - 64, width), F32)
    streams[2].sum_send(0)
    for j in range(wide // width):
        base = 4 * unit + j * width
        acc[base : base + width, :] = dg(act[:, j * width : (j + 1) * width], branch[...], 0, 0)
    streams[3].sum_send(0)
    for j in range(wide // width):
        base = 5 * unit + j * width
        acc[base : base + width, :] = dg(n1_keep[...], hidden[:, j * width : (j + 1) * width], 0, 0)
    streams[4].sum_send(0)
    run_sum(streams[2:], range(1, steps))
    run_share(streams[2:], steps)


def back(parts, trig, tok, x1, n2, grad_x2, gain1, gain2, w_in, w_out, w_qkv, mid, small):
    frames, width = tok.shape
    sp = parts.shape[0]
    chunk = min(256, frames)
    count = frames // chunk
    wide = w_in.shape[1]
    rows = 6 * 4 * width
    steps = len(axis_bits())
    staged = exchange_plan(8 * width, steps, 0)[1] + 4 * exchange_plan(4 * width, steps, 0)[1]
    return pl.pallas_call(
        functools.partial(back_kernel, sp, chunk),
        out_shape=[
            jax.ShapeDtypeStruct((frames, width), BF16),
            jax.ShapeDtypeStruct((rows, width), BF16),
        ],
        in_specs=[pl.BlockSpec(memory_space=pl.ANY)] + [VMEM] * 12,
        out_specs=[VMEM] * 2,
        scratch_shapes=[
            pltpu.VMEM(parts.shape, BF16),
            pltpu.VMEM((3 * width, frames), BF16),
            pltpu.VMEM((frames, width), BF16),
            pltpu.VMEM((frames, width), BF16),
            pltpu.VMEM((frames, wide), BF16),
            pltpu.VMEM((frames, wide), BF16),
            pltpu.VMEM((8, width), F32),
            pltpu.VMEM((rows, width), F32),
            pltpu.VMEM((staged, width), BF16),
            pltpu.VMEM((staged, width), BF16),
            DMA((sp - 1, count)),
            DMA((sp - 1, count)),
            DMA((count,)),
            DMA((5, 2 * steps)),
            DMA((5, 2 * steps)),
        ],
        compiler_params=pltpu.CompilerParams(
            collective_id=6, has_side_effects=True, vmem_limit_bytes=VMEM_LIMIT
        ),
        name="back",
    )(parts, trig, tok, x1, n2, grad_x2, gain1, gain2, w_in, w_out, w_qkv, mid, small)


def unpack_kernel(full, in_two, out_two, point_one, point_two, out_weight, qkv, in_one, out_one, small):
    width = full.shape[1]

    def block(base):
        return full[base : base + width, :].astype(F32)

    unit = 4 * width
    for j in range(4):
        cols = slice(j * width, (j + 1) * width)
        in_two[:, cols] = block(j * width)
        out_two[cols, :] = block(unit + j * width)
        out_one[cols, :] = block(4 * unit + j * width)
        in_one[:, cols] = block(5 * unit + j * width)
    base = 2 * unit
    for j in range(2):
        point_one[:, j * width : (j + 1) * width] = block(base + j * width)
    point_two[...] = block(base + 2 * width)
    out_weight[...] = block(base + 3 * width)
    base = 3 * unit
    head_dim = width // HEADS
    for part in range(3):
        rows = [
            full[base + (3 * head + part) * head_dim : base + (3 * head + part + 1) * head_dim, :]
            for head in range(HEADS)
        ]
        qkv[:, part * width : (part + 1) * width] = jnp.concatenate(rows, axis=0).astype(F32).T
    small[...] = full[base + 3 * width : base + 3 * width + 64, :].astype(F32)


def unpack(full):
    width = full.shape[1]
    shapes = [
        (width, 4 * width), (4 * width, width), (width, 2 * width), (width, width), (width, width),
        (width, 3 * width), (width, 4 * width), (4 * width, width), (64, width),
    ]
    return pl.pallas_call(
        unpack_kernel,
        out_shape=[jax.ShapeDtypeStruct(shape, F32) for shape in shapes],
        in_specs=[VMEM],
        out_specs=[VMEM] * len(shapes),
        compiler_params=pltpu.CompilerParams(vmem_limit_bytes=VMEM_LIMIT),
        name="unpack",
    )(full)


def on_device(
    tokens, ln1_gain, ffn1_in, ffn1_out, ln2_gain, w_qkv, w_out, ln3_gain, w_point1, depthwise,
    bn_gain, bn_bias, w_point2, ln4_gain, ffn2_in, ffn2_out, ln5_gain, lengths, cotangent,
):
    width = tokens.shape[2]
    sp, dp = lax.axis_size("sp"), lax.axis_size("dp")
    assert HEADS == sp
    head_dim = width // HEADS
    half = head_dim // 2
    taps = depthwise.shape[0]
    turns = 10000.0 ** (-np.arange(half, dtype=np.float64) / half) / (2 * np.pi)
    high = np.round(turns * 4096.0) / 4096.0
    freq = jnp.asarray(np.stack([high, turns - high], axis=1), F32)
    qkv_rows = w_qkv.T.reshape(3, HEADS, head_dim, width).transpose(1, 0, 2, 3).reshape(3 * width, width)
    x1, n2, trig, heads = front(
        lengths, tokens[0], ln1_gain, ffn1_in, ffn1_out, ln2_gain, qkv_rows, freq, sp
    )
    context, raw_context, log_sums = attend(heads, lengths)
    output, grad_x2, grad_context, mid, small, bn_grads = middle(
        lengths, context, x1, cotangent[0], ln3_gain, ln4_gain, ln5_gain, w_out, w_point1, depthwise,
        bn_gain, bn_bias, w_point2, ffn2_in, ffn2_out, dp,
    )
    grad_heads = attend_back(heads, lengths, raw_context, log_sums, grad_context)
    input_grad, full = back(
        grad_heads, trig, tokens[0], x1, n2, grad_x2, ln1_gain, ln2_gain, ffn1_in, ffn1_out, qkv_rows,
        mid, small,
    )
    in_two, out_two, point_one, point_two, out_weight, qkv, in_one, out_one, small = unpack(full)
    return (
        output[None], input_grad[None], small[0], in_one, out_one, small[1], qkv, out_weight,
        small[2], point_one, small[8 : 8 + taps], bn_grads[0], bn_grads[1], point_two, small[3],
        in_two, out_two, small[4],
    )


def solution(mesh):
    split = P("dp", "sp", None)
    return jax.shard_map(
        on_device,
        mesh=mesh,
        in_specs=(split,) + (P(),) * 16 + (P("dp", None), split),
        out_specs=(split, split) + (P(),) * 16,
        check_vma=False,
    )
```

```python
import functools

import jax
import jax.numpy as jnp
import numpy as np
from jax import lax
from jax.experimental import pallas as pl
from jax.experimental.pallas import tpu as pltpu
from jax.sharding import PartitionSpec as P

HEADS = 4
EPS = 1e-05
NEG = -1e30
LN2 = float(np.log(2.0))
F32 = jnp.float32
BF16 = jnp.bfloat16
I32 = jnp.int32
MESH = pl.DeviceIdType.MESH
VMEM = pl.BlockSpec(memory_space=pltpu.VMEM)
SMEM = pl.BlockSpec(memory_space=pltpu.SMEM)
DMA = pltpu.SemaphoreType.DMA
VMEM_LIMIT = 56 * 2**20


def dg(left, right, left_dim, right_dim):
    return lax.dot_general(
        left, right, (((left_dim,), (right_dim,)), ((), ())), preferred_element_type=F32
    )


def rows_at(index, count):
    return pl.ds(pl.multiple_of(index * count, count), count)


def greet(devices):
    for device in devices:
        pl.semaphore_signal(pltpu.get_barrier_semaphore(), inc=1, device_id=device, device_id_type=MESH)


def await_greetings(devices):
    pl.semaphore_wait(pltpu.get_barrier_semaphore(), len(devices))


def flipped(axis, mask):
    me, step = lax.axis_index(axis), 1
    out = me
    while step <= mask:
        if mask & step:
            out = out + step - 2 * step * lax.rem(me // step, 2)
        step *= 2
    return out


def peer_at(sp_mask, dp_mask):
    return (flipped("dp", dp_mask), flipped("sp", sp_mask))


def sp_peers(count):
    return [peer_at(mask, 0) for mask in range(1, count)]


def row_of(ref):
    return ref[...].astype(F32).reshape(1, ref.shape[0])


def frame_cols(device, frames, c, chunk):
    return pl.ds(pl.multiple_of(device * frames + c * chunk, chunk), chunk)


def ends_of(len_ref, items):
    ends, total = [], 0
    for item in range(items):
        total = total + len_ref[0, item]
        ends.append(total)
    return ends


def segment_row(first, count, ends):
    frame = first + lax.broadcasted_iota(I32, (1, count), 1)
    segment = jnp.zeros((1, count), I32)
    for end in ends:
        segment = segment + (frame >= end).astype(I32)
    return segment


def position_row(first, count, ends):
    frame = first + lax.broadcasted_iota(I32, (1, count), 1)
    start = jnp.zeros((1, count), I32)
    for end in ends:
        start = jnp.where(frame >= end, end, start)
    return (frame - start).astype(F32)


def block_bounds(first, count, ends, length):
    low, high = 0, length
    for end in ends:
        low = jnp.where(first >= end, end, low)
    for end in reversed(ends):
        high = jnp.where(first + count - 1 < end, end, high)
    return low, high


def onehot_rows(segment, items, other, same):
    row = lax.broadcasted_iota(I32, (16, segment.shape[1]), 0)
    return jnp.where(row <= items, jnp.where(row == segment, same, other), 0.0)


def norm_parts(rows):
    centre = rows - jnp.mean(rows, axis=-1, keepdims=True)
    inv = lax.rsqrt(jnp.mean(centre * centre, axis=-1, keepdims=True) + EPS)
    return centre * inv, inv


def norm_back(grad, hat, inv, gain):
    scaled = grad * gain
    first = jnp.mean(scaled, axis=-1, keepdims=True)
    second = jnp.mean(scaled * hat, axis=-1, keepdims=True)
    return inv * (scaled - first - hat * second)


def sigmoid(x):
    return 1.0 / (1.0 + jnp.exp(-x))


def sine_cosine(position, freq_hi, freq_lo):
    turns = position * freq_hi
    turns = turns - jnp.round(turns) + position * freq_lo
    turns = turns - jnp.round(turns)
    x = turns * float(np.pi)
    x2 = x * x
    s = x * (1 + x2 * (-1 / 6 + x2 * (1 / 120 + x2 * (-1 / 5040 + x2 * (1 / 362880 - x2 / 39916800)))))
    c = 1 + x2 * (-1 / 2 + x2 * (1 / 24 + x2 * (-1 / 720 + x2 * (1 / 40320 + x2 * (-1 / 3628800 + x2 / 479001600)))))
    return 2 * s * c, 1 - 2 * s * s


def front_kernel(
    sp, items, chunk, len_ref, tok, gain1, w_in, w_out, gain2, w_qkv, freq,
    x1_ref, n2_ref, trig, heads, parts, turned, send, recv, local,
):
    me = lax.axis_index("sp")
    frames = tok.shape[0]
    width = tok.shape[1]
    half = trig.shape[0] // 2
    peers = sp_peers(sp)
    greet(peers)
    turned[...] = w_qkv[...].T
    ends = ends_of(len_ref, items)
    scale = float(np.log2(np.e)) * (2 * half) ** -0.5

    def copies(c):
        cols = rows_at(c, chunk)
        out = [
            pltpu.make_async_remote_copy(
                src_ref=parts.at[peer[1], :, cols],
                dst_ref=heads.at[:, frame_cols(me, frames, c, chunk)],
                send_sem=send.at[i, c],
                recv_sem=recv.at[i, c],
                device_id=peer,
                device_id_type=MESH,
            )
            for i, peer in enumerate(peers)
        ]
        own = pltpu.make_async_copy(
            parts.at[me, :, cols], heads.at[:, frame_cols(me, frames, c, chunk)], local.at[c]
        )
        return out, own

    def step(c, carry):
        rows = rows_at(c, chunk)
        x = tok[rows, :].astype(F32)
        hat, _ = norm_parts(x)
        n1 = (hat * row_of(gain1)).astype(BF16)
        a = dg(n1, w_in[...], 1, 0)
        s = (a * sigmoid(a)).astype(BF16)
        x1 = x + 0.5 * dg(s, w_out[...], 1, 0)
        x1_ref[rows, :] = x1
        hat, _ = norm_parts(x1)
        n2 = (hat * row_of(gain2)).astype(BF16)
        n2_ref[rows, :] = n2
        joined = dg(turned[...], n2, 1, 1)
        sine, cosine = sine_cosine(
            position_row(me * frames + c * chunk, chunk, ends), freq[:, 0:1], freq[:, 1:2]
        )
        trig[0:half, rows] = sine
        trig[half:, rows] = cosine
        for head in range(sp):
            base = head * 2 * half
            for part, factor in ((0, scale), (1, 1.0)):
                low = part * width + base
                first, second = joined[low : low + half], joined[low + half : low + 2 * half]
                low = part * 2 * half
                parts[head, low : low + half, rows] = ((first * cosine - second * sine) * factor).astype(BF16)
                parts[head, low + half : low + 2 * half, rows] = (
                    (first * sine + second * cosine) * factor
                ).astype(BF16)
            low = 2 * width + base
            parts[head, 4 * half : 6 * half, rows] = joined[low : low + 2 * half].astype(BF16)

        @pl.when(c == 0)
        def _():
            await_greetings(peers)

        out, own = copies(c)
        for copy in out:
            copy.start()
        own.start()
        return carry

    lax.fori_loop(0, frames // chunk, step, 0)

    def finish(c, carry):
        out, own = copies(c)
        for copy in out:
            copy.wait()
        own.wait()
        return carry

    lax.fori_loop(0, frames // chunk, finish, 0)


def front(lengths, tok, gain1, w_in, w_out, gain2, w_qkv, freq, sp):
    frames, width = tok.shape
    chunk = min(256, frames)
    count = frames // chunk
    head_width = w_qkv.shape[1] // sp
    half = freq.shape[0]
    return pl.pallas_call(
        functools.partial(front_kernel, sp, lengths.shape[1], chunk),
        out_shape=[
            jax.ShapeDtypeStruct((frames, width), F32),
            jax.ShapeDtypeStruct((frames, width), BF16),
            jax.ShapeDtypeStruct((2 * half, frames), F32),
            jax.ShapeDtypeStruct((head_width, sp * frames), BF16),
        ],
        in_specs=[SMEM] + [VMEM] * 7,
        out_specs=[VMEM] * 4,
        scratch_shapes=[
            pltpu.VMEM((sp, head_width, frames), BF16),
            pltpu.VMEM((3 * width, width), BF16),
            DMA((sp - 1, count)),
            DMA((sp - 1, count)),
            DMA((count,)),
        ],
        compiler_params=pltpu.CompilerParams(
            collective_id=0, has_side_effects=True, vmem_limit_bytes=VMEM_LIMIT
        ),
        name="front",
    )(lengths, tok, gain1, w_in, w_out, gain2, w_qkv, freq)


def split_rows(value):
    row = lax.broadcasted_iota(I32, (16, value.shape[1]), 0)
    first = value.astype(BF16).astype(F32)
    second = (value - first).astype(BF16).astype(F32)
    third = value - first - second
    picked = jnp.where(row == 0, first, jnp.where(row == 1, second, third))
    return jnp.where(row < 3, picked, 0.0).astype(BF16)


def first_rows(count, columns):
    row = lax.broadcasted_iota(I32, (16, columns), 0)
    return jnp.where(row < count, 1.0, 0.0).astype(BF16)


def in_pieces(low, high, sizes, body, carry):
    for size in sizes:
        pieces = (high - low) // size
        carry = lax.fori_loop(
            0, pieces, lambda i, c, low=low, size=size: body(pl.multiple_of(low + i * size, sizes[-1]), size, c), carry
        )
        low = low + pieces * size
    return carry


def over_blocks(len_ref, ends, items, length, outer, sizes, body):
    unit = sizes[-1]
    start, stop, longest = 0, ends[0], len_ref[0, 0]
    for item in range(1, items):
        more = len_ref[0, item] > longest
        start = jnp.where(more, ends[item - 1], start)
        stop = jnp.where(more, ends[item], stop)
        longest = jnp.where(more, len_ref[0, item], longest)
    start, stop = start // unit * unit, (stop + unit - 1) // unit * unit

    def part(index, carry):
        low = jnp.where(index == 0, 0, jnp.where(index == 1, start, stop))
        high = jnp.where(index == 0, start, jnp.where(index == 1, stop, length))

        def block(at, size, carry):
            first, last = block_bounds(at, size, ends, length)
            body(at, size, first // unit * unit, (last + unit - 1) // unit * unit)
            return carry

        return in_pieces(low, high, outer, block, carry)

    lax.fori_loop(0, 3, part, 0)


def attend_kernel(items, outer, sizes, len_ref, x_ref, ctx_ref, o_ref, lse_ref, qa, ka, va):
    dim, length = x_ref.shape[0] // 3, x_ref.shape[1]
    ends = ends_of(len_ref, items)
    frames = min(1024, length)
    pad = jnp.zeros((dim - 32, frames), BF16)
    for first in range(0, length, frames):
        cols = slice(first, first + frames)
        segment = segment_row(first, frames, ends)
        query, key = x_ref[0:dim, cols], x_ref[dim : 2 * dim, cols]
        own = jnp.sum(query.astype(F32) * key.astype(F32), axis=0, keepdims=True)
        lse_ref[:, cols] = own
        qa[0:dim, cols] = query
        qa[dim : dim + 16, cols] = onehot_rows(segment, items, 0.0, 1.0).astype(BF16)
        qa[dim + 16 : dim + 32, cols] = split_rows(-own)
        qa[dim + 32 :, cols] = pad
        ka[cols, :] = jnp.concatenate(
            [key, onehot_rows(segment, items, NEG, 0.0).astype(BF16), first_rows(3, frames), pad], axis=0
        ).T
        va[0:dim, cols] = x_ref[2 * dim :, cols]
        va[dim:, cols] = first_rows(1, frames)

    def block_step(start, block, low, high):
        where = pl.ds(start, block)
        query = qa[:, where]

        def piece(at, size, acc):
            powers = jnp.exp2(dg(ka[pl.ds(at, size), :], query, 1, 0)).astype(BF16)
            return acc + dg(va[:, pl.ds(at, size)], powers, 1, 0)

        def store(acc, shift):
            total = acc[dim : dim + 1, :]
            value = acc[0:dim, :] / total
            ctx_ref[:, where] = value.astype(BF16)
            o_ref[:, where] = value
            lse_ref[:, where] = shift + jnp.log2(total)

        acc = in_pieces(low, high, sizes, piece, jnp.zeros((dim + 16, block), F32))
        own = lse_ref[:, where]
        store(acc, own)
        fits = jnp.min(jnp.where(acc[dim : dim + 1, :] < 2.0**60, 1.0, 0.0)) > 0.5

        @pl.when(jnp.logical_not(fits))
        def _():
            def maximum(at, size, top):
                return jnp.maximum(top, jnp.max(dg(ka[pl.ds(at, size), :], query, 1, 0), axis=0, keepdims=True))

            top = in_pieces(low, high, sizes[-1:], maximum, jnp.zeros((1, block), F32))

            def careful(at, size, acc):
                powers = jnp.exp2(dg(ka[pl.ds(at, size), :], query, 1, 0) - top).astype(BF16)
                return acc + dg(va[:, pl.ds(at, size)], powers, 1, 0)

            store(in_pieces(low, high, sizes[-1:], careful, jnp.zeros((dim + 16, block), F32)), own + top)

    over_blocks(len_ref, ends, items, length, outer, sizes, block_step)


def attend(x, lengths, outer=(1024, 512, 256), sizes=(2048, 1024, 512, 256)):
    rows, length = x.shape
    dim = rows // 3
    return pl.pallas_call(
        functools.partial(attend_kernel, lengths.shape[1], outer, sizes),
        out_shape=[
            jax.ShapeDtypeStruct((dim, length), BF16),
            jax.ShapeDtypeStruct((dim, length), F32),
            jax.ShapeDtypeStruct((1, length), F32),
        ],
        in_specs=[SMEM, VMEM],
        out_specs=[VMEM] * 3,
        scratch_shapes=[
            pltpu.VMEM((2 * dim, length), BF16),
            pltpu.VMEM((length, 2 * dim), BF16),
            pltpu.VMEM((dim + 16, length), BF16),
        ],
        compiler_params=pltpu.CompilerParams(vmem_limit_bytes=VMEM_LIMIT),
        name="attend",
    )(lengths, x)


def attend_back_kernel(
    items, outer, sizes, sub, len_ref, x_ref, o_ref, lse_ref, do_ref, g_ref, qa, ka, da, va, dq, dk, dv
):
    dim, length = x_ref.shape[0] // 3, x_ref.shape[1]
    ends = ends_of(len_ref, items)
    frames = min(1024, length)
    pad, wide_pad = jnp.zeros((dim - 32, frames), BF16), jnp.zeros((dim - 16, frames), BF16)
    for first in range(0, length, frames):
        cols = slice(first, first + frames)
        segment = segment_row(first, frames, ends)
        qa[cols, :] = jnp.concatenate(
            [
                x_ref[0:dim, cols],
                onehot_rows(segment, items, 0.0, 1.0).astype(BF16),
                split_rows(-lse_ref[:, cols]),
                pad,
            ],
            axis=0,
        ).T
        ka[0:dim, cols] = x_ref[dim : 2 * dim, cols]
        ka[dim : dim + 16, cols] = onehot_rows(segment, items, NEG, 0.0).astype(BF16)
        ka[dim + 16 : dim + 32, cols] = first_rows(3, frames)
        ka[dim + 32 :, cols] = pad
        grad = do_ref[:, cols]
        row_dot = jnp.sum(grad.astype(F32) * o_ref[:, cols], axis=0, keepdims=True)
        da[cols, :] = jnp.concatenate([grad, split_rows(-row_dot), wide_pad], axis=0).T
        va[0:dim, cols] = x_ref[2 * dim :, cols]
        va[dim : dim + 16, cols] = first_rows(3, frames)
        va[dim + 16 :, cols] = wide_pad
        dq[:, cols] = jnp.zeros((dim, frames), F32)

    def block_step(start, block, low, high):
        where = pl.ds(start, block)
        dk[...] = jnp.zeros_like(dk)
        dv[...] = jnp.zeros_like(dv)

        def piece(at, size, carry):
            rows = pl.ds(at, size)

            def score(u):
                cols = pl.ds(pl.multiple_of(start + u * sub, sub), sub)
                return dg(qa[rows, :], ka[:, cols], 1, 0), dg(da[rows, :], va[:, cols], 1, 0)

            count = block // sub
            grads = []
            ready = score(0)
            for u in range(count):
                scores, grad_probs = ready
                if u + 1 < count:
                    ready = score(u + 1)
                probs = jnp.exp2(scores)
                grad = (probs * grad_probs).astype(BF16)
                cols = slice(u * sub, (u + 1) * sub)
                dv[:, cols] += dg(do_ref[:, rows], probs.astype(BF16), 1, 0)
                dk[:, cols] += dg(x_ref[0:dim, rows], grad, 1, 0)
                grads.append(grad)
            dq[:, rows] += dg(ka[0:dim, where], jnp.concatenate(grads, axis=1), 1, 1)
            return carry

        in_pieces(low, high, sizes, piece, 0)
        g_ref[dim : 2 * dim, where] = (dk[:, 0:block] * LN2).astype(BF16)
        g_ref[2 * dim :, where] = dv[:, 0:block].astype(BF16)

    over_blocks(len_ref, ends, items, length, outer, sizes, block_step)
    for first in range(0, length, frames):
        cols = slice(first, first + frames)
        g_ref[0:dim, cols] = (dq[:, cols] * dim**-0.5).astype(BF16)


def attend_back(x, lengths, o, lse, do, outer=(512, 256), sizes=(2048, 1024, 512, 256), sub=256):
    rows, length = x.shape
    dim = rows // 3
    return pl.pallas_call(
        functools.partial(attend_back_kernel, lengths.shape[1], outer, sizes, sub),
        out_shape=jax.ShapeDtypeStruct(x.shape, BF16),
        in_specs=[SMEM] + [VMEM] * 4,
        out_specs=VMEM,
        scratch_shapes=[
            pltpu.VMEM((length, 2 * dim), BF16),
            pltpu.VMEM((2 * dim, length), BF16),
            pltpu.VMEM((length, 2 * dim), BF16),
            pltpu.VMEM((2 * dim, length), BF16),
            pltpu.VMEM((dim, length), F32),
            pltpu.VMEM((dim, outer[0]), F32),
            pltpu.VMEM((dim, outer[0]), F32),
        ],
        compiler_params=pltpu.CompilerParams(vmem_limit_bytes=VMEM_LIMIT),
        name="attend_back",
    )(lengths, x, o, lse, do)


def axis_steps(axis):
    steps, step = [], 1
    while step < lax.axis_size(axis):
        steps.append((axis, step))
        step *= 2
    assert step == lax.axis_size(axis)
    return steps


def stage_plans():
    sp_steps, dp_steps = axis_steps("sp"), axis_steps("dp")
    plane, rest = sp_steps[1:] + dp_steps[:1], dp_steps[1:]

    def groups(steps):
        return [steps[i : i + 2] for i in range(0, len(steps), 2)]

    plans = [sp_steps[:1]] + groups(plane) + groups(rest), [sp_steps[:1]] + groups(rest) + groups(plane)
    return tuple([stage for stage in plan if stage] for plan in plans)


def stage_masks(stage):
    masks = []
    for number in range(1, 1 << len(stage)):
        mask = {"sp": 0, "dp": 0}
        for i, (axis, step) in enumerate(stage):
            if number & (1 << i):
                mask[axis] += step
        masks.append((mask["sp"], mask["dp"]))
    return masks


def place_in(stage, number):
    place = 0
    for i, (axis, step) in enumerate(stage):
        bit = lax.rem(lax.axis_index(axis) // step, 2)
        place = place + (1 << i) * (1 - bit if number & (1 << i) else bit)
    return place


def exchange_plan(rows, stages, offset=0):
    sizes, size = [], rows
    for stage in stages:
        group = 1 << len(stage)
        splits = size % (16 * group) == 0
        size = size // group if splits else size
        sizes.append((splits, size, offset))
        offset += (group - 1) * size
    return sizes, offset, size


class Reduction:
    def __init__(self, base, rows, staged, stages, acc, stage, land, full, send, recv):
        self.stages, self.acc, self.stage, self.land, self.full = stages, acc, stage, land, full
        self.send, self.recv, self.low = send, recv, base
        self.sizes, _, self.own = exchange_plan(rows, stages, staged)
        self.first_sem = [sum((1 << len(s)) - 1 for s in stages[:k]) for k in range(len(stages))]

    def at(self, low, size):
        return pl.ds(pl.multiple_of(low, 16), size)

    def slot(self, k, i):
        _, size, offset = self.sizes[k]
        return slice(offset + i * size, offset + (i + 1) * size)

    def copies(self, way, k):
        splits, size, _ = self.sizes[k]
        out = []
        for i, masks in enumerate(stage_masks(self.stages[k])):
            if way == 0:
                source = self.stage.at[self.slot(k, i if splits else 0), :]
                target = self.land.at[self.slot(k, i), :]
            else:
                source = target = self.full.at[self.at(self.low, size), :]
            out.append(
                pltpu.make_async_remote_copy(
                    src_ref=source,
                    dst_ref=target,
                    send_sem=self.send.at[way, self.first_sem[k] + i],
                    recv_sem=self.recv.at[way, self.first_sem[k] + i],
                    device_id=peer_at(*masks),
                    device_id_type=MESH,
                )
            )
        return out

    def sum_send(self, k):
        splits, size, _ = self.sizes[k]
        copies = self.copies(0, k)
        for i, copy in enumerate(copies):
            if splits:
                away = self.low + place_in(self.stages[k], i + 1) * size
                self.stage[self.slot(k, i), :] = self.acc[self.at(away, size), :].astype(BF16)
            elif i == 0:
                self.stage[self.slot(k, 0), :] = self.acc[self.at(self.low, size), :].astype(BF16)
            copy.start()

    def sum_recv(self, k):
        splits, size, _ = self.sizes[k]
        copies = self.copies(0, k)
        for copy in copies:
            copy.wait()
        values = [self.land[self.slot(k, i), :].astype(F32) for i in range(len(copies))]
        if splits:
            self.low = self.low + place_in(self.stages[k], 0) * size
            values = [self.acc[self.at(self.low, size), :]] + values
        else:
            values = [self.stage[self.slot(k, 0), :].astype(F32)] + values
        while len(values) > 1:
            values = [values[i] + values[i + 1] for i in range(0, len(values), 2)]
        self.acc[self.at(self.low, size), :] = values[0]

    def close(self):
        where = self.at(self.low, self.own)
        self.full[where, :] = self.acc[where, :].astype(BF16)

    def share_send(self, k):
        if self.sizes[k][0]:
            for copy in self.copies(1, k):
                copy.start()

    def share_recv(self, k):
        splits, size, _ = self.sizes[k]
        if splits:
            for copy in self.copies(1, k):
                copy.wait()
            self.low = self.low - place_in(self.stages[k], 0) * size


def advance(streams, position):
    for stream in streams:
        n = len(stream.stages)
        if 0 < position <= n:
            stream.sum_recv(position - 1)
        if position < n:
            stream.sum_send(position)
        else:
            if position == n:
                stream.close()
            else:
                stream.share_recv(2 * n - position)
            if position < 2 * n:
                stream.share_send(2 * n - 1 - position)


def reduction_scratch(rows_list):
    plan, _ = stage_plans()
    staged = sum(max(exchange_plan(rows, stages)[1] for stages in stage_plans()) for rows in rows_list)
    sems = sum((1 << len(stage)) - 1 for stage in plan)
    return staged, (len(rows_list), 2, sems)


def make_streams(items, acc, stage, land, full, send, recv):
    streams, staged = [], 0
    for i, (base, rows, order) in enumerate(items):
        stages = stage_plans()[order]
        streams.append(
            Reduction(base, rows, staged, stages, acc, stage, land, full, send.at[i], recv.at[i])
        )
        staged += max(exchange_plan(rows, plan)[1] for plan in stage_plans())
    return streams


def all_masks(sp):
    masks = [(mask, 0) for mask in range(1, sp)]
    for plan in stage_plans():
        for stage in plan:
            masks += [m for m in stage_masks(stage) if m not in masks]
    return masks


def halves_of(ref, rows):
    return jnp.concatenate([ref[0, rows, :], ref[1, rows, :]], axis=1)


def combine(entries):
    count = sum(e[2] for e in entries)
    safe = jnp.maximum(count, 1.0)
    mean = sum(e[2] * e[0] for e in entries) / safe
    spread = sum(e[1] + e[2] * (e[0] - mean) * (e[0] - mean) for e in entries)
    return mean, spread, count


def pick(ref):
    return ref[0:1, :], ref[1:2, :], ref[2:3, :]


def total(entries):
    return tuple(sum(e[i] for e in entries) for i in range(3))


def middle_kernel(
    sp, dp, items, taps, chunk, block, len_ref, parts, x1_ref, cot, gain3, gain4, gain5, w_out, w_point1,
    depthwise, bn_gain, bn_bias, w_point2, w_in, w_down,
    out_ref, grad_x2, heads, mid, point_two, bn_grads, full,
    ctx, x2_ref, n3_keep, point, glu, conv, low_lim, high_lim, act, hidden, n4_keep, branch, swish, branch2,
    grad_x3, grad_y, grad_conv, grad_glu, grad_point, branch3, back_parts, tap_sums, edge_out, edge_in,
    send_box, near_box, far_box, sums, acc, stage, land,
    send, recv, local, back_send, back_recv, back_local, rim_send, rim_recv, box_send, box_recv,
    sum_send, sum_recv,
):
    me, me_dp = lax.axis_index("sp"), lax.axis_index("dp")
    frames, width = x1_ref.shape
    lanes = width // 2
    reach = taps // 2
    count = frames // chunk
    peers = sp_peers(sp)
    far_peers = [peer_at(0, mask) for mask in range(1, dp)]
    masks = all_masks(sp)
    masks += [(0, mask) for mask in range(1, dp) if (0, mask) not in masks]
    greeted = [peer_at(*mask) for mask in masks]
    length = sp * frames
    ends = ends_of(len_ref, items)
    first_frame = me * frames

    def limits(b, carry):
        rows = rows_at(b, chunk)
        frame = first_frame + b * chunk + lax.broadcasted_iota(I32, (chunk, lanes), 0)
        low, high = jnp.zeros_like(frame), jnp.full_like(frame, length)
        for end in ends:
            low = jnp.where(frame >= end, end, low)
        for end in reversed(ends):
            high = jnp.where(frame < end, end, high)
        low_lim[rows, :] = low - frame
        high_lim[rows, :] = high - 1 - frame
        return carry

    for ref in (glu, grad_conv):
        for h in range(2):
            ref[h, 0:reach, :] = jnp.zeros((reach, lanes), F32)
            ref[h, reach + frames :, :] = jnp.zeros((reach, lanes), F32)
    edge_in[...] = jnp.zeros_like(edge_in)
    send_box[...] = jnp.zeros_like(send_box)
    greet(greeted)
    lax.fori_loop(0, count, limits, 0)
    tap_sums[...] = jnp.zeros_like(tap_sums)
    sums[...] = jnp.zeros_like(sums)
    await_greetings(greeted)

    def moves(c, source, target, send_sems, recv_sems, local_sems):
        out = [
            pltpu.make_async_remote_copy(
                src_ref=source(peer[1], c),
                dst_ref=target(me, c),
                send_sem=send_sems.at[i, c],
                recv_sem=recv_sems.at[i, c],
                device_id=peer,
                device_id_type=MESH,
            )
            for i, peer in enumerate(peers)
        ]
        return out + [pltpu.make_async_copy(source(me, c), target(me, c), local_sems.at[c])]

    def by_frames(ref):
        return lambda device, c: ref.at[:, frame_cols(device, frames, c, chunk)]

    def by_head(ref):
        return lambda device, c: ref.at[device, :, rows_at(c, chunk)]

    def context_moves(c):
        return moves(c, by_frames(parts), by_head(ctx), send, recv, local)

    def begin(c, carry):
        for copy in context_moves(c):
            copy.start()
        return carry

    lax.fori_loop(0, count, begin, 0)

    def open_step(c, carry):
        rows = rows_at(c, chunk)
        for copy in context_moves(c):
            copy.wait()
        context = ctx[:, :, rows].reshape(width, chunk)
        x2 = x1_ref[rows, :] + dg(context, w_out[...], 0, 0)
        x2_ref[rows, :] = x2
        hat, _ = norm_parts(x2)
        n3 = (hat * row_of(gain3)).astype(BF16)
        n3_keep[rows, :] = n3
        pair = dg(n3, w_point1[...], 1, 0)
        point[rows, :] = pair
        gated = (pair[:, :width] * sigmoid(pair[:, width:])).astype(BF16).astype(F32)
        where = pl.ds(pl.multiple_of(reach + c * chunk, 8), chunk)
        glu[0, where, :] = gated[:, :lanes]
        glu[1, where, :] = gated[:, lanes:]
        return carry

    lax.fori_loop(0, count, open_step, 0)

    def rim_copies(call, side, source, target):
        peer = (me_dp, me - 1 if side == 0 else me + 1)
        return pltpu.make_async_remote_copy(
            src_ref=source, dst_ref=target, send_sem=rim_send.at[call, side], recv_sem=rim_recv.at[call, side],
            device_id=peer, device_id_type=MESH,
        )

    def swap_rims(call, sources, targets):
        @pl.when(me > 0)
        def _():
            rim_copies(call, 0, sources[0], targets[1]).start()

        @pl.when(me < sp - 1)
        def _():
            rim_copies(call, 1, sources[1], targets[0]).start()

    def await_rims(call, sources, targets):
        @pl.when(me > 0)
        def _():
            rim_copies(call, 0, sources[0], targets[1]).wait_send()
            rim_copies(call, 1, sources[1], targets[0]).wait_recv()

        @pl.when(me < sp - 1)
        def _():
            rim_copies(call, 1, sources[1], targets[0]).wait_send()
            rim_copies(call, 0, sources[0], targets[1]).wait_recv()

    for side, rows in ((0, slice(reach, 2 * reach)), (1, slice(frames, frames + reach))):
        for h in range(2):
            edge_out[side, 0:reach, h * lanes : (h + 1) * lanes] = glu[h, rows, :]
    glu_rims = (
        [edge_out.at[0, 0:reach, :], edge_out.at[1, 0:reach, :]],
        [edge_in.at[0, 0:reach, :], edge_in.at[1, 0:reach, :]],
    )
    swap_rims(0, *glu_rims)

    zero = jnp.zeros((block, lanes), F32)

    def conv_step(b, carry):
        low, high = low_lim[rows_at(b, block), :], high_lim[rows_at(b, block), :]
        start = pl.multiple_of(b * block, block)
        result = [zero, zero]
        for tap in range(taps):
            shift = tap - reach
            inside = (low <= shift) if shift < 0 else (high >= shift)
            for h in range(2):
                view = glu.at[h, pl.ds(start, block + 2 * reach), :]
                term = jnp.where(inside, view[tap : tap + block, :], 0.0)
                result[h] = result[h] + depthwise[tap : tap + 1, h * lanes : (h + 1) * lanes].astype(F32) * term
        valid = (first_frame + start + lax.broadcasted_iota(I32, (block, lanes), 0)) < ends[-1]
        for h in range(2):
            conv[h, rows_at(b, block), :] = result[h]
            sums[0:1, h * lanes : (h + 1) * lanes] += jnp.sum(jnp.where(valid, result[h], 0.0), axis=0, keepdims=True)
        return carry

    blocks = frames // block
    lax.fori_loop(1, blocks - 1, conv_step, 0)
    await_rims(0, *glu_rims)
    for h in range(2):
        glu[h, 0:reach, :] = edge_in[0, 0:reach, h * lanes : (h + 1) * lanes]
        glu[h, reach + frames :, :] = edge_in[1, 0:reach, h * lanes : (h + 1) * lanes]
    conv_step(0, 0)
    conv_step(blocks - 1, 0)

    own_count = jnp.clip(ends[-1] - first_frame, 0, frames).astype(F32)
    own_mean = sums[0:1, :] / jnp.maximum(own_count, 1.0)
    sums[0:1, :] = jnp.zeros((1, width), F32)

    def spread_step(c, carry):
        rows = rows_at(c, chunk)
        valid = (first_frame + c * chunk + lax.broadcasted_iota(I32, (chunk, width), 0)) < ends[-1]
        apart = jnp.where(valid, halves_of(conv, rows) - own_mean, 0.0)
        sums[1:2, :] += jnp.sum(apart * apart, axis=0, keepdims=True)
        return carry

    lax.fori_loop(0, count, spread_step, 0)

    def box_copies(call, stage):
        group = peers if stage == 0 else far_peers
        target = near_box if stage == 0 else far_box
        base = 0 if stage == 0 else sp - 1
        return [
            pltpu.make_async_remote_copy(
                src_ref=send_box.at[call, stage],
                dst_ref=target.at[call, i],
                send_sem=box_send.at[call, base + i],
                recv_sem=box_recv.at[call, base + i],
                device_id=peer,
                device_id_type=MESH,
            )
            for i, peer in enumerate(group)
        ]

    def box_begin(call, stage, rows):
        for i, row in enumerate(rows):
            send_box[call, stage, i : i + 1, :] = row
        for copy in box_copies(call, stage):
            copy.start()

    def box_end(call, stage, rows, merge):
        target = near_box if stage == 0 else far_box
        copies = box_copies(call, stage)
        for copy in copies:
            copy.wait()
        return merge([rows] + [pick(target[call, i]) for i in range(len(copies))])

    stats = (own_mean, sums[1:2, :], jnp.full((1, width), 1.0, F32) * own_count)
    sums[1:2, :] = jnp.zeros((1, width), F32)
    box_begin(0, 0, stats)
    stats = box_end(0, 0, stats, combine)
    box_begin(0, 1, stats)
    mean, spread, frame_count = box_end(0, 1, stats, combine)
    inv_std = lax.rsqrt(spread / frame_count + EPS)
    norm_gain, norm_bias = row_of(bn_gain), row_of(bn_bias)

    def heart_step(c, carry):
        rows = rows_at(c, chunk)
        normed = (halves_of(conv, rows) - mean) * inv_std
        y = normed * norm_gain + norm_bias
        sig_y = sigmoid(y)
        w = (y * sig_y).astype(BF16)
        swish[rows, :] = w
        x3 = x2_ref[rows, :] + dg(w, w_point2[...], 1, 0)
        hat4, inv4 = norm_parts(x3)
        g4 = row_of(gain4)
        n4 = (hat4 * g4).astype(BF16)
        n4_keep[rows, :] = n4
        a = dg(n4, w_in[...], 1, 0)
        sig = sigmoid(a)
        s = (a * sig).astype(BF16)
        act[rows, :] = s
        x4 = x3 + 0.5 * dg(s, w_down[...], 1, 0)
        hat5, inv5 = norm_parts(x4)
        g5 = row_of(gain5)
        out_ref[rows, :] = (hat5 * g5).astype(BF16)
        top = cot[rows, :].astype(F32)
        mid[3 * width + 4 : 3 * width + 5, :] += jnp.sum(top * hat5, axis=0, keepdims=True)
        grad_x4 = norm_back(top, hat5, inv5, g5)
        low_grad = (0.5 * grad_x4).astype(BF16)
        branch[rows, :] = low_grad
        grad = dg(low_grad, w_down[...], 1, 1)
        low_hidden = (grad * (sig * (1.0 + a * (1.0 - sig)))).astype(BF16)
        hidden[rows, :] = low_hidden
        grad = dg(low_hidden, w_in[...], 1, 1)
        mid[3 * width + 3 : 3 * width + 4, :] += jnp.sum(grad * hat4, axis=0, keepdims=True)
        grad3 = grad_x4 + norm_back(grad, hat4, inv4, g4)
        grad_x3[rows, :] = grad3
        low_grad = grad3.astype(BF16)
        branch2[rows, :] = low_grad
        grad = dg(low_grad, w_point2[...], 1, 1) * (sig_y * (1.0 + y * (1.0 - sig_y)))
        grad_y[0, rows, :] = grad[:, :lanes]
        grad_y[1, rows, :] = grad[:, lanes:]
        sums[2:3, :] += jnp.sum(grad, axis=0, keepdims=True)
        sums[3:4, :] += jnp.sum(grad * normed, axis=0, keepdims=True)
        return carry

    mid[3 * width :, :] = jnp.zeros((width, width), F32)
    lax.fori_loop(0, count, heart_step, 0)

    pair = (sums[2:3, :], sums[3:4, :], jnp.zeros((1, width), F32))
    box_begin(1, 0, pair)
    for side, rows in ((0, slice(0, reach)), (1, slice(frames - reach, frames))):
        for h in range(2):
            cols = slice(h * lanes, (h + 1) * lanes)
            edge_out[side, reach : 2 * reach, cols] = grad_y[h, rows, :]
            edge_out[side, 2 * reach : 3 * reach, cols] = conv[h, rows, :]
    grad_rims = (
        [edge_out.at[0, reach : 3 * reach, :], edge_out.at[1, reach : 3 * reach, :]],
        [edge_in.at[0, reach : 3 * reach, :], edge_in.at[1, reach : 3 * reach, :]],
    )
    swap_rims(1, *grad_rims)
    wide = w_in.shape[1]
    streams = make_streams(
        [(0, wide, 0), (wide, wide, 1)], acc, stage, land, full, sum_send, sum_recv
    )
    steps = len(stage_plans()[0])
    for j in range(0, wide, width):
        acc[j : j + width, :] = dg(act[:, j : j + width], branch[...], 0, 0)
    advance(streams[:1], 0)
    pair = box_end(1, 0, pair, total)
    box_begin(1, 1, pair)
    for j in range(0, wide, width):
        acc[wide + j : wide + j + width, :] = dg(n4_keep[...], hidden[:, j : j + width], 0, 0)
    advance(streams[1:], 0)
    advance(streams[:1], 1)
    point_two[...] = dg(swish[...], branch2[...], 0, 0)
    advance(streams[1:], 1)
    await_rims(1, *grad_rims)
    bias_sum, gain_sum, _ = box_end(1, 1, pair, total)
    bn_grads[0:1, :] = gain_sum
    bn_grads[1:2, :] = bias_sum
    bn_grads[2:8, :] = jnp.zeros((6, width), F32)

    scale = norm_gain * inv_std
    slope = -inv_std * inv_std * norm_gain * gain_sum / frame_count
    shift_all = -inv_std * norm_gain * bias_sum / frame_count

    def conv_grad(grad, value, frame, h):
        cols = slice(h * lanes, (h + 1) * lanes)
        extra = (value - mean[:, cols]) * slope[:, cols] + shift_all[:, cols]
        return grad * scale[:, cols] + jnp.where(frame < ends[-1], extra, 0.0)

    def grad_conv_step(c, carry):
        rows = rows_at(c, chunk)
        frame = first_frame + c * chunk + lax.broadcasted_iota(I32, (chunk, lanes), 0)
        where = pl.ds(pl.multiple_of(reach + c * chunk, 8), chunk)
        for h in range(2):
            grad_conv[h, where, :] = conv_grad(grad_y[h, rows, :], conv[h, rows, :], frame, h)
        return carry

    lax.fori_loop(0, count, grad_conv_step, 0)
    for side, rows, begin_frame in (
        (0, slice(0, reach), first_frame - reach),
        (1, slice(reach + frames, 2 * reach + frames), first_frame + frames),
    ):
        frame = begin_frame + lax.broadcasted_iota(I32, (reach, lanes), 0)
        for h in range(2):
            cols = slice(h * lanes, (h + 1) * lanes)
            grad_conv[h, rows, :] = conv_grad(
                edge_in[side, reach : 2 * reach, cols], edge_in[side, 2 * reach : 3 * reach, cols], frame, h
            )

    def conv_back_step(b, carry):
        low, high = low_lim[rows_at(b, block), :], high_lim[rows_at(b, block), :]
        start = pl.multiple_of(b * block, block)
        result = [zero, zero]
        here = [glu[h, pl.ds(pl.multiple_of(reach + start, 8), block), :] for h in range(2)]
        for tap in range(taps):
            shift = reach - tap
            inside = (low <= shift) if shift < 0 else (high >= shift)
            at = reach + shift
            for h in range(2):
                view = grad_conv.at[h, pl.ds(start, block + 2 * reach), :]
                term = jnp.where(inside, view[at : at + block, :], 0.0)
                result[h] = result[h] + depthwise[tap : tap + 1, h * lanes : (h + 1) * lanes].astype(F32) * term
                tap_sums[tap, h] += jnp.sum((here[h] * term).reshape(block // 8, 8, lanes), axis=0)
        for h in range(2):
            grad_glu[h, rows_at(b, block), :] = result[h]
        return carry

    points = list(range(2, 2 * steps + 1))
    advance(streams, points.pop(0))
    lax.fori_loop(0, blocks // 2, conv_back_step, 0)
    advance(streams, points.pop(0))
    lax.fori_loop(blocks // 2, blocks, conv_back_step, 0)
    advance(streams, points.pop(0))

    def back_moves(c):
        return moves(c, by_head(back_parts), by_frames(heads), back_send, back_recv, back_local)

    def close_step(c, carry):
        rows = rows_at(c, chunk)
        grad = halves_of(grad_glu, rows)
        value, gate = point[rows, :width], sigmoid(point[rows, width:])
        low_grad = jnp.concatenate([grad * gate, grad * value * gate * (1.0 - gate)], axis=1).astype(BF16)
        grad_point[rows, :] = low_grad
        grad = dg(low_grad, w_point1[...], 1, 1)
        hat, inv = norm_parts(x2_ref[rows, :])
        mid[3 * width + 2 : 3 * width + 3, :] += jnp.sum(grad * hat, axis=0, keepdims=True)
        grad2 = grad_x3[rows, :] + norm_back(grad, hat, inv, row_of(gain3))
        grad_x2[rows, :] = grad2
        low_grad = grad2.astype(BF16)
        branch3[rows, :] = low_grad
        back_parts[:, :, rows] = dg(w_out[...], low_grad, 1, 1).astype(BF16).reshape(sp, width // sp, chunk)
        for copy in back_moves(c):
            copy.start()
        return carry

    lax.fori_loop(0, count // 2, close_step, 0)
    advance(streams, points.pop(0))
    lax.fori_loop(count // 2, count, close_step, 0)
    for j in range(2):
        mid[j * width : (j + 1) * width, :] = dg(n3_keep[...], grad_point[:, j * width : (j + 1) * width], 0, 0)
    mid[2 * width : 3 * width, :] = dg(ctx[...].reshape(width, frames), branch3[...], 1, 0)
    for tap in range(taps):
        row = 3 * width + 8 + tap
        for h in range(2):
            mid[row : row + 1, h * lanes : (h + 1) * lanes] = jnp.sum(tap_sums[tap, h], axis=0, keepdims=True)
    while points:
        advance(streams, points.pop(0))

    def finish(c, carry):
        for copy in back_moves(c):
            copy.wait()
        return carry

    lax.fori_loop(0, count, finish, 0)


def middle(
    lengths, parts, x1, cot, gain3, gain4, gain5, w_out, w_point1, depthwise, bn_gain, bn_bias, w_point2,
    w_in, w_down, dp,
):
    frames, width = x1.shape
    length = parts.shape[1]
    sp = length // frames
    wide = w_in.shape[1]
    taps = depthwise.shape[0]
    reach = taps // 2
    chunk = min(256, frames)
    count = frames // chunk
    lanes = width // 2
    staged, sems = reduction_scratch([wide, wide])
    keep, low_keep = pltpu.VMEM((frames, width), F32), pltpu.VMEM((frames, width), BF16)
    split = pltpu.VMEM((2, frames, lanes), F32)
    rimmed = pltpu.VMEM((2, frames + 2 * reach, lanes), F32)
    rims = pltpu.VMEM((2, 3 * reach, width), F32)
    moves = [DMA((sp - 1, count)), DMA((sp - 1, count)), DMA((count,))]
    return pl.pallas_call(
        functools.partial(middle_kernel, sp, dp, lengths.shape[1], taps, chunk, 32),
        out_shape=[
            jax.ShapeDtypeStruct((frames, width), BF16),
            jax.ShapeDtypeStruct((frames, width), F32),
            jax.ShapeDtypeStruct(parts.shape, BF16),
            jax.ShapeDtypeStruct((4 * width, width), F32),
            jax.ShapeDtypeStruct((width, width), F32),
            jax.ShapeDtypeStruct((8, width), F32),
            jax.ShapeDtypeStruct((2 * wide, width), BF16),
        ],
        in_specs=[SMEM, pl.BlockSpec(memory_space=pl.ANY)] + [VMEM] * 13,
        out_specs=[VMEM] * 7,
        scratch_shapes=[
            pltpu.VMEM((sp, width // sp, frames), BF16),
            keep,
            low_keep,
            pltpu.VMEM((frames, 2 * width), F32),
            rimmed,
            split,
            pltpu.VMEM((frames, lanes), I32),
            pltpu.VMEM((frames, lanes), I32),
            pltpu.VMEM((frames, wide), BF16),
            pltpu.VMEM((frames, wide), BF16),
            low_keep,
            low_keep,
            low_keep,
            low_keep,
            keep,
            split,
            rimmed,
            split,
            pltpu.VMEM((frames, 2 * width), BF16),
            low_keep,
            pltpu.VMEM((sp, width // sp, frames), BF16),
            pltpu.VMEM((taps, 2, 8, lanes), F32),
            rims,
            rims,
            pltpu.VMEM((2, 2, 8, width), F32),
            pltpu.VMEM((2, sp - 1, 8, width), F32),
            pltpu.VMEM((2, dp - 1, 8, width), F32),
            pltpu.VMEM((8, width), F32),
            pltpu.VMEM((2 * wide, width), F32),
            pltpu.VMEM((staged, width), BF16),
            pltpu.VMEM((staged, width), BF16),
        ]
        + moves
        + moves
        + [DMA((2, 2)), DMA((2, 2)), DMA((2, sp + dp - 2)), DMA((2, sp + dp - 2)), DMA(sems), DMA(sems)],
        compiler_params=pltpu.CompilerParams(
            collective_id=1, has_side_effects=True, vmem_limit_bytes=VMEM_LIMIT
        ),
        name="middle",
    )(
        lengths, parts, x1, cot, gain3, gain4, gain5, w_out, w_point1, depthwise, bn_gain, bn_bias, w_point2,
        w_in, w_down,
    )


def back_kernel(
    sp, chunk, parts, trig, tok, x1_ref, n2_ref, grad_x2, gain1, gain2, w_in, w_out, w_qkv, mid, point_two,
    grad_ref, full, heads, joined, n1_keep, hat_keep, branch, act, slope, hidden, grad_x1, gains, acc, stage, land,
    send, recv, local, sum_send, sum_recv,
):
    me = lax.axis_index("sp")
    frames, width = tok.shape
    wide = w_in.shape[1]
    half = trig.shape[0] // 2
    dim = 2 * half
    count = frames // chunk
    peers = sp_peers(sp)
    greeted = [peer_at(*mask) for mask in all_masks(sp)]
    greet(greeted)
    unit = 4 * width
    last = 4 * unit
    streams = make_streams(
        [(0, unit, 1), (unit, unit, 1), (2 * unit, unit, 0), (3 * unit, unit, 0), (last, 16, 0)],
        acc, stage, land, full, sum_send, sum_recv,
    )
    early, qkv, down, up, rest = ([stream] for stream in streams)
    acc[0:unit, :] = mid[...]
    acc[last : last + 16, :] = jnp.zeros((16, width), F32)
    gains[...] = jnp.zeros_like(gains)
    await_greetings(greeted)

    def copies(c):
        out = [
            pltpu.make_async_remote_copy(
                src_ref=parts.at[:, frame_cols(peer[1], frames, c, chunk)],
                dst_ref=heads.at[me, :, rows_at(c, chunk)],
                send_sem=send.at[i, c],
                recv_sem=recv.at[i, c],
                device_id=peer,
                device_id_type=MESH,
            )
            for i, peer in enumerate(peers)
        ]
        own = pltpu.make_async_copy(
            parts.at[:, frame_cols(me, frames, c, chunk)], heads.at[me, :, rows_at(c, chunk)], local.at[c]
        )
        return out + [own]

    def begin(c, carry):
        for copy in copies(c):
            copy.start()
        return carry

    lax.fori_loop(0, count, begin, 0)
    advance(early, 0)

    def again(c, carry):
        rows = rows_at(c, chunk)
        hat, inv = norm_parts(tok[rows, :].astype(F32))
        hat_keep[rows, :] = hat
        n1 = (hat * row_of(gain1)).astype(BF16)
        n1_keep[rows, :] = n1
        a = dg(n1, w_in[...], 1, 0)
        sig = sigmoid(a)
        act[rows, :] = (a * sig).astype(BF16)
        slope[rows, :] = sig * (1.0 + a * (1.0 - sig))
        return carry

    lax.fori_loop(0, count // 2, again, 0)
    advance(early, 1)
    lax.fori_loop(count // 2, count, again, 0)

    def arrive(c, carry):
        rows = rows_at(c, chunk)
        for copy in copies(c):
            copy.wait()
        sine, cosine = trig[0:half, rows], trig[half:, rows]
        for head in range(sp):
            for part in range(2):
                first = heads[head, part * dim : part * dim + half, rows].astype(F32)
                second = heads[head, part * dim + half : (part + 1) * dim, rows].astype(F32)
                low = part * width + head * dim
                joined[low : low + half, rows] = (first * cosine + second * sine).astype(BF16)
                joined[low + half : low + dim, rows] = (second * cosine - first * sine).astype(BF16)
            low = 2 * width + head * dim
            joined[low : low + dim, rows] = heads[head, 2 * dim : 3 * dim, rows]
        grad = dg(joined[:, rows], w_qkv[...], 0, 1)
        hat, inv = norm_parts(x1_ref[rows, :])
        gains[1:2, :] += jnp.sum(grad * hat, axis=0, keepdims=True)
        grad = grad_x2[rows, :] + norm_back(grad, hat, inv, row_of(gain2))
        grad_x1[rows, :] = grad
        branch[rows, :] = (0.5 * grad).astype(BF16)
        return carry

    steps = len(stage_plans()[0])
    points = list(range(2, 2 * steps + 1))
    for c in range(count):
        if c > 0 and points:
            advance(early, points.pop(0))
        lax.fori_loop(c, c + 1, arrive, 0)
    for j in range(0, wide, width):
        acc[2 * unit + j : 2 * unit + j + width, :] = dg(act[:, j : j + width], branch[...], 0, 0)
    advance(down, 0)
    acc[unit : unit + 3 * width, :] = dg(joined[...], n2_ref[...], 1, 0)
    acc[unit + 3 * width : 2 * unit, :] = point_two[...]
    advance(qkv, 0)

    def through(c, carry):
        rows = rows_at(c, chunk)
        grad = dg(branch[rows, :], w_out[...], 1, 1)
        low_hidden = (grad * slope[rows, :]).astype(BF16)
        hidden[rows, :] = low_hidden
        grad = dg(low_hidden, w_in[...], 1, 1)
        hat = hat_keep[rows, :]
        gains[0:1, :] += jnp.sum(grad * hat, axis=0, keepdims=True)
        _, inv = norm_parts(tok[rows, :].astype(F32))
        grad_ref[rows, :] = (grad_x1[rows, :] + norm_back(grad, hat, inv, row_of(gain1))).astype(BF16)
        return carry

    lax.fori_loop(0, count, through, 0)
    for j in range(0, wide, width):
        acc[3 * unit + j : 3 * unit + j + width, :] = dg(n1_keep[...], hidden[:, j : j + width], 0, 0)
    advance(up, 0)
    acc[last : last + 8, :] = gains[...]
    advance(rest, 0)
    while points:
        advance(early, points.pop(0))
    for position in range(1, 2 * steps + 1):
        advance(down + qkv + up + rest, position)


def back(parts, trig, tok, x1, n2, grad_x2, gain1, gain2, w_in, w_out, w_qkv, mid, point_two):
    frames, width = tok.shape
    head_width, length = parts.shape
    sp = length // frames
    chunk = min(256, frames)
    count = frames // chunk
    wide = w_in.shape[1]
    rows = 16 * width + 16
    staged, sems = reduction_scratch([4 * width] * 4 + [16])
    low_keep, keep = pltpu.VMEM((frames, width), BF16), pltpu.VMEM((frames, width), F32)
    return pl.pallas_call(
        functools.partial(back_kernel, sp, chunk),
        out_shape=[
            jax.ShapeDtypeStruct((frames, width), BF16),
            jax.ShapeDtypeStruct((rows, width), BF16),
        ],
        in_specs=[pl.BlockSpec(memory_space=pl.ANY)] + [VMEM] * 12,
        out_specs=[VMEM] * 2,
        scratch_shapes=[
            pltpu.VMEM((sp, head_width, frames), BF16),
            pltpu.VMEM((3 * width, frames), BF16),
            low_keep,
            keep,
            low_keep,
            pltpu.VMEM((frames, wide), BF16),
            pltpu.VMEM((frames, wide), F32),
            pltpu.VMEM((frames, wide), BF16),
            keep,
            pltpu.VMEM((8, width), F32),
            pltpu.VMEM((rows, width), F32),
            pltpu.VMEM((staged, width), BF16),
            pltpu.VMEM((staged, width), BF16),
            DMA((sp - 1, count)),
            DMA((sp - 1, count)),
            DMA((count,)),
            DMA(sems),
            DMA(sems),
        ],
        compiler_params=pltpu.CompilerParams(
            collective_id=2, has_side_effects=True, vmem_limit_bytes=VMEM_LIMIT
        ),
        name="back",
    )(parts, trig, tok, x1, n2, grad_x2, gain1, gain2, w_in, w_out, w_qkv, mid, point_two)


def unpack_kernel(
    taps, full_two, full, bn_grads, output, input_grad,
    output_to, input_to, gain1_to, in_one_to, out_one_to, gain2_to, qkv_to, out_weight_to, gain3_to, point_one_to,
    depthwise_to, bn_gain_to, bn_bias_to, point_two_to, gain4_to, in_two_to, out_two_to, gain5_to,
    in_one, out_one, qkv, point_one, point_two, out_weight, in_two, out_two, depthwise, sems,
):
    width = full.shape[1]
    unit = 4 * width
    copies = []

    def send(source, target):
        copies.append(pltpu.make_async_copy(source, target, sems.at[len(copies)]))
        copies[-1].start()

    def block(ref, base):
        return ref[base : base + width, :].astype(F32)

    send(output, output_to)
    send(input_grad, input_to)
    for j in range(0, unit, width):
        out_two[j : j + width, :] = block(full_two, j)
    send(out_two, out_two_to)
    for j in range(0, unit, width):
        in_two[:, j : j + width] = block(full_two, unit + j)
    send(in_two, in_two_to)
    for j in range(0, unit, width):
        out_one[j : j + width, :] = block(full, 2 * unit + j)
    send(out_one, out_one_to)
    for j in range(0, unit, width):
        in_one[:, j : j + width] = block(full, 3 * unit + j)
    send(in_one, in_one_to)
    for j in range(0, 2 * width, width):
        point_one[:, j : j + width] = block(full, j)
    send(point_one, point_one_to)
    out_weight[...] = block(full, 2 * width)
    send(out_weight, out_weight_to)
    point_two[...] = block(full, unit + 3 * width)
    send(point_two, point_two_to)
    for j in range(0, 3 * width, width):
        qkv[:, j : j + width] = block(full, unit + j).T
    send(qkv, qkv_to)
    small = full[3 * width : 3 * width + 64, :].astype(F32)
    depthwise[...] = small[8 : 8 + taps]
    send(depthwise, depthwise_to)
    rest = full[4 * unit : 4 * unit + 16, :].astype(F32)
    for ref, row in (
        (gain1_to, rest[0]), (gain2_to, rest[1]), (gain3_to, small[2]), (gain4_to, small[3]), (gain5_to, small[4]),
        (bn_gain_to, bn_grads[0, :]), (bn_bias_to, bn_grads[1, :]),
    ):
        ref[...] = row
    for copy in copies:
        copy.wait()


def unpack(full_two, full, bn_grads, output, input_grad, taps):
    width = full.shape[1]
    row, square, tall, flat = (width,), (width, width), (4 * width, width), (width, 4 * width)
    thrice, twice = (width, 3 * width), (width, 2 * width)
    anywhere = pl.BlockSpec(memory_space=pl.ANY)
    shapes = [
        output.shape, input_grad.shape, row, flat, tall, row, thrice, square, row, twice, (taps, width), row, row,
        square, row, flat, tall, row,
    ]
    return pl.pallas_call(
        functools.partial(unpack_kernel, taps),
        out_shape=[jax.ShapeDtypeStruct(shape, F32 if i > 1 else BF16) for i, shape in enumerate(shapes)],
        in_specs=[VMEM] * 5,
        out_specs=[VMEM if shape == row else anywhere for shape in shapes],
        scratch_shapes=[
            pltpu.VMEM(shape, F32)
            for shape in (flat, tall, thrice, twice, square, square, flat, tall, (taps, width))
        ]
        + [DMA((11,))],
        compiler_params=pltpu.CompilerParams(vmem_limit_bytes=VMEM_LIMIT),
        name="unpack",
    )(full_two, full, bn_grads, output, input_grad)


def on_device(
    tokens, ln1_gain, ffn1_in, ffn1_out, ln2_gain, w_qkv, w_out, ln3_gain, w_point1, depthwise,
    bn_gain, bn_bias, w_point2, ln4_gain, ffn2_in, ffn2_out, ln5_gain, lengths, cotangent,
):
    width = tokens.shape[2]
    sp, dp = lax.axis_size("sp"), lax.axis_size("dp")
    assert HEADS == sp and ffn1_in.shape[1] == ffn2_in.shape[1] == 4 * width
    half = width // HEADS // 2
    turns = 10000.0 ** (-np.arange(half, dtype=np.float64) / half) / (2 * np.pi)
    high = np.round(turns * 4096.0) / 4096.0
    freq = jnp.asarray(np.stack([high, turns - high], axis=1), F32)
    x1, n2, trig, heads = front(lengths, tokens[0], ln1_gain, ffn1_in, ffn1_out, ln2_gain, w_qkv, freq, sp)
    context, raw_context, log_sums = attend(heads, lengths)
    output, grad_x2, grad_context, mid, point_two, bn_grads, full_two = middle(
        lengths, context, x1, cotangent[0], ln3_gain, ln4_gain, ln5_gain, w_out, w_point1, depthwise,
        bn_gain, bn_bias, w_point2, ffn2_in, ffn2_out, dp,
    )
    grad_heads = attend_back(heads, lengths, raw_context, log_sums, grad_context)
    input_grad, full = back(
        grad_heads, trig, tokens[0], x1, n2, grad_x2, ln1_gain, ln2_gain, ffn1_in, ffn1_out, w_qkv, mid, point_two
    )
    results = unpack(full_two, full, bn_grads, output, input_grad, depthwise.shape[0])
    return (results[0][None], results[1][None]) + tuple(results[2:])


def solution(mesh):
    split = P("dp", "sp", None)
    return jax.shard_map(
        on_device,
        mesh=mesh,
        in_specs=(split,) + (P(),) * 16 + (P("dp", None), split),
        out_specs=(split, split) + (P(),) * 16,
        check_vma=False,
    )
```

```python
import functools

import jax
import jax.numpy as jnp
import numpy as np
from jax import lax
from jax.experimental import pallas as pl
from jax.experimental.pallas import tpu as pltpu
from jax.sharding import PartitionSpec as P

HEADS = 4
EPS = 1e-05
NEG = -1e30
LN2 = float(np.log(2.0))
F32 = jnp.float32
BF16 = jnp.bfloat16
I32 = jnp.int32
MESH = pl.DeviceIdType.MESH
VMEM = pl.BlockSpec(memory_space=pltpu.VMEM)
SMEM = pl.BlockSpec(memory_space=pltpu.SMEM)
DMA = pltpu.SemaphoreType.DMA
VMEM_LIMIT = 56 * 2**20


def dg(left, right, left_dim, right_dim):
    return lax.dot_general(
        left, right, (((left_dim,), (right_dim,)), ((), ())), preferred_element_type=F32
    )


def rows_at(index, count):
    return pl.ds(pl.multiple_of(index * count, count), count)


def greet(devices):
    for device in devices:
        pl.semaphore_signal(pltpu.get_barrier_semaphore(), inc=1, device_id=device, device_id_type=MESH)


def await_greetings(devices):
    pl.semaphore_wait(pltpu.get_barrier_semaphore(), len(devices))


def flipped(axis, mask):
    me, step = lax.axis_index(axis), 1
    out = me
    while step <= mask:
        if mask & step:
            out = out + step - 2 * step * lax.rem(me // step, 2)
        step *= 2
    return out


def peer_at(sp_mask, dp_mask):
    return (flipped("dp", dp_mask), flipped("sp", sp_mask))


def sp_peers(count):
    return [peer_at(mask, 0) for mask in range(1, count)]


def row_of(ref):
    return ref[...].astype(F32).reshape(1, ref.shape[0])


def frame_cols(device, frames, c, chunk):
    return pl.ds(pl.multiple_of(device * frames + c * chunk, chunk), chunk)


def ends_of(len_ref, items):
    ends, total = [], 0
    for item in range(items):
        total = total + len_ref[0, item]
        ends.append(total)
    return ends


def segment_row(first, count, ends):
    frame = first + lax.broadcasted_iota(I32, (1, count), 1)
    segment = jnp.zeros((1, count), I32)
    for end in ends:
        segment = segment + (frame >= end).astype(I32)
    return segment


def position_row(first, count, ends):
    frame = first + lax.broadcasted_iota(I32, (1, count), 1)
    start = jnp.zeros((1, count), I32)
    for end in ends:
        start = jnp.where(frame >= end, end, start)
    return (frame - start).astype(F32)


def onehot_rows(segment, items, other, same):
    row = lax.broadcasted_iota(I32, (16, segment.shape[1]), 0)
    return jnp.where(row <= items, jnp.where(row == segment, same, other), 0.0)


def norm_parts(rows):
    centre = rows - jnp.mean(rows, axis=-1, keepdims=True)
    inv = lax.rsqrt(jnp.mean(centre * centre, axis=-1, keepdims=True) + EPS)
    return centre * inv, inv


def norm_back(grad, hat, inv, gain):
    scaled = grad * gain
    first = jnp.mean(scaled, axis=-1, keepdims=True)
    second = jnp.mean(scaled * hat, axis=-1, keepdims=True)
    return inv * (scaled - first - hat * second)


def sigmoid(x):
    return 1.0 / (1.0 + jnp.exp(-x))


def sine_cosine(position, freq_hi, freq_lo):
    turns = position * freq_hi
    turns = turns - jnp.round(turns) + position * freq_lo
    turns = turns - jnp.round(turns)
    x = turns * float(np.pi)
    x2 = x * x
    s = x * (1 + x2 * (-1 / 6 + x2 * (1 / 120 + x2 * (-1 / 5040 + x2 * (1 / 362880 - x2 / 39916800)))))
    c = 1 + x2 * (-1 / 2 + x2 * (1 / 24 + x2 * (-1 / 720 + x2 * (1 / 40320 + x2 * (-1 / 3628800 + x2 / 479001600)))))
    return 2 * s * c, 1 - 2 * s * s


def split_rows(value):
    row = lax.broadcasted_iota(I32, (16, value.shape[1]), 0)
    first = value.astype(BF16).astype(F32)
    second = (value - first).astype(BF16).astype(F32)
    third = value - first - second
    picked = jnp.where(row == 0, first, jnp.where(row == 1, second, third))
    return jnp.where(row < 3, picked, 0.0).astype(BF16)


def first_rows(count, columns):
    row = lax.broadcasted_iota(I32, (16, columns), 0)
    return jnp.where(row < count, 1.0, 0.0).astype(BF16)


def query_rows(query, segment, items, shift):
    pad = jnp.zeros((query.shape[0] - 32, query.shape[1]), BF16)
    return jnp.concatenate([query, onehot_rows(segment, items, 0.0, 1.0).astype(BF16), split_rows(shift), pad], axis=0)


def key_rows(key, segment, items):
    pad = jnp.zeros((key.shape[0] - 32, key.shape[1]), BF16)
    return jnp.concatenate(
        [key, onehot_rows(segment, items, NEG, 0.0).astype(BF16), first_rows(3, key.shape[1]), pad], axis=0
    )


def lay_queries(near, slot, frames, first, ends, items, dim, qa, lse):
    cols = slice(slot * frames, (slot + 1) * frames)
    segment = segment_row(first, frames, ends)
    for h in range(2):
        query = near[slot, h * dim : (h + 1) * dim, :]
        key = near[slot, (2 + h) * dim : (3 + h) * dim, :]
        own = jnp.sum(query.astype(F32) * key.astype(F32), axis=0, keepdims=True)
        lse[h : h + 1, cols] = own
        qa[h, :, cols] = query_rows(query, segment, items, -own)


def lay_keys(key, value, rows, first, ends, items, h, ka, va):
    dim, count = key.shape
    ka[h, rows, :] = key_rows(key, segment_row(first, count, ends), items).T
    va[h, 0:dim, rows] = value
    va[h, dim:, rows] = first_rows(1, count)


def front_kernel(
    items, chunk, block, len_ref, tok, gain1, w_in, w_out, gain2, w_qkv, freq,
    x1_ref, n2_ref, trig, act, slope, near, far, ctx, o_ref, lse, flag,
    parts, turned, qa, ka, va, acc, send, recv,
):
    me = lax.axis_index("sp")
    core, pair = lax.rem(me, 2), me // 2
    frames, width = tok.shape
    half = trig.shape[0] // 2
    dim = 2 * half
    count = frames // chunk
    peers = [peer_at(mask, 0) for mask in (1, 2, 3)]
    greet(peers)
    turned[...] = w_qkv[...].T
    ends = ends_of(len_ref, items)
    scale = float(np.log2(np.e)) * dim**-0.5

    def copies(c):
        cols = rows_at(c, chunk)
        ways = (
            (parts.at[1 - core, :, cols], near.at[core, :, cols]),
            (parts.at[core, 2 * dim :, cols], far.at[core, :, cols]),
            (parts.at[1 - core, 2 * dim :, cols], far.at[core, :, cols]),
        )
        return [
            pltpu.make_async_remote_copy(
                src_ref=source, dst_ref=target, send_sem=send.at[i, c], recv_sem=recv.at[i, c],
                device_id=peers[i], device_id_type=MESH,
            )
            for i, (source, target) in enumerate(ways)
        ]

    def step(c, carry):
        rows = rows_at(c, chunk)
        x = tok[rows, :].astype(F32)
        hat, _ = norm_parts(x)
        n1 = (hat * row_of(gain1)).astype(BF16)
        a = dg(n1, w_in[...], 1, 0)
        sig = sigmoid(a)
        s = (a * sig).astype(BF16)
        act[rows, :] = s
        slope[rows, :] = (sig * (1.0 + a * (1.0 - sig))).astype(BF16)
        x1 = x + 0.5 * dg(s, w_out[...], 1, 0)
        x1_ref[rows, :] = x1
        hat, _ = norm_parts(x1)
        n2 = (hat * row_of(gain2)).astype(BF16)
        n2_ref[rows, :] = n2
        joined = dg(turned[...], n2, 1, 1)
        sine, cosine = sine_cosine(
            position_row(me * frames + c * chunk, chunk, ends), freq[:, 0:1], freq[:, 1:2]
        )
        trig[0:half, rows] = sine
        trig[half:, rows] = cosine
        for p in range(2):
            for j in range(2):
                for part, factor in ((0, scale), (1, 1.0)):
                    low = part * width + (2 * p + j) * dim
                    first, second = joined[low : low + half], joined[low + half : low + dim]
                    low = (2 * part + j) * dim
                    parts[p, low : low + half, rows] = ((first * cosine - second * sine) * factor).astype(BF16)
                    parts[p, low + half : low + dim, rows] = (
                        (first * sine + second * cosine) * factor
                    ).astype(BF16)
                low = 2 * width + (2 * p + j) * dim
                parts[p, (4 + j) * dim : (5 + j) * dim, rows] = joined[low : low + dim].astype(BF16)

        @pl.when(c == 0)
        def _():
            await_greetings(peers)

        for copy in copies(c):
            copy.start()
        near[core, :, rows] = parts[core, :, rows]
        return carry

    lax.fori_loop(0, count, step, 0)

    def near_arrives(c, carry):
        copies(c)[0].wait()
        return carry

    lax.fori_loop(0, count, near_arrives, 0)
    reach = 2 * frames
    for slot in range(2):
        first = (2 * pair + slot) * frames
        lay_queries(near, slot, frames, first, ends, items, dim, qa, lse)
        for h in range(2):
            lay_keys(
                near[slot, (2 + h) * dim : (3 + h) * dim, :], near[slot, (4 + h) * dim : (5 + h) * dim, :],
                slice(slot * frames, (slot + 1) * frames), first, ends, items, h, ka, va,
            )

    def near_step(i, carry):
        h, cols = i // (reach // block), rows_at(lax.rem(i, reach // block), block)
        powers = jnp.exp2(dg(ka[h, 0:reach, :], qa[h, :, cols], 1, 0)).astype(BF16)
        acc[h, :, cols] = dg(va[h, :, 0:reach], powers, 1, 0)
        return carry

    lax.fori_loop(0, 2 * reach // block, near_step, 0)
    wide = min(1024, reach)

    def far_step(c, carry):
        for copy in copies(c)[1:]:
            copy.wait()
        cols = rows_at(c, chunk)
        for slot in range(2):
            first = (2 * (1 - pair) + slot) * frames + c * chunk
            rows = pl.ds(pl.multiple_of(reach + (2 * c + slot) * chunk, chunk), chunk)
            for h in range(2):
                lay_keys(
                    far[slot, h * dim : (h + 1) * dim, cols], far[slot, (2 + h) * dim : (3 + h) * dim, cols],
                    rows, first, ends, items, h, ka, va,
                )
        rows = pl.ds(pl.multiple_of(reach + 2 * c * chunk, 2 * chunk), 2 * chunk)

        def inner(i, carry):
            h, cols = i // (reach // wide), rows_at(lax.rem(i, reach // wide), wide)
            powers = jnp.exp2(dg(ka[h, rows, :], qa[h, :, cols], 1, 0)).astype(BF16)
            acc[h, :, cols] += dg(va[h, :, rows], powers, 1, 0)
            return carry

        return lax.fori_loop(0, 2 * reach // wide, inner, carry)

    lax.fori_loop(0, count, far_step, 0)
    bad = jnp.zeros((1, reach), F32)
    for h in range(2):
        total = acc[h, dim : dim + 1, :]
        value = acc[h, 0:dim, :] / total
        ctx[h] = value.astype(BF16)
        o_ref[h] = value
        lse[h : h + 1, :] = lse[h : h + 1, :] + jnp.log2(total)
        bad = jnp.maximum(bad, jnp.where(total < 2.0**60, 0.0, 1.0))
    flag[...] = jnp.broadcast_to(jnp.max(bad, axis=1, keepdims=True), flag.shape)


def front(lengths, tok, gain1, w_in, w_out, gain2, w_qkv, freq):
    frames, width = tok.shape
    wide = w_in.shape[1]
    chunk = min(256, frames)
    count = frames // chunk
    dim = width // HEADS
    reach = 2 * frames
    return pl.pallas_call(
        functools.partial(front_kernel, lengths.shape[1], chunk, min(512, reach)),
        out_shape=[
            jax.ShapeDtypeStruct((frames, width), F32),
            jax.ShapeDtypeStruct((frames, width), BF16),
            jax.ShapeDtypeStruct((dim, frames), F32),
            jax.ShapeDtypeStruct((frames, wide), BF16),
            jax.ShapeDtypeStruct((frames, wide), BF16),
            jax.ShapeDtypeStruct((2, 6 * dim, frames), BF16),
            jax.ShapeDtypeStruct((2, 4 * dim, frames), BF16),
            jax.ShapeDtypeStruct((2, dim, reach), BF16),
            jax.ShapeDtypeStruct((2, dim, reach), F32),
            jax.ShapeDtypeStruct((2, reach), F32),
            jax.ShapeDtypeStruct((8, 128), F32),
        ],
        in_specs=[SMEM] + [VMEM] * 7,
        out_specs=[VMEM] * 11,
        scratch_shapes=[
            pltpu.VMEM((2, 6 * dim, frames), BF16),
            pltpu.VMEM((3 * width, width), BF16),
            pltpu.VMEM((2, 2 * dim, reach), BF16),
            pltpu.VMEM((2, 2 * reach, 2 * dim), BF16),
            pltpu.VMEM((2, dim + 16, 2 * reach), BF16),
            pltpu.VMEM((2, dim + 16, reach), F32),
            DMA((3, count)),
            DMA((3, count)),
        ],
        compiler_params=pltpu.CompilerParams(
            collective_id=0, has_side_effects=True, vmem_limit_bytes=VMEM_LIMIT
        ),
        name="front",
    )(lengths, tok, gain1, w_in, w_out, gain2, w_qkv, freq)


def repair_kernel(
    items, block, len_ref, flag, near_hbm, far_hbm, ctx_in, o_in, lse_in, ctx_hbm, o_hbm, lse_hbm,
    near, far, ctx, o_ref, lse, qa, ka, va, sems,
):
    @pl.when(jnp.max(flag[...]) > 0.5)
    def _():
        pair = lax.axis_index("sp") // 2
        frames, dim = near.shape[2], near.shape[1] // 6
        reach = 2 * frames
        ends = ends_of(len_ref, items)
        loads = [
            pltpu.make_async_copy(near_hbm, near, sems.at[0]),
            pltpu.make_async_copy(far_hbm, far, sems.at[1]),
        ]
        for copy in loads:
            copy.start()
        for copy in loads:
            copy.wait()
        for slot in range(2):
            first, other = (2 * pair + slot) * frames, (2 * (1 - pair) + slot) * frames
            lay_queries(near, slot, frames, first, ends, items, dim, qa, lse)
            for h in range(2):
                lay_keys(
                    near[slot, (2 + h) * dim : (3 + h) * dim, :], near[slot, (4 + h) * dim : (5 + h) * dim, :],
                    slice(slot * frames, (slot + 1) * frames), first, ends, items, h, ka, va,
                )
                lay_keys(
                    far[slot, h * dim : (h + 1) * dim, :], far[slot, (2 + h) * dim : (3 + h) * dim, :],
                    slice(reach + slot * frames, reach + (slot + 1) * frames), other, ends, items, h, ka, va,
                )

        def step(i, carry):
            h, cols = i // (reach // block), rows_at(lax.rem(i, reach // block), block)
            query = qa[h, :, cols]

            def highest(j, top):
                scores = dg(ka[h, rows_at(j, block), :], query, 1, 0)
                return jnp.maximum(top, jnp.max(scores, axis=0, keepdims=True))

            top = lax.fori_loop(0, 2 * reach // block, highest, jnp.zeros((1, block), F32))

            def add(j, total):
                rows = rows_at(j, block)
                powers = jnp.exp2(dg(ka[h, rows, :], query, 1, 0) - top).astype(BF16)
                return total + dg(va[h, :, rows], powers, 1, 0)

            total = lax.fori_loop(0, 2 * reach // block, add, jnp.zeros((dim + 16, block), F32))
            value = total[0:dim, :] / total[dim : dim + 1, :]
            ctx[h, :, cols] = value.astype(BF16)
            o_ref[h, :, cols] = value
            change = top + jnp.log2(total[dim : dim + 1, :])
            row = lax.broadcasted_iota(I32, (2, block), 0)
            lse[:, cols] = lse[:, cols] + jnp.where(row == h, change, 0.0)
            return carry

        lax.fori_loop(0, 2 * reach // block, step, 0)
        stores = [
            pltpu.make_async_copy(ctx, ctx_hbm, sems.at[2]),
            pltpu.make_async_copy(o_ref, o_hbm, sems.at[3]),
            pltpu.make_async_copy(lse, lse_hbm, sems.at[4]),
        ]
        for copy in stores:
            copy.start()
        for copy in stores:
            copy.wait()


def repair(lengths, flag, near, far, ctx, o, lse):
    dim, reach = ctx.shape[1:]
    anywhere = pl.BlockSpec(memory_space=pl.ANY)
    return pl.pallas_call(
        functools.partial(repair_kernel, lengths.shape[1], min(512, reach)),
        out_shape=[jax.ShapeDtypeStruct(x.shape, x.dtype) for x in (ctx, o, lse)],
        in_specs=[SMEM, VMEM] + [anywhere] * 5,
        out_specs=[anywhere] * 3,
        input_output_aliases={4: 0, 5: 1, 6: 2},
        scratch_shapes=[
            pltpu.VMEM(near.shape, BF16),
            pltpu.VMEM(far.shape, BF16),
            pltpu.VMEM(ctx.shape, BF16),
            pltpu.VMEM(o.shape, F32),
            pltpu.VMEM(lse.shape, F32),
            pltpu.VMEM((2, 2 * dim, reach), BF16),
            pltpu.VMEM((2, 2 * reach, 2 * dim), BF16),
            pltpu.VMEM((2, dim + 16, 2 * reach), BF16),
            DMA((5,)),
        ],
        compiler_params=pltpu.CompilerParams(vmem_limit_bytes=VMEM_LIMIT),
        name="repair",
    )(lengths, flag, near, far, ctx, o, lse)


def axis_steps(axis):
    steps, step = [], 1
    while step < lax.axis_size(axis):
        steps.append((axis, step))
        step *= 2
    assert step == lax.axis_size(axis)
    return steps


def stage_plans():
    sp_steps, dp_steps = axis_steps("sp"), axis_steps("dp")
    plane, rest = sp_steps[1:] + dp_steps[:1], dp_steps[1:]

    def groups(steps):
        return [steps[i : i + 2] for i in range(0, len(steps), 2)]

    plans = [sp_steps[:1]] + groups(plane) + groups(rest), [sp_steps[:1]] + groups(rest) + groups(plane)
    return tuple([stage for stage in plan if stage] for plan in plans)


def stage_masks(stage):
    masks = []
    for number in range(1, 1 << len(stage)):
        mask = {"sp": 0, "dp": 0}
        for i, (axis, step) in enumerate(stage):
            if number & (1 << i):
                mask[axis] += step
        masks.append((mask["sp"], mask["dp"]))
    return masks


def place_in(stage, number):
    place = 0
    for i, (axis, step) in enumerate(stage):
        bit = lax.rem(lax.axis_index(axis) // step, 2)
        place = place + (1 << i) * (1 - bit if number & (1 << i) else bit)
    return place


def exchange_plan(rows, stages, offset=0):
    sizes, size = [], rows
    for stage in stages:
        group = 1 << len(stage)
        splits = size % (16 * group) == 0
        size = size // group if splits else size
        sizes.append((splits, size, offset))
        offset += (group - 1) * size
    return sizes, offset, size


class Reduction:
    def __init__(self, base, rows, staged, stages, acc, stage, land, full, send, recv):
        self.stages, self.acc, self.stage, self.land, self.full = stages, acc, stage, land, full
        self.send, self.recv, self.base = send, recv, base
        self.sizes, _, self.own = exchange_plan(rows, stages, staged)
        self.first_sem = [sum((1 << len(s)) - 1 for s in stages[:k]) for k in range(len(stages))]

    def at(self, low, size):
        return pl.ds(pl.multiple_of(low, 16), size)

    def low(self, k):
        return self.base + sum(
            place_in(self.stages[j], 0) * self.sizes[j][1] for j in range(k) if self.sizes[j][0]
        )

    def slot(self, k, i):
        _, size, offset = self.sizes[k]
        return slice(offset + i * size, offset + (i + 1) * size)

    def copies(self, way, k):
        splits, size, _ = self.sizes[k]
        out = []
        for i, masks in enumerate(stage_masks(self.stages[k])):
            if way == 0:
                source = self.stage.at[self.slot(k, i if splits else 0), :]
                target = self.land.at[self.slot(k, i), :]
            else:
                source = target = self.full.at[self.at(self.low(k + 1), size), :]
            out.append(
                pltpu.make_async_remote_copy(
                    src_ref=source,
                    dst_ref=target,
                    send_sem=self.send.at[way, self.first_sem[k] + i],
                    recv_sem=self.recv.at[way, self.first_sem[k] + i],
                    device_id=peer_at(*masks),
                    device_id_type=MESH,
                )
            )
        return out

    def sum_send(self, k):
        splits, size, _ = self.sizes[k]
        copies = self.copies(0, k)
        for i, copy in enumerate(copies):
            if splits:
                away = self.low(k) + place_in(self.stages[k], i + 1) * size
                self.stage[self.slot(k, i), :] = self.acc[self.at(away, size), :].astype(BF16)
            elif i == 0:
                self.stage[self.slot(k, 0), :] = self.acc[self.at(self.low(k), size), :].astype(BF16)
            copy.start()

    def sum_recv(self, k):
        splits, size, _ = self.sizes[k]
        copies = self.copies(0, k)
        for copy in copies:
            copy.wait()
        values = [self.land[self.slot(k, i), :].astype(F32) for i in range(len(copies))]
        if splits:
            values = [self.acc[self.at(self.low(k + 1), size), :]] + values
        else:
            values = [self.stage[self.slot(k, 0), :].astype(F32)] + values
        while len(values) > 1:
            values = [values[i] + values[i + 1] for i in range(0, len(values), 2)]
        self.acc[self.at(self.low(k + 1), size), :] = values[0]

    def close(self):
        where = self.at(self.low(len(self.stages)), self.own)
        self.full[where, :] = self.acc[where, :].astype(BF16)

    def share_send(self, k):
        if self.sizes[k][0]:
            for copy in self.copies(1, k):
                copy.start()

    def share_recv(self, k):
        if self.sizes[k][0]:
            for copy in self.copies(1, k):
                copy.wait()


def advance(streams, position):
    for stream in streams:
        n = len(stream.stages)
        if 0 < position <= n:
            stream.sum_recv(position - 1)
        if position < n:
            stream.sum_send(position)
        else:
            if position == n:
                stream.close()
            else:
                stream.share_recv(2 * n - position)
            if position < 2 * n:
                stream.share_send(2 * n - 1 - position)


def reduction_scratch(rows_list):
    plan, _ = stage_plans()
    staged = sum(max(exchange_plan(rows, stages)[1] for stages in stage_plans()) for rows in rows_list)
    sems = sum((1 << len(stage)) - 1 for stage in plan)
    return staged, (len(rows_list), 2, sems)


def make_streams(items, acc, stage, land, full, send, recv):
    streams, staged = [], 0
    for i, (base, rows, order) in enumerate(items):
        stages = stage_plans()[order]
        streams.append(
            Reduction(base, rows, staged, stages, acc, stage, land, full, send.at[i], recv.at[i])
        )
        staged += max(exchange_plan(rows, plan)[1] for plan in stage_plans())
    return streams


def all_masks(sp):
    masks = [(mask, 0) for mask in range(1, sp)]
    for plan in stage_plans():
        for stage in plan:
            masks += [m for m in stage_masks(stage) if m not in masks]
    return masks


def halves_of(ref, rows):
    return jnp.concatenate([ref[0, rows, :], ref[1, rows, :]], axis=1)


def combine(entries):
    count = sum(e[2] for e in entries)
    safe = jnp.maximum(count, 1.0)
    mean = sum(e[2] * e[0] for e in entries) / safe
    spread = sum(e[1] + e[2] * (e[0] - mean) * (e[0] - mean) for e in entries)
    return mean, spread, count


def pick(ref):
    return ref[0:1, :], ref[1:2, :], ref[2:3, :]


def total(entries):
    return tuple(sum(e[i] for e in entries) for i in range(3))


def middle_kernel(
    sp, dp, items, taps, chunk, block, len_ref, parts, x1_ref, cot, gain3, gain4, gain5, w_out, w_point1,
    depthwise, bn_gain, bn_bias, w_point2, w_in, w_down,
    out_ref, grad_x2, heads, mid, point_two, bn_grads, two,
    ctx, x2_ref, n3_keep, point, glu, conv, low_lim, high_lim, act, hidden, n4_keep, branch, swish, branch2,
    grad_x3, grad_y, grad_conv, grad_glu, grad_point, branch3, back_parts, tap_sums, edge_out, edge_in,
    send_box, near_box, far_box, sums,
    send, recv, local, back_send, back_recv, back_local, rim_send, rim_recv, box_send, box_recv,
):
    me, me_dp = lax.axis_index("sp"), lax.axis_index("dp")
    frames, width = x1_ref.shape
    lanes = width // 2
    reach = taps // 2
    count = frames // chunk
    peers = sp_peers(sp)
    far_peers = [peer_at(0, mask) for mask in range(1, dp)]
    greeted = peers + far_peers
    core = lax.rem(me, 2)
    sibling = peer_at(1, 0)
    length = sp * frames
    ends = ends_of(len_ref, items)
    first_frame = me * frames

    def limits(b, carry):
        rows = rows_at(b, chunk)
        frame = first_frame + b * chunk + lax.broadcasted_iota(I32, (chunk, lanes), 0)
        low, high = jnp.zeros_like(frame), jnp.full_like(frame, length)
        for end in ends:
            low = jnp.where(frame >= end, end, low)
        for end in reversed(ends):
            high = jnp.where(frame < end, end, high)
        low_lim[rows, :] = low - frame
        high_lim[rows, :] = high - 1 - frame
        return carry

    for ref in (glu, grad_conv):
        for h in range(2):
            ref[h, 0:reach, :] = jnp.zeros((reach, lanes), F32)
            ref[h, reach + frames :, :] = jnp.zeros((reach, lanes), F32)
    edge_in[...] = jnp.zeros_like(edge_in)
    send_box[...] = jnp.zeros_like(send_box)
    greet(greeted)
    lax.fori_loop(0, count, limits, 0)
    tap_sums[...] = jnp.zeros_like(tap_sums)
    sums[...] = jnp.zeros_like(sums)
    await_greetings(greeted)

    def moves(c, source, target, send_sems, recv_sems, local_sems):
        return [
            pltpu.make_async_remote_copy(
                src_ref=source(1 - core, c), dst_ref=target(core, c),
                send_sem=send_sems.at[c], recv_sem=recv_sems.at[c],
                device_id=sibling, device_id_type=MESH,
            ),
            pltpu.make_async_copy(source(core, c), target(core, c), local_sems.at[c]),
        ]

    def by_frames(ref):
        return lambda slot, c: ref.at[:, :, frame_cols(slot, frames, c, chunk)]

    def by_head(ref):
        return lambda slot, c: ref.at[slot, :, :, rows_at(c, chunk)]

    def context_moves(c):
        return moves(c, by_frames(parts), by_head(ctx), send, recv, local)

    def begin(c, carry):
        for copy in context_moves(c):
            copy.start()
        return carry

    lax.fori_loop(0, count, begin, 0)

    def open_step(c, carry):
        rows = rows_at(c, chunk)
        for copy in context_moves(c):
            copy.wait()
        context = ctx[:, :, :, rows].reshape(width, chunk)
        x2 = x1_ref[rows, :] + dg(context, w_out[...], 0, 0)
        x2_ref[rows, :] = x2
        hat, _ = norm_parts(x2)
        n3 = (hat * row_of(gain3)).astype(BF16)
        n3_keep[rows, :] = n3
        pair = dg(n3, w_point1[...], 1, 0)
        point[rows, :] = pair
        gated = (pair[:, :width] * sigmoid(pair[:, width:])).astype(BF16).astype(F32)
        where = pl.ds(pl.multiple_of(reach + c * chunk, 8), chunk)
        glu[0, where, :] = gated[:, :lanes]
        glu[1, where, :] = gated[:, lanes:]
        return carry

    lax.fori_loop(0, count, open_step, 0)

    def rim_copies(call, side, source, target):
        peer = (me_dp, me - 1 if side == 0 else me + 1)
        return pltpu.make_async_remote_copy(
            src_ref=source, dst_ref=target, send_sem=rim_send.at[call, side], recv_sem=rim_recv.at[call, side],
            device_id=peer, device_id_type=MESH,
        )

    def swap_rims(call, sources, targets):
        @pl.when(me > 0)
        def _():
            rim_copies(call, 0, sources[0], targets[1]).start()

        @pl.when(me < sp - 1)
        def _():
            rim_copies(call, 1, sources[1], targets[0]).start()

    def await_rims(call, sources, targets):
        @pl.when(me > 0)
        def _():
            rim_copies(call, 0, sources[0], targets[1]).wait_send()
            rim_copies(call, 1, sources[1], targets[0]).wait_recv()

        @pl.when(me < sp - 1)
        def _():
            rim_copies(call, 1, sources[1], targets[0]).wait_send()
            rim_copies(call, 0, sources[0], targets[1]).wait_recv()

    for side, rows in ((0, slice(reach, 2 * reach)), (1, slice(frames, frames + reach))):
        for h in range(2):
            edge_out[side, 0:reach, h * lanes : (h + 1) * lanes] = glu[h, rows, :]
    glu_rims = (
        [edge_out.at[0, 0:reach, :], edge_out.at[1, 0:reach, :]],
        [edge_in.at[0, 0:reach, :], edge_in.at[1, 0:reach, :]],
    )
    swap_rims(0, *glu_rims)

    zero = jnp.zeros((block, lanes), F32)

    def conv_step(b, carry):
        low, high = low_lim[rows_at(b, block), :], high_lim[rows_at(b, block), :]
        start = pl.multiple_of(b * block, block)
        result = [zero, zero]
        for tap in range(taps):
            shift = tap - reach
            inside = (low <= shift) if shift < 0 else (high >= shift)
            for h in range(2):
                view = glu.at[h, pl.ds(start, block + 2 * reach), :]
                term = jnp.where(inside, view[tap : tap + block, :], 0.0)
                result[h] = result[h] + depthwise[tap : tap + 1, h * lanes : (h + 1) * lanes].astype(F32) * term
        valid = (first_frame + start + lax.broadcasted_iota(I32, (block, lanes), 0)) < ends[-1]
        for h in range(2):
            conv[h, rows_at(b, block), :] = result[h]
            sums[0:1, h * lanes : (h + 1) * lanes] += jnp.sum(jnp.where(valid, result[h], 0.0), axis=0, keepdims=True)
        return carry

    blocks = frames // block
    lax.fori_loop(1, blocks - 1, conv_step, 0)
    await_rims(0, *glu_rims)
    for h in range(2):
        glu[h, 0:reach, :] = edge_in[0, 0:reach, h * lanes : (h + 1) * lanes]
        glu[h, reach + frames :, :] = edge_in[1, 0:reach, h * lanes : (h + 1) * lanes]
    conv_step(0, 0)
    conv_step(blocks - 1, 0)

    own_count = jnp.clip(ends[-1] - first_frame, 0, frames).astype(F32)
    own_mean = sums[0:1, :] / jnp.maximum(own_count, 1.0)
    sums[0:1, :] = jnp.zeros((1, width), F32)

    def spread_step(c, carry):
        rows = rows_at(c, chunk)
        valid = (first_frame + c * chunk + lax.broadcasted_iota(I32, (chunk, width), 0)) < ends[-1]
        apart = jnp.where(valid, halves_of(conv, rows) - own_mean, 0.0)
        sums[1:2, :] += jnp.sum(apart * apart, axis=0, keepdims=True)
        return carry

    lax.fori_loop(0, count, spread_step, 0)

    def box_copies(call, stage):
        group = peers if stage == 0 else far_peers
        target = near_box if stage == 0 else far_box
        base = 0 if stage == 0 else sp - 1
        return [
            pltpu.make_async_remote_copy(
                src_ref=send_box.at[call, stage],
                dst_ref=target.at[call, i],
                send_sem=box_send.at[call, base + i],
                recv_sem=box_recv.at[call, base + i],
                device_id=peer,
                device_id_type=MESH,
            )
            for i, peer in enumerate(group)
        ]

    def box_begin(call, stage, rows):
        for i, row in enumerate(rows):
            send_box[call, stage, i : i + 1, :] = row
        for copy in box_copies(call, stage):
            copy.start()

    def box_end(call, stage, rows, merge):
        target = near_box if stage == 0 else far_box
        copies = box_copies(call, stage)
        for copy in copies:
            copy.wait()
        return merge([rows] + [pick(target[call, i]) for i in range(len(copies))])

    stats = (own_mean, sums[1:2, :], jnp.full((1, width), 1.0, F32) * own_count)
    sums[1:2, :] = jnp.zeros((1, width), F32)
    box_begin(0, 0, stats)
    stats = box_end(0, 0, stats, combine)
    box_begin(0, 1, stats)
    mean, spread, frame_count = box_end(0, 1, stats, combine)
    inv_std = lax.rsqrt(spread / frame_count + EPS)
    norm_gain, norm_bias = row_of(bn_gain), row_of(bn_bias)

    def heart_step(c, carry):
        rows = rows_at(c, chunk)
        normed = (halves_of(conv, rows) - mean) * inv_std
        y = normed * norm_gain + norm_bias
        sig_y = sigmoid(y)
        w = (y * sig_y).astype(BF16)
        swish[rows, :] = w
        x3 = x2_ref[rows, :] + dg(w, w_point2[...], 1, 0)
        hat4, inv4 = norm_parts(x3)
        g4 = row_of(gain4)
        n4 = (hat4 * g4).astype(BF16)
        n4_keep[rows, :] = n4
        a = dg(n4, w_in[...], 1, 0)
        sig = sigmoid(a)
        s = (a * sig).astype(BF16)
        act[rows, :] = s
        x4 = x3 + 0.5 * dg(s, w_down[...], 1, 0)
        hat5, inv5 = norm_parts(x4)
        g5 = row_of(gain5)
        out_ref[rows, :] = (hat5 * g5).astype(BF16)
        top = cot[rows, :].astype(F32)
        mid[3 * width + 4 : 3 * width + 5, :] += jnp.sum(top * hat5, axis=0, keepdims=True)
        grad_x4 = norm_back(top, hat5, inv5, g5)
        low_grad = (0.5 * grad_x4).astype(BF16)
        branch[rows, :] = low_grad
        grad = dg(low_grad, w_down[...], 1, 1)
        low_hidden = (grad * (sig * (1.0 + a * (1.0 - sig)))).astype(BF16)
        hidden[rows, :] = low_hidden
        grad = dg(low_hidden, w_in[...], 1, 1)
        mid[3 * width + 3 : 3 * width + 4, :] += jnp.sum(grad * hat4, axis=0, keepdims=True)
        grad3 = grad_x4 + norm_back(grad, hat4, inv4, g4)
        grad_x3[rows, :] = grad3
        low_grad = grad3.astype(BF16)
        branch2[rows, :] = low_grad
        grad = dg(low_grad, w_point2[...], 1, 1) * (sig_y * (1.0 + y * (1.0 - sig_y)))
        grad_y[0, rows, :] = grad[:, :lanes]
        grad_y[1, rows, :] = grad[:, lanes:]
        sums[2:3, :] += jnp.sum(grad, axis=0, keepdims=True)
        sums[3:4, :] += jnp.sum(grad * normed, axis=0, keepdims=True)
        return carry

    mid[3 * width :, :] = jnp.zeros((width, width), F32)
    lax.fori_loop(0, count, heart_step, 0)

    pair = (sums[2:3, :], sums[3:4, :], jnp.zeros((1, width), F32))
    box_begin(1, 0, pair)
    for side, rows in ((0, slice(0, reach)), (1, slice(frames - reach, frames))):
        for h in range(2):
            cols = slice(h * lanes, (h + 1) * lanes)
            edge_out[side, reach : 2 * reach, cols] = grad_y[h, rows, :]
            edge_out[side, 2 * reach : 3 * reach, cols] = conv[h, rows, :]
    grad_rims = (
        [edge_out.at[0, reach : 3 * reach, :], edge_out.at[1, reach : 3 * reach, :]],
        [edge_in.at[0, reach : 3 * reach, :], edge_in.at[1, reach : 3 * reach, :]],
    )
    swap_rims(1, *grad_rims)
    wide = w_in.shape[1]
    for j in range(0, wide, width):
        two[j : j + width, :] = dg(act[:, j : j + width], branch[...], 0, 0).astype(BF16)
    pair = box_end(1, 0, pair, total)
    box_begin(1, 1, pair)
    for j in range(0, wide, width):
        two[wide + j : wide + j + width, :] = dg(n4_keep[...], hidden[:, j : j + width], 0, 0).astype(BF16)
    point_two[...] = dg(swish[...], branch2[...], 0, 0)
    await_rims(1, *grad_rims)
    bias_sum, gain_sum, _ = box_end(1, 1, pair, total)
    bn_grads[0:1, :] = gain_sum
    bn_grads[1:2, :] = bias_sum
    bn_grads[2:8, :] = jnp.zeros((6, width), F32)

    scale = norm_gain * inv_std
    slope = -inv_std * inv_std * norm_gain * gain_sum / frame_count
    shift_all = -inv_std * norm_gain * bias_sum / frame_count

    def conv_grad(grad, value, frame, h):
        cols = slice(h * lanes, (h + 1) * lanes)
        extra = (value - mean[:, cols]) * slope[:, cols] + shift_all[:, cols]
        return grad * scale[:, cols] + jnp.where(frame < ends[-1], extra, 0.0)

    def grad_conv_step(c, carry):
        rows = rows_at(c, chunk)
        frame = first_frame + c * chunk + lax.broadcasted_iota(I32, (chunk, lanes), 0)
        where = pl.ds(pl.multiple_of(reach + c * chunk, 8), chunk)
        for h in range(2):
            grad_conv[h, where, :] = conv_grad(grad_y[h, rows, :], conv[h, rows, :], frame, h)
        return carry

    lax.fori_loop(0, count, grad_conv_step, 0)
    for side, rows, begin_frame in (
        (0, slice(0, reach), first_frame - reach),
        (1, slice(reach + frames, 2 * reach + frames), first_frame + frames),
    ):
        frame = begin_frame + lax.broadcasted_iota(I32, (reach, lanes), 0)
        for h in range(2):
            cols = slice(h * lanes, (h + 1) * lanes)
            grad_conv[h, rows, :] = conv_grad(
                edge_in[side, reach : 2 * reach, cols], edge_in[side, 2 * reach : 3 * reach, cols], frame, h
            )

    def conv_back_step(b, carry):
        low, high = low_lim[rows_at(b, block), :], high_lim[rows_at(b, block), :]
        start = pl.multiple_of(b * block, block)
        result = [zero, zero]
        here = [glu[h, pl.ds(pl.multiple_of(reach + start, 8), block), :] for h in range(2)]
        for tap in range(taps):
            shift = reach - tap
            inside = (low <= shift) if shift < 0 else (high >= shift)
            at = reach + shift
            for h in range(2):
                view = grad_conv.at[h, pl.ds(start, block + 2 * reach), :]
                term = jnp.where(inside, view[at : at + block, :], 0.0)
                result[h] = result[h] + depthwise[tap : tap + 1, h * lanes : (h + 1) * lanes].astype(F32) * term
                tap_sums[tap, h] += jnp.sum((here[h] * term).reshape(block // 8, 8, lanes), axis=0)
        for h in range(2):
            grad_glu[h, rows_at(b, block), :] = result[h]
        return carry

    lax.fori_loop(0, blocks, conv_back_step, 0)

    def back_moves(c):
        return moves(c, by_head(back_parts), by_frames(heads), back_send, back_recv, back_local)

    def close_step(c, carry):
        rows = rows_at(c, chunk)
        grad = halves_of(grad_glu, rows)
        value, gate = point[rows, :width], sigmoid(point[rows, width:])
        low_grad = jnp.concatenate([grad * gate, grad * value * gate * (1.0 - gate)], axis=1).astype(BF16)
        grad_point[rows, :] = low_grad
        grad = dg(low_grad, w_point1[...], 1, 1)
        hat, inv = norm_parts(x2_ref[rows, :])
        mid[3 * width + 2 : 3 * width + 3, :] += jnp.sum(grad * hat, axis=0, keepdims=True)
        grad2 = grad_x3[rows, :] + norm_back(grad, hat, inv, row_of(gain3))
        grad_x2[rows, :] = grad2
        low_grad = grad2.astype(BF16)
        branch3[rows, :] = low_grad
        back_parts[:, :, :, rows] = dg(w_out[...], low_grad, 1, 1).astype(BF16).reshape(2, 2, width // 4, chunk)
        for copy in back_moves(c):
            copy.start()
        return carry

    lax.fori_loop(0, count, close_step, 0)
    for j in range(2):
        mid[j * width : (j + 1) * width, :] = dg(n3_keep[...], grad_point[:, j * width : (j + 1) * width], 0, 0)
    mid[2 * width : 3 * width, :] = dg(ctx[...].reshape(width, frames), branch3[...], 1, 0)
    for tap in range(taps):
        row = 3 * width + 8 + tap
        for h in range(2):
            mid[row : row + 1, h * lanes : (h + 1) * lanes] = jnp.sum(tap_sums[tap, h], axis=0, keepdims=True)

    def finish(c, carry):
        for copy in back_moves(c):
            copy.wait()
        return carry

    lax.fori_loop(0, count, finish, 0)


def middle(
    lengths, parts, x1, cot, gain3, gain4, gain5, w_out, w_point1, depthwise, bn_gain, bn_bias, w_point2,
    w_in, w_down, dp,
):
    frames, width = x1.shape
    sp = lax.axis_size("sp")
    assert sp == HEADS == 4
    paired = pltpu.VMEM((2, 2, width // 4, frames), BF16)
    wide = w_in.shape[1]
    taps = depthwise.shape[0]
    reach = taps // 2
    chunk = min(256, frames)
    count = frames // chunk
    lanes = width // 2
    keep, low_keep = pltpu.VMEM((frames, width), F32), pltpu.VMEM((frames, width), BF16)
    split = pltpu.VMEM((2, frames, lanes), F32)
    rimmed = pltpu.VMEM((2, frames + 2 * reach, lanes), F32)
    rims = pltpu.VMEM((2, 3 * reach, width), F32)
    moves = [DMA((count,)), DMA((count,)), DMA((count,))]
    return pl.pallas_call(
        functools.partial(middle_kernel, sp, dp, lengths.shape[1], taps, chunk, 32),
        out_shape=[
            jax.ShapeDtypeStruct((frames, width), BF16),
            jax.ShapeDtypeStruct((frames, width), F32),
            jax.ShapeDtypeStruct(parts.shape, BF16),
            jax.ShapeDtypeStruct((4 * width, width), F32),
            jax.ShapeDtypeStruct((width, width), F32),
            jax.ShapeDtypeStruct((8, width), F32),
            jax.ShapeDtypeStruct((2 * wide, width), BF16),
        ],
        in_specs=[SMEM, pl.BlockSpec(memory_space=pl.ANY)] + [VMEM] * 13,
        out_specs=[VMEM] * 7,
        scratch_shapes=[
            paired,
            keep,
            low_keep,
            pltpu.VMEM((frames, 2 * width), F32),
            rimmed,
            split,
            pltpu.VMEM((frames, lanes), I32),
            pltpu.VMEM((frames, lanes), I32),
            pltpu.VMEM((frames, wide), BF16),
            pltpu.VMEM((frames, wide), BF16),
            low_keep,
            low_keep,
            low_keep,
            low_keep,
            keep,
            split,
            rimmed,
            split,
            pltpu.VMEM((frames, 2 * width), BF16),
            low_keep,
            paired,
            pltpu.VMEM((taps, 2, 8, lanes), F32),
            rims,
            rims,
            pltpu.VMEM((2, 2, 8, width), F32),
            pltpu.VMEM((2, sp - 1, 8, width), F32),
            pltpu.VMEM((2, dp - 1, 8, width), F32),
            pltpu.VMEM((8, width), F32),
        ]
        + moves
        + moves
        + [DMA((2, 2)), DMA((2, 2)), DMA((2, sp + dp - 2)), DMA((2, sp + dp - 2))],
        compiler_params=pltpu.CompilerParams(
            collective_id=1, has_side_effects=True, vmem_limit_bytes=VMEM_LIMIT
        ),
        name="middle",
    )(
        lengths, parts, x1, cot, gain3, gain4, gain5, w_out, w_point1, depthwise, bn_gain, bn_bias, w_point2,
        w_in, w_down,
    )


def back_kernel(
    sp, items, chunk, block, sub, len_ref, near, far, o_ref, lse_ref, do_ref, trig, gain1, gain2, two, mid, point_two,
    tok_hbm, x1_hbm, n2_hbm, x2_hbm, act_hbm, slope_hbm, w_in_hbm, w_out_hbm, w_qkv_hbm,
    grad_ref, full,
    tok, x1_ref, n2_ref, grad_x2, act, slope, w_in, w_out, w_qkv,
    qa, qt, ka, da, va, dq, far_out, near_out, dq_out, far_kv, near_kv, near_dq,
    joined, branch, hidden, grad_x1, gains, acc, stage, land,
    load_sems, far_send, far_recv, near_send, near_recv, sum_send, sum_recv,
):
    me, dp = lax.axis_index("sp"), lax.axis_index("dp")
    core, pair = lax.rem(me, 2), me // 2
    sibling = peer_at(1, 0)
    frames, width = tok.shape
    wide = w_in.shape[1]
    half = trig.shape[0] // 2
    dim = 2 * half
    count = frames // chunk
    reach = 2 * frames
    greeted = [peer_at(*mask) for mask in all_masks(sp)]
    greet(greeted)
    loads = [
        pltpu.make_async_copy(source, target, load_sems.at[i])
        for i, (source, target) in enumerate(
            (
                (x1_hbm, x1_ref), (x2_hbm, grad_x2), (w_qkv_hbm, w_qkv), (n2_hbm, n2_ref), (act_hbm, act),
                (w_out_hbm, w_out), (slope_hbm, slope), (w_in_hbm, w_in), (tok_hbm, tok),
            )
        )
    ]
    for copy in loads:
        copy.start()
    unit = 4 * width
    last = 6 * unit
    streams = make_streams(
        [
            (0, unit, 1), (unit, unit, 1), (2 * unit, unit, 1),
            (3 * unit, unit, 1), (4 * unit, unit, 0), (5 * unit, unit, 0), (last, 16, 0),
        ],
        acc, stage, land, full, sum_send, sum_recv,
    )
    early, (qkv, down, up, rest) = streams[:3], ([stream] for stream in streams[3:])
    steps = len(stage_plans()[0])
    acc[0 : 2 * unit, :] = two[...].astype(F32)
    acc[2 * unit : 3 * unit, :] = mid[...]
    acc[last : last + 16, :] = jnp.zeros((16, width), F32)
    gains[...] = jnp.zeros_like(gains)
    ends = ends_of(len_ref, items)
    wide_pad = jnp.zeros((dim - 16, frames), BF16)
    for slot in range(2):
        cols = slice(slot * frames, (slot + 1) * frames)
        far_cols = slice(reach + slot * frames, reach + (slot + 1) * frames)
        segment = segment_row((2 * pair + slot) * frames, frames, ends)
        far_segment = segment_row((2 * (1 - pair) + slot) * frames, frames, ends)
        for h in range(2):
            query = near[slot, h * dim : (h + 1) * dim, :]
            qt[h, :, cols] = query
            qa[h, cols, :] = query_rows(query, segment, items, -lse_ref[h : h + 1, cols]).T
            grad = do_ref[h, :, cols]
            row_dot = jnp.sum(grad.astype(F32) * o_ref[h, :, cols], axis=0, keepdims=True)
            da[h, cols, :] = jnp.concatenate([grad, split_rows(-row_dot), wide_pad], axis=0).T
            ka[h, :, cols] = key_rows(near[slot, (2 + h) * dim : (3 + h) * dim, :], segment, items)
            ka[h, :, far_cols] = key_rows(far[slot, h * dim : (h + 1) * dim, :], far_segment, items)
            for where, value in (
                (cols, near[slot, (4 + h) * dim : (5 + h) * dim, :]),
                (far_cols, far[slot, (2 + h) * dim : (3 + h) * dim, :]),
            ):
                va[h, 0:dim, where] = value
                va[h, dim : dim + 16, where] = first_rows(3, frames)
                va[h, dim + 16 :, where] = wide_pad
    for h in range(2):
        dq[h] = jnp.zeros((dim, reach), F32)
    await_greetings(greeted)

    def attend_block(h, at):
        dk, dv, grads = [], [], []

        def score(u):
            cols = pl.ds(pl.multiple_of(at + u * sub, sub), sub)
            return dg(qa[h], ka[h, :, cols], 1, 0), dg(da[h], va[h, :, cols], 1, 0)

        ready = score(0)
        for u in range(block // sub):
            scores, grad_probs = ready
            if u + 1 < block // sub:
                ready = score(u + 1)
            probs = jnp.exp2(scores)
            grad = (probs * grad_probs).astype(BF16)
            dv.append(dg(do_ref[h], probs.astype(BF16), 1, 0).astype(BF16))
            dk.append((dg(qt[h], grad, 1, 0) * LN2).astype(BF16))
            grads.append(grad)
        dq[h] += dg(ka[h, 0:dim, pl.ds(pl.multiple_of(at, block), block)], jnp.concatenate(grads, axis=1), 1, 1)
        return jnp.concatenate(dk, axis=1), jnp.concatenate(dv, axis=1)

    per = frames // block

    def keep(ref, slot, h, cols, block_grads):
        for i, value in enumerate(block_grads):
            ref[slot, 2 * i + h, :, cols] = value

    def far_copy(b):
        cols = rows_at(lax.rem(b, per), block)
        return pltpu.make_async_remote_copy(
            src_ref=far_out.at[b // per, :, :, cols], dst_ref=far_kv.at[core, :, :, cols],
            send_sem=far_send.at[b], recv_sem=far_recv.at[core, lax.rem(b, per)],
            device_id=(dp, 2 * (1 - pair) + b // per), device_id_type=MESH,
        )

    def far_step(t, carry):
        b, h = t // 2, lax.rem(t, 2)
        cols = rows_at(lax.rem(b, per), block)
        keep(far_out, b // per, h, cols, attend_block(h, reach + b * block))

        @pl.when(h == 1)
        def _():
            far_copy(b).start()

        for position in range(steps + 1):
            @pl.when(t == 1 + position * 2)
            def _():
                advance(early, position)

        return carry

    lax.fori_loop(0, 4 * per, far_step, 0)

    def near_copy(b):
        cols = rows_at(b, block)
        return pltpu.make_async_remote_copy(
            src_ref=near_out.at[:, :, cols], dst_ref=near_kv.at[core, :, :, cols],
            send_sem=near_send.at[b], recv_sem=near_recv.at[b], device_id=sibling, device_id_type=MESH,
        )

    def sibling_step(t, carry):
        b, h = t // 2, lax.rem(t, 2)
        block_grads = attend_block(h, (1 - core) * frames + b * block)
        for i, value in enumerate(block_grads):
            near_out[2 * i + h, :, rows_at(b, block)] = value

        @pl.when(h == 1)
        def _():
            near_copy(b).start()

        for position in range(steps + 1, 2 * steps):
            @pl.when(t == 2 * (position - steps - 1))
            def _():
                advance(early, position)

        return carry

    lax.fori_loop(0, 2 * per, sibling_step, 0)

    def own_step(t, carry):
        b, h = t // 2, lax.rem(t, 2)
        keep(near_kv, core, h, rows_at(b, block), attend_block(h, core * frames + b * block))

        @pl.when(t == 0)
        def _():
            advance(early, 2 * steps)

        return carry

    lax.fori_loop(0, 2 * per, own_step, 0)
    for h in range(2):
        dq_out[h] = (dq[h, :, pl.ds(pl.multiple_of((1 - core) * frames, frames), frames)] * dim**-0.5).astype(BF16)
    dq_copy = pltpu.make_async_remote_copy(
        src_ref=dq_out, dst_ref=near_dq.at[core], send_sem=near_send.at[per], recv_sem=near_recv.at[per],
        device_id=sibling, device_id_type=MESH,
    )
    dq_copy.start()
    for h in range(2):
        near_dq[core, h] = (dq[h, :, pl.ds(pl.multiple_of(core * frames, frames), frames)] * dim**-0.5).astype(BF16)
    for copy in loads:
        copy.wait()
    for b in range(2 * per):
        far_copy(b).wait_send()
    for source in range(2):
        for b in range(per):
            pltpu.make_async_remote_copy(
                src_ref=far_out.at[0, :, :, rows_at(b, block)], dst_ref=far_kv.at[source, :, :, rows_at(b, block)],
                send_sem=far_send.at[b], recv_sem=far_recv.at[source, b], device_id=sibling, device_id_type=MESH,
            ).wait_recv()
    for b in range(per):
        near_copy(b).wait()

    def turn_back(first, second, rows, low):
        sine, cosine = trig[0:half, rows], trig[half:, rows]
        joined[low : low + half, rows] = (first * cosine + second * sine).astype(BF16)
        joined[low + half : low + dim, rows] = (second * cosine - first * sine).astype(BF16)

    def keys_step(c, carry):
        rows = rows_at(c, chunk)
        for p in range(2):
            for h in range(2):
                head = 2 * p + h

                def both(i, low, high):
                    return near_kv[p, i, low:high, rows].astype(F32) + far_kv[p, i, low:high, rows].astype(F32)

                turn_back(both(h, 0, half), both(h, half, dim), rows, width + head * dim)
                low = 2 * width + head * dim
                joined[low : low + dim, rows] = both(2 + h, 0, dim).astype(BF16)
        return carry

    lax.fori_loop(0, count, keys_step, 0)
    dq_copy.wait()

    def arrive(c, carry):
        rows = rows_at(c, chunk)
        for p in range(2):
            for h in range(2):
                turn_back(
                    near_dq[p, h, 0:half, rows].astype(F32), near_dq[p, h, half:dim, rows].astype(F32), rows,
                    (2 * p + h) * dim,
                )
        grad = dg(joined[:, rows], w_qkv[...], 0, 1)
        hat, inv = norm_parts(x1_ref[rows, :])
        gains[1:2, :] += jnp.sum(grad * hat, axis=0, keepdims=True)
        grad = grad_x2[rows, :] + norm_back(grad, hat, inv, row_of(gain2))
        grad_x1[rows, :] = grad
        branch[rows, :] = (0.5 * grad).astype(BF16)
        return carry

    lax.fori_loop(0, count, arrive, 0)
    for j in range(0, wide, width):
        acc[4 * unit + j : 4 * unit + j + width, :] = dg(act[:, j : j + width], branch[...], 0, 0)
    advance(down, 0)
    acc[3 * unit : 3 * unit + 3 * width, :] = dg(joined[...], n2_ref[...], 1, 0)
    acc[3 * unit + 3 * width : 4 * unit, :] = point_two[...]
    advance(qkv, 0)

    def through(c, carry):
        rows = rows_at(c, chunk)
        grad = dg(branch[rows, :], w_out[...], 1, 1)
        low_hidden = (grad * slope[rows, :].astype(F32)).astype(BF16)
        hidden[rows, :] = low_hidden
        grad = dg(low_hidden, w_in[...], 1, 1)
        hat, inv = norm_parts(tok[rows, :].astype(F32))
        gains[0:1, :] += jnp.sum(grad * hat, axis=0, keepdims=True)
        gain = row_of(gain1)
        grad_ref[rows, :] = (grad_x1[rows, :] + norm_back(grad, hat, inv, gain)).astype(BF16)
        n2_ref[rows, :] = (hat * gain).astype(BF16)
        return carry

    lax.fori_loop(0, count, through, 0)
    for j in range(0, wide, width):
        acc[5 * unit + j : 5 * unit + j + width, :] = dg(n2_ref[...], hidden[:, j : j + width], 0, 0)
    advance(up, 0)
    acc[last : last + 8, :] = gains[...]
    advance(rest, 0)
    for position in range(1, 2 * steps + 1):
        advance(down + qkv + up + rest, position)


def back(
    lengths, near, far, o, lse, do, trig, gain1, gain2, two, mid, point_two,
    tok, x1, n2, grad_x2, act, slope, w_in, w_out, w_qkv,
):
    frames, width = tok.shape
    sp = lax.axis_size("sp")
    chunk = min(256, frames)
    block = min(512, frames)
    count, per = frames // chunk, frames // block
    wide = w_in.shape[1]
    dim = width // HEADS
    reach = 2 * frames
    rows = 24 * width + 16
    staged, sems = reduction_scratch([4 * width] * 6 + [16])
    low_keep, keep = pltpu.VMEM((frames, width), BF16), pltpu.VMEM((frames, width), F32)
    return pl.pallas_call(
        functools.partial(back_kernel, sp, lengths.shape[1], chunk, block, min(256, block)),
        out_shape=[
            jax.ShapeDtypeStruct((frames, width), BF16),
            jax.ShapeDtypeStruct((rows, width), BF16),
        ],
        in_specs=[SMEM] + [VMEM] * 11 + [pl.BlockSpec(memory_space=pl.ANY)] * 9,
        out_specs=[VMEM] * 2,
        scratch_shapes=[
            low_keep,
            keep,
            low_keep,
            keep,
            pltpu.VMEM((frames, wide), BF16),
            pltpu.VMEM((frames, wide), BF16),
            pltpu.VMEM(w_in.shape, BF16),
            pltpu.VMEM(w_out.shape, BF16),
            pltpu.VMEM(w_qkv.shape, BF16),
            pltpu.VMEM((2, reach, 2 * dim), BF16),
            pltpu.VMEM((2, dim, reach), BF16),
            pltpu.VMEM((2, 2 * dim, 2 * reach), BF16),
            pltpu.VMEM((2, reach, 2 * dim), BF16),
            pltpu.VMEM((2, 2 * dim, 2 * reach), BF16),
            pltpu.VMEM((2, dim, reach), F32),
            pltpu.VMEM((2, 4, dim, frames), BF16),
            pltpu.VMEM((4, dim, frames), BF16),
            pltpu.VMEM((2, dim, frames), BF16),
            pltpu.VMEM((2, 4, dim, frames), BF16),
            pltpu.VMEM((2, 4, dim, frames), BF16),
            pltpu.VMEM((2, 2, dim, frames), BF16),
            pltpu.VMEM((3 * width, frames), BF16),
            low_keep,
            pltpu.VMEM((frames, wide), BF16),
            keep,
            pltpu.VMEM((8, width), F32),
            pltpu.VMEM((rows, width), F32),
            pltpu.VMEM((staged, width), BF16),
            pltpu.VMEM((staged, width), BF16),
            DMA((9,)),
            DMA((2 * per,)),
            DMA((2, per)),
            DMA((per + 1,)),
            DMA((per + 1,)),
            DMA(sems),
            DMA(sems),
        ],
        compiler_params=pltpu.CompilerParams(
            collective_id=2, has_side_effects=True, vmem_limit_bytes=VMEM_LIMIT
        ),
        name="back",
    )(
        lengths, near, far, o, lse, do, trig, gain1, gain2, two, mid, point_two,
        tok, x1, n2, grad_x2, act, slope, w_in, w_out, w_qkv,
    )


def unpack_kernel(
    taps, full, bn_grads, output, input_grad,
    output_to, input_to, gain1_to, in_one_to, out_one_to, gain2_to, qkv_to, out_weight_to, gain3_to, point_one_to,
    depthwise_to, bn_gain_to, bn_bias_to, point_two_to, gain4_to, in_two_to, out_two_to, gain5_to,
    in_one, out_one, qkv, point_one, point_two, out_weight, in_two, out_two, depthwise, sems,
):
    width = full.shape[1]
    unit = 4 * width
    copies = []

    def send(source, target):
        copies.append(pltpu.make_async_copy(source, target, sems.at[len(copies)]))
        copies[-1].start()

    def block(ref, base):
        return ref[base : base + width, :].astype(F32)

    send(output, output_to)
    send(input_grad, input_to)
    for j in range(0, unit, width):
        out_two[j : j + width, :] = block(full, j)
    send(out_two, out_two_to)
    for j in range(0, unit, width):
        in_two[:, j : j + width] = block(full, unit + j)
    send(in_two, in_two_to)
    for j in range(0, unit, width):
        out_one[j : j + width, :] = block(full, 4 * unit + j)
    send(out_one, out_one_to)
    for j in range(0, unit, width):
        in_one[:, j : j + width] = block(full, 5 * unit + j)
    send(in_one, in_one_to)
    for j in range(0, 2 * width, width):
        point_one[:, j : j + width] = block(full, 2 * unit + j)
    send(point_one, point_one_to)
    out_weight[...] = block(full, 2 * unit + 2 * width)
    send(out_weight, out_weight_to)
    point_two[...] = block(full, 3 * unit + 3 * width)
    send(point_two, point_two_to)
    for j in range(0, 3 * width, width):
        qkv[:, j : j + width] = block(full, 3 * unit + j).T
    send(qkv, qkv_to)
    small = full[2 * unit + 3 * width : 2 * unit + 3 * width + 64, :].astype(F32)
    depthwise[...] = small[8 : 8 + taps]
    send(depthwise, depthwise_to)
    rest = full[6 * unit : 6 * unit + 16, :].astype(F32)
    for ref, row in (
        (gain1_to, rest[0]), (gain2_to, rest[1]), (gain3_to, small[2]), (gain4_to, small[3]), (gain5_to, small[4]),
        (bn_gain_to, bn_grads[0, :]), (bn_bias_to, bn_grads[1, :]),
    ):
        ref[...] = row
    for copy in copies:
        copy.wait()


def unpack(full, bn_grads, output, input_grad, taps):
    width = full.shape[1]
    row, square, tall, flat = (width,), (width, width), (4 * width, width), (width, 4 * width)
    thrice, twice = (width, 3 * width), (width, 2 * width)
    anywhere = pl.BlockSpec(memory_space=pl.ANY)
    shapes = [
        output.shape, input_grad.shape, row, flat, tall, row, thrice, square, row, twice, (taps, width), row, row,
        square, row, flat, tall, row,
    ]
    return pl.pallas_call(
        functools.partial(unpack_kernel, taps),
        out_shape=[jax.ShapeDtypeStruct(shape, F32 if i > 1 else BF16) for i, shape in enumerate(shapes)],
        in_specs=[VMEM] * 4,
        out_specs=[VMEM if shape == row else anywhere for shape in shapes],
        scratch_shapes=[
            pltpu.VMEM(shape, F32)
            for shape in (flat, tall, thrice, twice, square, square, flat, tall, (taps, width))
        ]
        + [DMA((11,))],
        compiler_params=pltpu.CompilerParams(vmem_limit_bytes=VMEM_LIMIT),
        name="unpack",
    )(full, bn_grads, output, input_grad)


def on_device(
    tokens, ln1_gain, ffn1_in, ffn1_out, ln2_gain, w_qkv, w_out, ln3_gain, w_point1, depthwise,
    bn_gain, bn_bias, w_point2, ln4_gain, ffn2_in, ffn2_out, ln5_gain, lengths, cotangent,
):
    width = tokens.shape[2]
    sp, dp = lax.axis_size("sp"), lax.axis_size("dp")
    assert HEADS == sp and ffn1_in.shape[1] == ffn2_in.shape[1] == 4 * width
    half = width // HEADS // 2
    turns = 10000.0 ** (-np.arange(half, dtype=np.float64) / half) / (2 * np.pi)
    high = np.round(turns * 4096.0) / 4096.0
    freq = jnp.asarray(np.stack([high, turns - high], axis=1), F32)
    x1, n2, trig, act, slope, near, far, context, raw_context, log_sums, flag = front(
        lengths, tokens[0], ln1_gain, ffn1_in, ffn1_out, ln2_gain, w_qkv, freq
    )
    context, raw_context, log_sums = repair(lengths, flag, near, far, context, raw_context, log_sums)
    output, grad_x2, grad_context, mid, point_two, bn_grads, two = middle(
        lengths, context, x1, cotangent[0], ln3_gain, ln4_gain, ln5_gain, w_out, w_point1, depthwise,
        bn_gain, bn_bias, w_point2, ffn2_in, ffn2_out, dp,
    )
    input_grad, full = back(
        lengths, near, far, raw_context, log_sums, grad_context, trig, ln1_gain, ln2_gain, two, mid, point_two,
        tokens[0], x1, n2, grad_x2, act, slope, ffn1_in, ffn1_out, w_qkv,
    )
    results = unpack(full, bn_grads, output, input_grad, depthwise.shape[0])
    return (results[0][None], results[1][None]) + tuple(results[2:])


def solution(mesh):
    split = P("dp", "sp", None)
    return jax.shard_map(
        on_device,
        mesh=mesh,
        in_specs=(split,) + (P(),) * 16 + (P("dp", None), split),
        out_specs=(split, split) + (P(),) * 16,
        check_vma=False,
    )
```

```python
import functools

import jax
import jax.numpy as jnp
import numpy as np
from jax import lax
from jax.experimental import pallas as pl
from jax.experimental.pallas import tpu as pltpu
from jax.sharding import PartitionSpec as P

HEADS = 4
EPS = 1e-05
NEG = -1e30
LN2 = float(np.log(2.0))
F32 = jnp.float32
BF16 = jnp.bfloat16
I32 = jnp.int32
MESH = pl.DeviceIdType.MESH
VMEM = pl.BlockSpec(memory_space=pltpu.VMEM)
SMEM = pl.BlockSpec(memory_space=pltpu.SMEM)
DMA = pltpu.SemaphoreType.DMA
VMEM_LIMIT = 56 * 2**20
EARLY_TIMES = (0, 1, 3, 5, 9, 11, 13)


def dg(left, right, left_dim, right_dim):
    return lax.dot_general(
        left, right, (((left_dim,), (right_dim,)), ((), ())), preferred_element_type=F32
    )


def rows_at(index, count):
    return pl.ds(pl.multiple_of(index * count, count), count)


def start_copies(pairs, sems):
    copies = [pltpu.make_async_copy(source, target, sems.at[i]) for i, (source, target) in enumerate(pairs)]
    for copy in copies:
        copy.start()
    return copies


def wait_all(copies):
    for copy in copies:
        copy.wait()


def greet(devices):
    for device in devices:
        pl.semaphore_signal(pltpu.get_barrier_semaphore(), inc=1, device_id=device, device_id_type=MESH)


def await_greetings(devices):
    pl.semaphore_wait(pltpu.get_barrier_semaphore(), len(devices))


def flipped(axis, mask):
    me, step = lax.axis_index(axis), 1
    out = me
    while step <= mask:
        if mask & step:
            out = out + step - 2 * step * lax.rem(me // step, 2)
        step *= 2
    return out


def peer_at(sp_mask, dp_mask):
    return (flipped("dp", dp_mask), flipped("sp", sp_mask))


def sp_peers(count):
    return [peer_at(mask, 0) for mask in range(1, count)]


def row_of(ref):
    return ref[...].astype(F32).reshape(1, ref.shape[0])


def frame_cols(device, frames, c, chunk):
    return pl.ds(pl.multiple_of(device * frames + c * chunk, chunk), chunk)


def ends_of(len_ref, items):
    ends, total = [], 0
    for item in range(items):
        total = total + len_ref[0, item]
        ends.append(total)
    return ends


def segment_row(first, count, ends):
    frame = first + lax.broadcasted_iota(I32, (1, count), 1)
    segment = jnp.zeros((1, count), I32)
    for end in ends:
        segment = segment + (frame >= end).astype(I32)
    return segment


def position_row(first, count, ends):
    frame = first + lax.broadcasted_iota(I32, (1, count), 1)
    start = jnp.zeros((1, count), I32)
    for end in ends:
        start = jnp.where(frame >= end, end, start)
    return (frame - start).astype(F32)


def onehot_rows(segment, items, other, same):
    row = lax.broadcasted_iota(I32, (16, segment.shape[1]), 0)
    return jnp.where(row <= items, jnp.where(row == segment, same, other), 0.0)


def norm_parts(rows):
    centre = rows - jnp.mean(rows, axis=-1, keepdims=True)
    inv = lax.rsqrt(jnp.mean(centre * centre, axis=-1, keepdims=True) + EPS)
    return centre * inv, inv


def norm_back(grad, hat, inv, gain):
    scaled = grad * gain
    first = jnp.mean(scaled, axis=-1, keepdims=True)
    second = jnp.mean(scaled * hat, axis=-1, keepdims=True)
    return inv * (scaled - first - hat * second)


def sigmoid(x):
    return 1.0 / (1.0 + jnp.exp(-x))


def sine_cosine(position, freq_hi, freq_lo):
    turns = position * freq_hi
    turns = turns - jnp.round(turns) + position * freq_lo
    turns = turns - jnp.round(turns)
    x = turns * float(np.pi)
    x2 = x * x
    s = x * (1 + x2 * (-1 / 6 + x2 * (1 / 120 + x2 * (-1 / 5040 + x2 * (1 / 362880 - x2 / 39916800)))))
    c = 1 + x2 * (-1 / 2 + x2 * (1 / 24 + x2 * (-1 / 720 + x2 * (1 / 40320 + x2 * (-1 / 3628800 + x2 / 479001600)))))
    return 2 * s * c, 1 - 2 * s * s


def split_rows(value):
    row = lax.broadcasted_iota(I32, (16, value.shape[1]), 0)
    first = value.astype(BF16).astype(F32)
    second = (value - first).astype(BF16).astype(F32)
    third = value - first - second
    picked = jnp.where(row == 0, first, jnp.where(row == 1, second, third))
    return jnp.where(row < 3, picked, 0.0).astype(BF16)


def first_rows(count, columns):
    row = lax.broadcasted_iota(I32, (16, columns), 0)
    return jnp.where(row < count, 1.0, 0.0).astype(BF16)


def query_rows(query, segment, items, shift):
    pad = jnp.zeros((query.shape[0] - 32, query.shape[1]), BF16)
    return jnp.concatenate([query, onehot_rows(segment, items, 0.0, 1.0).astype(BF16), split_rows(shift), pad], axis=0)


def key_rows(key, segment, items):
    pad = jnp.zeros((key.shape[0] - 32, key.shape[1]), BF16)
    return jnp.concatenate(
        [key, onehot_rows(segment, items, NEG, 0.0).astype(BF16), first_rows(3, key.shape[1]), pad], axis=0
    )


def lay_queries(near, slot, frames, first, ends, items, dim, qa, lse):
    cols = slice(slot * frames, (slot + 1) * frames)
    segment = segment_row(first, frames, ends)
    for h in range(2):
        query = near[slot, h * dim : (h + 1) * dim, :]
        key = near[slot, (2 + h) * dim : (3 + h) * dim, :]
        own = jnp.sum(query.astype(F32) * key.astype(F32), axis=0, keepdims=True)
        lse[h : h + 1, cols] = own
        qa[h, :, cols] = query_rows(query, segment, items, -own)


def lay_keys(key, value, rows, first, ends, items, h, ka, va):
    dim, count = key.shape
    ka[h, rows, :] = key_rows(key, segment_row(first, count, ends), items).T
    va[h, 0:dim, rows] = value
    va[h, dim:, rows] = first_rows(1, count)


def front_kernel(
    items, chunk, block, len_ref, tok, gain1, w_in, w_out, gain2, w_qkv, freq,
    x1_hbm, n2_hbm, trig_hbm, act_hbm, slope_hbm, near_hbm, far_hbm, ctx_hbm, o_hbm, lse, flag,
    x1_ref, n2_ref, trig, act, slope, near, far, ctx, o_ref,
    parts, turned, qa, ka, va, acc, send, recv, out_sems, last_sems,
):
    me = lax.axis_index("sp")
    core, pair = lax.rem(me, 2), me // 2
    frames, width = tok.shape
    half = trig.shape[0] // 2
    dim = 2 * half
    count = frames // chunk
    peers = [peer_at(mask, 0) for mask in (1, 2, 3)]
    greet(peers)
    turned[...] = w_qkv[...].T
    ends = ends_of(len_ref, items)
    scale = float(np.log2(np.e)) * dim**-0.5

    def copies(c):
        cols = rows_at(c, chunk)
        ways = (
            (parts.at[1 - core, :, cols], near.at[core, :, cols]),
            (parts.at[core, 2 * dim :, cols], far.at[core, :, cols]),
            (parts.at[1 - core, 2 * dim :, cols], far.at[core, :, cols]),
        )
        return [
            pltpu.make_async_remote_copy(
                src_ref=source, dst_ref=target, send_sem=send.at[i, c], recv_sem=recv.at[i, c],
                device_id=peers[i], device_id_type=MESH,
            )
            for i, (source, target) in enumerate(ways)
        ]

    def results(c):
        rows = rows_at(c, chunk)
        pairs = [(ref.at[rows, :], hbm.at[rows, :]) for ref, hbm in (
            (x1_ref, x1_hbm), (n2_ref, n2_hbm), (act, act_hbm), (slope, slope_hbm)
        )]
        return [pltpu.make_async_copy(source, target, out_sems.at[i, c]) for i, (source, target) in enumerate(pairs)]

    def step(c, carry):
        rows = rows_at(c, chunk)
        x = tok[rows, :].astype(F32)
        hat, _ = norm_parts(x)
        n1 = (hat * row_of(gain1)).astype(BF16)
        a = dg(n1, w_in[...], 1, 0)
        sig = sigmoid(a)
        s = (a * sig).astype(BF16)
        act[rows, :] = s
        slope[rows, :] = (sig * (1.0 + a * (1.0 - sig))).astype(BF16)
        x1 = x + 0.5 * dg(s, w_out[...], 1, 0)
        x1_ref[rows, :] = x1
        hat, _ = norm_parts(x1)
        n2 = (hat * row_of(gain2)).astype(BF16)
        n2_ref[rows, :] = n2
        joined = dg(turned[...], n2, 1, 1)
        sine, cosine = sine_cosine(
            position_row(me * frames + c * chunk, chunk, ends), freq[:, 0:1], freq[:, 1:2]
        )
        trig[0:half, rows] = sine
        trig[half:, rows] = cosine
        for p in range(2):
            for j in range(2):
                for part, factor in ((0, scale), (1, 1.0)):
                    low = part * width + (2 * p + j) * dim
                    first, second = joined[low : low + half], joined[low + half : low + dim]
                    low = (2 * part + j) * dim
                    parts[p, low : low + half, rows] = ((first * cosine - second * sine) * factor).astype(BF16)
                    parts[p, low + half : low + dim, rows] = (
                        (first * sine + second * cosine) * factor
                    ).astype(BF16)
                low = 2 * width + (2 * p + j) * dim
                parts[p, (4 + j) * dim : (5 + j) * dim, rows] = joined[low : low + dim].astype(BF16)

        @pl.when(c == 0)
        def _():
            await_greetings(peers)

        for copy in copies(c):
            copy.start()
        near[core, :, rows] = parts[core, :, rows]
        for copy in results(c):
            copy.start()
        return carry

    lax.fori_loop(0, count, step, 0)

    def near_arrives(c, carry):
        copies(c)[0].wait()
        return carry

    lax.fori_loop(0, count, near_arrives, 0)
    leaving = start_copies([(near, near_hbm), (trig, trig_hbm)], last_sems)
    reach = 2 * frames
    for slot in range(2):
        first = (2 * pair + slot) * frames
        lay_queries(near, slot, frames, first, ends, items, dim, qa, lse)
        for h in range(2):
            lay_keys(
                near[slot, (2 + h) * dim : (3 + h) * dim, :], near[slot, (4 + h) * dim : (5 + h) * dim, :],
                slice(slot * frames, (slot + 1) * frames), first, ends, items, h, ka, va,
            )

    def near_step(i, carry):
        h, cols = i // (reach // block), rows_at(lax.rem(i, reach // block), block)
        powers = jnp.exp2(dg(ka[h, 0:reach, :], qa[h, :, cols], 1, 0)).astype(BF16)
        acc[h, :, cols] = dg(va[h, :, 0:reach], powers, 1, 0)
        return carry

    lax.fori_loop(0, 2 * reach // block, near_step, 0)
    wide = min(1024, reach)

    def far_step(c, carry):
        for copy in copies(c)[1:]:
            copy.wait()
        cols = rows_at(c, chunk)
        for slot in range(2):
            first = (2 * (1 - pair) + slot) * frames + c * chunk
            rows = pl.ds(pl.multiple_of(reach + (2 * c + slot) * chunk, chunk), chunk)
            for h in range(2):
                lay_keys(
                    far[slot, h * dim : (h + 1) * dim, cols], far[slot, (2 + h) * dim : (3 + h) * dim, cols],
                    rows, first, ends, items, h, ka, va,
                )
        rows = pl.ds(pl.multiple_of(reach + 2 * c * chunk, 2 * chunk), 2 * chunk)

        def inner(i, carry):
            h, cols = i // (reach // wide), rows_at(lax.rem(i, reach // wide), wide)
            powers = jnp.exp2(dg(ka[h, rows, :], qa[h, :, cols], 1, 0)).astype(BF16)
            acc[h, :, cols] += dg(va[h, :, rows], powers, 1, 0)
            return carry

        return lax.fori_loop(0, 2 * reach // wide, inner, carry)

    lax.fori_loop(0, count, far_step, 0)
    leaving += start_copies([(far, far_hbm)], last_sems.at[pl.ds(2, 1)])
    bad = jnp.zeros((1, reach), F32)
    for h in range(2):
        total = acc[h, dim : dim + 1, :]
        value = acc[h, 0:dim, :] / total
        ctx[h] = value.astype(BF16)
        o_ref[h] = value
        leaving += start_copies([(ctx.at[h], ctx_hbm.at[h]), (o_ref.at[h], o_hbm.at[h])], last_sems.at[pl.ds(3 + 2 * h, 2)])
        lse[h : h + 1, :] = lse[h : h + 1, :] + jnp.log2(total)
        bad = jnp.maximum(bad, jnp.where(total < 2.0**60, 0.0, 1.0))
    flag[...] = jnp.broadcast_to(jnp.max(bad, axis=1, keepdims=True), flag.shape)
    for c in range(count):
        wait_all(results(c))
    wait_all(leaving)


def front(lengths, tok, gain1, w_in, w_out, gain2, w_qkv, freq):
    frames, width = tok.shape
    wide = w_in.shape[1]
    chunk = min(256, frames)
    count = frames // chunk
    dim = width // HEADS
    reach = 2 * frames
    return pl.pallas_call(
        functools.partial(front_kernel, lengths.shape[1], chunk, min(512, reach)),
        out_shape=[
            jax.ShapeDtypeStruct((frames, width), F32),
            jax.ShapeDtypeStruct((frames, width), BF16),
            jax.ShapeDtypeStruct((dim, frames), F32),
            jax.ShapeDtypeStruct((frames, wide), BF16),
            jax.ShapeDtypeStruct((frames, wide), BF16),
            jax.ShapeDtypeStruct((2, 6 * dim, frames), BF16),
            jax.ShapeDtypeStruct((2, 4 * dim, frames), BF16),
            jax.ShapeDtypeStruct((2, dim, reach), BF16),
            jax.ShapeDtypeStruct((2, dim, reach), F32),
            jax.ShapeDtypeStruct((2, reach), F32),
            jax.ShapeDtypeStruct((8, 128), F32),
        ],
        in_specs=[SMEM] + [VMEM] * 7,
        out_specs=[pl.BlockSpec(memory_space=pl.ANY)] * 9 + [VMEM] * 2,
        scratch_shapes=[
            pltpu.VMEM((frames, width), F32),
            pltpu.VMEM((frames, width), BF16),
            pltpu.VMEM((dim, frames), F32),
            pltpu.VMEM((frames, wide), BF16),
            pltpu.VMEM((frames, wide), BF16),
            pltpu.VMEM((2, 6 * dim, frames), BF16),
            pltpu.VMEM((2, 4 * dim, frames), BF16),
            pltpu.VMEM((2, dim, reach), BF16),
            pltpu.VMEM((2, dim, reach), F32),
            pltpu.VMEM((2, 6 * dim, frames), BF16),
            pltpu.VMEM((3 * width, width), BF16),
            pltpu.VMEM((2, 2 * dim, reach), BF16),
            pltpu.VMEM((2, 2 * reach, 2 * dim), BF16),
            pltpu.VMEM((2, dim + 16, 2 * reach), BF16),
            pltpu.VMEM((2, dim + 16, reach), F32),
            DMA((3, count)),
            DMA((3, count)),
            DMA((4, count)),
            DMA((7,)),
        ],
        compiler_params=pltpu.CompilerParams(
            collective_id=0, has_side_effects=True, vmem_limit_bytes=VMEM_LIMIT
        ),
        name="front",
    )(lengths, tok, gain1, w_in, w_out, gain2, w_qkv, freq)


def repair_kernel(
    items, block, len_ref, flag, near_hbm, far_hbm, ctx_in, o_in, lse_in, ctx_hbm, o_hbm, lse_hbm,
    near, far, ctx, o_ref, lse, qa, ka, va, sems,
):
    @pl.when(jnp.max(flag[...]) > 0.5)
    def _():
        pair = lax.axis_index("sp") // 2
        frames, dim = near.shape[2], near.shape[1] // 6
        reach = 2 * frames
        ends = ends_of(len_ref, items)
        loads = [
            pltpu.make_async_copy(near_hbm, near, sems.at[0]),
            pltpu.make_async_copy(far_hbm, far, sems.at[1]),
        ]
        for copy in loads:
            copy.start()
        for copy in loads:
            copy.wait()
        for slot in range(2):
            first, other = (2 * pair + slot) * frames, (2 * (1 - pair) + slot) * frames
            lay_queries(near, slot, frames, first, ends, items, dim, qa, lse)
            for h in range(2):
                lay_keys(
                    near[slot, (2 + h) * dim : (3 + h) * dim, :], near[slot, (4 + h) * dim : (5 + h) * dim, :],
                    slice(slot * frames, (slot + 1) * frames), first, ends, items, h, ka, va,
                )
                lay_keys(
                    far[slot, h * dim : (h + 1) * dim, :], far[slot, (2 + h) * dim : (3 + h) * dim, :],
                    slice(reach + slot * frames, reach + (slot + 1) * frames), other, ends, items, h, ka, va,
                )

        def step(i, carry):
            h, cols = i // (reach // block), rows_at(lax.rem(i, reach // block), block)
            query = qa[h, :, cols]

            def highest(j, top):
                scores = dg(ka[h, rows_at(j, block), :], query, 1, 0)
                return jnp.maximum(top, jnp.max(scores, axis=0, keepdims=True))

            top = lax.fori_loop(0, 2 * reach // block, highest, jnp.zeros((1, block), F32))

            def add(j, total):
                rows = rows_at(j, block)
                powers = jnp.exp2(dg(ka[h, rows, :], query, 1, 0) - top).astype(BF16)
                return total + dg(va[h, :, rows], powers, 1, 0)

            total = lax.fori_loop(0, 2 * reach // block, add, jnp.zeros((dim + 16, block), F32))
            value = total[0:dim, :] / total[dim : dim + 1, :]
            ctx[h, :, cols] = value.astype(BF16)
            o_ref[h, :, cols] = value
            change = top + jnp.log2(total[dim : dim + 1, :])
            row = lax.broadcasted_iota(I32, (2, block), 0)
            lse[:, cols] = lse[:, cols] + jnp.where(row == h, change, 0.0)
            return carry

        lax.fori_loop(0, 2 * reach // block, step, 0)
        stores = [
            pltpu.make_async_copy(ctx, ctx_hbm, sems.at[2]),
            pltpu.make_async_copy(o_ref, o_hbm, sems.at[3]),
            pltpu.make_async_copy(lse, lse_hbm, sems.at[4]),
        ]
        for copy in stores:
            copy.start()
        for copy in stores:
            copy.wait()


def repair(lengths, flag, near, far, ctx, o, lse):
    dim, reach = ctx.shape[1:]
    anywhere = pl.BlockSpec(memory_space=pl.ANY)
    return pl.pallas_call(
        functools.partial(repair_kernel, lengths.shape[1], min(512, reach)),
        out_shape=[jax.ShapeDtypeStruct(x.shape, x.dtype) for x in (ctx, o, lse)],
        in_specs=[SMEM, VMEM] + [anywhere] * 5,
        out_specs=[anywhere] * 3,
        input_output_aliases={4: 0, 5: 1, 6: 2},
        scratch_shapes=[
            pltpu.VMEM(near.shape, BF16),
            pltpu.VMEM(far.shape, BF16),
            pltpu.VMEM(ctx.shape, BF16),
            pltpu.VMEM(o.shape, F32),
            pltpu.VMEM(lse.shape, F32),
            pltpu.VMEM((2, 2 * dim, reach), BF16),
            pltpu.VMEM((2, 2 * reach, 2 * dim), BF16),
            pltpu.VMEM((2, dim + 16, 2 * reach), BF16),
            DMA((5,)),
        ],
        compiler_params=pltpu.CompilerParams(vmem_limit_bytes=VMEM_LIMIT),
        name="repair",
    )(lengths, flag, near, far, ctx, o, lse)


def axis_steps(axis):
    steps, step = [], 1
    while step < lax.axis_size(axis):
        steps.append((axis, step))
        step *= 2
    assert step == lax.axis_size(axis)
    return steps


def stage_plans():
    sp_steps, dp_steps = axis_steps("sp"), axis_steps("dp")
    plane, rest = sp_steps[1:] + dp_steps[:1], dp_steps[1:]

    def groups(steps):
        return [steps[i : i + 2] for i in range(0, len(steps), 2)]

    plans = (
        groups(plane) + groups(rest),
        groups(rest) + groups(plane),
        [dp_steps[:1]] + groups(rest) + groups(sp_steps[1:]),
    )
    return tuple([sp_steps[:1]] + [stage for stage in plan if stage] for plan in plans)


def stage_masks(stage):
    masks = []
    for number in range(1, 1 << len(stage)):
        mask = {"sp": 0, "dp": 0}
        for i, (axis, step) in enumerate(stage):
            if number & (1 << i):
                mask[axis] += step
        masks.append((mask["sp"], mask["dp"]))
    return masks


def place_in(stage, number):
    place = 0
    for i, (axis, step) in enumerate(stage):
        bit = lax.rem(lax.axis_index(axis) // step, 2)
        place = place + (1 << i) * (1 - bit if number & (1 << i) else bit)
    return place


def exchange_plan(rows, stages, offset=0):
    sizes, size = [], rows
    for stage in stages:
        group = 1 << len(stage)
        splits = size % (16 * group) == 0
        size = size // group if splits else size
        sizes.append((splits, size, offset))
        offset += (group - 1) * size
    return sizes, offset, size


class Reduction:
    def __init__(self, base, rows, staged, stages, acc, stage, land, full, send, recv):
        self.stages, self.acc, self.stage, self.land, self.full = stages, acc, stage, land, full
        self.send, self.recv, self.base = send, recv, base
        self.sizes, _, self.own = exchange_plan(rows, stages, staged)
        self.first_sem = [sum((1 << len(s)) - 1 for s in stages[:k]) for k in range(len(stages))]

    def at(self, low, size):
        return pl.ds(pl.multiple_of(low, 16), size)

    def low(self, k):
        return self.base + sum(
            place_in(self.stages[j], 0) * self.sizes[j][1] for j in range(k) if self.sizes[j][0]
        )

    def slot(self, k, i):
        _, size, offset = self.sizes[k]
        return slice(offset + i * size, offset + (i + 1) * size)

    def copies(self, way, k):
        splits, size, _ = self.sizes[k]
        out = []
        for i, masks in enumerate(stage_masks(self.stages[k])):
            if way == 0:
                source = self.stage.at[self.slot(k, i if splits else 0), :]
                target = self.land.at[self.slot(k, i), :]
            else:
                source = target = self.full.at[self.at(self.low(k + 1), size), :]
            out.append(
                pltpu.make_async_remote_copy(
                    src_ref=source,
                    dst_ref=target,
                    send_sem=self.send.at[way, self.first_sem[k] + i],
                    recv_sem=self.recv.at[way, self.first_sem[k] + i],
                    device_id=peer_at(*masks),
                    device_id_type=MESH,
                )
            )
        return out

    def sum_send(self, k):
        splits, size, _ = self.sizes[k]
        copies = self.copies(0, k)
        for i, copy in enumerate(copies):
            if splits:
                away = self.low(k) + place_in(self.stages[k], i + 1) * size
                self.stage[self.slot(k, i), :] = self.acc[self.at(away, size), :].astype(BF16)
            elif i == 0:
                self.stage[self.slot(k, 0), :] = self.acc[self.at(self.low(k), size), :].astype(BF16)
            copy.start()

    def sum_recv(self, k):
        splits, size, _ = self.sizes[k]
        copies = self.copies(0, k)
        for copy in copies:
            copy.wait()
        values = [self.land[self.slot(k, i), :].astype(F32) for i in range(len(copies))]
        if splits:
            values = [self.acc[self.at(self.low(k + 1), size), :]] + values
        else:
            values = [self.stage[self.slot(k, 0), :].astype(F32)] + values
        while len(values) > 1:
            values = [values[i] + values[i + 1] for i in range(0, len(values), 2)]
        self.acc[self.at(self.low(k + 1), size), :] = values[0]

    def close(self):
        where = self.at(self.low(len(self.stages)), self.own)
        self.full[where, :] = self.acc[where, :].astype(BF16)

    def share_send(self, k):
        if self.sizes[k][0]:
            for copy in self.copies(1, k):
                copy.start()

    def share_recv(self, k):
        if self.sizes[k][0]:
            for copy in self.copies(1, k):
                copy.wait()


def advance(streams, position):
    for stream in streams:
        n = len(stream.stages)
        if 0 < position <= n:
            stream.sum_recv(position - 1)
        if position < n:
            stream.sum_send(position)
        else:
            if position == n:
                stream.close()
            else:
                stream.share_recv(2 * n - position)
            if position < 2 * n:
                stream.share_send(2 * n - 1 - position)


def reduction_scratch(rows_list):
    staged = sum(max(exchange_plan(rows, stages)[1] for stages in stage_plans()) for rows in rows_list)
    sems = max(sum((1 << len(stage)) - 1 for stage in plan) for plan in stage_plans())
    return staged, (len(rows_list), 2, sems)


def make_streams(items, acc, stage, land, full, send, recv):
    streams, staged = [], 0
    for i, (base, rows, order) in enumerate(items):
        stages = stage_plans()[order]
        streams.append(
            Reduction(base, rows, staged, stages, acc, stage, land, full, send.at[i], recv.at[i])
        )
        staged += max(exchange_plan(rows, plan)[1] for plan in stage_plans())
    return streams


def all_masks(sp):
    masks = [(mask, 0) for mask in range(1, sp)]
    for plan in stage_plans():
        for stage in plan:
            masks += [m for m in stage_masks(stage) if m not in masks]
    return masks


def halves_of(ref, rows):
    return jnp.concatenate([ref[0, rows, :], ref[1, rows, :]], axis=1)


def combine(entries):
    count = sum(e[2] for e in entries)
    safe = jnp.maximum(count, 1.0)
    mean = sum(e[2] * e[0] for e in entries) / safe
    spread = sum(e[1] + e[2] * (e[0] - mean) * (e[0] - mean) for e in entries)
    return mean, spread, count


def pick(ref):
    return ref[0:1, :], ref[1:2, :], ref[2:3, :]


def total(entries):
    return tuple(sum(e[i] for e in entries) for i in range(3))


def middle_kernel(
    sp, dp, items, taps, chunk, block, len_ref, parts, x1_hbm, cot_hbm, gain3, gain4, gain5, w_out_hbm,
    w_point1_hbm, depthwise, bn_gain, bn_bias, w_point2_hbm, w_in_hbm, w_down_hbm,
    out_hbm, x2_hbm, heads, mid_hbm, point_two_hbm, bn_grads, two_hbm,
    x1_ref, cot, w_out, w_point1, w_point2, w_in, w_down, out_ref, grad_x2, mid, point_two, two, load_sems, out_sems,
    ctx, x2_ref, n3_keep, point, glu, conv, low_lim, high_lim, act, hidden, n4_keep, branch, swish, branch2,
    grad_x3, grad_y, grad_conv, grad_glu, grad_point, branch3, back_parts, tap_sums, edge_out, edge_in,
    send_box, near_box, far_box, sums,
    send, recv, local, back_send, back_recv, back_local, rim_send, rim_recv, box_send, box_recv,
):
    me, me_dp = lax.axis_index("sp"), lax.axis_index("dp")
    frames, width = x1_ref.shape
    lanes = width // 2
    reach = taps // 2
    count = frames // chunk
    peers = sp_peers(sp)
    far_peers = [peer_at(0, mask) for mask in range(1, dp)]
    greeted = peers + far_peers
    core = lax.rem(me, 2)
    sibling = peer_at(1, 0)
    length = sp * frames
    ends = ends_of(len_ref, items)
    first_frame = me * frames

    def limits(b, carry):
        rows = rows_at(b, chunk)
        frame = first_frame + b * chunk + lax.broadcasted_iota(I32, (chunk, lanes), 0)
        low, high = jnp.zeros_like(frame), jnp.full_like(frame, length)
        for end in ends:
            low = jnp.where(frame >= end, end, low)
        for end in reversed(ends):
            high = jnp.where(frame < end, end, high)
        low_lim[rows, :] = low - frame
        high_lim[rows, :] = high - 1 - frame
        return carry

    for ref in (glu, grad_conv):
        for h in range(2):
            ref[h, 0:reach, :] = jnp.zeros((reach, lanes), F32)
            ref[h, reach + frames :, :] = jnp.zeros((reach, lanes), F32)
    edge_in[...] = jnp.zeros_like(edge_in)
    send_box[...] = jnp.zeros_like(send_box)
    greet(greeted)
    loads = start_copies(
        [
            (w_out_hbm, w_out), (x1_hbm, x1_ref), (w_point1_hbm, w_point1), (w_point2_hbm, w_point2),
            (w_in_hbm, w_in), (w_down_hbm, w_down), (cot_hbm, cot),
        ],
        load_sems,
    )
    lax.fori_loop(0, count, limits, 0)
    tap_sums[...] = jnp.zeros_like(tap_sums)
    sums[...] = jnp.zeros_like(sums)
    await_greetings(greeted)

    def moves(c, source, target, send_sems, recv_sems, local_sems):
        return [
            pltpu.make_async_remote_copy(
                src_ref=source(1 - core, c), dst_ref=target(core, c),
                send_sem=send_sems.at[c], recv_sem=recv_sems.at[c],
                device_id=sibling, device_id_type=MESH,
            ),
            pltpu.make_async_copy(source(core, c), target(core, c), local_sems.at[c]),
        ]

    def by_frames(ref):
        return lambda slot, c: ref.at[:, :, frame_cols(slot, frames, c, chunk)]

    def by_head(ref):
        return lambda slot, c: ref.at[slot, :, :, rows_at(c, chunk)]

    def context_moves(c):
        return moves(c, by_frames(parts), by_head(ctx), send, recv, local)

    def begin(c, carry):
        for copy in context_moves(c):
            copy.start()
        return carry

    lax.fori_loop(0, count, begin, 0)
    wait_all(loads[:3])

    def open_step(c, carry):
        rows = rows_at(c, chunk)
        for copy in context_moves(c):
            copy.wait()
        context = ctx[:, :, :, rows].reshape(width, chunk)
        x2 = x1_ref[rows, :] + dg(context, w_out[...], 0, 0)
        x2_ref[rows, :] = x2
        hat, _ = norm_parts(x2)
        n3 = (hat * row_of(gain3)).astype(BF16)
        n3_keep[rows, :] = n3
        pair = dg(n3, w_point1[...], 1, 0)
        point[rows, :] = pair
        gated = (pair[:, :width] * sigmoid(pair[:, width:])).astype(BF16).astype(F32)
        where = pl.ds(pl.multiple_of(reach + c * chunk, 8), chunk)
        glu[0, where, :] = gated[:, :lanes]
        glu[1, where, :] = gated[:, lanes:]
        return carry

    lax.fori_loop(0, count, open_step, 0)

    def rim_copies(call, side, source, target):
        peer = (me_dp, me - 1 if side == 0 else me + 1)
        return pltpu.make_async_remote_copy(
            src_ref=source, dst_ref=target, send_sem=rim_send.at[call, side], recv_sem=rim_recv.at[call, side],
            device_id=peer, device_id_type=MESH,
        )

    def swap_rims(call, sources, targets):
        @pl.when(me > 0)
        def _():
            rim_copies(call, 0, sources[0], targets[1]).start()

        @pl.when(me < sp - 1)
        def _():
            rim_copies(call, 1, sources[1], targets[0]).start()

    def await_rims(call, sources, targets):
        @pl.when(me > 0)
        def _():
            rim_copies(call, 0, sources[0], targets[1]).wait_send()
            rim_copies(call, 1, sources[1], targets[0]).wait_recv()

        @pl.when(me < sp - 1)
        def _():
            rim_copies(call, 1, sources[1], targets[0]).wait_send()
            rim_copies(call, 0, sources[0], targets[1]).wait_recv()

    for side, rows in ((0, slice(reach, 2 * reach)), (1, slice(frames, frames + reach))):
        for h in range(2):
            edge_out[side, 0:reach, h * lanes : (h + 1) * lanes] = glu[h, rows, :]
    glu_rims = (
        [edge_out.at[0, 0:reach, :], edge_out.at[1, 0:reach, :]],
        [edge_in.at[0, 0:reach, :], edge_in.at[1, 0:reach, :]],
    )
    swap_rims(0, *glu_rims)

    zero = jnp.zeros((block, lanes), F32)

    def conv_step(b, carry):
        low, high = low_lim[rows_at(b, block), :], high_lim[rows_at(b, block), :]
        start = pl.multiple_of(b * block, block)
        result = [zero, zero]
        for tap in range(taps):
            shift = tap - reach
            inside = (low <= shift) if shift < 0 else (high >= shift)
            for h in range(2):
                view = glu.at[h, pl.ds(start, block + 2 * reach), :]
                term = jnp.where(inside, view[tap : tap + block, :], 0.0)
                result[h] = result[h] + depthwise[tap : tap + 1, h * lanes : (h + 1) * lanes].astype(F32) * term
        valid = (first_frame + start + lax.broadcasted_iota(I32, (block, lanes), 0)) < ends[-1]
        for h in range(2):
            conv[h, rows_at(b, block), :] = result[h]
            sums[0:1, h * lanes : (h + 1) * lanes] += jnp.sum(jnp.where(valid, result[h], 0.0), axis=0, keepdims=True)
        return carry

    blocks = frames // block
    lax.fori_loop(1, blocks - 1, conv_step, 0)
    await_rims(0, *glu_rims)
    for h in range(2):
        glu[h, 0:reach, :] = edge_in[0, 0:reach, h * lanes : (h + 1) * lanes]
        glu[h, reach + frames :, :] = edge_in[1, 0:reach, h * lanes : (h + 1) * lanes]
    conv_step(0, 0)
    conv_step(blocks - 1, 0)

    own_count = jnp.clip(ends[-1] - first_frame, 0, frames).astype(F32)
    own_mean = sums[0:1, :] / jnp.maximum(own_count, 1.0)
    sums[0:1, :] = jnp.zeros((1, width), F32)

    def spread_step(c, carry):
        rows = rows_at(c, chunk)
        valid = (first_frame + c * chunk + lax.broadcasted_iota(I32, (chunk, width), 0)) < ends[-1]
        apart = jnp.where(valid, halves_of(conv, rows) - own_mean, 0.0)
        sums[1:2, :] += jnp.sum(apart * apart, axis=0, keepdims=True)
        return carry

    lax.fori_loop(0, count, spread_step, 0)

    def box_copies(call, stage):
        group = peers if stage == 0 else far_peers
        target = near_box if stage == 0 else far_box
        base = 0 if stage == 0 else sp - 1
        return [
            pltpu.make_async_remote_copy(
                src_ref=send_box.at[call, stage],
                dst_ref=target.at[call, i],
                send_sem=box_send.at[call, base + i],
                recv_sem=box_recv.at[call, base + i],
                device_id=peer,
                device_id_type=MESH,
            )
            for i, peer in enumerate(group)
        ]

    def box_begin(call, stage, rows):
        for i, row in enumerate(rows):
            send_box[call, stage, i : i + 1, :] = row
        for copy in box_copies(call, stage):
            copy.start()

    def box_end(call, stage, rows, merge):
        target = near_box if stage == 0 else far_box
        copies = box_copies(call, stage)
        for copy in copies:
            copy.wait()
        return merge([rows] + [pick(target[call, i]) for i in range(len(copies))])

    stats = (own_mean, sums[1:2, :], jnp.full((1, width), 1.0, F32) * own_count)
    sums[1:2, :] = jnp.zeros((1, width), F32)
    box_begin(0, 0, stats)
    stats = box_end(0, 0, stats, combine)
    box_begin(0, 1, stats)
    mean, spread, frame_count = box_end(0, 1, stats, combine)
    inv_std = lax.rsqrt(spread / frame_count + EPS)
    norm_gain, norm_bias = row_of(bn_gain), row_of(bn_bias)

    def heart_step(c, carry):
        rows = rows_at(c, chunk)
        normed = (halves_of(conv, rows) - mean) * inv_std
        y = normed * norm_gain + norm_bias
        sig_y = sigmoid(y)
        w = (y * sig_y).astype(BF16)
        swish[rows, :] = w
        x3 = x2_ref[rows, :] + dg(w, w_point2[...], 1, 0)
        hat4, inv4 = norm_parts(x3)
        g4 = row_of(gain4)
        n4 = (hat4 * g4).astype(BF16)
        n4_keep[rows, :] = n4
        a = dg(n4, w_in[...], 1, 0)
        sig = sigmoid(a)
        s = (a * sig).astype(BF16)
        act[rows, :] = s
        x4 = x3 + 0.5 * dg(s, w_down[...], 1, 0)
        hat5, inv5 = norm_parts(x4)
        g5 = row_of(gain5)
        out_ref[rows, :] = (hat5 * g5).astype(BF16)
        top = cot[rows, :].astype(F32)
        mid[3 * width + 4 : 3 * width + 5, :] += jnp.sum(top * hat5, axis=0, keepdims=True)
        grad_x4 = norm_back(top, hat5, inv5, g5)
        low_grad = (0.5 * grad_x4).astype(BF16)
        branch[rows, :] = low_grad
        grad = dg(low_grad, w_down[...], 1, 1)
        low_hidden = (grad * (sig * (1.0 + a * (1.0 - sig)))).astype(BF16)
        hidden[rows, :] = low_hidden
        grad = dg(low_hidden, w_in[...], 1, 1)
        mid[3 * width + 3 : 3 * width + 4, :] += jnp.sum(grad * hat4, axis=0, keepdims=True)
        grad3 = grad_x4 + norm_back(grad, hat4, inv4, g4)
        grad_x3[rows, :] = grad3
        low_grad = grad3.astype(BF16)
        branch2[rows, :] = low_grad
        grad = dg(low_grad, w_point2[...], 1, 1) * (sig_y * (1.0 + y * (1.0 - sig_y)))
        grad_y[0, rows, :] = grad[:, :lanes]
        grad_y[1, rows, :] = grad[:, lanes:]
        sums[2:3, :] += jnp.sum(grad, axis=0, keepdims=True)
        sums[3:4, :] += jnp.sum(grad * normed, axis=0, keepdims=True)
        return carry

    mid[3 * width :, :] = jnp.zeros((width, width), F32)
    wait_all(loads[3:])
    lax.fori_loop(0, count, heart_step, 0)
    leaving = start_copies([(out_ref, out_hbm)], out_sems)

    pair = (sums[2:3, :], sums[3:4, :], jnp.zeros((1, width), F32))
    box_begin(1, 0, pair)
    for side, rows in ((0, slice(0, reach)), (1, slice(frames - reach, frames))):
        for h in range(2):
            cols = slice(h * lanes, (h + 1) * lanes)
            edge_out[side, reach : 2 * reach, cols] = grad_y[h, rows, :]
            edge_out[side, 2 * reach : 3 * reach, cols] = conv[h, rows, :]
    grad_rims = (
        [edge_out.at[0, reach : 3 * reach, :], edge_out.at[1, reach : 3 * reach, :]],
        [edge_in.at[0, reach : 3 * reach, :], edge_in.at[1, reach : 3 * reach, :]],
    )
    swap_rims(1, *grad_rims)
    wide = w_in.shape[1]
    for j in range(0, wide, width):
        two[j : j + width, :] = dg(act[:, j : j + width], branch[...], 0, 0)
    pair = box_end(1, 0, pair, total)
    box_begin(1, 1, pair)
    for j in range(0, wide, width):
        two[wide + j : wide + j + width, :] = dg(n4_keep[...], hidden[:, j : j + width], 0, 0)
    point_two[...] = dg(swish[...], branch2[...], 0, 0)
    leaving += start_copies([(two, two_hbm), (point_two, point_two_hbm)], out_sems.at[pl.ds(1, 2)])
    await_rims(1, *grad_rims)
    bias_sum, gain_sum, _ = box_end(1, 1, pair, total)
    bn_grads[0:1, :] = gain_sum
    bn_grads[1:2, :] = bias_sum
    bn_grads[2:8, :] = jnp.zeros((6, width), F32)

    scale = norm_gain * inv_std
    slope = -inv_std * inv_std * norm_gain * gain_sum / frame_count
    shift_all = -inv_std * norm_gain * bias_sum / frame_count

    def conv_grad(grad, value, frame, h):
        cols = slice(h * lanes, (h + 1) * lanes)
        extra = (value - mean[:, cols]) * slope[:, cols] + shift_all[:, cols]
        return grad * scale[:, cols] + jnp.where(frame < ends[-1], extra, 0.0)

    def grad_conv_step(c, carry):
        rows = rows_at(c, chunk)
        frame = first_frame + c * chunk + lax.broadcasted_iota(I32, (chunk, lanes), 0)
        where = pl.ds(pl.multiple_of(reach + c * chunk, 8), chunk)
        for h in range(2):
            grad_conv[h, where, :] = conv_grad(grad_y[h, rows, :], conv[h, rows, :], frame, h)
        return carry

    lax.fori_loop(0, count, grad_conv_step, 0)
    for side, rows, begin_frame in (
        (0, slice(0, reach), first_frame - reach),
        (1, slice(reach + frames, 2 * reach + frames), first_frame + frames),
    ):
        frame = begin_frame + lax.broadcasted_iota(I32, (reach, lanes), 0)
        for h in range(2):
            cols = slice(h * lanes, (h + 1) * lanes)
            grad_conv[h, rows, :] = conv_grad(
                edge_in[side, reach : 2 * reach, cols], edge_in[side, 2 * reach : 3 * reach, cols], frame, h
            )

    def conv_back_step(b, carry):
        low, high = low_lim[rows_at(b, block), :], high_lim[rows_at(b, block), :]
        start = pl.multiple_of(b * block, block)
        result = [zero, zero]
        here = [glu[h, pl.ds(pl.multiple_of(reach + start, 8), block), :] for h in range(2)]
        for tap in range(taps):
            shift = reach - tap
            inside = (low <= shift) if shift < 0 else (high >= shift)
            at = reach + shift
            for h in range(2):
                view = grad_conv.at[h, pl.ds(start, block + 2 * reach), :]
                term = jnp.where(inside, view[at : at + block, :], 0.0)
                result[h] = result[h] + depthwise[tap : tap + 1, h * lanes : (h + 1) * lanes].astype(F32) * term
                tap_sums[tap, h] += jnp.sum((here[h] * term).reshape(block // 8, 8, lanes), axis=0)
        for h in range(2):
            grad_glu[h, rows_at(b, block), :] = result[h]
        return carry

    lax.fori_loop(0, blocks, conv_back_step, 0)

    def back_moves(c):
        return moves(c, by_head(back_parts), by_frames(heads), back_send, back_recv, back_local)

    def close_step(c, carry):
        rows = rows_at(c, chunk)
        grad = halves_of(grad_glu, rows)
        value, gate = point[rows, :width], sigmoid(point[rows, width:])
        low_grad = jnp.concatenate([grad * gate, grad * value * gate * (1.0 - gate)], axis=1).astype(BF16)
        grad_point[rows, :] = low_grad
        grad = dg(low_grad, w_point1[...], 1, 1)
        hat, inv = norm_parts(x2_ref[rows, :])
        mid[3 * width + 2 : 3 * width + 3, :] += jnp.sum(grad * hat, axis=0, keepdims=True)
        grad2 = grad_x3[rows, :] + norm_back(grad, hat, inv, row_of(gain3))
        grad_x2[rows, :] = grad2
        low_grad = grad2.astype(BF16)
        branch3[rows, :] = low_grad
        back_parts[:, :, :, rows] = dg(w_out[...], low_grad, 1, 1).astype(BF16).reshape(2, 2, width // 4, chunk)
        for copy in back_moves(c):
            copy.start()
        return carry

    lax.fori_loop(0, count, close_step, 0)
    leaving += start_copies([(grad_x2, x2_hbm)], out_sems.at[pl.ds(3, 1)])
    for j in range(2):
        mid[j * width : (j + 1) * width, :] = dg(n3_keep[...], grad_point[:, j * width : (j + 1) * width], 0, 0)
    mid[2 * width : 3 * width, :] = dg(ctx[...].reshape(width, frames), branch3[...], 1, 0)
    for tap in range(taps):
        row = 3 * width + 8 + tap
        for h in range(2):
            mid[row : row + 1, h * lanes : (h + 1) * lanes] = jnp.sum(tap_sums[tap, h], axis=0, keepdims=True)

    leaving += start_copies([(mid, mid_hbm)], out_sems.at[pl.ds(4, 1)])

    def finish(c, carry):
        for copy in back_moves(c):
            copy.wait()
        return carry

    lax.fori_loop(0, count, finish, 0)
    wait_all(leaving)


def middle(
    lengths, parts, x1, cot, gain3, gain4, gain5, w_out, w_point1, depthwise, bn_gain, bn_bias, w_point2,
    w_in, w_down, dp,
):
    frames, width = x1.shape
    sp = lax.axis_size("sp")
    assert sp == HEADS == 4
    anywhere = pl.BlockSpec(memory_space=pl.ANY)
    paired = pltpu.VMEM((2, 2, width // 4, frames), BF16)
    wide = w_in.shape[1]
    taps = depthwise.shape[0]
    reach = taps // 2
    chunk = min(256, frames)
    count = frames // chunk
    lanes = width // 2
    keep, low_keep = pltpu.VMEM((frames, width), F32), pltpu.VMEM((frames, width), BF16)
    split = pltpu.VMEM((2, frames, lanes), F32)
    rimmed = pltpu.VMEM((2, frames + 2 * reach, lanes), F32)
    rims = pltpu.VMEM((2, 3 * reach, width), F32)
    moves = [DMA((count,)), DMA((count,)), DMA((count,))]
    return pl.pallas_call(
        functools.partial(middle_kernel, sp, dp, lengths.shape[1], taps, chunk, 32),
        out_shape=[
            jax.ShapeDtypeStruct((frames, width), BF16),
            jax.ShapeDtypeStruct((frames, width), F32),
            jax.ShapeDtypeStruct(parts.shape, BF16),
            jax.ShapeDtypeStruct((4 * width, width), F32),
            jax.ShapeDtypeStruct((width, width), F32),
            jax.ShapeDtypeStruct((8, width), F32),
            jax.ShapeDtypeStruct((2 * wide, width), F32),
        ],
        in_specs=[
            SMEM, anywhere, anywhere, anywhere, VMEM, VMEM, VMEM, anywhere, anywhere, VMEM, VMEM, VMEM, anywhere,
            anywhere, anywhere,
        ],
        out_specs=[anywhere, anywhere, VMEM, anywhere, anywhere, VMEM, anywhere],
        scratch_shapes=[
            keep,
            low_keep,
            pltpu.VMEM(w_out.shape, BF16),
            pltpu.VMEM(w_point1.shape, BF16),
            pltpu.VMEM(w_point2.shape, BF16),
            pltpu.VMEM(w_in.shape, BF16),
            pltpu.VMEM(w_down.shape, BF16),
            low_keep,
            keep,
            pltpu.VMEM((4 * width, width), F32),
            pltpu.VMEM((width, width), F32),
            pltpu.VMEM((2 * wide, width), F32),
            DMA((7,)),
            DMA((5,)),
            paired,
            keep,
            low_keep,
            pltpu.VMEM((frames, 2 * width), F32),
            rimmed,
            split,
            pltpu.VMEM((frames, lanes), I32),
            pltpu.VMEM((frames, lanes), I32),
            pltpu.VMEM((frames, wide), BF16),
            pltpu.VMEM((frames, wide), BF16),
            low_keep,
            low_keep,
            low_keep,
            low_keep,
            keep,
            split,
            rimmed,
            split,
            pltpu.VMEM((frames, 2 * width), BF16),
            low_keep,
            paired,
            pltpu.VMEM((taps, 2, 8, lanes), F32),
            rims,
            rims,
            pltpu.VMEM((2, 2, 8, width), F32),
            pltpu.VMEM((2, sp - 1, 8, width), F32),
            pltpu.VMEM((2, dp - 1, 8, width), F32),
            pltpu.VMEM((8, width), F32),
        ]
        + moves
        + moves
        + [DMA((2, 2)), DMA((2, 2)), DMA((2, sp + dp - 2)), DMA((2, sp + dp - 2))],
        compiler_params=pltpu.CompilerParams(
            collective_id=1, has_side_effects=True, vmem_limit_bytes=VMEM_LIMIT
        ),
        name="middle",
    )(
        lengths, parts, x1, cot, gain3, gain4, gain5, w_out, w_point1, depthwise, bn_gain, bn_bias, w_point2,
        w_in, w_down,
    )


def back_kernel(
    sp, items, chunk, block, sub, len_ref, lse_ref, gain1, gain2,
    near_hbm, far_hbm, o_hbm, do_hbm, trig_hbm, two_hbm, mid_hbm, point_two_hbm, tok_hbm, x1_hbm, n2_hbm, x2_hbm, act_hbm, slope_hbm, w_in_hbm, w_out_hbm, w_qkv_hbm,
    grad_ref, full,
    near, far, o_ref, do_ref, trig, tok, x1_ref, n2_ref, grad_x2, act, slope, w_in, w_out, w_qkv,
    qa, qt, ka, da, va, dq, far_out, near_out, dq_out, far_kv, near_kv, near_dq,
    joined, branch, hidden, grad_x1, gains, acc, stage, land,
    load_sems, far_send, far_recv, near_send, near_recv, sum_send, sum_recv,
):
    me, dp = lax.axis_index("sp"), lax.axis_index("dp")
    core, pair = lax.rem(me, 2), me // 2
    sibling = peer_at(1, 0)
    frames, width = tok.shape
    wide = w_in.shape[1]
    half = trig.shape[0] // 2
    dim = 2 * half
    count = frames // chunk
    reach = 2 * frames
    greeted = [peer_at(*mask) for mask in all_masks(sp)]
    greet(greeted)
    unit = 4 * width
    last = 6 * unit
    loads = start_copies(
        [
            (near_hbm, near), (do_hbm, do_ref), (o_hbm, o_ref), (far_hbm, far),
            (two_hbm, acc.at[0 : 2 * unit, :]), (mid_hbm, acc.at[2 * unit : 3 * unit, :]),
            (point_two_hbm, acc.at[3 * unit + 3 * width : 4 * unit, :]), (trig_hbm, trig),
            (x1_hbm, x1_ref), (x2_hbm, grad_x2), (w_qkv_hbm, w_qkv), (n2_hbm, n2_ref), (act_hbm, act),
            (w_out_hbm, w_out), (slope_hbm, slope), (w_in_hbm, w_in), (tok_hbm, tok),
        ],
        load_sems,
    )
    streams = make_streams(
        [
            (0, unit, 2), (unit, unit, 2), (2 * unit, unit, 2),
            (3 * unit, unit, 1), (4 * unit, unit, 0), (5 * unit, unit, 0), (last, 16, 0),
        ],
        acc, stage, land, full, sum_send, sum_recv,
    )
    early, (qkv, down, up, rest) = streams[:3], ([stream] for stream in streams[3:])
    steps = len(stage_plans()[0])
    acc[last : last + 16, :] = jnp.zeros((16, width), F32)
    gains[...] = jnp.zeros_like(gains)
    for h in range(2):
        dq[h] = jnp.zeros((dim, reach), F32)
    wait_all(loads[:4])
    ends = ends_of(len_ref, items)
    wide_pad = jnp.zeros((dim - 16, frames), BF16)
    for slot in range(2):
        cols = slice(slot * frames, (slot + 1) * frames)
        far_cols = slice(reach + slot * frames, reach + (slot + 1) * frames)
        segment = segment_row((2 * pair + slot) * frames, frames, ends)
        far_segment = segment_row((2 * (1 - pair) + slot) * frames, frames, ends)
        for h in range(2):
            query = near[slot, h * dim : (h + 1) * dim, :]
            qt[h, :, cols] = query
            qa[h, cols, :] = query_rows(query, segment, items, -lse_ref[h : h + 1, cols]).T
            grad = do_ref[h, :, cols]
            row_dot = jnp.sum(grad.astype(F32) * o_ref[h, :, cols], axis=0, keepdims=True)
            da[h, cols, :] = jnp.concatenate([grad, split_rows(-row_dot), wide_pad], axis=0).T
            ka[h, :, cols] = key_rows(near[slot, (2 + h) * dim : (3 + h) * dim, :], segment, items)
            ka[h, :, far_cols] = key_rows(far[slot, h * dim : (h + 1) * dim, :], far_segment, items)
            for where, value in (
                (cols, near[slot, (4 + h) * dim : (5 + h) * dim, :]),
                (far_cols, far[slot, (2 + h) * dim : (3 + h) * dim, :]),
            ):
                va[h, 0:dim, where] = value
                va[h, dim : dim + 16, where] = first_rows(3, frames)
                va[h, dim + 16 :, where] = wide_pad
    await_greetings(greeted)
    wait_all(loads[4:6])

    def attend_block(h, at):
        dk, dv, grads = [], [], []

        def score(u):
            cols = pl.ds(pl.multiple_of(at + u * sub, sub), sub)
            return dg(qa[h], ka[h, :, cols], 1, 0), dg(da[h], va[h, :, cols], 1, 0)

        ready = score(0)
        for u in range(block // sub):
            scores, grad_probs = ready
            if u + 1 < block // sub:
                ready = score(u + 1)
            probs = jnp.exp2(scores)
            grad = (probs * grad_probs).astype(BF16)
            dv.append(dg(do_ref[h], probs.astype(BF16), 1, 0).astype(BF16))
            dk.append((dg(qt[h], grad, 1, 0) * LN2).astype(BF16))
            grads.append(grad)
        dq[h] += dg(ka[h, 0:dim, pl.ds(pl.multiple_of(at, block), block)], jnp.concatenate(grads, axis=1), 1, 1)
        return jnp.concatenate(dk, axis=1), jnp.concatenate(dv, axis=1)

    per = frames // block

    def keep(ref, slot, h, cols, block_grads):
        for i, value in enumerate(block_grads):
            ref[slot, 2 * i + h, :, cols] = value

    def far_copy(b):
        cols = rows_at(lax.rem(b, per), block)
        return pltpu.make_async_remote_copy(
            src_ref=far_out.at[b // per, :, :, cols], dst_ref=far_kv.at[core, :, :, cols],
            send_sem=far_send.at[b], recv_sem=far_recv.at[core, lax.rem(b, per)],
            device_id=(dp, 2 * (1 - pair) + b // per), device_id_type=MESH,
        )

    times = EARLY_TIMES[: 2 * len(early[0].stages) + 1]
    remaining = list(range(len(times), 2 * len(early[0].stages) + 1))

    def early_steps(t):
        for position, time in enumerate(times):
            for i, stream in enumerate(early):
                @pl.when(t == min(time + i, 8 * per - 1))
                def _():
                    advance([stream], position)

    def far_step(t, carry):
        b, h = t // 2, lax.rem(t, 2)
        cols = rows_at(lax.rem(b, per), block)
        keep(far_out, b // per, h, cols, attend_block(h, reach + b * block))

        @pl.when(h == 1)
        def _():
            far_copy(b).start()

        early_steps(t)
        return carry

    lax.fori_loop(0, 4 * per, far_step, 0)

    def near_copy(b):
        cols = rows_at(b, block)
        return pltpu.make_async_remote_copy(
            src_ref=near_out.at[:, :, cols], dst_ref=near_kv.at[core, :, :, cols],
            send_sem=near_send.at[b], recv_sem=near_recv.at[b], device_id=sibling, device_id_type=MESH,
        )

    def sibling_step(t, carry):
        b, h = t // 2, lax.rem(t, 2)
        block_grads = attend_block(h, (1 - core) * frames + b * block)
        for i, value in enumerate(block_grads):
            near_out[2 * i + h, :, rows_at(b, block)] = value

        @pl.when(h == 1)
        def _():
            near_copy(b).start()

        early_steps(t + 4 * per)
        return carry

    lax.fori_loop(0, 2 * per, sibling_step, 0)

    def own_step(t, carry):
        b, h = t // 2, lax.rem(t, 2)
        keep(near_kv, core, h, rows_at(b, block), attend_block(h, core * frames + b * block))

        early_steps(t + 6 * per)
        return carry

    lax.fori_loop(0, 2 * per, own_step, 0)
    for h in range(2):
        dq_out[h] = (dq[h, :, pl.ds(pl.multiple_of((1 - core) * frames, frames), frames)] * dim**-0.5).astype(BF16)
    dq_copy = pltpu.make_async_remote_copy(
        src_ref=dq_out, dst_ref=near_dq.at[core], send_sem=near_send.at[per], recv_sem=near_recv.at[per],
        device_id=sibling, device_id_type=MESH,
    )
    dq_copy.start()
    for h in range(2):
        near_dq[core, h] = (dq[h, :, pl.ds(pl.multiple_of(core * frames, frames), frames)] * dim**-0.5).astype(BF16)
    wait_all(loads[6:])
    for b in range(2 * per):
        far_copy(b).wait_send()
    for source in range(2):
        for b in range(per):
            pltpu.make_async_remote_copy(
                src_ref=far_out.at[0, :, :, rows_at(b, block)], dst_ref=far_kv.at[source, :, :, rows_at(b, block)],
                send_sem=far_send.at[b], recv_sem=far_recv.at[source, b], device_id=sibling, device_id_type=MESH,
            ).wait_recv()
    for b in range(per):
        near_copy(b).wait()

    def turn_back(first, second, rows, low):
        sine, cosine = trig[0:half, rows], trig[half:, rows]
        joined[low : low + half, rows] = (first * cosine + second * sine).astype(BF16)
        joined[low + half : low + dim, rows] = (second * cosine - first * sine).astype(BF16)

    def keys_step(c, carry):
        rows = rows_at(c, chunk)
        for p in range(2):
            for h in range(2):
                head = 2 * p + h

                def both(i, low, high):
                    return near_kv[p, i, low:high, rows].astype(F32) + far_kv[p, i, low:high, rows].astype(F32)

                turn_back(both(h, 0, half), both(h, half, dim), rows, width + head * dim)
                low = 2 * width + head * dim
                joined[low : low + dim, rows] = both(2 + h, 0, dim).astype(BF16)
        return carry

    lax.fori_loop(0, count, keys_step, 0)
    dq_copy.wait()

    def arrive(c, carry):
        rows = rows_at(c, chunk)
        for p in range(2):
            for h in range(2):
                turn_back(
                    near_dq[p, h, 0:half, rows].astype(F32), near_dq[p, h, half:dim, rows].astype(F32), rows,
                    (2 * p + h) * dim,
                )
        grad = dg(joined[:, rows], w_qkv[...], 0, 1)
        hat, inv = norm_parts(x1_ref[rows, :])
        gains[1:2, :] += jnp.sum(grad * hat, axis=0, keepdims=True)
        grad = grad_x2[rows, :] + norm_back(grad, hat, inv, row_of(gain2))
        grad_x1[rows, :] = grad
        branch[rows, :] = (0.5 * grad).astype(BF16)
        return carry

    lax.fori_loop(0, count, arrive, 0)
    for j in range(0, wide, width):
        acc[4 * unit + j : 4 * unit + j + width, :] = dg(act[:, j : j + width], branch[...], 0, 0)
    advance(down, 0)
    acc[3 * unit : 3 * unit + 3 * width, :] = dg(joined[...], n2_ref[...], 1, 0)
    advance(qkv, 0)

    def through(c, carry):
        rows = rows_at(c, chunk)
        grad = dg(branch[rows, :], w_out[...], 1, 1)
        hidden[rows, :] = (grad * slope[rows, :].astype(F32)).astype(BF16)
        hat, _ = norm_parts(tok[rows, :].astype(F32))
        n2_ref[rows, :] = (hat * row_of(gain1)).astype(BF16)
        return carry

    lax.fori_loop(0, count, through, 0)
    for j in range(0, wide, width):
        acc[5 * unit + j : 5 * unit + j + width, :] = dg(n2_ref[...], hidden[:, j : j + width], 0, 0)
    advance(up, 0)
    advance(down + qkv, 1)

    def last_step(c, carry):
        rows = rows_at(c, chunk)
        grad = dg(hidden[rows, :], w_in[...], 1, 1)
        hat, inv = norm_parts(tok[rows, :].astype(F32))
        gains[0:1, :] += jnp.sum(grad * hat, axis=0, keepdims=True)
        grad_ref[rows, :] = (grad_x1[rows, :] + norm_back(grad, hat, inv, row_of(gain1))).astype(BF16)
        return carry

    lax.fori_loop(0, count // 2, last_step, 0)
    advance(up, 1)
    lax.fori_loop(count // 2, count, last_step, 0)
    acc[last : last + 8, :] = gains[...]
    advance(rest, 0)
    advance(down + qkv, 2)
    advance(rest, 1)
    for position in range(2, 2 * steps + 1):
        if position < 2 * steps:
            advance(down + qkv, position + 1)
        advance(up + rest, position)
        if remaining:
            advance(early, remaining.pop(0))
    while remaining:
        advance(early, remaining.pop(0))


def back(
    lengths, near, far, o, lse, do, trig, gain1, gain2, two, mid, point_two,
    tok, x1, n2, grad_x2, act, slope, w_in, w_out, w_qkv,
):
    frames, width = tok.shape
    sp = lax.axis_size("sp")
    chunk = min(256, frames)
    block = min(512, frames)
    count, per = frames // chunk, frames // block
    wide = w_in.shape[1]
    dim = width // HEADS
    reach = 2 * frames
    rows = 24 * width + 16
    staged, sems = reduction_scratch([4 * width] * 6 + [16])
    low_keep, keep = pltpu.VMEM((frames, width), BF16), pltpu.VMEM((frames, width), F32)
    return pl.pallas_call(
        functools.partial(back_kernel, sp, lengths.shape[1], chunk, block, min(256, block)),
        out_shape=[
            jax.ShapeDtypeStruct((frames, width), BF16),
            jax.ShapeDtypeStruct((rows, width), BF16),
        ],
        in_specs=[SMEM] + [VMEM] * 3 + [pl.BlockSpec(memory_space=pl.ANY)] * 17,
        out_specs=[VMEM] * 2,
        scratch_shapes=[
            pltpu.VMEM(near.shape, BF16),
            pltpu.VMEM(far.shape, BF16),
            pltpu.VMEM(o.shape, F32),
            pltpu.VMEM(do.shape, BF16),
            pltpu.VMEM(trig.shape, F32),
            low_keep,
            keep,
            low_keep,
            keep,
            pltpu.VMEM((frames, wide), BF16),
            pltpu.VMEM((frames, wide), BF16),
            pltpu.VMEM(w_in.shape, BF16),
            pltpu.VMEM(w_out.shape, BF16),
            pltpu.VMEM(w_qkv.shape, BF16),
            pltpu.VMEM((2, reach, 2 * dim), BF16),
            pltpu.VMEM((2, dim, reach), BF16),
            pltpu.VMEM((2, 2 * dim, 2 * reach), BF16),
            pltpu.VMEM((2, reach, 2 * dim), BF16),
            pltpu.VMEM((2, 2 * dim, 2 * reach), BF16),
            pltpu.VMEM((2, dim, reach), F32),
            pltpu.VMEM((2, 4, dim, frames), BF16),
            pltpu.VMEM((4, dim, frames), BF16),
            pltpu.VMEM((2, dim, frames), BF16),
            pltpu.VMEM((2, 4, dim, frames), BF16),
            pltpu.VMEM((2, 4, dim, frames), BF16),
            pltpu.VMEM((2, 2, dim, frames), BF16),
            pltpu.VMEM((3 * width, frames), BF16),
            low_keep,
            pltpu.VMEM((frames, wide), BF16),
            keep,
            pltpu.VMEM((8, width), F32),
            pltpu.VMEM((rows, width), F32),
            pltpu.VMEM((staged, width), BF16),
            pltpu.VMEM((staged, width), BF16),
            DMA((17,)),
            DMA((2 * per,)),
            DMA((2, per)),
            DMA((per + 1,)),
            DMA((per + 1,)),
            DMA(sems),
            DMA(sems),
        ],
        compiler_params=pltpu.CompilerParams(
            collective_id=2, has_side_effects=True, vmem_limit_bytes=VMEM_LIMIT
        ),
        name="back",
    )(
        lengths, lse, gain1, gain2, near, far, o, do, trig, two, mid, point_two,
        tok, x1, n2, grad_x2, act, slope, w_in, w_out, w_qkv,
    )


def unpack_kernel(
    taps, full, bn_grads, output, input_grad,
    output_to, input_to, gain1_to, in_one_to, out_one_to, gain2_to, qkv_to, out_weight_to, gain3_to, point_one_to,
    depthwise_to, bn_gain_to, bn_bias_to, point_two_to, gain4_to, in_two_to, out_two_to, gain5_to,
    in_one, out_one, qkv, point_one, point_two, out_weight, in_two, out_two, depthwise, sems,
):
    width = full.shape[1]
    unit = 4 * width
    copies = []

    def send(source, target):
        copies.append(pltpu.make_async_copy(source, target, sems.at[len(copies)]))
        copies[-1].start()

    def block(ref, base):
        return ref[base : base + width, :].astype(F32)

    send(output, output_to)
    send(input_grad, input_to)
    for j in range(0, unit, width):
        out_two[j : j + width, :] = block(full, j)
    send(out_two, out_two_to)
    for j in range(0, unit, width):
        in_two[:, j : j + width] = block(full, unit + j)
    send(in_two, in_two_to)
    for j in range(0, unit, width):
        out_one[j : j + width, :] = block(full, 4 * unit + j)
    send(out_one, out_one_to)
    for j in range(0, unit, width):
        in_one[:, j : j + width] = block(full, 5 * unit + j)
    send(in_one, in_one_to)
    for j in range(0, 2 * width, width):
        point_one[:, j : j + width] = block(full, 2 * unit + j)
    send(point_one, point_one_to)
    out_weight[...] = block(full, 2 * unit + 2 * width)
    send(out_weight, out_weight_to)
    point_two[...] = block(full, 3 * unit + 3 * width)
    send(point_two, point_two_to)
    for j in range(0, 3 * width, width):
        qkv[:, j : j + width] = block(full, 3 * unit + j).T
    send(qkv, qkv_to)
    small = full[2 * unit + 3 * width : 2 * unit + 3 * width + 64, :].astype(F32)
    depthwise[...] = small[8 : 8 + taps]
    send(depthwise, depthwise_to)
    rest = full[6 * unit : 6 * unit + 16, :].astype(F32)
    for ref, row in (
        (gain1_to, rest[0]), (gain2_to, rest[1]), (gain3_to, small[2]), (gain4_to, small[3]), (gain5_to, small[4]),
        (bn_gain_to, bn_grads[0, :]), (bn_bias_to, bn_grads[1, :]),
    ):
        ref[...] = row
    for copy in copies:
        copy.wait()


def unpack(full, bn_grads, output, input_grad, taps):
    width = full.shape[1]
    row, square, tall, flat = (width,), (width, width), (4 * width, width), (width, 4 * width)
    thrice, twice = (width, 3 * width), (width, 2 * width)
    anywhere = pl.BlockSpec(memory_space=pl.ANY)
    shapes = [
        output.shape, input_grad.shape, row, flat, tall, row, thrice, square, row, twice, (taps, width), row, row,
        square, row, flat, tall, row,
    ]
    return pl.pallas_call(
        functools.partial(unpack_kernel, taps),
        out_shape=[jax.ShapeDtypeStruct(shape, F32 if i > 1 else BF16) for i, shape in enumerate(shapes)],
        in_specs=[VMEM] * 4,
        out_specs=[VMEM if shape == row else anywhere for shape in shapes],
        scratch_shapes=[
            pltpu.VMEM(shape, F32)
            for shape in (flat, tall, thrice, twice, square, square, flat, tall, (taps, width))
        ]
        + [DMA((11,))],
        compiler_params=pltpu.CompilerParams(vmem_limit_bytes=VMEM_LIMIT),
        name="unpack",
    )(full, bn_grads, output, input_grad)


def on_device(
    tokens, ln1_gain, ffn1_in, ffn1_out, ln2_gain, w_qkv, w_out, ln3_gain, w_point1, depthwise,
    bn_gain, bn_bias, w_point2, ln4_gain, ffn2_in, ffn2_out, ln5_gain, lengths, cotangent,
):
    width = tokens.shape[2]
    sp, dp = lax.axis_size("sp"), lax.axis_size("dp")
    assert HEADS == sp and ffn1_in.shape[1] == ffn2_in.shape[1] == 4 * width
    half = width // HEADS // 2
    turns = 10000.0 ** (-np.arange(half, dtype=np.float64) / half) / (2 * np.pi)
    high = np.round(turns * 4096.0) / 4096.0
    freq = jnp.asarray(np.stack([high, turns - high], axis=1), F32)
    x1, n2, trig, act, slope, near, far, context, raw_context, log_sums, flag = front(
        lengths, tokens[0], ln1_gain, ffn1_in, ffn1_out, ln2_gain, w_qkv, freq
    )
    context, raw_context, log_sums = repair(lengths, flag, near, far, context, raw_context, log_sums)
    output, grad_x2, grad_context, mid, point_two, bn_grads, two = middle(
        lengths, context, x1, cotangent[0], ln3_gain, ln4_gain, ln5_gain, w_out, w_point1, depthwise,
        bn_gain, bn_bias, w_point2, ffn2_in, ffn2_out, dp,
    )
    input_grad, full = back(
        lengths, near, far, raw_context, log_sums, grad_context, trig, ln1_gain, ln2_gain, two, mid, point_two,
        tokens[0], x1, n2, grad_x2, act, slope, ffn1_in, ffn1_out, w_qkv,
    )
    results = unpack(full, bn_grads, output, input_grad, depthwise.shape[0])
    return (results[0][None], results[1][None]) + tuple(results[2:])


def solution(mesh):
    split = P("dp", "sp", None)
    return jax.shard_map(
        on_device,
        mesh=mesh,
        in_specs=(split,) + (P(),) * 16 + (P("dp", None), split),
        out_specs=(split, split) + (P(),) * 16,
        check_vma=False,
    )
```

```python
import functools

import jax
import jax.numpy as jnp
import numpy as np
from jax import lax
from jax.experimental import pallas as pl
from jax.experimental.pallas import tpu as pltpu
from jax.sharding import PartitionSpec as P

HEADS = 4
EPS = 1e-05
NEG = -1e30
LN2 = float(np.log(2.0))
F32 = jnp.float32
BF16 = jnp.bfloat16
I32 = jnp.int32
MESH = pl.DeviceIdType.MESH
VMEM = pl.BlockSpec(memory_space=pltpu.VMEM)
SMEM = pl.BlockSpec(memory_space=pltpu.SMEM)
DMA = pltpu.SemaphoreType.DMA
VMEM_LIMIT = 56 * 2**20
PARTIAL_TIMES = (0, 3, 5, 10, 14)
FRESH_TIMES = (0, 1, 4, 7, 11, 13)


def dg(left, right, left_dim, right_dim):
    return lax.dot_general(
        left, right, (((left_dim,), (right_dim,)), ((), ())), preferred_element_type=F32
    )


def rows_at(index, count):
    return pl.ds(pl.multiple_of(index * count, count), count)


def start_copies(pairs, sems):
    copies = [pltpu.make_async_copy(source, target, sems.at[i]) for i, (source, target) in enumerate(pairs)]
    for copy in copies:
        copy.start()
    return copies


def wait_all(copies):
    for copy in copies:
        copy.wait()


def greet(devices):
    for device in devices:
        pl.semaphore_signal(pltpu.get_barrier_semaphore(), inc=1, device_id=device, device_id_type=MESH)


def await_greetings(devices):
    pl.semaphore_wait(pltpu.get_barrier_semaphore(), len(devices))


def flipped(axis, mask):
    me, step = lax.axis_index(axis), 1
    out = me
    while step <= mask:
        if mask & step:
            out = out + step - 2 * step * lax.rem(me // step, 2)
        step *= 2
    return out


def peer_at(sp_mask, dp_mask):
    return (flipped("dp", dp_mask), flipped("sp", sp_mask))


def sp_peers(count):
    return [peer_at(mask, 0) for mask in range(1, count)]


def row_of(ref):
    return ref[...].astype(F32).reshape(1, ref.shape[0])


def frame_cols(device, frames, c, chunk):
    return pl.ds(pl.multiple_of(device * frames + c * chunk, chunk), chunk)


def ends_of(len_ref, items):
    ends, total = [], 0
    for item in range(items):
        total = total + len_ref[0, item]
        ends.append(total)
    return ends


def segment_row(first, count, ends):
    frame = first + lax.broadcasted_iota(I32, (1, count), 1)
    segment = jnp.zeros((1, count), I32)
    for end in ends:
        segment = segment + (frame >= end).astype(I32)
    return segment


def position_row(first, count, ends):
    frame = first + lax.broadcasted_iota(I32, (1, count), 1)
    start = jnp.zeros((1, count), I32)
    for end in ends:
        start = jnp.where(frame >= end, end, start)
    return (frame - start).astype(F32)


def onehot_rows(segment, items, other, same):
    row = lax.broadcasted_iota(I32, (16, segment.shape[1]), 0)
    return jnp.where(row <= items, jnp.where(row == segment, same, other), 0.0)


def norm_parts(rows):
    centre = rows - jnp.mean(rows, axis=-1, keepdims=True)
    inv = lax.rsqrt(jnp.mean(centre * centre, axis=-1, keepdims=True) + EPS)
    return centre * inv, inv


def norm_back(grad, hat, inv, gain):
    scaled = grad * gain
    first = jnp.mean(scaled, axis=-1, keepdims=True)
    second = jnp.mean(scaled * hat, axis=-1, keepdims=True)
    return inv * (scaled - first - hat * second)


def sigmoid(x):
    return 1.0 / (1.0 + jnp.exp(-x))


def sine_cosine(position, freq_hi, freq_lo):
    turns = position * freq_hi
    turns = turns - jnp.round(turns) + position * freq_lo
    turns = turns - jnp.round(turns)
    x = turns * float(np.pi)
    x2 = x * x
    s = x * (1 + x2 * (-1 / 6 + x2 * (1 / 120 + x2 * (-1 / 5040 + x2 * (1 / 362880 - x2 / 39916800)))))
    c = 1 + x2 * (-1 / 2 + x2 * (1 / 24 + x2 * (-1 / 720 + x2 * (1 / 40320 + x2 * (-1 / 3628800 + x2 / 479001600)))))
    return 2 * s * c, 1 - 2 * s * s


def split_rows(value):
    row = lax.broadcasted_iota(I32, (16, value.shape[1]), 0)
    first = value.astype(BF16).astype(F32)
    second = (value - first).astype(BF16).astype(F32)
    third = value - first - second
    picked = jnp.where(row == 0, first, jnp.where(row == 1, second, third))
    return jnp.where(row < 3, picked, 0.0).astype(BF16)


def first_rows(count, columns):
    row = lax.broadcasted_iota(I32, (16, columns), 0)
    return jnp.where(row < count, 1.0, 0.0).astype(BF16)


def query_rows(query, segment, items, shift):
    pad = jnp.zeros((query.shape[0] - 32, query.shape[1]), BF16)
    return jnp.concatenate([query, onehot_rows(segment, items, 0.0, 1.0).astype(BF16), split_rows(shift), pad], axis=0)


def key_rows(key, segment, items):
    pad = jnp.zeros((key.shape[0] - 32, key.shape[1]), BF16)
    return jnp.concatenate(
        [key, onehot_rows(segment, items, NEG, 0.0).astype(BF16), first_rows(3, key.shape[1]), pad], axis=0
    )


def lay_queries(near, slot, frames, first, ends, items, dim, qa, lse):
    cols = slice(slot * frames, (slot + 1) * frames)
    segment = segment_row(first, frames, ends)
    for h in range(2):
        query = near[slot, h * dim : (h + 1) * dim, :]
        key = near[slot, (2 + h) * dim : (3 + h) * dim, :]
        own = jnp.sum(query.astype(F32) * key.astype(F32), axis=0, keepdims=True)
        lse[h : h + 1, cols] = own
        qa[h, :, cols] = query_rows(query, segment, items, -own)


def lay_keys(key, value, rows, first, ends, items, h, ka, va):
    dim, count = key.shape
    ka[h, rows, :] = key_rows(key, segment_row(first, count, ends), items).T
    va[h, 0:dim, rows] = value
    va[h, dim:, rows] = first_rows(1, count)


def front_kernel(
    items, chunk, block, len_ref, tok, gain1, w_in, w_out, gain2, w_qkv, freq,
    x1_hbm, n2_hbm, trig_hbm, act_hbm, slope_hbm, near_hbm, far_hbm, ctx_hbm, o_hbm, lse, flag,
    x1_ref, n2_ref, trig, act, slope, near, far, ctx, o_ref,
    parts, turned, qa, ka, va, acc, send, recv, out_sems, last_sems,
):
    me = lax.axis_index("sp")
    core, pair = lax.rem(me, 2), me // 2
    frames, width = tok.shape
    half = trig.shape[0] // 2
    dim = 2 * half
    count = frames // chunk
    peers = [peer_at(mask, 0) for mask in (1, 2, 3)]
    greet(peers)
    turned[...] = w_qkv[...].T
    ends = ends_of(len_ref, items)
    scale = float(np.log2(np.e)) * dim**-0.5

    def copies(c):
        cols = rows_at(c, chunk)
        ways = (
            (parts.at[1 - core, :, cols], near.at[core, :, cols]),
            (parts.at[core, 2 * dim :, cols], far.at[core, :, cols]),
            (parts.at[1 - core, 2 * dim :, cols], far.at[core, :, cols]),
        )
        return [
            pltpu.make_async_remote_copy(
                src_ref=source, dst_ref=target, send_sem=send.at[i, c], recv_sem=recv.at[i, c],
                device_id=peers[i], device_id_type=MESH,
            )
            for i, (source, target) in enumerate(ways)
        ]

    def results(c):
        rows = rows_at(c, chunk)
        pairs = [(ref.at[rows, :], hbm.at[rows, :]) for ref, hbm in (
            (x1_ref, x1_hbm), (n2_ref, n2_hbm), (act, act_hbm), (slope, slope_hbm)
        )]
        return [pltpu.make_async_copy(source, target, out_sems.at[i, c]) for i, (source, target) in enumerate(pairs)]

    def step(c, carry):
        rows = rows_at(c, chunk)
        x = tok[rows, :].astype(F32)
        hat, _ = norm_parts(x)
        n1 = (hat * row_of(gain1)).astype(BF16)
        a = dg(n1, w_in[...], 1, 0)
        sig = sigmoid(a)
        s = (a * sig).astype(BF16)
        act[rows, :] = s
        slope[rows, :] = (sig * (1.0 + a * (1.0 - sig))).astype(BF16)
        x1 = x + 0.5 * dg(s, w_out[...], 1, 0)
        x1_ref[rows, :] = x1
        hat, _ = norm_parts(x1)
        n2 = (hat * row_of(gain2)).astype(BF16)
        n2_ref[rows, :] = n2
        joined = dg(turned[...], n2, 1, 1)
        sine, cosine = sine_cosine(
            position_row(me * frames + c * chunk, chunk, ends), freq[:, 0:1], freq[:, 1:2]
        )
        trig[0:half, rows] = sine
        trig[half:, rows] = cosine
        for p in range(2):
            for j in range(2):
                for part, factor in ((0, scale), (1, 1.0)):
                    low = part * width + (2 * p + j) * dim
                    first, second = joined[low : low + half], joined[low + half : low + dim]
                    low = (2 * part + j) * dim
                    parts[p, low : low + half, rows] = ((first * cosine - second * sine) * factor).astype(BF16)
                    parts[p, low + half : low + dim, rows] = (
                        (first * sine + second * cosine) * factor
                    ).astype(BF16)
                low = 2 * width + (2 * p + j) * dim
                parts[p, (4 + j) * dim : (5 + j) * dim, rows] = joined[low : low + dim].astype(BF16)

        @pl.when(c == 0)
        def _():
            await_greetings(peers)

        for copy in copies(c):
            copy.start()
        near[core, :, rows] = parts[core, :, rows]
        for copy in results(c):
            copy.start()
        return carry

    lax.fori_loop(0, count, step, 0)

    def near_arrives(c, carry):
        copies(c)[0].wait()
        return carry

    lax.fori_loop(0, count, near_arrives, 0)
    leaving = start_copies([(near, near_hbm), (trig, trig_hbm)], last_sems)
    reach = 2 * frames
    for slot in range(2):
        first = (2 * pair + slot) * frames
        lay_queries(near, slot, frames, first, ends, items, dim, qa, lse)
        for h in range(2):
            lay_keys(
                near[slot, (2 + h) * dim : (3 + h) * dim, :], near[slot, (4 + h) * dim : (5 + h) * dim, :],
                slice(slot * frames, (slot + 1) * frames), first, ends, items, h, ka, va,
            )

    def near_step(i, carry):
        h, cols = i // (reach // block), rows_at(lax.rem(i, reach // block), block)
        powers = jnp.exp2(dg(ka[h, 0:reach, :], qa[h, :, cols], 1, 0)).astype(BF16)
        acc[h, :, cols] = dg(va[h, :, 0:reach], powers, 1, 0)
        return carry

    lax.fori_loop(0, 2 * reach // block, near_step, 0)
    wide = min(1024, reach)

    def far_step(c, carry):
        for copy in copies(c)[1:]:
            copy.wait()
        cols = rows_at(c, chunk)
        for slot in range(2):
            first = (2 * (1 - pair) + slot) * frames + c * chunk
            rows = pl.ds(pl.multiple_of(reach + (2 * c + slot) * chunk, chunk), chunk)
            for h in range(2):
                lay_keys(
                    far[slot, h * dim : (h + 1) * dim, cols], far[slot, (2 + h) * dim : (3 + h) * dim, cols],
                    rows, first, ends, items, h, ka, va,
                )
        rows = pl.ds(pl.multiple_of(reach + 2 * c * chunk, 2 * chunk), 2 * chunk)

        def inner(i, carry):
            h, cols = i // (reach // wide), rows_at(lax.rem(i, reach // wide), wide)
            powers = jnp.exp2(dg(ka[h, rows, :], qa[h, :, cols], 1, 0)).astype(BF16)
            acc[h, :, cols] += dg(va[h, :, rows], powers, 1, 0)
            return carry

        return lax.fori_loop(0, 2 * reach // wide, inner, carry)

    lax.fori_loop(0, count, far_step, 0)
    leaving += start_copies([(far, far_hbm)], last_sems.at[pl.ds(2, 1)])
    bad = jnp.zeros((1, reach), F32)
    for h in range(2):
        total = acc[h, dim : dim + 1, :]
        value = acc[h, 0:dim, :] / total
        ctx[h] = value.astype(BF16)
        o_ref[h] = value
        leaving += start_copies([(ctx.at[h], ctx_hbm.at[h]), (o_ref.at[h], o_hbm.at[h])], last_sems.at[pl.ds(3 + 2 * h, 2)])
        lse[h : h + 1, :] = lse[h : h + 1, :] + jnp.log2(total)
        bad = jnp.maximum(bad, jnp.where(total < 2.0**60, 0.0, 1.0))
    flag[...] = jnp.broadcast_to(jnp.max(bad, axis=1, keepdims=True), flag.shape)
    for c in range(count):
        wait_all(results(c))
    wait_all(leaving)


def front(lengths, tok, gain1, w_in, w_out, gain2, w_qkv, freq):
    frames, width = tok.shape
    wide = w_in.shape[1]
    chunk = min(256, frames)
    count = frames // chunk
    dim = width // HEADS
    reach = 2 * frames
    return pl.pallas_call(
        functools.partial(front_kernel, lengths.shape[1], chunk, min(512, reach)),
        out_shape=[
            jax.ShapeDtypeStruct((frames, width), F32),
            jax.ShapeDtypeStruct((frames, width), BF16),
            jax.ShapeDtypeStruct((dim, frames), F32),
            jax.ShapeDtypeStruct((frames, wide), BF16),
            jax.ShapeDtypeStruct((frames, wide), BF16),
            jax.ShapeDtypeStruct((2, 6 * dim, frames), BF16),
            jax.ShapeDtypeStruct((2, 4 * dim, frames), BF16),
            jax.ShapeDtypeStruct((2, dim, reach), BF16),
            jax.ShapeDtypeStruct((2, dim, reach), F32),
            jax.ShapeDtypeStruct((2, reach), F32),
            jax.ShapeDtypeStruct((8, 128), F32),
        ],
        in_specs=[SMEM] + [VMEM] * 7,
        out_specs=[pl.BlockSpec(memory_space=pl.ANY)] * 9 + [VMEM] * 2,
        scratch_shapes=[
            pltpu.VMEM((frames, width), F32),
            pltpu.VMEM((frames, width), BF16),
            pltpu.VMEM((dim, frames), F32),
            pltpu.VMEM((frames, wide), BF16),
            pltpu.VMEM((frames, wide), BF16),
            pltpu.VMEM((2, 6 * dim, frames), BF16),
            pltpu.VMEM((2, 4 * dim, frames), BF16),
            pltpu.VMEM((2, dim, reach), BF16),
            pltpu.VMEM((2, dim, reach), F32),
            pltpu.VMEM((2, 6 * dim, frames), BF16),
            pltpu.VMEM((3 * width, width), BF16),
            pltpu.VMEM((2, 2 * dim, reach), BF16),
            pltpu.VMEM((2, 2 * reach, 2 * dim), BF16),
            pltpu.VMEM((2, dim + 16, 2 * reach), BF16),
            pltpu.VMEM((2, dim + 16, reach), F32),
            DMA((3, count)),
            DMA((3, count)),
            DMA((4, count)),
            DMA((7,)),
        ],
        compiler_params=pltpu.CompilerParams(
            collective_id=0, has_side_effects=True, vmem_limit_bytes=VMEM_LIMIT
        ),
        name="front",
    )(lengths, tok, gain1, w_in, w_out, gain2, w_qkv, freq)


def repair_kernel(
    items, block, len_ref, flag, near_hbm, far_hbm, ctx_in, o_in, lse_in, ctx_hbm, o_hbm, lse_hbm,
    near, far, ctx, o_ref, lse, qa, ka, va, sems,
):
    @pl.when(jnp.max(flag[...]) > 0.5)
    def _():
        pair = lax.axis_index("sp") // 2
        frames, dim = near.shape[2], near.shape[1] // 6
        reach = 2 * frames
        ends = ends_of(len_ref, items)
        loads = [
            pltpu.make_async_copy(near_hbm, near, sems.at[0]),
            pltpu.make_async_copy(far_hbm, far, sems.at[1]),
        ]
        for copy in loads:
            copy.start()
        for copy in loads:
            copy.wait()
        for slot in range(2):
            first, other = (2 * pair + slot) * frames, (2 * (1 - pair) + slot) * frames
            lay_queries(near, slot, frames, first, ends, items, dim, qa, lse)
            for h in range(2):
                lay_keys(
                    near[slot, (2 + h) * dim : (3 + h) * dim, :], near[slot, (4 + h) * dim : (5 + h) * dim, :],
                    slice(slot * frames, (slot + 1) * frames), first, ends, items, h, ka, va,
                )
                lay_keys(
                    far[slot, h * dim : (h + 1) * dim, :], far[slot, (2 + h) * dim : (3 + h) * dim, :],
                    slice(reach + slot * frames, reach + (slot + 1) * frames), other, ends, items, h, ka, va,
                )

        def step(i, carry):
            h, cols = i // (reach // block), rows_at(lax.rem(i, reach // block), block)
            query = qa[h, :, cols]

            def highest(j, top):
                scores = dg(ka[h, rows_at(j, block), :], query, 1, 0)
                return jnp.maximum(top, jnp.max(scores, axis=0, keepdims=True))

            top = lax.fori_loop(0, 2 * reach // block, highest, jnp.zeros((1, block), F32))

            def add(j, total):
                rows = rows_at(j, block)
                powers = jnp.exp2(dg(ka[h, rows, :], query, 1, 0) - top).astype(BF16)
                return total + dg(va[h, :, rows], powers, 1, 0)

            total = lax.fori_loop(0, 2 * reach // block, add, jnp.zeros((dim + 16, block), F32))
            value = total[0:dim, :] / total[dim : dim + 1, :]
            ctx[h, :, cols] = value.astype(BF16)
            o_ref[h, :, cols] = value
            change = top + jnp.log2(total[dim : dim + 1, :])
            row = lax.broadcasted_iota(I32, (2, block), 0)
            lse[:, cols] = lse[:, cols] + jnp.where(row == h, change, 0.0)
            return carry

        lax.fori_loop(0, 2 * reach // block, step, 0)
        stores = [
            pltpu.make_async_copy(ctx, ctx_hbm, sems.at[2]),
            pltpu.make_async_copy(o_ref, o_hbm, sems.at[3]),
            pltpu.make_async_copy(lse, lse_hbm, sems.at[4]),
        ]
        for copy in stores:
            copy.start()
        for copy in stores:
            copy.wait()


def repair(lengths, flag, near, far, ctx, o, lse):
    dim, reach = ctx.shape[1:]
    anywhere = pl.BlockSpec(memory_space=pl.ANY)
    return pl.pallas_call(
        functools.partial(repair_kernel, lengths.shape[1], min(512, reach)),
        out_shape=[jax.ShapeDtypeStruct(x.shape, x.dtype) for x in (ctx, o, lse)],
        in_specs=[SMEM, VMEM] + [anywhere] * 5,
        out_specs=[anywhere] * 3,
        input_output_aliases={4: 0, 5: 1, 6: 2},
        scratch_shapes=[
            pltpu.VMEM(near.shape, BF16),
            pltpu.VMEM(far.shape, BF16),
            pltpu.VMEM(ctx.shape, BF16),
            pltpu.VMEM(o.shape, F32),
            pltpu.VMEM(lse.shape, F32),
            pltpu.VMEM((2, 2 * dim, reach), BF16),
            pltpu.VMEM((2, 2 * reach, 2 * dim), BF16),
            pltpu.VMEM((2, dim + 16, 2 * reach), BF16),
            DMA((5,)),
        ],
        compiler_params=pltpu.CompilerParams(vmem_limit_bytes=VMEM_LIMIT),
        name="repair",
    )(lengths, flag, near, far, ctx, o, lse)


def axis_steps(axis):
    steps, step = [], 1
    while step < lax.axis_size(axis):
        steps.append((axis, step))
        step *= 2
    assert step == lax.axis_size(axis)
    return steps


def stage_plans():
    sp_steps, dp_steps = axis_steps("sp"), axis_steps("dp")
    plane, rest = sp_steps[1:] + dp_steps[:1], dp_steps[1:]

    def groups(steps):
        return [steps[i : i + 2] for i in range(0, len(steps), 2)]

    plans = (
        groups(plane) + groups(rest),
        groups(rest) + groups(plane),
        [dp_steps[:1]] + groups(rest) + groups(sp_steps[1:]),
    )
    return tuple([sp_steps[:1]] + [stage for stage in plan if stage] for plan in plans)


def stage_masks(stage):
    masks = []
    for number in range(1, 1 << len(stage)):
        mask = {"sp": 0, "dp": 0}
        for i, (axis, step) in enumerate(stage):
            if number & (1 << i):
                mask[axis] += step
        masks.append((mask["sp"], mask["dp"]))
    return masks


def place_in(stage, number):
    place = 0
    for i, (axis, step) in enumerate(stage):
        bit = lax.rem(lax.axis_index(axis) // step, 2)
        place = place + (1 << i) * (1 - bit if number & (1 << i) else bit)
    return place


def exchange_plan(rows, stages, offset=0):
    sizes, size = [], rows
    for stage in stages:
        group = 1 << len(stage)
        splits = size % (16 * group) == 0
        size = size // group if splits else size
        sizes.append((splits, size, offset))
        offset += (group - 1) * size
    return sizes, offset, size


class Reduction:
    def __init__(self, base, rows, staged, stages, acc, stage, land, full, send, recv):
        self.stages, self.acc, self.stage, self.land, self.full = stages, acc, stage, land, full
        self.send, self.recv, self.base = send, recv, base
        self.sizes, _, self.own = exchange_plan(rows, stages, staged)
        self.first_sem = [sum((1 << len(s)) - 1 for s in stages[:k]) for k in range(len(stages))]

    def at(self, low, size):
        return pl.ds(pl.multiple_of(low, 16), size)

    def low(self, k):
        return self.base + sum(
            place_in(self.stages[j], 0) * self.sizes[j][1] for j in range(k) if self.sizes[j][0]
        )

    def slot(self, k, i):
        _, size, offset = self.sizes[k]
        return slice(offset + i * size, offset + (i + 1) * size)

    def copies(self, way, k):
        splits, size, _ = self.sizes[k]
        out = []
        for i, masks in enumerate(stage_masks(self.stages[k])):
            if way == 0:
                source = self.stage.at[self.slot(k, i if splits else 0), :]
                target = self.land.at[self.slot(k, i), :]
            else:
                source = target = self.full.at[self.at(self.low(k + 1), size), :]
            out.append(
                pltpu.make_async_remote_copy(
                    src_ref=source,
                    dst_ref=target,
                    send_sem=self.send.at[way, self.first_sem[k] + i],
                    recv_sem=self.recv.at[way, self.first_sem[k] + i],
                    device_id=peer_at(*masks),
                    device_id_type=MESH,
                )
            )
        return out

    def sum_send(self, k):
        splits, size, _ = self.sizes[k]
        copies = self.copies(0, k)
        for i, copy in enumerate(copies):
            if splits:
                away = self.low(k) + place_in(self.stages[k], i + 1) * size
                self.stage[self.slot(k, i), :] = self.acc[self.at(away, size), :].astype(BF16)
            elif i == 0:
                self.stage[self.slot(k, 0), :] = self.acc[self.at(self.low(k), size), :].astype(BF16)
            copy.start()

    def sum_recv(self, k):
        splits, size, _ = self.sizes[k]
        copies = self.copies(0, k)
        for copy in copies:
            copy.wait()
        values = [self.land[self.slot(k, i), :].astype(F32) for i in range(len(copies))]
        if splits:
            values = [self.acc[self.at(self.low(k + 1), size), :]] + values
        else:
            values = [self.stage[self.slot(k, 0), :].astype(F32)] + values
        while len(values) > 1:
            values = [values[i] + values[i + 1] for i in range(0, len(values), 2)]
        self.acc[self.at(self.low(k + 1), size), :] = values[0]

    def close(self):
        where = self.at(self.low(len(self.stages)), self.own)
        self.full[where, :] = self.acc[where, :].astype(BF16)

    def share_send(self, k):
        if self.sizes[k][0]:
            for copy in self.copies(1, k):
                copy.start()

    def share_recv(self, k):
        if self.sizes[k][0]:
            for copy in self.copies(1, k):
                copy.wait()


def advance(streams, position):
    for stream in streams:
        n = len(stream.stages)
        if 0 < position <= n:
            stream.sum_recv(position - 1)
        if position < n:
            stream.sum_send(position)
        else:
            if position == n:
                stream.close()
            else:
                stream.share_recv(2 * n - position)
            if position < 2 * n:
                stream.share_send(2 * n - 1 - position)


def reduction_scratch(rows_list):
    staged = sum(max(exchange_plan(rows, stages)[1] for stages in stage_plans()) for rows in rows_list)
    sems = max(sum((1 << len(stage)) - 1 for stage in plan) for plan in stage_plans())
    return staged, (len(rows_list), 2, sems)


def make_streams(items, acc, stage, land, full, send, recv):
    streams, staged = [], 0
    for i, (base, rows, order) in enumerate(items):
        stages = stage_plans()[order]
        streams.append(
            Reduction(base, rows, staged, stages, acc, stage, land, full, send.at[i], recv.at[i])
        )
        staged += max(exchange_plan(rows, plan)[1] for plan in stage_plans())
    return streams


def all_masks(sp):
    masks = [(mask, 0) for mask in range(1, sp)]
    for plan in stage_plans():
        for stage in plan:
            masks += [m for m in stage_masks(stage) if m not in masks]
    return masks


def halves_of(ref, rows):
    return jnp.concatenate([ref[0, rows, :], ref[1, rows, :]], axis=1)


def combine(entries):
    count = sum(e[2] for e in entries)
    safe = jnp.maximum(count, 1.0)
    mean = sum(e[2] * e[0] for e in entries) / safe
    spread = sum(e[1] + e[2] * (e[0] - mean) * (e[0] - mean) for e in entries)
    return mean, spread, count


def pick(ref):
    return ref[0:1, :], ref[1:2, :], ref[2:3, :]


def total(entries):
    return tuple(sum(e[i] for e in entries) for i in range(3))


def middle_kernel(
    sp, dp, items, taps, chunk, block, len_ref, parts, x1_hbm, cot_hbm, gain3, gain4, gain5, w_out_hbm,
    w_point1_hbm, depthwise, bn_gain, bn_bias, w_point2_hbm, w_in_hbm, w_down_hbm,
    out_hbm, x2_hbm, heads, mid_hbm, point_two_hbm, bn_grads, partial,
    x1_ref, cot, w_out, w_point1, w_point2, w_in, w_down, out_ref, grad_x2, mid, point_two, two, load_sems, out_sems,
    stage, land, sum_send, sum_recv,
    ctx, x2_ref, n3_keep, point, glu, conv, low_lim, high_lim, act, hidden, n4_keep, branch, swish, branch2,
    grad_x3, grad_y, grad_conv, grad_glu, grad_point, branch3, back_parts, tap_sums, edge_out, edge_in,
    send_box, near_box, far_box, sums,
    send, recv, local, back_send, back_recv, back_local, rim_send, rim_recv, box_send, box_recv,
):
    me, me_dp = lax.axis_index("sp"), lax.axis_index("dp")
    frames, width = x1_ref.shape
    lanes = width // 2
    reach = taps // 2
    count = frames // chunk
    peers = sp_peers(sp)
    far_peers = [peer_at(0, mask) for mask in range(1, dp)]
    masks = all_masks(sp)
    masks += [(0, mask) for mask in range(1, dp) if (0, mask) not in masks]
    greeted = [peer_at(*mask) for mask in masks]
    core = lax.rem(me, 2)
    sibling = peer_at(1, 0)
    length = sp * frames
    ends = ends_of(len_ref, items)
    first_frame = me * frames

    def limits(b, carry):
        rows = rows_at(b, chunk)
        frame = first_frame + b * chunk + lax.broadcasted_iota(I32, (chunk, lanes), 0)
        low, high = jnp.zeros_like(frame), jnp.full_like(frame, length)
        for end in ends:
            low = jnp.where(frame >= end, end, low)
        for end in reversed(ends):
            high = jnp.where(frame < end, end, high)
        low_lim[rows, :] = low - frame
        high_lim[rows, :] = high - 1 - frame
        return carry

    for ref in (glu, grad_conv):
        for h in range(2):
            ref[h, 0:reach, :] = jnp.zeros((reach, lanes), F32)
            ref[h, reach + frames :, :] = jnp.zeros((reach, lanes), F32)
    edge_in[...] = jnp.zeros_like(edge_in)
    send_box[...] = jnp.zeros_like(send_box)
    greet(greeted)
    loads = start_copies(
        [
            (w_out_hbm, w_out), (x1_hbm, x1_ref), (w_point1_hbm, w_point1), (w_point2_hbm, w_point2),
            (w_in_hbm, w_in), (w_down_hbm, w_down), (cot_hbm, cot),
        ],
        load_sems,
    )
    lax.fori_loop(0, count, limits, 0)
    tap_sums[...] = jnp.zeros_like(tap_sums)
    sums[...] = jnp.zeros_like(sums)
    await_greetings(greeted)

    def moves(c, source, target, send_sems, recv_sems, local_sems):
        return [
            pltpu.make_async_remote_copy(
                src_ref=source(1 - core, c), dst_ref=target(core, c),
                send_sem=send_sems.at[c], recv_sem=recv_sems.at[c],
                device_id=sibling, device_id_type=MESH,
            ),
            pltpu.make_async_copy(source(core, c), target(core, c), local_sems.at[c]),
        ]

    def by_frames(ref):
        return lambda slot, c: ref.at[:, :, frame_cols(slot, frames, c, chunk)]

    def by_head(ref):
        return lambda slot, c: ref.at[slot, :, :, rows_at(c, chunk)]

    def context_moves(c):
        return moves(c, by_frames(parts), by_head(ctx), send, recv, local)

    def begin(c, carry):
        for copy in context_moves(c):
            copy.start()
        return carry

    lax.fori_loop(0, count, begin, 0)
    wait_all(loads[:3])

    def open_step(c, carry):
        rows = rows_at(c, chunk)
        for copy in context_moves(c):
            copy.wait()
        context = ctx[:, :, :, rows].reshape(width, chunk)
        x2 = x1_ref[rows, :] + dg(context, w_out[...], 0, 0)
        x2_ref[rows, :] = x2
        hat, _ = norm_parts(x2)
        n3 = (hat * row_of(gain3)).astype(BF16)
        n3_keep[rows, :] = n3
        pair = dg(n3, w_point1[...], 1, 0)
        point[rows, :] = pair
        gated = (pair[:, :width] * sigmoid(pair[:, width:])).astype(BF16).astype(F32)
        where = pl.ds(pl.multiple_of(reach + c * chunk, 8), chunk)
        glu[0, where, :] = gated[:, :lanes]
        glu[1, where, :] = gated[:, lanes:]
        return carry

    lax.fori_loop(0, count, open_step, 0)

    def rim_copies(call, side, source, target):
        peer = (me_dp, me - 1 if side == 0 else me + 1)
        return pltpu.make_async_remote_copy(
            src_ref=source, dst_ref=target, send_sem=rim_send.at[call, side], recv_sem=rim_recv.at[call, side],
            device_id=peer, device_id_type=MESH,
        )

    def swap_rims(call, sources, targets):
        @pl.when(me > 0)
        def _():
            rim_copies(call, 0, sources[0], targets[1]).start()

        @pl.when(me < sp - 1)
        def _():
            rim_copies(call, 1, sources[1], targets[0]).start()

    def await_rims(call, sources, targets):
        @pl.when(me > 0)
        def _():
            rim_copies(call, 0, sources[0], targets[1]).wait_send()
            rim_copies(call, 1, sources[1], targets[0]).wait_recv()

        @pl.when(me < sp - 1)
        def _():
            rim_copies(call, 1, sources[1], targets[0]).wait_send()
            rim_copies(call, 0, sources[0], targets[1]).wait_recv()

    for side, rows in ((0, slice(reach, 2 * reach)), (1, slice(frames, frames + reach))):
        for h in range(2):
            edge_out[side, 0:reach, h * lanes : (h + 1) * lanes] = glu[h, rows, :]
    glu_rims = (
        [edge_out.at[0, 0:reach, :], edge_out.at[1, 0:reach, :]],
        [edge_in.at[0, 0:reach, :], edge_in.at[1, 0:reach, :]],
    )
    swap_rims(0, *glu_rims)

    zero = jnp.zeros((block, lanes), F32)

    def conv_step(b, carry):
        low, high = low_lim[rows_at(b, block), :], high_lim[rows_at(b, block), :]
        start = pl.multiple_of(b * block, block)
        result = [zero, zero]
        for tap in range(taps):
            shift = tap - reach
            inside = (low <= shift) if shift < 0 else (high >= shift)
            for h in range(2):
                view = glu.at[h, pl.ds(start, block + 2 * reach), :]
                term = jnp.where(inside, view[tap : tap + block, :], 0.0)
                result[h] = result[h] + depthwise[tap : tap + 1, h * lanes : (h + 1) * lanes].astype(F32) * term
        valid = (first_frame + start + lax.broadcasted_iota(I32, (block, lanes), 0)) < ends[-1]
        for h in range(2):
            conv[h, rows_at(b, block), :] = result[h]
            sums[0:1, h * lanes : (h + 1) * lanes] += jnp.sum(jnp.where(valid, result[h], 0.0), axis=0, keepdims=True)
        return carry

    blocks = frames // block
    lax.fori_loop(1, blocks - 1, conv_step, 0)
    await_rims(0, *glu_rims)
    for h in range(2):
        glu[h, 0:reach, :] = edge_in[0, 0:reach, h * lanes : (h + 1) * lanes]
        glu[h, reach + frames :, :] = edge_in[1, 0:reach, h * lanes : (h + 1) * lanes]
    conv_step(0, 0)
    conv_step(blocks - 1, 0)

    own_count = jnp.clip(ends[-1] - first_frame, 0, frames).astype(F32)
    own_mean = sums[0:1, :] / jnp.maximum(own_count, 1.0)
    sums[0:1, :] = jnp.zeros((1, width), F32)

    def spread_step(c, carry):
        rows = rows_at(c, chunk)
        valid = (first_frame + c * chunk + lax.broadcasted_iota(I32, (chunk, width), 0)) < ends[-1]
        apart = jnp.where(valid, halves_of(conv, rows) - own_mean, 0.0)
        sums[1:2, :] += jnp.sum(apart * apart, axis=0, keepdims=True)
        return carry

    lax.fori_loop(0, count, spread_step, 0)

    def box_copies(call, stage):
        group = peers if stage == 0 else far_peers
        target = near_box if stage == 0 else far_box
        base = 0 if stage == 0 else sp - 1
        return [
            pltpu.make_async_remote_copy(
                src_ref=send_box.at[call, stage],
                dst_ref=target.at[call, i],
                send_sem=box_send.at[call, base + i],
                recv_sem=box_recv.at[call, base + i],
                device_id=peer,
                device_id_type=MESH,
            )
            for i, peer in enumerate(group)
        ]

    def box_begin(call, stage, rows):
        for i, row in enumerate(rows):
            send_box[call, stage, i : i + 1, :] = row
        for copy in box_copies(call, stage):
            copy.start()

    def box_end(call, stage, rows, merge):
        target = near_box if stage == 0 else far_box
        copies = box_copies(call, stage)
        for copy in copies:
            copy.wait()
        return merge([rows] + [pick(target[call, i]) for i in range(len(copies))])

    stats = (own_mean, sums[1:2, :], jnp.full((1, width), 1.0, F32) * own_count)
    sums[1:2, :] = jnp.zeros((1, width), F32)
    box_begin(0, 0, stats)
    stats = box_end(0, 0, stats, combine)
    box_begin(0, 1, stats)
    mean, spread, frame_count = box_end(0, 1, stats, combine)
    inv_std = lax.rsqrt(spread / frame_count + EPS)
    norm_gain, norm_bias = row_of(bn_gain), row_of(bn_bias)

    def heart_step(c, carry):
        rows = rows_at(c, chunk)
        normed = (halves_of(conv, rows) - mean) * inv_std
        y = normed * norm_gain + norm_bias
        sig_y = sigmoid(y)
        w = (y * sig_y).astype(BF16)
        swish[rows, :] = w
        x3 = x2_ref[rows, :] + dg(w, w_point2[...], 1, 0)
        hat4, inv4 = norm_parts(x3)
        g4 = row_of(gain4)
        n4 = (hat4 * g4).astype(BF16)
        n4_keep[rows, :] = n4
        a = dg(n4, w_in[...], 1, 0)
        sig = sigmoid(a)
        s = (a * sig).astype(BF16)
        act[rows, :] = s
        x4 = x3 + 0.5 * dg(s, w_down[...], 1, 0)
        hat5, inv5 = norm_parts(x4)
        g5 = row_of(gain5)
        out_ref[rows, :] = (hat5 * g5).astype(BF16)
        top = cot[rows, :].astype(F32)
        mid[3 * width + 4 : 3 * width + 5, :] += jnp.sum(top * hat5, axis=0, keepdims=True)
        grad_x4 = norm_back(top, hat5, inv5, g5)
        low_grad = (0.5 * grad_x4).astype(BF16)
        branch[rows, :] = low_grad
        grad = dg(low_grad, w_down[...], 1, 1)
        low_hidden = (grad * (sig * (1.0 + a * (1.0 - sig)))).astype(BF16)
        hidden[rows, :] = low_hidden
        grad = dg(low_hidden, w_in[...], 1, 1)
        mid[3 * width + 3 : 3 * width + 4, :] += jnp.sum(grad * hat4, axis=0, keepdims=True)
        grad3 = grad_x4 + norm_back(grad, hat4, inv4, g4)
        grad_x3[rows, :] = grad3
        low_grad = grad3.astype(BF16)
        branch2[rows, :] = low_grad
        grad = dg(low_grad, w_point2[...], 1, 1) * (sig_y * (1.0 + y * (1.0 - sig_y)))
        grad_y[0, rows, :] = grad[:, :lanes]
        grad_y[1, rows, :] = grad[:, lanes:]
        sums[2:3, :] += jnp.sum(grad, axis=0, keepdims=True)
        sums[3:4, :] += jnp.sum(grad * normed, axis=0, keepdims=True)
        return carry

    mid[3 * width :, :] = jnp.zeros((width, width), F32)
    wait_all(loads[3:])
    lax.fori_loop(0, count, heart_step, 0)
    leaving = start_copies([(out_ref, out_hbm)], out_sems)

    pair = (sums[2:3, :], sums[3:4, :], jnp.zeros((1, width), F32))
    box_begin(1, 0, pair)
    for side, rows in ((0, slice(0, reach)), (1, slice(frames - reach, frames))):
        for h in range(2):
            cols = slice(h * lanes, (h + 1) * lanes)
            edge_out[side, reach : 2 * reach, cols] = grad_y[h, rows, :]
            edge_out[side, 2 * reach : 3 * reach, cols] = conv[h, rows, :]
    grad_rims = (
        [edge_out.at[0, reach : 3 * reach, :], edge_out.at[1, reach : 3 * reach, :]],
        [edge_in.at[0, reach : 3 * reach, :], edge_in.at[1, reach : 3 * reach, :]],
    )
    swap_rims(1, *grad_rims)
    wide = w_in.shape[1]
    streams = make_streams([(0, wide, 2), (wide, wide, 2)], two, stage, land, None, sum_send, sum_recv)
    early_stages = len(stage_plans()[2]) - 1
    for j in range(0, wide, width):
        two[j : j + width, :] = dg(act[:, j : j + width], branch[...], 0, 0)
    advance(streams[:1], 0)
    pair = box_end(1, 0, pair, total)
    box_begin(1, 1, pair)
    for j in range(0, wide, width):
        two[wide + j : wide + j + width, :] = dg(n4_keep[...], hidden[:, j : j + width], 0, 0)
    advance(streams[1:], 0)
    advance(streams[:1], 1)
    point_two[...] = dg(swish[...], branch2[...], 0, 0)
    leaving += start_copies([(point_two, point_two_hbm)], out_sems.at[pl.ds(1, 1)])
    advance(streams[1:], 1)
    await_rims(1, *grad_rims)
    bias_sum, gain_sum, _ = box_end(1, 1, pair, total)
    bn_grads[0:1, :] = gain_sum
    bn_grads[1:2, :] = bias_sum
    bn_grads[2:8, :] = jnp.zeros((6, width), F32)

    scale = norm_gain * inv_std
    slope = -inv_std * inv_std * norm_gain * gain_sum / frame_count
    shift_all = -inv_std * norm_gain * bias_sum / frame_count

    def conv_grad(grad, value, frame, h):
        cols = slice(h * lanes, (h + 1) * lanes)
        extra = (value - mean[:, cols]) * slope[:, cols] + shift_all[:, cols]
        return grad * scale[:, cols] + jnp.where(frame < ends[-1], extra, 0.0)

    def grad_conv_step(c, carry):
        rows = rows_at(c, chunk)
        frame = first_frame + c * chunk + lax.broadcasted_iota(I32, (chunk, lanes), 0)
        where = pl.ds(pl.multiple_of(reach + c * chunk, 8), chunk)
        for h in range(2):
            grad_conv[h, where, :] = conv_grad(grad_y[h, rows, :], conv[h, rows, :], frame, h)
        return carry

    lax.fori_loop(0, count, grad_conv_step, 0)
    for side, rows, begin_frame in (
        (0, slice(0, reach), first_frame - reach),
        (1, slice(reach + frames, 2 * reach + frames), first_frame + frames),
    ):
        frame = begin_frame + lax.broadcasted_iota(I32, (reach, lanes), 0)
        for h in range(2):
            cols = slice(h * lanes, (h + 1) * lanes)
            grad_conv[h, rows, :] = conv_grad(
                edge_in[side, reach : 2 * reach, cols], edge_in[side, 2 * reach : 3 * reach, cols], frame, h
            )

    def conv_back_step(b, carry):
        low, high = low_lim[rows_at(b, block), :], high_lim[rows_at(b, block), :]
        start = pl.multiple_of(b * block, block)
        result = [zero, zero]
        here = [glu[h, pl.ds(pl.multiple_of(reach + start, 8), block), :] for h in range(2)]
        for tap in range(taps):
            shift = reach - tap
            inside = (low <= shift) if shift < 0 else (high >= shift)
            at = reach + shift
            for h in range(2):
                view = grad_conv.at[h, pl.ds(start, block + 2 * reach), :]
                term = jnp.where(inside, view[at : at + block, :], 0.0)
                result[h] = result[h] + depthwise[tap : tap + 1, h * lanes : (h + 1) * lanes].astype(F32) * term
                tap_sums[tap, h] += jnp.sum((here[h] * term).reshape(block // 8, 8, lanes), axis=0)
        for h in range(2):
            grad_glu[h, rows_at(b, block), :] = result[h]
        return carry

    lax.fori_loop(0, blocks // 2, conv_back_step, 0)
    advance(streams, 2)
    lax.fori_loop(blocks // 2, blocks, conv_back_step, 0)

    def back_moves(c):
        return moves(c, by_head(back_parts), by_frames(heads), back_send, back_recv, back_local)

    def close_step(c, carry):
        rows = rows_at(c, chunk)
        grad = halves_of(grad_glu, rows)
        value, gate = point[rows, :width], sigmoid(point[rows, width:])
        low_grad = jnp.concatenate([grad * gate, grad * value * gate * (1.0 - gate)], axis=1).astype(BF16)
        grad_point[rows, :] = low_grad
        grad = dg(low_grad, w_point1[...], 1, 1)
        hat, inv = norm_parts(x2_ref[rows, :])
        mid[3 * width + 2 : 3 * width + 3, :] += jnp.sum(grad * hat, axis=0, keepdims=True)
        grad2 = grad_x3[rows, :] + norm_back(grad, hat, inv, row_of(gain3))
        grad_x2[rows, :] = grad2
        low_grad = grad2.astype(BF16)
        branch3[rows, :] = low_grad
        back_parts[:, :, :, rows] = dg(w_out[...], low_grad, 1, 1).astype(BF16).reshape(2, 2, width // 4, chunk)
        for copy in back_moves(c):
            copy.start()
        return carry

    lax.fori_loop(0, count, close_step, 0)
    leaving += start_copies([(grad_x2, x2_hbm)], out_sems.at[pl.ds(3, 1)])
    for j in range(2):
        mid[j * width : (j + 1) * width, :] = dg(n3_keep[...], grad_point[:, j * width : (j + 1) * width], 0, 0)
    mid[2 * width : 3 * width, :] = dg(ctx[...].reshape(width, frames), branch3[...], 1, 0)
    for tap in range(taps):
        row = 3 * width + 8 + tap
        for h in range(2):
            mid[row : row + 1, h * lanes : (h + 1) * lanes] = jnp.sum(tap_sums[tap, h], axis=0, keepdims=True)

    leaving += start_copies([(mid, mid_hbm)], out_sems.at[pl.ds(4, 1)])

    def finish(c, carry):
        for copy in back_moves(c):
            copy.wait()
        return carry

    lax.fori_loop(0, count, finish, 0)
    for position in range(3, early_stages):
        advance(streams, position)
    size = streams[0].sizes[early_stages - 1][1]
    for i, stream in enumerate(streams):
        stream.sum_recv(early_stages - 1)
        partial[i * size : (i + 1) * size, :] = two[stream.at(stream.low(early_stages), size), :]
    wait_all(leaving)


def middle(
    lengths, parts, x1, cot, gain3, gain4, gain5, w_out, w_point1, depthwise, bn_gain, bn_bias, w_point2,
    w_in, w_down, dp,
):
    frames, width = x1.shape
    sp = lax.axis_size("sp")
    assert sp == HEADS == 4
    anywhere = pl.BlockSpec(memory_space=pl.ANY)
    paired = pltpu.VMEM((2, 2, width // 4, frames), BF16)
    wide = w_in.shape[1]
    staged, sems = reduction_scratch([wide, wide])
    stages = stage_plans()[2]
    part = exchange_plan(wide, stages[:-1])[2]
    taps = depthwise.shape[0]
    reach = taps // 2
    chunk = min(256, frames)
    count = frames // chunk
    lanes = width // 2
    keep, low_keep = pltpu.VMEM((frames, width), F32), pltpu.VMEM((frames, width), BF16)
    split = pltpu.VMEM((2, frames, lanes), F32)
    rimmed = pltpu.VMEM((2, frames + 2 * reach, lanes), F32)
    rims = pltpu.VMEM((2, 3 * reach, width), F32)
    moves = [DMA((count,)), DMA((count,)), DMA((count,))]
    return pl.pallas_call(
        functools.partial(middle_kernel, sp, dp, lengths.shape[1], taps, chunk, 32),
        out_shape=[
            jax.ShapeDtypeStruct((frames, width), BF16),
            jax.ShapeDtypeStruct((frames, width), F32),
            jax.ShapeDtypeStruct(parts.shape, BF16),
            jax.ShapeDtypeStruct((4 * width, width), F32),
            jax.ShapeDtypeStruct((width, width), F32),
            jax.ShapeDtypeStruct((8, width), F32),
            jax.ShapeDtypeStruct((2 * part, width), F32),
        ],
        in_specs=[
            SMEM, anywhere, anywhere, anywhere, VMEM, VMEM, VMEM, anywhere, anywhere, VMEM, VMEM, VMEM, anywhere,
            anywhere, anywhere,
        ],
        out_specs=[anywhere, anywhere, VMEM, anywhere, anywhere, VMEM, VMEM],
        scratch_shapes=[
            keep,
            low_keep,
            pltpu.VMEM(w_out.shape, BF16),
            pltpu.VMEM(w_point1.shape, BF16),
            pltpu.VMEM(w_point2.shape, BF16),
            pltpu.VMEM(w_in.shape, BF16),
            pltpu.VMEM(w_down.shape, BF16),
            low_keep,
            keep,
            pltpu.VMEM((4 * width, width), F32),
            pltpu.VMEM((width, width), F32),
            pltpu.VMEM((2 * wide, width), F32),
            DMA((7,)),
            DMA((5,)),
            pltpu.VMEM((staged, width), BF16),
            pltpu.VMEM((staged, width), BF16),
            DMA(sems),
            DMA(sems),
            paired,
            keep,
            low_keep,
            pltpu.VMEM((frames, 2 * width), F32),
            rimmed,
            split,
            pltpu.VMEM((frames, lanes), I32),
            pltpu.VMEM((frames, lanes), I32),
            pltpu.VMEM((frames, wide), BF16),
            pltpu.VMEM((frames, wide), BF16),
            low_keep,
            low_keep,
            low_keep,
            low_keep,
            keep,
            split,
            rimmed,
            split,
            pltpu.VMEM((frames, 2 * width), BF16),
            low_keep,
            paired,
            pltpu.VMEM((taps, 2, 8, lanes), F32),
            rims,
            rims,
            pltpu.VMEM((2, 2, 8, width), F32),
            pltpu.VMEM((2, sp - 1, 8, width), F32),
            pltpu.VMEM((2, dp - 1, 8, width), F32),
            pltpu.VMEM((8, width), F32),
        ]
        + moves
        + moves
        + [DMA((2, 2)), DMA((2, 2)), DMA((2, sp + dp - 2)), DMA((2, sp + dp - 2))],
        compiler_params=pltpu.CompilerParams(
            collective_id=1, has_side_effects=True, vmem_limit_bytes=VMEM_LIMIT
        ),
        name="middle",
    )(
        lengths, parts, x1, cot, gain3, gain4, gain5, w_out, w_point1, depthwise, bn_gain, bn_bias, w_point2,
        w_in, w_down,
    )


def back_kernel(
    sp, items, chunk, block, sub, len_ref, lse_ref, gain1, gain2, partial,
    near_hbm, far_hbm, o_hbm, do_hbm, trig_hbm, mid_hbm, point_two_hbm, tok_hbm, x1_hbm, n2_hbm, x2_hbm, act_hbm, slope_hbm, w_in_hbm, w_out_hbm, w_qkv_hbm,
    grad_ref, full,
    near, far, o_ref, do_ref, trig, tok, x1_ref, n2_ref, grad_x2, act, slope, w_in, w_out, w_qkv,
    qa, qt, ka, da, va, dq, turned, far_out, near_out, dq_out, far_kv, near_kv, near_dq,
    joined, branch, hidden, grad_x1, gains, acc, stage, land,
    load_sems, far_send, far_recv, near_send, near_recv, sum_send, sum_recv,
):
    me, dp = lax.axis_index("sp"), lax.axis_index("dp")
    core, pair = lax.rem(me, 2), me // 2
    sibling = peer_at(1, 0)
    frames, width = tok.shape
    wide = w_in.shape[1]
    half = trig.shape[0] // 2
    dim = 2 * half
    count = frames // chunk
    reach = 2 * frames
    greeted = [peer_at(*mask) for mask in all_masks(sp)]
    greet(greeted)
    unit = 4 * width
    last = 6 * unit
    loads = start_copies(
        [
            (near_hbm, near), (do_hbm, do_ref), (o_hbm, o_ref), (far_hbm, far),
            (mid_hbm, acc.at[2 * unit : 3 * unit, :]),
            (point_two_hbm, acc.at[3 * unit + 3 * width : 4 * unit, :]), (trig_hbm, trig),
            (x1_hbm, x1_ref), (x2_hbm, grad_x2), (w_qkv_hbm, w_qkv), (n2_hbm, n2_ref), (act_hbm, act),
            (w_out_hbm, w_out), (slope_hbm, slope), (w_in_hbm, w_in), (tok_hbm, tok),
        ],
        load_sems,
    )
    streams = make_streams(
        [
            (0, unit, 2), (unit, unit, 2), (2 * unit, unit, 2),
            (3 * unit, unit, 1), (4 * unit, unit, 0), (5 * unit, unit, 0), (last, 16, 0),
        ],
        acc, stage, land, full, sum_send, sum_recv,
    )
    early, (qkv, down, up, rest) = streams[:3], ([stream] for stream in streams[3:])
    steps = len(stage_plans()[0])
    acc[last : last + 16, :] = jnp.zeros((16, width), F32)
    gains[...] = jnp.zeros_like(gains)
    for h in range(2):
        dq[h] = jnp.zeros((dim, reach), F32)
    wait_all(loads[:4])
    ends = ends_of(len_ref, items)
    wide_pad = jnp.zeros((dim - 16, frames), BF16)
    for slot in range(2):
        cols = slice(slot * frames, (slot + 1) * frames)
        far_cols = slice(reach + slot * frames, reach + (slot + 1) * frames)
        segment = segment_row((2 * pair + slot) * frames, frames, ends)
        far_segment = segment_row((2 * (1 - pair) + slot) * frames, frames, ends)
        for h in range(2):
            query = near[slot, h * dim : (h + 1) * dim, :]
            qt[h, :, cols] = query
            qa[h, cols, :] = query_rows(query, segment, items, -lse_ref[h : h + 1, cols]).T
            grad = do_ref[h, :, cols]
            row_dot = jnp.sum(grad.astype(F32) * o_ref[h, :, cols], axis=0, keepdims=True)
            da[h, cols, :] = jnp.concatenate([grad, split_rows(-row_dot), wide_pad], axis=0).T
            ka[h, :, cols] = key_rows(near[slot, (2 + h) * dim : (3 + h) * dim, :], segment, items)
            ka[h, :, far_cols] = key_rows(far[slot, h * dim : (h + 1) * dim, :], far_segment, items)
            for where, value in (
                (cols, near[slot, (4 + h) * dim : (5 + h) * dim, :]),
                (far_cols, far[slot, (2 + h) * dim : (3 + h) * dim, :]),
            ):
                va[h, 0:dim, where] = value
                va[h, dim : dim + 16, where] = first_rows(3, frames)
                va[h, dim + 16 :, where] = wide_pad
    await_greetings(greeted)
    wait_all(loads[4:5])

    def attend_block(h, at):
        dk, dv = [], []

        def score(u):
            cols = pl.ds(pl.multiple_of(at + u * sub, sub), sub)
            return dg(qa[h], ka[h, :, cols], 1, 0), dg(da[h], va[h, :, cols], 1, 0)

        ready = score(0)
        for u in range(block // sub):
            scores, grad_probs = ready
            if u + 1 < block // sub:
                ready = score(u + 1)
            probs = jnp.exp2(scores)
            grad = (probs * grad_probs).astype(BF16)
            dv.append(dg(do_ref[h], probs.astype(BF16), 1, 0).astype(BF16))
            dk.append((dg(qt[h], grad, 1, 0) * LN2).astype(BF16))
            turned[u * sub : (u + 1) * sub, :] = grad.T
        dq[h] += dg(ka[h, 0:dim, pl.ds(pl.multiple_of(at, block), block)], turned[...], 1, 0)
        return jnp.concatenate(dk, axis=1), jnp.concatenate(dv, axis=1)

    per = frames // block

    def keep(ref, slot, h, cols, block_grads):
        for i, value in enumerate(block_grads):
            ref[slot, 2 * i + h, :, cols] = value

    def far_copy(b):
        cols = rows_at(lax.rem(b, per), block)
        return pltpu.make_async_remote_copy(
            src_ref=far_out.at[b // per, :, :, cols], dst_ref=far_kv.at[core, :, :, cols],
            send_sem=far_send.at[b], recv_sem=far_recv.at[core, lax.rem(b, per)],
            device_id=(dp, 2 * (1 - pair) + b // per), device_id_type=MESH,
        )

    done = len(early[0].stages) - 1
    size = early[0].sizes[done - 1][1]
    for i, stream in enumerate(early[:2]):
        acc[stream.at(stream.low(done), size), :] = partial[i * size : (i + 1) * size, :]
    schedule, remaining = {}, []
    for stream, times, first in zip(early, (PARTIAL_TIMES, PARTIAL_TIMES, FRESH_TIMES), (done, done, 0)):
        positions = range(first, 2 * len(stream.stages) + 1)
        for position, time in zip(positions, times):
            schedule.setdefault(time, []).append((stream, position, position == first))
        remaining.append([(stream, position) for position in positions[len(times) :]])

    def early_steps(t):
        for time, moves in schedule.items():
            @pl.when(t == min(time, 8 * per - 1))
            def _():
                for stream, position, opening in moves:
                    if opening:
                        stream.sum_send(position)
                    else:
                        advance([stream], position)

    def late_steps():
        for moves in remaining:
            if moves:
                stream, position = moves.pop(0)
                advance([stream], position)

    def far_step(t, carry):
        b, h = t // 2, lax.rem(t, 2)
        cols = rows_at(lax.rem(b, per), block)
        keep(far_out, b // per, h, cols, attend_block(h, reach + b * block))

        @pl.when(h == 1)
        def _():
            far_copy(b).start()

        early_steps(t)
        return carry

    lax.fori_loop(0, 4 * per, far_step, 0)

    def near_copy(b):
        cols = rows_at(b, block)
        return pltpu.make_async_remote_copy(
            src_ref=near_out.at[:, :, cols], dst_ref=near_kv.at[core, :, :, cols],
            send_sem=near_send.at[b], recv_sem=near_recv.at[b], device_id=sibling, device_id_type=MESH,
        )

    def sibling_step(t, carry):
        b, h = t // 2, lax.rem(t, 2)
        block_grads = attend_block(h, (1 - core) * frames + b * block)
        for i, value in enumerate(block_grads):
            near_out[2 * i + h, :, rows_at(b, block)] = value

        @pl.when(h == 1)
        def _():
            near_copy(b).start()

        early_steps(t + 4 * per)
        return carry

    lax.fori_loop(0, 2 * per, sibling_step, 0)

    def own_step(t, carry):
        b, h = t // 2, lax.rem(t, 2)
        keep(near_kv, core, h, rows_at(b, block), attend_block(h, core * frames + b * block))

        early_steps(t + 6 * per)
        return carry

    lax.fori_loop(0, 2 * per, own_step, 0)
    for h in range(2):
        dq_out[h] = (dq[h, :, pl.ds(pl.multiple_of((1 - core) * frames, frames), frames)] * dim**-0.5).astype(BF16)
    dq_copy = pltpu.make_async_remote_copy(
        src_ref=dq_out, dst_ref=near_dq.at[core], send_sem=near_send.at[per], recv_sem=near_recv.at[per],
        device_id=sibling, device_id_type=MESH,
    )
    dq_copy.start()
    for h in range(2):
        near_dq[core, h] = (dq[h, :, pl.ds(pl.multiple_of(core * frames, frames), frames)] * dim**-0.5).astype(BF16)
    wait_all(loads[5:])
    for b in range(2 * per):
        far_copy(b).wait_send()
    for source in range(2):
        for b in range(per):
            pltpu.make_async_remote_copy(
                src_ref=far_out.at[0, :, :, rows_at(b, block)], dst_ref=far_kv.at[source, :, :, rows_at(b, block)],
                send_sem=far_send.at[b], recv_sem=far_recv.at[source, b], device_id=sibling, device_id_type=MESH,
            ).wait_recv()
    for b in range(per):
        near_copy(b).wait()

    def turn_back(first, second, rows, low):
        sine, cosine = trig[0:half, rows], trig[half:, rows]
        joined[low : low + half, rows] = (first * cosine + second * sine).astype(BF16)
        joined[low + half : low + dim, rows] = (second * cosine - first * sine).astype(BF16)

    def keys_step(c, carry):
        rows = rows_at(c, chunk)
        for p in range(2):
            for h in range(2):
                head = 2 * p + h

                def both(i, low, high):
                    return near_kv[p, i, low:high, rows].astype(F32) + far_kv[p, i, low:high, rows].astype(F32)

                turn_back(both(h, 0, half), both(h, half, dim), rows, width + head * dim)
                low = 2 * width + head * dim
                joined[low : low + dim, rows] = both(2 + h, 0, dim).astype(BF16)
        return carry

    lax.fori_loop(0, count, keys_step, 0)
    dq_copy.wait()

    def arrive(c, carry):
        rows = rows_at(c, chunk)
        for p in range(2):
            for h in range(2):
                turn_back(
                    near_dq[p, h, 0:half, rows].astype(F32), near_dq[p, h, half:dim, rows].astype(F32), rows,
                    (2 * p + h) * dim,
                )
        grad = dg(joined[:, rows], w_qkv[...], 0, 1)
        hat, inv = norm_parts(x1_ref[rows, :])
        gains[1:2, :] += jnp.sum(grad * hat, axis=0, keepdims=True)
        grad = grad_x2[rows, :] + norm_back(grad, hat, inv, row_of(gain2))
        grad_x1[rows, :] = grad
        branch[rows, :] = (0.5 * grad).astype(BF16)
        return carry

    lax.fori_loop(0, count, arrive, 0)
    for j in range(0, wide, width):
        acc[4 * unit + j : 4 * unit + j + width, :] = dg(act[:, j : j + width], branch[...], 0, 0)
    advance(down, 0)
    acc[3 * unit : 3 * unit + 3 * width, :] = dg(joined[...], n2_ref[...], 1, 0)
    advance(qkv, 0)

    def through(c, carry):
        rows = rows_at(c, chunk)
        grad = dg(branch[rows, :], w_out[...], 1, 1)
        hidden[rows, :] = (grad * slope[rows, :].astype(F32)).astype(BF16)
        hat, _ = norm_parts(tok[rows, :].astype(F32))
        n2_ref[rows, :] = (hat * row_of(gain1)).astype(BF16)
        return carry

    lax.fori_loop(0, count, through, 0)
    advance(down + qkv, 1)
    for j in range(0, wide, width):
        acc[5 * unit + j : 5 * unit + j + width, :] = dg(n2_ref[...], hidden[:, j : j + width], 0, 0)
    advance(up, 0)

    def last_step(c, carry):
        rows = rows_at(c, chunk)
        grad = dg(hidden[rows, :], w_in[...], 1, 1)
        hat, inv = norm_parts(tok[rows, :].astype(F32))
        gains[0:1, :] += jnp.sum(grad * hat, axis=0, keepdims=True)
        grad_ref[rows, :] = (grad_x1[rows, :] + norm_back(grad, hat, inv, row_of(gain1))).astype(BF16)
        return carry

    lax.fori_loop(0, count // 2, last_step, 0)
    advance(up, 1)
    lax.fori_loop(count // 2, count, last_step, 0)
    acc[last : last + 8, :] = gains[...]
    advance(rest, 0)
    for position in range(2, 2 * steps + 1):
        advance(down + qkv + up, position)
        advance(rest, position - 1)
        late_steps()
    advance(rest, 2 * steps)
    while any(remaining):
        late_steps()


def back(
    lengths, near, far, o, lse, do, trig, gain1, gain2, partial, mid, point_two,
    tok, x1, n2, grad_x2, act, slope, w_in, w_out, w_qkv,
):
    frames, width = tok.shape
    sp = lax.axis_size("sp")
    chunk = min(256, frames)
    block = min(512, frames)
    count, per = frames // chunk, frames // block
    wide = w_in.shape[1]
    dim = width // HEADS
    reach = 2 * frames
    rows = 24 * width + 16
    staged, sems = reduction_scratch([4 * width] * 6 + [16])
    low_keep, keep = pltpu.VMEM((frames, width), BF16), pltpu.VMEM((frames, width), F32)
    return pl.pallas_call(
        functools.partial(back_kernel, sp, lengths.shape[1], chunk, block, min(128, block)),
        out_shape=[
            jax.ShapeDtypeStruct((frames, width), BF16),
            jax.ShapeDtypeStruct((rows, width), BF16),
        ],
        in_specs=[SMEM] + [VMEM] * 4 + [pl.BlockSpec(memory_space=pl.ANY)] * 16,
        out_specs=[VMEM] * 2,
        scratch_shapes=[
            pltpu.VMEM(near.shape, BF16),
            pltpu.VMEM(far.shape, BF16),
            pltpu.VMEM(o.shape, F32),
            pltpu.VMEM(do.shape, BF16),
            pltpu.VMEM(trig.shape, F32),
            low_keep,
            keep,
            low_keep,
            keep,
            pltpu.VMEM((frames, wide), BF16),
            pltpu.VMEM((frames, wide), BF16),
            pltpu.VMEM(w_in.shape, BF16),
            pltpu.VMEM(w_out.shape, BF16),
            pltpu.VMEM(w_qkv.shape, BF16),
            pltpu.VMEM((2, reach, 2 * dim), BF16),
            pltpu.VMEM((2, dim, reach), BF16),
            pltpu.VMEM((2, 2 * dim, 2 * reach), BF16),
            pltpu.VMEM((2, reach, 2 * dim), BF16),
            pltpu.VMEM((2, 2 * dim, 2 * reach), BF16),
            pltpu.VMEM((2, dim, reach), F32),
            pltpu.VMEM((block, reach), BF16),
            pltpu.VMEM((2, 4, dim, frames), BF16),
            pltpu.VMEM((4, dim, frames), BF16),
            pltpu.VMEM((2, dim, frames), BF16),
            pltpu.VMEM((2, 4, dim, frames), BF16),
            pltpu.VMEM((2, 4, dim, frames), BF16),
            pltpu.VMEM((2, 2, dim, frames), BF16),
            pltpu.VMEM((3 * width, frames), BF16),
            low_keep,
            pltpu.VMEM((frames, wide), BF16),
            keep,
            pltpu.VMEM((8, width), F32),
            pltpu.VMEM((rows, width), F32),
            pltpu.VMEM((staged, width), BF16),
            pltpu.VMEM((staged, width), BF16),
            DMA((16,)),
            DMA((2 * per,)),
            DMA((2, per)),
            DMA((per + 1,)),
            DMA((per + 1,)),
            DMA(sems),
            DMA(sems),
        ],
        compiler_params=pltpu.CompilerParams(
            collective_id=2, has_side_effects=True, vmem_limit_bytes=VMEM_LIMIT
        ),
        name="back",
    )(
        lengths, lse, gain1, gain2, partial, near, far, o, do, trig, mid, point_two,
        tok, x1, n2, grad_x2, act, slope, w_in, w_out, w_qkv,
    )


def unpack_kernel(
    taps, full, bn_grads, output, input_grad,
    output_to, input_to, gain1_to, in_one_to, out_one_to, gain2_to, qkv_to, out_weight_to, gain3_to, point_one_to,
    depthwise_to, bn_gain_to, bn_bias_to, point_two_to, gain4_to, in_two_to, out_two_to, gain5_to,
    in_one, out_one, qkv, point_one, point_two, out_weight, in_two, out_two, depthwise, sems,
):
    width = full.shape[1]
    unit = 4 * width
    copies = []

    def send(source, target):
        copies.append(pltpu.make_async_copy(source, target, sems.at[len(copies)]))
        copies[-1].start()

    def block(ref, base):
        return ref[base : base + width, :].astype(F32)

    send(output, output_to)
    send(input_grad, input_to)
    for j in range(0, unit, width):
        out_two[j : j + width, :] = block(full, j)
    send(out_two, out_two_to)
    for j in range(0, unit, width):
        in_two[:, j : j + width] = block(full, unit + j)
    send(in_two, in_two_to)
    for j in range(0, unit, width):
        out_one[j : j + width, :] = block(full, 4 * unit + j)
    send(out_one, out_one_to)
    for j in range(0, unit, width):
        in_one[:, j : j + width] = block(full, 5 * unit + j)
    send(in_one, in_one_to)
    for j in range(0, 2 * width, width):
        point_one[:, j : j + width] = block(full, 2 * unit + j)
    send(point_one, point_one_to)
    out_weight[...] = block(full, 2 * unit + 2 * width)
    send(out_weight, out_weight_to)
    point_two[...] = block(full, 3 * unit + 3 * width)
    send(point_two, point_two_to)
    for j in range(0, 3 * width, width):
        qkv[:, j : j + width] = block(full, 3 * unit + j).T
    send(qkv, qkv_to)
    small = full[2 * unit + 3 * width : 2 * unit + 3 * width + 64, :].astype(F32)
    depthwise[...] = small[8 : 8 + taps]
    send(depthwise, depthwise_to)
    rest = full[6 * unit : 6 * unit + 16, :].astype(F32)
    for ref, row in (
        (gain1_to, rest[0]), (gain2_to, rest[1]), (gain3_to, small[2]), (gain4_to, small[3]), (gain5_to, small[4]),
        (bn_gain_to, bn_grads[0, :]), (bn_bias_to, bn_grads[1, :]),
    ):
        ref[...] = row
    for copy in copies:
        copy.wait()


def unpack(full, bn_grads, output, input_grad, taps):
    width = full.shape[1]
    row, square, tall, flat = (width,), (width, width), (4 * width, width), (width, 4 * width)
    thrice, twice = (width, 3 * width), (width, 2 * width)
    anywhere = pl.BlockSpec(memory_space=pl.ANY)
    shapes = [
        output.shape, input_grad.shape, row, flat, tall, row, thrice, square, row, twice, (taps, width), row, row,
        square, row, flat, tall, row,
    ]
    return pl.pallas_call(
        functools.partial(unpack_kernel, taps),
        out_shape=[jax.ShapeDtypeStruct(shape, F32 if i > 1 else BF16) for i, shape in enumerate(shapes)],
        in_specs=[VMEM] * 4,
        out_specs=[VMEM if shape == row else anywhere for shape in shapes],
        scratch_shapes=[
            pltpu.VMEM(shape, F32)
            for shape in (flat, tall, thrice, twice, square, square, flat, tall, (taps, width))
        ]
        + [DMA((11,))],
        compiler_params=pltpu.CompilerParams(vmem_limit_bytes=VMEM_LIMIT),
        name="unpack",
    )(full, bn_grads, output, input_grad)


def on_device(
    tokens, ln1_gain, ffn1_in, ffn1_out, ln2_gain, w_qkv, w_out, ln3_gain, w_point1, depthwise,
    bn_gain, bn_bias, w_point2, ln4_gain, ffn2_in, ffn2_out, ln5_gain, lengths, cotangent,
):
    width = tokens.shape[2]
    sp, dp = lax.axis_size("sp"), lax.axis_size("dp")
    assert HEADS == sp and ffn1_in.shape[1] == ffn2_in.shape[1] == 4 * width
    half = width // HEADS // 2
    turns = 10000.0 ** (-np.arange(half, dtype=np.float64) / half) / (2 * np.pi)
    high = np.round(turns * 4096.0) / 4096.0
    freq = jnp.asarray(np.stack([high, turns - high], axis=1), F32)
    x1, n2, trig, act, slope, near, far, context, raw_context, log_sums, flag = front(
        lengths, tokens[0], ln1_gain, ffn1_in, ffn1_out, ln2_gain, w_qkv, freq
    )
    context, raw_context, log_sums = repair(lengths, flag, near, far, context, raw_context, log_sums)
    output, grad_x2, grad_context, mid, point_two, bn_grads, partial = middle(
        lengths, context, x1, cotangent[0], ln3_gain, ln4_gain, ln5_gain, w_out, w_point1, depthwise,
        bn_gain, bn_bias, w_point2, ffn2_in, ffn2_out, dp,
    )
    input_grad, full = back(
        lengths, near, far, raw_context, log_sums, grad_context, trig, ln1_gain, ln2_gain, partial, mid, point_two,
        tokens[0], x1, n2, grad_x2, act, slope, ffn1_in, ffn1_out, w_qkv,
    )
    results = unpack(full, bn_grads, output, input_grad, depthwise.shape[0])
    return (results[0][None], results[1][None]) + tuple(results[2:])


def solution(mesh):
    split = P("dp", "sp", None)
    return jax.shard_map(
        on_device,
        mesh=mesh,
        in_specs=(split,) + (P(),) * 16 + (P("dp", None), split),
        out_specs=(split, split) + (P(),) * 16,
        check_vma=False,
    )
```

```python
import functools

import jax
import jax.numpy as jnp
import numpy as np
from jax import lax
from jax.experimental import pallas as pl
from jax.experimental.pallas import tpu as pltpu
from jax.sharding import PartitionSpec as P

HEADS = 4
EPS = 1e-05
NEG = -1e30
LN2 = float(np.log(2.0))
F32 = jnp.float32
BF16 = jnp.bfloat16
I32 = jnp.int32
MESH = pl.DeviceIdType.MESH
VMEM = pl.BlockSpec(memory_space=pltpu.VMEM)
SMEM = pl.BlockSpec(memory_space=pltpu.SMEM)
DMA = pltpu.SemaphoreType.DMA
VMEM_LIMIT = 56 * 2**20
PARTIAL_TIMES = (0, 4, 8, 13)
FRESH_TIMES = (0, 2, 5, 9, 13)


def dg(left, right, left_dim, right_dim):
    return lax.dot_general(
        left, right, (((left_dim,), (right_dim,)), ((), ())), preferred_element_type=F32
    )


def rows_at(index, count):
    return pl.ds(pl.multiple_of(index * count, count), count)


def start_copies(pairs, sems):
    copies = [pltpu.make_async_copy(source, target, sems.at[i]) for i, (source, target) in enumerate(pairs)]
    for copy in copies:
        copy.start()
    return copies


def wait_all(copies):
    for copy in copies:
        copy.wait()


def greet(devices):
    for device in devices:
        pl.semaphore_signal(pltpu.get_barrier_semaphore(), inc=1, device_id=device, device_id_type=MESH)


def await_greetings(devices):
    pl.semaphore_wait(pltpu.get_barrier_semaphore(), len(devices))


def flipped(axis, mask):
    me, step = lax.axis_index(axis), 1
    out = me
    while step <= mask:
        if mask & step:
            out = out + step - 2 * step * lax.rem(me // step, 2)
        step *= 2
    return out


def peer_at(sp_mask, dp_mask):
    return (flipped("dp", dp_mask), flipped("sp", sp_mask))


def sp_peers(count):
    return [peer_at(mask, 0) for mask in range(1, count)]


def row_of(ref):
    return ref[...].astype(F32).reshape(1, ref.shape[0])


def frame_cols(device, frames, c, chunk):
    return pl.ds(pl.multiple_of(device * frames + c * chunk, chunk), chunk)


def ends_of(len_ref, items):
    ends, total = [], 0
    for item in range(items):
        total = total + len_ref[0, item]
        ends.append(total)
    return ends


def segment_row(first, count, ends):
    frame = first + lax.broadcasted_iota(I32, (1, count), 1)
    segment = jnp.zeros((1, count), I32)
    for end in ends:
        segment = segment + (frame >= end).astype(I32)
    return segment


def position_row(first, count, ends):
    frame = first + lax.broadcasted_iota(I32, (1, count), 1)
    start = jnp.zeros((1, count), I32)
    for end in ends:
        start = jnp.where(frame >= end, end, start)
    return (frame - start).astype(F32)


def onehot_rows(segment, items, other, same):
    row = lax.broadcasted_iota(I32, (16, segment.shape[1]), 0)
    return jnp.where(row <= items, jnp.where(row == segment, same, other), 0.0)


def norm_parts(rows):
    centre = rows - jnp.mean(rows, axis=-1, keepdims=True)
    inv = lax.rsqrt(jnp.mean(centre * centre, axis=-1, keepdims=True) + EPS)
    return centre * inv, inv


def norm_back(grad, hat, inv, gain):
    scaled = grad * gain
    first = jnp.mean(scaled, axis=-1, keepdims=True)
    second = jnp.mean(scaled * hat, axis=-1, keepdims=True)
    return inv * (scaled - first - hat * second)


def sigmoid(x):
    return 0.5 * jnp.tanh(0.5 * x) + 0.5


def sine_cosine(position, freq_hi, freq_lo):
    turns = position * freq_hi
    turns = turns - jnp.round(turns) + position * freq_lo
    turns = turns - jnp.round(turns)
    x = turns * float(np.pi)
    x2 = x * x
    s = x * (1 + x2 * (-1 / 6 + x2 * (1 / 120 + x2 * (-1 / 5040 + x2 * (1 / 362880 - x2 / 39916800)))))
    c = 1 + x2 * (-1 / 2 + x2 * (1 / 24 + x2 * (-1 / 720 + x2 * (1 / 40320 + x2 * (-1 / 3628800 + x2 / 479001600)))))
    return 2 * s * c, 1 - 2 * s * s


def split_rows(value):
    row = lax.broadcasted_iota(I32, (16, value.shape[1]), 0)
    first = value.astype(BF16).astype(F32)
    second = (value - first).astype(BF16).astype(F32)
    third = value - first - second
    picked = jnp.where(row == 0, first, jnp.where(row == 1, second, third))
    return jnp.where(row < 3, picked, 0.0).astype(BF16)


def first_rows(count, columns):
    row = lax.broadcasted_iota(I32, (16, columns), 0)
    return jnp.where(row < count, 1.0, 0.0).astype(BF16)


def query_rows(query, segment, items, shift):
    pad = jnp.zeros((query.shape[0] - 32, query.shape[1]), BF16)
    return jnp.concatenate([query, onehot_rows(segment, items, 0.0, 1.0).astype(BF16), split_rows(shift), pad], axis=0)


def key_rows(key, segment, items):
    pad = jnp.zeros((key.shape[0] - 32, key.shape[1]), BF16)
    return jnp.concatenate(
        [key, onehot_rows(segment, items, NEG, 0.0).astype(BF16), first_rows(3, key.shape[1]), pad], axis=0
    )


def lay_queries(near, slot, frames, first, ends, items, dim, qa, lse):
    cols = slice(slot * frames, (slot + 1) * frames)
    segment = segment_row(first, frames, ends)
    for h in range(2):
        query = near[slot, h * dim : (h + 1) * dim, :]
        key = near[slot, (2 + h) * dim : (3 + h) * dim, :]
        own = jnp.sum(query.astype(F32) * key.astype(F32), axis=0, keepdims=True)
        lse[h : h + 1, cols] = own
        qa[h, :, cols] = query_rows(query, segment, items, -own)


def lay_keys(key, value, rows, first, ends, items, h, ka, va):
    dim, count = key.shape
    ka[h, rows, :] = key_rows(key, segment_row(first, count, ends), items).T
    va[h, 0:dim, rows] = value
    va[h, dim:, rows] = first_rows(1, count)


def front_kernel(
    items, chunk, block, len_ref, tok, gain1, w_in, w_out, gain2, w_qkv, freq,
    x1_hbm, n2_hbm, trig_hbm, act_hbm, slope_hbm, near_hbm, far_hbm, ctx_hbm, o_hbm, lse, flag,
    x1_ref, n2_ref, trig, act, slope, near, far, ctx, o_ref,
    parts, turned, qa, ka, va, acc, send, recv, out_sems, last_sems,
):
    me = lax.axis_index("sp")
    core, pair = lax.rem(me, 2), me // 2
    frames, width = tok.shape
    half = trig.shape[0] // 2
    dim = 2 * half
    count = frames // chunk
    peers = [peer_at(mask, 0) for mask in (1, 2, 3)]
    greet(peers)
    turned[...] = w_qkv[...].T
    ends = ends_of(len_ref, items)
    scale = float(np.log2(np.e)) * dim**-0.5

    def copies(c):
        cols = rows_at(c, chunk)
        ways = (
            (parts.at[1 - core, :, cols], near.at[core, :, cols]),
            (parts.at[core, 2 * dim :, cols], far.at[core, :, cols]),
            (parts.at[1 - core, 2 * dim :, cols], far.at[core, :, cols]),
        )
        return [
            pltpu.make_async_remote_copy(
                src_ref=source, dst_ref=target, send_sem=send.at[i, c], recv_sem=recv.at[i, c],
                device_id=peers[i], device_id_type=MESH,
            )
            for i, (source, target) in enumerate(ways)
        ]

    def results(c):
        rows = rows_at(c, chunk)
        pairs = [(ref.at[rows, :], hbm.at[rows, :]) for ref, hbm in (
            (x1_ref, x1_hbm), (n2_ref, n2_hbm), (act, act_hbm), (slope, slope_hbm)
        )]
        return [pltpu.make_async_copy(source, target, out_sems.at[i, c]) for i, (source, target) in enumerate(pairs)]

    def step(c, carry):
        rows = rows_at(c, chunk)
        x = tok[rows, :].astype(F32)
        hat, _ = norm_parts(x)
        n1 = (hat * row_of(gain1)).astype(BF16)
        a = dg(n1, w_in[...], 1, 0)
        sig = sigmoid(a)
        s = (a * sig).astype(BF16)
        act[rows, :] = s
        slope[rows, :] = (sig * (1.0 + a * (1.0 - sig))).astype(BF16)
        x1 = x + 0.5 * dg(s, w_out[...], 1, 0)
        x1_ref[rows, :] = x1
        hat, _ = norm_parts(x1)
        n2 = (hat * row_of(gain2)).astype(BF16)
        n2_ref[rows, :] = n2
        joined = dg(turned[...], n2, 1, 1)
        sine, cosine = sine_cosine(
            position_row(me * frames + c * chunk, chunk, ends), freq[:, 0:1], freq[:, 1:2]
        )
        trig[0:half, rows] = sine
        trig[half:, rows] = cosine
        for p in range(2):
            for j in range(2):
                for part, factor in ((0, scale), (1, 1.0)):
                    low = part * width + (2 * p + j) * dim
                    first, second = joined[low : low + half], joined[low + half : low + dim]
                    low = (2 * part + j) * dim
                    parts[p, low : low + half, rows] = ((first * cosine - second * sine) * factor).astype(BF16)
                    parts[p, low + half : low + dim, rows] = (
                        (first * sine + second * cosine) * factor
                    ).astype(BF16)
                low = 2 * width + (2 * p + j) * dim
                parts[p, (4 + j) * dim : (5 + j) * dim, rows] = joined[low : low + dim].astype(BF16)

        @pl.when(c == 0)
        def _():
            await_greetings(peers)

        for copy in copies(c):
            copy.start()
        near[core, :, rows] = parts[core, :, rows]
        for copy in results(c):
            copy.start()
        return carry

    lax.fori_loop(0, count, step, 0)

    def near_arrives(c, carry):
        copies(c)[0].wait()
        return carry

    lax.fori_loop(0, count, near_arrives, 0)
    leaving = start_copies([(near, near_hbm), (trig, trig_hbm)], last_sems)
    reach = 2 * frames
    for slot in range(2):
        first = (2 * pair + slot) * frames
        lay_queries(near, slot, frames, first, ends, items, dim, qa, lse)
        for h in range(2):
            lay_keys(
                near[slot, (2 + h) * dim : (3 + h) * dim, :], near[slot, (4 + h) * dim : (5 + h) * dim, :],
                slice(slot * frames, (slot + 1) * frames), first, ends, items, h, ka, va,
            )

    def near_step(i, carry):
        h, cols = i // (reach // block), rows_at(lax.rem(i, reach // block), block)
        powers = jnp.exp2(dg(ka[h, 0:reach, :], qa[h, :, cols], 1, 0)).astype(BF16)
        acc[h, :, cols] = dg(va[h, :, 0:reach], powers, 1, 0)
        return carry

    lax.fori_loop(0, 2 * reach // block, near_step, 0)
    wide = min(1024, reach)

    def far_step(c, carry):
        for copy in copies(c)[1:]:
            copy.wait()
        cols = rows_at(c, chunk)
        for slot in range(2):
            first = (2 * (1 - pair) + slot) * frames + c * chunk
            rows = pl.ds(pl.multiple_of(reach + (2 * c + slot) * chunk, chunk), chunk)
            for h in range(2):
                lay_keys(
                    far[slot, h * dim : (h + 1) * dim, cols], far[slot, (2 + h) * dim : (3 + h) * dim, cols],
                    rows, first, ends, items, h, ka, va,
                )
        rows = pl.ds(pl.multiple_of(reach + 2 * c * chunk, 2 * chunk), 2 * chunk)

        def inner(i, carry):
            h, cols = i // (reach // wide), rows_at(lax.rem(i, reach // wide), wide)
            powers = jnp.exp2(dg(ka[h, rows, :], qa[h, :, cols], 1, 0)).astype(BF16)
            acc[h, :, cols] += dg(va[h, :, rows], powers, 1, 0)
            return carry

        return lax.fori_loop(0, 2 * reach // wide, inner, carry)

    lax.fori_loop(0, count, far_step, 0)
    leaving += start_copies([(far, far_hbm)], last_sems.at[pl.ds(2, 1)])
    bad = jnp.zeros((1, reach), F32)
    for h in range(2):
        total = acc[h, dim : dim + 1, :]
        value = acc[h, 0:dim, :] / total
        ctx[h] = value.astype(BF16)
        o_ref[h] = value
        leaving += start_copies([(ctx.at[h], ctx_hbm.at[h]), (o_ref.at[h], o_hbm.at[h])], last_sems.at[pl.ds(3 + 2 * h, 2)])
        lse[h : h + 1, :] = lse[h : h + 1, :] + jnp.log2(total)
        bad = jnp.maximum(bad, jnp.where(total < 2.0**60, 0.0, 1.0))
    flag[...] = jnp.broadcast_to(jnp.max(bad, axis=1, keepdims=True), flag.shape)
    for c in range(count):
        wait_all(results(c))
    wait_all(leaving)


def front(lengths, tok, gain1, w_in, w_out, gain2, w_qkv, freq):
    frames, width = tok.shape
    wide = w_in.shape[1]
    chunk = min(256, frames)
    count = frames // chunk
    dim = width // HEADS
    reach = 2 * frames
    return pl.pallas_call(
        functools.partial(front_kernel, lengths.shape[1], chunk, min(512, reach)),
        out_shape=[
            jax.ShapeDtypeStruct((frames, width), F32),
            jax.ShapeDtypeStruct((frames, width), BF16),
            jax.ShapeDtypeStruct((dim, frames), F32),
            jax.ShapeDtypeStruct((frames, wide), BF16),
            jax.ShapeDtypeStruct((frames, wide), BF16),
            jax.ShapeDtypeStruct((2, 6 * dim, frames), BF16),
            jax.ShapeDtypeStruct((2, 4 * dim, frames), BF16),
            jax.ShapeDtypeStruct((2, dim, reach), BF16),
            jax.ShapeDtypeStruct((2, dim, reach), F32),
            jax.ShapeDtypeStruct((2, reach), F32),
            jax.ShapeDtypeStruct((8, 128), F32),
        ],
        in_specs=[SMEM] + [VMEM] * 7,
        out_specs=[pl.BlockSpec(memory_space=pl.ANY)] * 9 + [VMEM] * 2,
        scratch_shapes=[
            pltpu.VMEM((frames, width), F32),
            pltpu.VMEM((frames, width), BF16),
            pltpu.VMEM((dim, frames), F32),
            pltpu.VMEM((frames, wide), BF16),
            pltpu.VMEM((frames, wide), BF16),
            pltpu.VMEM((2, 6 * dim, frames), BF16),
            pltpu.VMEM((2, 4 * dim, frames), BF16),
            pltpu.VMEM((2, dim, reach), BF16),
            pltpu.VMEM((2, dim, reach), F32),
            pltpu.VMEM((2, 6 * dim, frames), BF16),
            pltpu.VMEM((3 * width, width), BF16),
            pltpu.VMEM((2, 2 * dim, reach), BF16),
            pltpu.VMEM((2, 2 * reach, 2 * dim), BF16),
            pltpu.VMEM((2, dim + 16, 2 * reach), BF16),
            pltpu.VMEM((2, dim + 16, reach), F32),
            DMA((3, count)),
            DMA((3, count)),
            DMA((4, count)),
            DMA((7,)),
        ],
        compiler_params=pltpu.CompilerParams(
            collective_id=0, has_side_effects=True, vmem_limit_bytes=VMEM_LIMIT
        ),
        name="front",
    )(lengths, tok, gain1, w_in, w_out, gain2, w_qkv, freq)


def repair_kernel(
    items, block, len_ref, flag, near_hbm, far_hbm, ctx_in, o_in, lse_in, ctx_hbm, o_hbm, lse_hbm,
    near, far, ctx, o_ref, lse, qa, ka, va, sems,
):
    @pl.when(jnp.max(flag[...]) > 0.5)
    def _():
        pair = lax.axis_index("sp") // 2
        frames, dim = near.shape[2], near.shape[1] // 6
        reach = 2 * frames
        ends = ends_of(len_ref, items)
        loads = [
            pltpu.make_async_copy(near_hbm, near, sems.at[0]),
            pltpu.make_async_copy(far_hbm, far, sems.at[1]),
        ]
        for copy in loads:
            copy.start()
        for copy in loads:
            copy.wait()
        for slot in range(2):
            first, other = (2 * pair + slot) * frames, (2 * (1 - pair) + slot) * frames
            lay_queries(near, slot, frames, first, ends, items, dim, qa, lse)
            for h in range(2):
                lay_keys(
                    near[slot, (2 + h) * dim : (3 + h) * dim, :], near[slot, (4 + h) * dim : (5 + h) * dim, :],
                    slice(slot * frames, (slot + 1) * frames), first, ends, items, h, ka, va,
                )
                lay_keys(
                    far[slot, h * dim : (h + 1) * dim, :], far[slot, (2 + h) * dim : (3 + h) * dim, :],
                    slice(reach + slot * frames, reach + (slot + 1) * frames), other, ends, items, h, ka, va,
                )

        def step(i, carry):
            h, cols = i // (reach // block), rows_at(lax.rem(i, reach // block), block)
            query = qa[h, :, cols]

            def highest(j, top):
                scores = dg(ka[h, rows_at(j, block), :], query, 1, 0)
                return jnp.maximum(top, jnp.max(scores, axis=0, keepdims=True))

            top = lax.fori_loop(0, 2 * reach // block, highest, jnp.zeros((1, block), F32))

            def add(j, total):
                rows = rows_at(j, block)
                powers = jnp.exp2(dg(ka[h, rows, :], query, 1, 0) - top).astype(BF16)
                return total + dg(va[h, :, rows], powers, 1, 0)

            total = lax.fori_loop(0, 2 * reach // block, add, jnp.zeros((dim + 16, block), F32))
            value = total[0:dim, :] / total[dim : dim + 1, :]
            ctx[h, :, cols] = value.astype(BF16)
            o_ref[h, :, cols] = value
            change = top + jnp.log2(total[dim : dim + 1, :])
            row = lax.broadcasted_iota(I32, (2, block), 0)
            lse[:, cols] = lse[:, cols] + jnp.where(row == h, change, 0.0)
            return carry

        lax.fori_loop(0, 2 * reach // block, step, 0)
        stores = [
            pltpu.make_async_copy(ctx, ctx_hbm, sems.at[2]),
            pltpu.make_async_copy(o_ref, o_hbm, sems.at[3]),
            pltpu.make_async_copy(lse, lse_hbm, sems.at[4]),
        ]
        for copy in stores:
            copy.start()
        for copy in stores:
            copy.wait()


def repair(lengths, flag, near, far, ctx, o, lse):
    dim, reach = ctx.shape[1:]
    anywhere = pl.BlockSpec(memory_space=pl.ANY)
    return pl.pallas_call(
        functools.partial(repair_kernel, lengths.shape[1], min(512, reach)),
        out_shape=[jax.ShapeDtypeStruct(x.shape, x.dtype) for x in (ctx, o, lse)],
        in_specs=[SMEM, VMEM] + [anywhere] * 5,
        out_specs=[anywhere] * 3,
        input_output_aliases={4: 0, 5: 1, 6: 2},
        scratch_shapes=[
            pltpu.VMEM(near.shape, BF16),
            pltpu.VMEM(far.shape, BF16),
            pltpu.VMEM(ctx.shape, BF16),
            pltpu.VMEM(o.shape, F32),
            pltpu.VMEM(lse.shape, F32),
            pltpu.VMEM((2, 2 * dim, reach), BF16),
            pltpu.VMEM((2, 2 * reach, 2 * dim), BF16),
            pltpu.VMEM((2, dim + 16, 2 * reach), BF16),
            DMA((5,)),
        ],
        compiler_params=pltpu.CompilerParams(vmem_limit_bytes=VMEM_LIMIT),
        name="repair",
    )(lengths, flag, near, far, ctx, o, lse)


def axis_steps(axis):
    steps, step = [], 1
    while step < lax.axis_size(axis):
        steps.append((axis, step))
        step *= 2
    assert step == lax.axis_size(axis)
    return steps


def stage_plans():
    sp_steps, dp_steps = axis_steps("sp"), axis_steps("dp")
    plane, rest = sp_steps[1:] + dp_steps[:1], dp_steps[1:]

    def groups(steps):
        return [steps[i : i + 2] for i in range(0, len(steps), 2)]

    plans = (
        groups(plane) + groups(rest),
        groups(rest) + groups(plane),
        [dp_steps[:1]] + groups(rest) + groups(sp_steps[1:]),
    )
    return tuple([sp_steps[:1]] + [stage for stage in plan if stage] for plan in plans)


def stage_masks(stage):
    masks = []
    for number in range(1, 1 << len(stage)):
        mask = {"sp": 0, "dp": 0}
        for i, (axis, step) in enumerate(stage):
            if number & (1 << i):
                mask[axis] += step
        masks.append((mask["sp"], mask["dp"]))
    return masks


def place_in(stage, number):
    place = 0
    for i, (axis, step) in enumerate(stage):
        bit = lax.rem(lax.axis_index(axis) // step, 2)
        place = place + (1 << i) * (1 - bit if number & (1 << i) else bit)
    return place


def exchange_plan(rows, stages, offset=0):
    sizes, size = [], rows
    for stage in stages:
        group = 1 << len(stage)
        splits = size % (16 * group) == 0
        size = size // group if splits else size
        sizes.append((splits, size, offset))
        offset += (group - 1) * size
    return sizes, offset, size


class Reduction:
    def __init__(self, base, rows, staged, stages, acc, stage, land, full, send, recv):
        self.stages, self.acc, self.stage, self.land, self.full = stages, acc, stage, land, full
        self.send, self.recv, self.base = send, recv, base
        self.sizes, _, self.own = exchange_plan(rows, stages, staged)
        self.first_sem = [sum((1 << len(s)) - 1 for s in stages[:k]) for k in range(len(stages))]

    def at(self, low, size):
        return pl.ds(pl.multiple_of(low, 16), size)

    def low(self, k):
        return self.base + sum(
            place_in(self.stages[j], 0) * self.sizes[j][1] for j in range(k) if self.sizes[j][0]
        )

    def slot(self, k, i):
        _, size, offset = self.sizes[k]
        return slice(offset + i * size, offset + (i + 1) * size)

    def copies(self, way, k):
        splits, size, _ = self.sizes[k]
        out = []
        for i, masks in enumerate(stage_masks(self.stages[k])):
            if way == 0:
                source = self.stage.at[self.slot(k, i if splits else 0), :]
                target = self.land.at[self.slot(k, i), :]
            else:
                source = target = self.full.at[self.at(self.low(k + 1), size), :]
            out.append(
                pltpu.make_async_remote_copy(
                    src_ref=source,
                    dst_ref=target,
                    send_sem=self.send.at[way, self.first_sem[k] + i],
                    recv_sem=self.recv.at[way, self.first_sem[k] + i],
                    device_id=peer_at(*masks),
                    device_id_type=MESH,
                )
            )
        return out

    def sum_send(self, k):
        splits, size, _ = self.sizes[k]
        copies = self.copies(0, k)
        for i, copy in enumerate(copies):
            if splits:
                away = self.low(k) + place_in(self.stages[k], i + 1) * size
                self.stage[self.slot(k, i), :] = self.acc[self.at(away, size), :].astype(BF16)
            elif i == 0:
                self.stage[self.slot(k, 0), :] = self.acc[self.at(self.low(k), size), :].astype(BF16)
            copy.start()

    def sum_recv(self, k):
        splits, size, _ = self.sizes[k]
        copies = self.copies(0, k)
        for copy in copies:
            copy.wait()
        values = [self.land[self.slot(k, i), :].astype(F32) for i in range(len(copies))]
        if splits:
            values = [self.acc[self.at(self.low(k + 1), size), :]] + values
        else:
            values = [self.stage[self.slot(k, 0), :].astype(F32)] + values
        while len(values) > 1:
            values = [values[i] + values[i + 1] for i in range(0, len(values), 2)]
        self.acc[self.at(self.low(k + 1), size), :] = values[0]

    def close(self):
        where = self.at(self.low(len(self.stages)), self.own)
        self.full[where, :] = self.acc[where, :].astype(BF16)

    def share_send(self, k):
        if self.sizes[k][0]:
            for copy in self.copies(1, k):
                copy.start()

    def share_recv(self, k):
        if self.sizes[k][0]:
            for copy in self.copies(1, k):
                copy.wait()


def advance(streams, position):
    for stream in streams:
        n = len(stream.stages)
        if 0 < position <= n:
            stream.sum_recv(position - 1)
        if position < n:
            stream.sum_send(position)
        else:
            if position == n:
                stream.close()
            else:
                stream.share_recv(2 * n - position)
            if position < 2 * n:
                stream.share_send(2 * n - 1 - position)


def reduction_scratch(rows_list):
    staged = sum(max(exchange_plan(rows, stages)[1] for stages in stage_plans()) for rows in rows_list)
    sems = max(sum((1 << len(stage)) - 1 for stage in plan) for plan in stage_plans())
    return staged, (len(rows_list), 2, sems)


def make_streams(items, acc, stage, land, full, send, recv):
    streams, staged = [], 0
    for i, (base, rows, order) in enumerate(items):
        stages = stage_plans()[order]
        streams.append(
            Reduction(base, rows, staged, stages, acc, stage, land, full, send.at[i], recv.at[i])
        )
        staged += max(exchange_plan(rows, plan)[1] for plan in stage_plans())
    return streams


def all_masks(sp):
    masks = [(mask, 0) for mask in range(1, sp)]
    for plan in stage_plans():
        for stage in plan:
            masks += [m for m in stage_masks(stage) if m not in masks]
    return masks


def halves_of(ref, rows):
    return jnp.concatenate([ref[0, rows, :], ref[1, rows, :]], axis=1)


def combine(entries):
    count = sum(e[2] for e in entries)
    safe = jnp.maximum(count, 1.0)
    mean = sum(e[2] * e[0] for e in entries) / safe
    spread = sum(e[1] + e[2] * (e[0] - mean) * (e[0] - mean) for e in entries)
    return mean, spread, count


def pick(ref):
    return ref[0:1, :], ref[1:2, :], ref[2:3, :]


def total(entries):
    return tuple(sum(e[i] for e in entries) for i in range(3))


def middle_kernel(
    sp, dp, items, taps, chunk, block, len_ref, parts, x1_hbm, cot_hbm, gain3, gain4, gain5, w_out_hbm,
    w_point1_hbm, depthwise, bn_gain, bn_bias, w_point2_hbm, w_in_hbm, w_down_hbm,
    out_hbm, x2_hbm, heads, mid_hbm, point_two_hbm, bn_grads, partial,
    x1_ref, cot, w_out, w_point1, w_point2, w_in, w_down, out_ref, grad_x2, mid, point_two, two, load_sems, out_sems,
    stage, land, sum_send, sum_recv,
    ctx, x2_ref, n3_keep, point, glu, conv, low_lim, high_lim, act, hidden, n4_keep, branch, swish, branch2,
    grad_x3, grad_y, grad_conv, grad_glu, grad_point, branch3, back_parts, tap_sums, edge_out, edge_in,
    send_box, near_box, far_box, sums,
    send, recv, local, back_send, back_recv, back_local, rim_send, rim_recv, box_send, box_recv,
):
    me, me_dp = lax.axis_index("sp"), lax.axis_index("dp")
    frames, width = x1_ref.shape
    lanes = width // 2
    reach = taps // 2
    count = frames // chunk
    peers = sp_peers(sp)
    far_peers = [peer_at(0, mask) for mask in range(1, dp)]
    masks = all_masks(sp)
    masks += [(0, mask) for mask in range(1, dp) if (0, mask) not in masks]
    greeted = [peer_at(*mask) for mask in masks]
    core = lax.rem(me, 2)
    sibling = peer_at(1, 0)
    length = sp * frames
    ends = ends_of(len_ref, items)
    first_frame = me * frames

    def limits(b, carry):
        rows = rows_at(b, chunk)
        frame = first_frame + b * chunk + lax.broadcasted_iota(I32, (chunk, lanes), 0)
        low, high = jnp.zeros_like(frame), jnp.full_like(frame, length)
        for end in ends:
            low = jnp.where(frame >= end, end, low)
        for end in reversed(ends):
            high = jnp.where(frame < end, end, high)
        low_lim[rows, :] = low - frame
        high_lim[rows, :] = high - 1 - frame
        return carry

    for ref in (glu, grad_conv):
        for h in range(2):
            ref[h, 0:reach, :] = jnp.zeros((reach, lanes), F32)
            ref[h, reach + frames :, :] = jnp.zeros((reach, lanes), F32)
    edge_in[...] = jnp.zeros_like(edge_in)
    send_box[...] = jnp.zeros_like(send_box)
    greet(greeted)
    loads = start_copies(
        [
            (w_out_hbm, w_out), (x1_hbm, x1_ref), (w_point1_hbm, w_point1), (w_point2_hbm, w_point2),
            (w_in_hbm, w_in), (w_down_hbm, w_down), (cot_hbm, cot),
        ],
        load_sems,
    )
    lax.fori_loop(0, count, limits, 0)
    tap_sums[...] = jnp.zeros_like(tap_sums)
    sums[...] = jnp.zeros_like(sums)
    await_greetings(greeted)

    def moves(c, source, target, send_sems, recv_sems, local_sems):
        return [
            pltpu.make_async_remote_copy(
                src_ref=source(1 - core, c), dst_ref=target(core, c),
                send_sem=send_sems.at[c], recv_sem=recv_sems.at[c],
                device_id=sibling, device_id_type=MESH,
            ),
            pltpu.make_async_copy(source(core, c), target(core, c), local_sems.at[c]),
        ]

    def by_frames(ref):
        return lambda slot, c: ref.at[:, :, frame_cols(slot, frames, c, chunk)]

    def by_head(ref):
        return lambda slot, c: ref.at[slot, :, :, rows_at(c, chunk)]

    def context_moves(c):
        return moves(c, by_frames(parts), by_head(ctx), send, recv, local)

    def begin(c, carry):
        for copy in context_moves(c):
            copy.start()
        return carry

    lax.fori_loop(0, count, begin, 0)
    wait_all(loads[:3])

    def open_step(c, carry):
        rows = rows_at(c, chunk)
        for copy in context_moves(c):
            copy.wait()
        context = ctx[:, :, :, rows].reshape(width, chunk)
        x2 = x1_ref[rows, :] + dg(context, w_out[...], 0, 0)
        x2_ref[rows, :] = x2
        hat, _ = norm_parts(x2)
        n3 = (hat * row_of(gain3)).astype(BF16)
        n3_keep[rows, :] = n3
        pair = dg(n3, w_point1[...], 1, 0)
        point[rows, :] = pair
        gated = (pair[:, :width] * sigmoid(pair[:, width:])).astype(BF16).astype(F32)
        where = pl.ds(pl.multiple_of(reach + c * chunk, 8), chunk)
        glu[0, where, :] = gated[:, :lanes]
        glu[1, where, :] = gated[:, lanes:]
        return carry

    lax.fori_loop(0, count, open_step, 0)

    def rim_copies(call, side, source, target):
        peer = (me_dp, me - 1 if side == 0 else me + 1)
        return pltpu.make_async_remote_copy(
            src_ref=source, dst_ref=target, send_sem=rim_send.at[call, side], recv_sem=rim_recv.at[call, side],
            device_id=peer, device_id_type=MESH,
        )

    def swap_rims(call, sources, targets):
        @pl.when(me > 0)
        def _():
            rim_copies(call, 0, sources[0], targets[1]).start()

        @pl.when(me < sp - 1)
        def _():
            rim_copies(call, 1, sources[1], targets[0]).start()

    def await_rims(call, sources, targets):
        @pl.when(me > 0)
        def _():
            rim_copies(call, 0, sources[0], targets[1]).wait_send()
            rim_copies(call, 1, sources[1], targets[0]).wait_recv()

        @pl.when(me < sp - 1)
        def _():
            rim_copies(call, 1, sources[1], targets[0]).wait_send()
            rim_copies(call, 0, sources[0], targets[1]).wait_recv()

    for side, rows in ((0, slice(reach, 2 * reach)), (1, slice(frames, frames + reach))):
        for h in range(2):
            edge_out[side, 0:reach, h * lanes : (h + 1) * lanes] = glu[h, rows, :]
    glu_rims = (
        [edge_out.at[0, 0:reach, :], edge_out.at[1, 0:reach, :]],
        [edge_in.at[0, 0:reach, :], edge_in.at[1, 0:reach, :]],
    )
    swap_rims(0, *glu_rims)

    zero = jnp.zeros((block, lanes), F32)

    def conv_step(b, carry):
        low, high = low_lim[rows_at(b, block), :], high_lim[rows_at(b, block), :]
        start = pl.multiple_of(b * block, block)
        result = [zero, zero]
        for tap in range(taps):
            shift = tap - reach
            inside = (low <= shift) if shift < 0 else (high >= shift)
            for h in range(2):
                view = glu.at[h, pl.ds(start, block + 2 * reach), :]
                term = jnp.where(inside, view[tap : tap + block, :], 0.0)
                result[h] = result[h] + depthwise[tap : tap + 1, h * lanes : (h + 1) * lanes].astype(F32) * term
        valid = (first_frame + start + lax.broadcasted_iota(I32, (block, lanes), 0)) < ends[-1]
        for h in range(2):
            conv[h, rows_at(b, block), :] = result[h]
            sums[0:1, h * lanes : (h + 1) * lanes] += jnp.sum(jnp.where(valid, result[h], 0.0), axis=0, keepdims=True)
        return carry

    blocks = frames // block
    lax.fori_loop(1, blocks - 1, conv_step, 0)
    await_rims(0, *glu_rims)
    for h in range(2):
        glu[h, 0:reach, :] = edge_in[0, 0:reach, h * lanes : (h + 1) * lanes]
        glu[h, reach + frames :, :] = edge_in[1, 0:reach, h * lanes : (h + 1) * lanes]
    conv_step(0, 0)
    conv_step(blocks - 1, 0)

    own_count = jnp.clip(ends[-1] - first_frame, 0, frames).astype(F32)
    own_mean = sums[0:1, :] / jnp.maximum(own_count, 1.0)
    sums[0:1, :] = jnp.zeros((1, width), F32)

    def spread_step(c, carry):
        rows = rows_at(c, chunk)
        valid = (first_frame + c * chunk + lax.broadcasted_iota(I32, (chunk, width), 0)) < ends[-1]
        apart = jnp.where(valid, halves_of(conv, rows) - own_mean, 0.0)
        sums[1:2, :] += jnp.sum(apart * apart, axis=0, keepdims=True)
        return carry

    lax.fori_loop(0, count, spread_step, 0)

    def box_copies(call, stage):
        group = peers if stage == 0 else far_peers
        target = near_box if stage == 0 else far_box
        base = 0 if stage == 0 else sp - 1
        return [
            pltpu.make_async_remote_copy(
                src_ref=send_box.at[call, stage],
                dst_ref=target.at[call, i],
                send_sem=box_send.at[call, base + i],
                recv_sem=box_recv.at[call, base + i],
                device_id=peer,
                device_id_type=MESH,
            )
            for i, peer in enumerate(group)
        ]

    def box_begin(call, stage, rows):
        for i, row in enumerate(rows):
            send_box[call, stage, i : i + 1, :] = row
        for copy in box_copies(call, stage):
            copy.start()

    def box_end(call, stage, rows, merge):
        target = near_box if stage == 0 else far_box
        copies = box_copies(call, stage)
        for copy in copies:
            copy.wait()
        return merge([rows] + [pick(target[call, i]) for i in range(len(copies))])

    stats = (own_mean, sums[1:2, :], jnp.full((1, width), 1.0, F32) * own_count)
    sums[1:2, :] = jnp.zeros((1, width), F32)
    box_begin(0, 0, stats)
    stats = box_end(0, 0, stats, combine)
    box_begin(0, 1, stats)
    mean, spread, frame_count = box_end(0, 1, stats, combine)
    inv_std = lax.rsqrt(spread / frame_count + EPS)
    norm_gain, norm_bias = row_of(bn_gain), row_of(bn_bias)

    def heart_step(c, carry):
        rows = rows_at(c, chunk)
        normed = (halves_of(conv, rows) - mean) * inv_std
        y = normed * norm_gain + norm_bias
        sig_y = sigmoid(y)
        w = (y * sig_y).astype(BF16)
        swish[rows, :] = w
        x3 = x2_ref[rows, :] + dg(w, w_point2[...], 1, 0)
        hat4, inv4 = norm_parts(x3)
        g4 = row_of(gain4)
        n4 = (hat4 * g4).astype(BF16)
        n4_keep[rows, :] = n4
        a = dg(n4, w_in[...], 1, 0)
        sig = sigmoid(a)
        s = (a * sig).astype(BF16)
        act[rows, :] = s
        x4 = x3 + 0.5 * dg(s, w_down[...], 1, 0)
        hat5, inv5 = norm_parts(x4)
        g5 = row_of(gain5)
        out_ref[rows, :] = (hat5 * g5).astype(BF16)
        top = cot[rows, :].astype(F32)
        mid[3 * width + 4 : 3 * width + 5, :] += jnp.sum(top * hat5, axis=0, keepdims=True)
        grad_x4 = norm_back(top, hat5, inv5, g5)
        low_grad = (0.5 * grad_x4).astype(BF16)
        branch[rows, :] = low_grad
        grad = dg(low_grad, w_down[...], 1, 1)
        low_hidden = (grad * (sig * (1.0 + a * (1.0 - sig)))).astype(BF16)
        hidden[rows, :] = low_hidden
        grad = dg(low_hidden, w_in[...], 1, 1)
        mid[3 * width + 3 : 3 * width + 4, :] += jnp.sum(grad * hat4, axis=0, keepdims=True)
        grad3 = grad_x4 + norm_back(grad, hat4, inv4, g4)
        grad_x3[rows, :] = grad3
        low_grad = grad3.astype(BF16)
        branch2[rows, :] = low_grad
        grad = dg(low_grad, w_point2[...], 1, 1) * (sig_y * (1.0 + y * (1.0 - sig_y)))
        grad_y[0, rows, :] = grad[:, :lanes]
        grad_y[1, rows, :] = grad[:, lanes:]
        sums[2:3, :] += jnp.sum(grad, axis=0, keepdims=True)
        sums[3:4, :] += jnp.sum(grad * normed, axis=0, keepdims=True)
        return carry

    mid[3 * width :, :] = jnp.zeros((width, width), F32)
    wait_all(loads[3:])
    lax.fori_loop(0, count, heart_step, 0)
    leaving = start_copies([(out_ref, out_hbm)], out_sems)

    pair = (sums[2:3, :], sums[3:4, :], jnp.zeros((1, width), F32))
    box_begin(1, 0, pair)
    for side, rows in ((0, slice(0, reach)), (1, slice(frames - reach, frames))):
        for h in range(2):
            cols = slice(h * lanes, (h + 1) * lanes)
            edge_out[side, reach : 2 * reach, cols] = grad_y[h, rows, :]
            edge_out[side, 2 * reach : 3 * reach, cols] = conv[h, rows, :]
    grad_rims = (
        [edge_out.at[0, reach : 3 * reach, :], edge_out.at[1, reach : 3 * reach, :]],
        [edge_in.at[0, reach : 3 * reach, :], edge_in.at[1, reach : 3 * reach, :]],
    )
    swap_rims(1, *grad_rims)
    wide = w_in.shape[1]
    streams = make_streams([(0, wide, 2), (wide, wide, 2)], two, stage, land, None, sum_send, sum_recv)
    early_stages = len(stage_plans()[2]) - 1
    for j in range(0, wide, width):
        two[j : j + width, :] = dg(act[:, j : j + width], branch[...], 0, 0)
    advance(streams[:1], 0)
    pair = box_end(1, 0, pair, total)
    box_begin(1, 1, pair)
    for j in range(0, wide, width):
        two[wide + j : wide + j + width, :] = dg(n4_keep[...], hidden[:, j : j + width], 0, 0)
    advance(streams[1:], 0)
    advance(streams[:1], 1)
    point_two[...] = dg(swish[...], branch2[...], 0, 0)
    leaving += start_copies([(point_two, point_two_hbm)], out_sems.at[pl.ds(1, 1)])
    advance(streams[1:], 1)
    await_rims(1, *grad_rims)
    bias_sum, gain_sum, _ = box_end(1, 1, pair, total)
    bn_grads[0:1, :] = gain_sum
    bn_grads[1:2, :] = bias_sum
    bn_grads[2:8, :] = jnp.zeros((6, width), F32)

    scale = norm_gain * inv_std
    slope = -inv_std * inv_std * norm_gain * gain_sum / frame_count
    shift_all = -inv_std * norm_gain * bias_sum / frame_count

    def conv_grad(grad, value, frame, h):
        cols = slice(h * lanes, (h + 1) * lanes)
        extra = (value - mean[:, cols]) * slope[:, cols] + shift_all[:, cols]
        return grad * scale[:, cols] + jnp.where(frame < ends[-1], extra, 0.0)

    def grad_conv_step(c, carry):
        rows = rows_at(c, chunk)
        frame = first_frame + c * chunk + lax.broadcasted_iota(I32, (chunk, lanes), 0)
        where = pl.ds(pl.multiple_of(reach + c * chunk, 8), chunk)
        for h in range(2):
            grad_conv[h, where, :] = conv_grad(grad_y[h, rows, :], conv[h, rows, :], frame, h)
        return carry

    lax.fori_loop(0, count, grad_conv_step, 0)
    for side, rows, begin_frame in (
        (0, slice(0, reach), first_frame - reach),
        (1, slice(reach + frames, 2 * reach + frames), first_frame + frames),
    ):
        frame = begin_frame + lax.broadcasted_iota(I32, (reach, lanes), 0)
        for h in range(2):
            cols = slice(h * lanes, (h + 1) * lanes)
            grad_conv[h, rows, :] = conv_grad(
                edge_in[side, reach : 2 * reach, cols], edge_in[side, 2 * reach : 3 * reach, cols], frame, h
            )

    def conv_back_step(b, carry):
        low, high = low_lim[rows_at(b, block), :], high_lim[rows_at(b, block), :]
        start = pl.multiple_of(b * block, block)
        result = [zero, zero]
        here = [glu[h, pl.ds(pl.multiple_of(reach + start, 8), block), :] for h in range(2)]
        for tap in range(taps):
            shift = reach - tap
            inside = (low <= shift) if shift < 0 else (high >= shift)
            at = reach + shift
            for h in range(2):
                view = grad_conv.at[h, pl.ds(start, block + 2 * reach), :]
                term = jnp.where(inside, view[at : at + block, :], 0.0)
                result[h] = result[h] + depthwise[tap : tap + 1, h * lanes : (h + 1) * lanes].astype(F32) * term
                tap_sums[tap, h] += jnp.sum((here[h] * term).reshape(block // 8, 8, lanes), axis=0)
        for h in range(2):
            grad_glu[h, rows_at(b, block), :] = result[h]
        return carry

    lax.fori_loop(0, blocks // 2, conv_back_step, 0)
    advance(streams, 2)
    lax.fori_loop(blocks // 2, blocks, conv_back_step, 0)

    def back_moves(c):
        return moves(c, by_head(back_parts), by_frames(heads), back_send, back_recv, back_local)

    def close_step(c, carry):
        rows = rows_at(c, chunk)
        grad = halves_of(grad_glu, rows)
        value, gate = point[rows, :width], sigmoid(point[rows, width:])
        low_grad = jnp.concatenate([grad * gate, grad * value * gate * (1.0 - gate)], axis=1).astype(BF16)
        grad_point[rows, :] = low_grad
        grad = dg(low_grad, w_point1[...], 1, 1)
        hat, inv = norm_parts(x2_ref[rows, :])
        mid[3 * width + 2 : 3 * width + 3, :] += jnp.sum(grad * hat, axis=0, keepdims=True)
        grad2 = grad_x3[rows, :] + norm_back(grad, hat, inv, row_of(gain3))
        grad_x2[rows, :] = grad2
        low_grad = grad2.astype(BF16)
        branch3[rows, :] = low_grad
        back_parts[:, :, :, rows] = dg(w_out[...], low_grad, 1, 1).astype(BF16).reshape(2, 2, width // 4, chunk)
        for copy in back_moves(c):
            copy.start()
        return carry

    lax.fori_loop(0, count, close_step, 0)
    leaving += start_copies([(grad_x2, x2_hbm)], out_sems.at[pl.ds(3, 1)])
    for j in range(2):
        mid[j * width : (j + 1) * width, :] = dg(n3_keep[...], grad_point[:, j * width : (j + 1) * width], 0, 0)
    mid[2 * width : 3 * width, :] = dg(ctx[...].reshape(width, frames), branch3[...], 1, 0)
    for tap in range(taps):
        row = 3 * width + 8 + tap
        for h in range(2):
            mid[row : row + 1, h * lanes : (h + 1) * lanes] = jnp.sum(tap_sums[tap, h], axis=0, keepdims=True)

    leaving += start_copies([(mid, mid_hbm)], out_sems.at[pl.ds(4, 1)])

    def finish(c, carry):
        for copy in back_moves(c):
            copy.wait()
        return carry

    lax.fori_loop(0, count, finish, 0)
    for position in range(3, early_stages):
        advance(streams, position)
    size = streams[0].sizes[early_stages - 1][1]
    for i, stream in enumerate(streams):
        stream.sum_recv(early_stages - 1)
        partial[i * size : (i + 1) * size, :] = two[stream.at(stream.low(early_stages), size), :]
    wait_all(leaving)


def middle(
    lengths, parts, x1, cot, gain3, gain4, gain5, w_out, w_point1, depthwise, bn_gain, bn_bias, w_point2,
    w_in, w_down, dp,
):
    frames, width = x1.shape
    sp = lax.axis_size("sp")
    assert sp == HEADS == 4
    anywhere = pl.BlockSpec(memory_space=pl.ANY)
    paired = pltpu.VMEM((2, 2, width // 4, frames), BF16)
    wide = w_in.shape[1]
    staged, sems = reduction_scratch([wide, wide])
    stages = stage_plans()[2]
    part = exchange_plan(wide, stages[:-1])[2]
    taps = depthwise.shape[0]
    reach = taps // 2
    chunk = min(256, frames)
    count = frames // chunk
    lanes = width // 2
    keep, low_keep = pltpu.VMEM((frames, width), F32), pltpu.VMEM((frames, width), BF16)
    split = pltpu.VMEM((2, frames, lanes), F32)
    rimmed = pltpu.VMEM((2, frames + 2 * reach, lanes), F32)
    rims = pltpu.VMEM((2, 3 * reach, width), F32)
    moves = [DMA((count,)), DMA((count,)), DMA((count,))]
    return pl.pallas_call(
        functools.partial(middle_kernel, sp, dp, lengths.shape[1], taps, chunk, 64),
        out_shape=[
            jax.ShapeDtypeStruct((frames, width), BF16),
            jax.ShapeDtypeStruct((frames, width), F32),
            jax.ShapeDtypeStruct(parts.shape, BF16),
            jax.ShapeDtypeStruct((4 * width, width), F32),
            jax.ShapeDtypeStruct((width, width), F32),
            jax.ShapeDtypeStruct((8, width), F32),
            jax.ShapeDtypeStruct((2 * part, width), F32),
        ],
        in_specs=[
            SMEM, anywhere, anywhere, anywhere, VMEM, VMEM, VMEM, anywhere, anywhere, VMEM, VMEM, VMEM, anywhere,
            anywhere, anywhere,
        ],
        out_specs=[anywhere, anywhere, VMEM, anywhere, anywhere, VMEM, VMEM],
        scratch_shapes=[
            keep,
            low_keep,
            pltpu.VMEM(w_out.shape, BF16),
            pltpu.VMEM(w_point1.shape, BF16),
            pltpu.VMEM(w_point2.shape, BF16),
            pltpu.VMEM(w_in.shape, BF16),
            pltpu.VMEM(w_down.shape, BF16),
            low_keep,
            keep,
            pltpu.VMEM((4 * width, width), F32),
            pltpu.VMEM((width, width), F32),
            pltpu.VMEM((2 * wide, width), F32),
            DMA((7,)),
            DMA((5,)),
            pltpu.VMEM((staged, width), BF16),
            pltpu.VMEM((staged, width), BF16),
            DMA(sems),
            DMA(sems),
            paired,
            keep,
            low_keep,
            pltpu.VMEM((frames, 2 * width), F32),
            rimmed,
            split,
            pltpu.VMEM((frames, lanes), I32),
            pltpu.VMEM((frames, lanes), I32),
            pltpu.VMEM((frames, wide), BF16),
            pltpu.VMEM((frames, wide), BF16),
            low_keep,
            low_keep,
            low_keep,
            low_keep,
            keep,
            split,
            rimmed,
            split,
            pltpu.VMEM((frames, 2 * width), BF16),
            low_keep,
            paired,
            pltpu.VMEM((taps, 2, 8, lanes), F32),
            rims,
            rims,
            pltpu.VMEM((2, 2, 8, width), F32),
            pltpu.VMEM((2, sp - 1, 8, width), F32),
            pltpu.VMEM((2, dp - 1, 8, width), F32),
            pltpu.VMEM((8, width), F32),
        ]
        + moves
        + moves
        + [DMA((2, 2)), DMA((2, 2)), DMA((2, sp + dp - 2)), DMA((2, sp + dp - 2))],
        compiler_params=pltpu.CompilerParams(
            collective_id=1, has_side_effects=True, vmem_limit_bytes=VMEM_LIMIT
        ),
        name="middle",
    )(
        lengths, parts, x1, cot, gain3, gain4, gain5, w_out, w_point1, depthwise, bn_gain, bn_bias, w_point2,
        w_in, w_down,
    )


def back_kernel(
    sp, items, chunk, block, sub, len_ref, lse_ref, gain1, gain2, partial,
    near_hbm, far_hbm, o_hbm, do_hbm, trig_hbm, mid_hbm, point_two_hbm, tok_hbm, x1_hbm, n2_hbm, x2_hbm, act_hbm, slope_hbm, w_in_hbm, w_out_hbm, w_qkv_hbm,
    grad_ref, full,
    near, far, o_ref, do_ref, trig, tok, x1_ref, n2_ref, grad_x2, act, slope, w_in, w_out, w_qkv,
    qa, qt, ka, da, va, dq, turned, far_out, near_out, dq_out, far_kv, near_kv, near_dq,
    joined, branch, hidden, grad_x1, gains, acc, stage, land,
    load_sems, far_send, far_recv, near_send, near_recv, sum_send, sum_recv,
):
    me, dp = lax.axis_index("sp"), lax.axis_index("dp")
    core, pair = lax.rem(me, 2), me // 2
    sibling = peer_at(1, 0)
    frames, width = tok.shape
    wide = w_in.shape[1]
    half = trig.shape[0] // 2
    dim = 2 * half
    count = frames // chunk
    reach = 2 * frames
    greeted = [peer_at(*mask) for mask in all_masks(sp)]
    greet(greeted)
    unit = 4 * width
    last = 6 * unit
    loads = start_copies(
        [
            (near_hbm, near), (do_hbm, do_ref), (o_hbm, o_ref), (far_hbm, far),
            (mid_hbm, acc.at[2 * unit : 3 * unit, :]),
            (point_two_hbm, acc.at[3 * unit + 3 * width : 4 * unit, :]), (trig_hbm, trig),
            (x1_hbm, x1_ref), (x2_hbm, grad_x2), (w_qkv_hbm, w_qkv), (n2_hbm, n2_ref), (act_hbm, act),
            (w_out_hbm, w_out), (slope_hbm, slope), (w_in_hbm, w_in), (tok_hbm, tok),
        ],
        load_sems,
    )
    streams = make_streams(
        [
            (0, unit, 2), (unit, unit, 2), (2 * unit, unit, 2),
            (3 * unit, unit, 1), (4 * unit, unit, 0), (5 * unit, unit, 0), (last, 16, 0),
        ],
        acc, stage, land, full, sum_send, sum_recv,
    )
    early, (qkv, down, up, rest) = streams[:3], ([stream] for stream in streams[3:])
    steps = len(stage_plans()[0])
    acc[last : last + 16, :] = jnp.zeros((16, width), F32)
    gains[...] = jnp.zeros_like(gains)
    for h in range(2):
        dq[h] = jnp.zeros((dim, reach), F32)
    wait_all(loads[:4])
    ends = ends_of(len_ref, items)
    wide_pad = jnp.zeros((dim - 16, frames), BF16)
    for slot in range(2):
        cols = slice(slot * frames, (slot + 1) * frames)
        far_cols = slice(reach + slot * frames, reach + (slot + 1) * frames)
        segment = segment_row((2 * pair + slot) * frames, frames, ends)
        far_segment = segment_row((2 * (1 - pair) + slot) * frames, frames, ends)
        for h in range(2):
            query = near[slot, h * dim : (h + 1) * dim, :]
            qt[h, :, cols] = query
            qa[h, cols, :] = query_rows(query, segment, items, -lse_ref[h : h + 1, cols]).T
            grad = do_ref[h, :, cols]
            row_dot = jnp.sum(grad.astype(F32) * o_ref[h, :, cols], axis=0, keepdims=True)
            da[h, cols, :] = jnp.concatenate([grad, split_rows(-row_dot), wide_pad], axis=0).T
            ka[h, :, cols] = key_rows(near[slot, (2 + h) * dim : (3 + h) * dim, :], segment, items)
            ka[h, :, far_cols] = key_rows(far[slot, h * dim : (h + 1) * dim, :], far_segment, items)
            for where, value in (
                (cols, near[slot, (4 + h) * dim : (5 + h) * dim, :]),
                (far_cols, far[slot, (2 + h) * dim : (3 + h) * dim, :]),
            ):
                va[h, 0:dim, where] = value
                va[h, dim : dim + 16, where] = first_rows(3, frames)
                va[h, dim + 16 :, where] = wide_pad
    wait_all(loads[4:5])

    def attend_block(h, at):
        dk, dv = [], []

        def score(u):
            cols = pl.ds(pl.multiple_of(at + u * sub, sub), sub)
            return dg(qa[h], ka[h, :, cols], 1, 0), dg(da[h], va[h, :, cols], 1, 0)

        ready = score(0)
        for u in range(block // sub):
            scores, grad_probs = ready
            if u + 1 < block // sub:
                ready = score(u + 1)
            probs = jnp.exp2(scores)
            grad = (probs * grad_probs).astype(BF16)
            dv.append(dg(do_ref[h], probs.astype(BF16), 1, 0).astype(BF16))
            dk.append((dg(qt[h], grad, 1, 0) * LN2).astype(BF16))
            turned[u * sub : (u + 1) * sub, :] = grad.T
        dq[h] += dg(ka[h, 0:dim, pl.ds(pl.multiple_of(at, block), block)], turned[...], 1, 0)
        return jnp.concatenate(dk, axis=1), jnp.concatenate(dv, axis=1)

    per = frames // block

    def keep(ref, slot, h, cols, block_grads):
        for i, value in enumerate(block_grads):
            ref[slot, 2 * i + h, :, cols] = value

    def far_copy(b):
        cols = rows_at(lax.rem(b, per), block)
        return pltpu.make_async_remote_copy(
            src_ref=far_out.at[b // per, :, :, cols], dst_ref=far_kv.at[core, :, :, cols],
            send_sem=far_send.at[b], recv_sem=far_recv.at[core, lax.rem(b, per)],
            device_id=(dp, 2 * (1 - pair) + b // per), device_id_type=MESH,
        )

    done = len(early[0].stages) - 1
    size = early[0].sizes[done - 1][1]
    for i, stream in enumerate(early[:2]):
        acc[stream.at(stream.low(done), size), :] = partial[i * size : (i + 1) * size, :]
    schedule, remaining = {}, []
    for stream, times, first in zip(early, (PARTIAL_TIMES, PARTIAL_TIMES, FRESH_TIMES), (done, done, 0)):
        positions = range(first, 2 * len(stream.stages) + 1)
        for position, time in zip(positions, times):
            schedule.setdefault(time, []).append((stream, position, position == first))
        remaining.append([(stream, position) for position in positions[len(times) :]])

    def early_steps(t):
        for time, moves in schedule.items():
            @pl.when(t == min(time, 8 * per - 1))
            def _():
                for stream, position, opening in moves:
                    if opening:
                        stream.sum_send(position)
                    else:
                        advance([stream], position)

    def late_steps():
        for moves in remaining:
            if moves:
                stream, position = moves.pop(0)
                advance([stream], position)

    def far_step(t, carry):
        b, h = t // 2, lax.rem(t, 2)
        cols = rows_at(lax.rem(b, per), block)
        keep(far_out, b // per, h, cols, attend_block(h, reach + b * block))

        @pl.when(t == 0)
        def _():
            await_greetings(greeted)

        @pl.when(h == 1)
        def _():
            far_copy(b).start()

        early_steps(t)
        return carry

    lax.fori_loop(0, 4 * per, far_step, 0)

    def near_copy(b):
        cols = rows_at(b, block)
        return pltpu.make_async_remote_copy(
            src_ref=near_out.at[:, :, cols], dst_ref=near_kv.at[core, :, :, cols],
            send_sem=near_send.at[b], recv_sem=near_recv.at[b], device_id=sibling, device_id_type=MESH,
        )

    def sibling_step(t, carry):
        b, h = t // 2, lax.rem(t, 2)
        block_grads = attend_block(h, (1 - core) * frames + b * block)
        for i, value in enumerate(block_grads):
            near_out[2 * i + h, :, rows_at(b, block)] = value

        @pl.when(h == 1)
        def _():
            near_copy(b).start()

        early_steps(t + 4 * per)
        return carry

    lax.fori_loop(0, 2 * per, sibling_step, 0)

    def own_step(t, carry):
        b, h = t // 2, lax.rem(t, 2)
        keep(near_kv, core, h, rows_at(b, block), attend_block(h, core * frames + b * block))

        early_steps(t + 6 * per)
        return carry

    lax.fori_loop(0, 2 * per, own_step, 0)
    for h in range(2):
        dq_out[h] = (dq[h, :, pl.ds(pl.multiple_of((1 - core) * frames, frames), frames)] * dim**-0.5).astype(BF16)
    dq_copy = pltpu.make_async_remote_copy(
        src_ref=dq_out, dst_ref=near_dq.at[core], send_sem=near_send.at[per], recv_sem=near_recv.at[per],
        device_id=sibling, device_id_type=MESH,
    )
    dq_copy.start()
    for h in range(2):
        near_dq[core, h] = (dq[h, :, pl.ds(pl.multiple_of(core * frames, frames), frames)] * dim**-0.5).astype(BF16)
    wait_all(loads[5:])
    for b in range(2 * per):
        far_copy(b).wait_send()
    for source in range(2):
        for b in range(per):
            pltpu.make_async_remote_copy(
                src_ref=far_out.at[0, :, :, rows_at(b, block)], dst_ref=far_kv.at[source, :, :, rows_at(b, block)],
                send_sem=far_send.at[b], recv_sem=far_recv.at[source, b], device_id=sibling, device_id_type=MESH,
            ).wait_recv()
    for b in range(per):
        near_copy(b).wait()

    def turn_back(first, second, rows, low):
        sine, cosine = trig[0:half, rows], trig[half:, rows]
        joined[low : low + half, rows] = (first * cosine + second * sine).astype(BF16)
        joined[low + half : low + dim, rows] = (second * cosine - first * sine).astype(BF16)

    def keys_step(c, carry):
        rows = rows_at(c, chunk)
        for p in range(2):
            for h in range(2):
                head = 2 * p + h

                def both(i, low, high):
                    return near_kv[p, i, low:high, rows].astype(F32) + far_kv[p, i, low:high, rows].astype(F32)

                turn_back(both(h, 0, half), both(h, half, dim), rows, width + head * dim)
                low = 2 * width + head * dim
                joined[low : low + dim, rows] = both(2 + h, 0, dim).astype(BF16)
        return carry

    lax.fori_loop(0, count, keys_step, 0)
    dq_copy.wait()

    def arrive(c, carry):
        rows = rows_at(c, chunk)
        for p in range(2):
            for h in range(2):
                turn_back(
                    near_dq[p, h, 0:half, rows].astype(F32), near_dq[p, h, half:dim, rows].astype(F32), rows,
                    (2 * p + h) * dim,
                )
        grad = dg(joined[:, rows], w_qkv[...], 0, 1)
        hat, inv = norm_parts(x1_ref[rows, :])
        gains[1:2, :] += jnp.sum(grad * hat, axis=0, keepdims=True)
        grad = grad_x2[rows, :] + norm_back(grad, hat, inv, row_of(gain2))
        grad_x1[rows, :] = grad
        branch[rows, :] = (0.5 * grad).astype(BF16)
        return carry

    lax.fori_loop(0, count, arrive, 0)
    for j in range(0, wide, width):
        acc[4 * unit + j : 4 * unit + j + width, :] = dg(act[:, j : j + width], branch[...], 0, 0)
    advance(down, 0)
    acc[3 * unit : 3 * unit + 3 * width, :] = dg(joined[...], n2_ref[...], 1, 0)
    advance(qkv, 0)

    def through(c, carry):
        rows = rows_at(c, chunk)
        grad = dg(branch[rows, :], w_out[...], 1, 1)
        hidden[rows, :] = (grad * slope[rows, :].astype(F32)).astype(BF16)
        hat, _ = norm_parts(tok[rows, :].astype(F32))
        n2_ref[rows, :] = (hat * row_of(gain1)).astype(BF16)
        return carry

    lax.fori_loop(0, count, through, 0)
    advance(down + qkv, 1)
    for j in range(0, wide, width):
        acc[5 * unit + j : 5 * unit + j + width, :] = dg(n2_ref[...], hidden[:, j : j + width], 0, 0)
    advance(up, 0)

    def last_step(c, carry):
        rows = rows_at(c, chunk)
        grad = dg(hidden[rows, :], w_in[...], 1, 1)
        hat, inv = norm_parts(tok[rows, :].astype(F32))
        gains[0:1, :] += jnp.sum(grad * hat, axis=0, keepdims=True)
        grad_ref[rows, :] = (grad_x1[rows, :] + norm_back(grad, hat, inv, row_of(gain1))).astype(BF16)
        return carry

    lax.fori_loop(0, count // 2, last_step, 0)
    advance(up, 1)
    lax.fori_loop(count // 2, count, last_step, 0)
    acc[last : last + 8, :] = gains[...]
    advance(rest, 0)
    for position in range(2, 2 * steps + 1):
        advance(down + qkv + up, position)
        advance(rest, position - 1)
        late_steps()
    advance(rest, 2 * steps)
    while any(remaining):
        late_steps()


def back(
    lengths, near, far, o, lse, do, trig, gain1, gain2, partial, mid, point_two,
    tok, x1, n2, grad_x2, act, slope, w_in, w_out, w_qkv,
):
    frames, width = tok.shape
    sp = lax.axis_size("sp")
    chunk = min(256, frames)
    block = min(512, frames)
    count, per = frames // chunk, frames // block
    wide = w_in.shape[1]
    dim = width // HEADS
    reach = 2 * frames
    rows = 24 * width + 16
    staged, sems = reduction_scratch([4 * width] * 6 + [16])
    low_keep, keep = pltpu.VMEM((frames, width), BF16), pltpu.VMEM((frames, width), F32)
    return pl.pallas_call(
        functools.partial(back_kernel, sp, lengths.shape[1], chunk, block, min(128, block)),
        out_shape=[
            jax.ShapeDtypeStruct((frames, width), BF16),
            jax.ShapeDtypeStruct((rows, width), BF16),
        ],
        in_specs=[SMEM] + [VMEM] * 4 + [pl.BlockSpec(memory_space=pl.ANY)] * 16,
        out_specs=[VMEM] * 2,
        scratch_shapes=[
            pltpu.VMEM(near.shape, BF16),
            pltpu.VMEM(far.shape, BF16),
            pltpu.VMEM(o.shape, F32),
            pltpu.VMEM(do.shape, BF16),
            pltpu.VMEM(trig.shape, F32),
            low_keep,
            keep,
            low_keep,
            keep,
            pltpu.VMEM((frames, wide), BF16),
            pltpu.VMEM((frames, wide), BF16),
            pltpu.VMEM(w_in.shape, BF16),
            pltpu.VMEM(w_out.shape, BF16),
            pltpu.VMEM(w_qkv.shape, BF16),
            pltpu.VMEM((2, reach, 2 * dim), BF16),
            pltpu.VMEM((2, dim, reach), BF16),
            pltpu.VMEM((2, 2 * dim, 2 * reach), BF16),
            pltpu.VMEM((2, reach, 2 * dim), BF16),
            pltpu.VMEM((2, 2 * dim, 2 * reach), BF16),
            pltpu.VMEM((2, dim, reach), F32),
            pltpu.VMEM((block, reach), BF16),
            pltpu.VMEM((2, 4, dim, frames), BF16),
            pltpu.VMEM((4, dim, frames), BF16),
            pltpu.VMEM((2, dim, frames), BF16),
            pltpu.VMEM((2, 4, dim, frames), BF16),
            pltpu.VMEM((2, 4, dim, frames), BF16),
            pltpu.VMEM((2, 2, dim, frames), BF16),
            pltpu.VMEM((3 * width, frames), BF16),
            low_keep,
            pltpu.VMEM((frames, wide), BF16),
            keep,
            pltpu.VMEM((8, width), F32),
            pltpu.VMEM((rows, width), F32),
            pltpu.VMEM((staged, width), BF16),
            pltpu.VMEM((staged, width), BF16),
            DMA((16,)),
            DMA((2 * per,)),
            DMA((2, per)),
            DMA((per + 1,)),
            DMA((per + 1,)),
            DMA(sems),
            DMA(sems),
        ],
        compiler_params=pltpu.CompilerParams(
            collective_id=2, has_side_effects=True, vmem_limit_bytes=VMEM_LIMIT
        ),
        name="back",
    )(
        lengths, lse, gain1, gain2, partial, near, far, o, do, trig, mid, point_two,
        tok, x1, n2, grad_x2, act, slope, w_in, w_out, w_qkv,
    )


def unpack_kernel(
    taps, full_hbm, bn_grads, output_hbm, input_hbm,
    output_to, input_to, gain1_to, in_one_to, out_one_to, gain2_to, qkv_to, out_weight_to, gain3_to, point_one_to,
    depthwise_to, bn_gain_to, bn_bias_to, point_two_to, gain4_to, in_two_to, out_two_to, gain5_to,
    full, output, input_grad, in_one, out_one, qkv, point_one, point_two, out_weight, in_two, out_two, depthwise,
    load_sems, sems,
):
    width = full.shape[1]
    unit = 4 * width
    copies = []
    pieces = [pl.ds(i * unit, unit) for i in range(6)] + [pl.ds(6 * unit, 16)]
    loads = start_copies(
        [(full_hbm.at[piece, :], full.at[piece, :]) for piece in pieces]
        + [(output_hbm, output), (input_hbm, input_grad)],
        load_sems,
    )

    def send(source, target):
        copies.append(pltpu.make_async_copy(source, target, sems.at[len(copies)]))
        copies[-1].start()

    def block(base):
        return full[base : base + width, :].astype(F32)

    loads[0].wait()
    for j in range(0, unit, width):
        out_two[j : j + width, :] = block(j)
    send(out_two, out_two_to)
    loads[1].wait()
    for j in range(0, unit, width):
        in_two[:, j : j + width] = block(unit + j)
    send(in_two, in_two_to)
    loads[2].wait()
    for j in range(0, 2 * width, width):
        point_one[:, j : j + width] = block(2 * unit + j)
    send(point_one, point_one_to)
    out_weight[...] = block(2 * unit + 2 * width)
    send(out_weight, out_weight_to)
    small = full[2 * unit + 3 * width : 2 * unit + 3 * width + 64, :].astype(F32)
    depthwise[...] = small[8 : 8 + taps]
    send(depthwise, depthwise_to)
    loads[3].wait()
    point_two[...] = block(3 * unit + 3 * width)
    send(point_two, point_two_to)
    for j in range(0, 3 * width, width):
        qkv[:, j : j + width] = block(3 * unit + j).T
    send(qkv, qkv_to)
    loads[4].wait()
    for j in range(0, unit, width):
        out_one[j : j + width, :] = block(4 * unit + j)
    send(out_one, out_one_to)
    loads[5].wait()
    for j in range(0, unit, width):
        in_one[:, j : j + width] = block(5 * unit + j)
    send(in_one, in_one_to)
    wait_all(loads[6:])
    send(output, output_to)
    send(input_grad, input_to)
    rest = full[6 * unit : 6 * unit + 16, :].astype(F32)
    for ref, row in (
        (gain1_to, rest[0]), (gain2_to, rest[1]), (gain3_to, small[2]), (gain4_to, small[3]), (gain5_to, small[4]),
        (bn_gain_to, bn_grads[0, :]), (bn_bias_to, bn_grads[1, :]),
    ):
        ref[...] = row
    wait_all(copies)


def unpack(full, bn_grads, output, input_grad, taps):
    width = full.shape[1]
    row, square, tall, flat = (width,), (width, width), (4 * width, width), (width, 4 * width)
    thrice, twice = (width, 3 * width), (width, 2 * width)
    anywhere = pl.BlockSpec(memory_space=pl.ANY)
    shapes = [
        output.shape, input_grad.shape, row, flat, tall, row, thrice, square, row, twice, (taps, width), row, row,
        square, row, flat, tall, row,
    ]
    return pl.pallas_call(
        functools.partial(unpack_kernel, taps),
        out_shape=[jax.ShapeDtypeStruct(shape, F32 if i > 1 else BF16) for i, shape in enumerate(shapes)],
        in_specs=[anywhere, VMEM, anywhere, anywhere],
        out_specs=[VMEM if shape == row else anywhere for shape in shapes],
        scratch_shapes=[
            pltpu.VMEM(full.shape, BF16),
            pltpu.VMEM(output.shape, BF16),
            pltpu.VMEM(input_grad.shape, BF16),
        ]
        + [
            pltpu.VMEM(shape, F32)
            for shape in (flat, tall, thrice, twice, square, square, flat, tall, (taps, width))
        ]
        + [DMA((9,)), DMA((11,))],
        compiler_params=pltpu.CompilerParams(vmem_limit_bytes=VMEM_LIMIT),
        name="unpack",
    )(full, bn_grads, output, input_grad)


def on_device(
    tokens, ln1_gain, ffn1_in, ffn1_out, ln2_gain, w_qkv, w_out, ln3_gain, w_point1, depthwise,
    bn_gain, bn_bias, w_point2, ln4_gain, ffn2_in, ffn2_out, ln5_gain, lengths, cotangent,
):
    width = tokens.shape[2]
    sp, dp = lax.axis_size("sp"), lax.axis_size("dp")
    assert HEADS == sp and ffn1_in.shape[1] == ffn2_in.shape[1] == 4 * width
    half = width // HEADS // 2
    turns = 10000.0 ** (-np.arange(half, dtype=np.float64) / half) / (2 * np.pi)
    high = np.round(turns * 4096.0) / 4096.0
    freq = jnp.asarray(np.stack([high, turns - high], axis=1), F32)
    x1, n2, trig, act, slope, near, far, context, raw_context, log_sums, flag = front(
        lengths, tokens[0], ln1_gain, ffn1_in, ffn1_out, ln2_gain, w_qkv, freq
    )
    context, raw_context, log_sums = repair(lengths, flag, near, far, context, raw_context, log_sums)
    output, grad_x2, grad_context, mid, point_two, bn_grads, partial = middle(
        lengths, context, x1, cotangent[0], ln3_gain, ln4_gain, ln5_gain, w_out, w_point1, depthwise,
        bn_gain, bn_bias, w_point2, ffn2_in, ffn2_out, dp,
    )
    input_grad, full = back(
        lengths, near, far, raw_context, log_sums, grad_context, trig, ln1_gain, ln2_gain, partial, mid, point_two,
        tokens[0], x1, n2, grad_x2, act, slope, ffn1_in, ffn1_out, w_qkv,
    )
    results = unpack(full, bn_grads, output, input_grad, depthwise.shape[0])
    return (results[0][None], results[1][None]) + tuple(results[2:])


def solution(mesh):
    split = P("dp", "sp", None)
    return jax.shard_map(
        on_device,
        mesh=mesh,
        in_specs=(split,) + (P(),) * 16 + (P("dp", None), split),
        out_specs=(split, split) + (P(),) * 16,
        check_vma=False,
    )
```

```python
import functools

import jax
import jax.numpy as jnp
import numpy as np
from jax import lax
from jax.experimental import pallas as pl
from jax.experimental.pallas import tpu as pltpu
from jax.sharding import PartitionSpec as P

HEADS = 4
EPS = 1e-05
NEG = -1e30
F32 = jnp.float32
BF16 = jnp.bfloat16
I32 = jnp.int32
MESH = pl.DeviceIdType.MESH
VMEM = pl.BlockSpec(memory_space=pltpu.VMEM)
SMEM = pl.BlockSpec(memory_space=pltpu.SMEM)
DMA = pltpu.SemaphoreType.DMA
VMEM_LIMIT = 56 * 2**20
PARTIAL_TIMES = (0, 4, 8, 13)
FRESH_TIMES = (0, 2, 5, 9, 13)


def dg(left, right, left_dim, right_dim):
    return lax.dot_general(
        left, right, (((left_dim,), (right_dim,)), ((), ())), preferred_element_type=F32
    )


def rows_at(index, count):
    return pl.ds(pl.multiple_of(index * count, count), count)


def start_copies(pairs, sems):
    copies = [pltpu.make_async_copy(source, target, sems.at[i]) for i, (source, target) in enumerate(pairs)]
    for copy in copies:
        copy.start()
    return copies


def wait_all(copies):
    for copy in copies:
        copy.wait()


def greet(devices):
    for device in devices:
        pl.semaphore_signal(pltpu.get_barrier_semaphore(), inc=1, device_id=device, device_id_type=MESH)


def await_greetings(devices):
    pl.semaphore_wait(pltpu.get_barrier_semaphore(), len(devices))


def flipped(axis, mask):
    me, step = lax.axis_index(axis), 1
    out = me
    while step <= mask:
        if mask & step:
            out = out + step - 2 * step * lax.rem(me // step, 2)
        step *= 2
    return out


def peer_at(sp_mask, dp_mask):
    return (flipped("dp", dp_mask), flipped("sp", sp_mask))


def sp_peers(count):
    return [peer_at(mask, 0) for mask in range(1, count)]


def row_of(ref):
    return ref[...].astype(F32).reshape(1, ref.shape[0])


def frame_cols(device, frames, c, chunk):
    return pl.ds(pl.multiple_of(device * frames + c * chunk, chunk), chunk)


def ends_of(len_ref, items):
    ends, total = [], 0
    for item in range(items):
        total = total + len_ref[0, item]
        ends.append(total)
    return ends


def segment_row(first, count, ends):
    frame = first + lax.broadcasted_iota(I32, (1, count), 1)
    segment = jnp.zeros((1, count), I32)
    for end in ends:
        segment = segment + (frame >= end).astype(I32)
    return segment


def position_row(first, count, ends):
    frame = first + lax.broadcasted_iota(I32, (1, count), 1)
    start = jnp.zeros((1, count), I32)
    for end in ends:
        start = jnp.where(frame >= end, end, start)
    return (frame - start).astype(F32)


def onehot_rows(segment, items, other, same):
    row = lax.broadcasted_iota(I32, (16, segment.shape[1]), 0)
    return jnp.where(row <= items, jnp.where(row == segment, same, other), 0.0)


def norm_parts(rows):
    centre = rows - jnp.mean(rows, axis=-1, keepdims=True)
    inv = lax.rsqrt(jnp.mean(centre * centre, axis=-1, keepdims=True) + EPS)
    return centre * inv, inv


def norm_back(grad, hat, inv, gain):
    scaled = grad * gain
    first = jnp.mean(scaled, axis=-1, keepdims=True)
    second = jnp.mean(scaled * hat, axis=-1, keepdims=True)
    return inv * (scaled - first - hat * second)


def sigmoid(x):
    return 0.5 * jnp.tanh(0.5 * x) + 0.5


def sine_cosine(position, freq_hi, freq_lo):
    turns = position * freq_hi
    turns = turns - jnp.round(turns) + position * freq_lo
    turns = turns - jnp.round(turns)
    x = turns * float(np.pi)
    x2 = x * x
    s = x * (1 + x2 * (-1 / 6 + x2 * (1 / 120 + x2 * (-1 / 5040 + x2 * (1 / 362880 - x2 / 39916800)))))
    c = 1 + x2 * (-1 / 2 + x2 * (1 / 24 + x2 * (-1 / 720 + x2 * (1 / 40320 + x2 * (-1 / 3628800 + x2 / 479001600)))))
    return 2 * s * c, 1 - 2 * s * s


def split_rows(value):
    row = lax.broadcasted_iota(I32, (16, value.shape[1]), 0)
    first = value.astype(BF16).astype(F32)
    second = (value - first).astype(BF16).astype(F32)
    third = value - first - second
    picked = jnp.where(row == 0, first, jnp.where(row == 1, second, third))
    return jnp.where(row < 3, picked, 0.0).astype(BF16)


def first_rows(count, columns):
    row = lax.broadcasted_iota(I32, (16, columns), 0)
    return jnp.where(row < count, 1.0, 0.0).astype(BF16)


def query_rows(query, segment, items, shift):
    pad = jnp.zeros((query.shape[0] - 32, query.shape[1]), BF16)
    return jnp.concatenate([query, onehot_rows(segment, items, 0.0, 1.0).astype(BF16), split_rows(shift), pad], axis=0)


def key_rows(key, segment, items):
    pad = jnp.zeros((key.shape[0] - 32, key.shape[1]), BF16)
    return jnp.concatenate(
        [key, onehot_rows(segment, items, NEG, 0.0).astype(BF16), first_rows(3, key.shape[1]), pad], axis=0
    )


def lay_queries(near, slot, frames, first, ends, items, dim, qa, lse):
    cols = slice(slot * frames, (slot + 1) * frames)
    segment = segment_row(first, frames, ends)
    for h in range(2):
        query = near[slot, h * dim : (h + 1) * dim, :]
        key = near[slot, (2 + h) * dim : (3 + h) * dim, :]
        own = jnp.sum(query.astype(F32) * key.astype(F32), axis=0, keepdims=True)
        lse[h : h + 1, cols] = own
        qa[h, :, cols] = query_rows(query, segment, items, -own)


def lay_keys(key, value, rows, first, ends, items, h, ka, va):
    dim, count = key.shape
    ka[h, rows, :] = key_rows(key, segment_row(first, count, ends), items).T
    va[h, 0:dim, rows] = value
    va[h, dim:, rows] = first_rows(1, count)


def front_kernel(
    items, chunk, block, len_ref, tok, gain1, w_in, w_out, gain2, w_qkv, freq,
    x1_hbm, n2_hbm, trig_hbm, act_hbm, slope_hbm, near_hbm, far_hbm, ctx_hbm, o_hbm, lse, flag,
    x1_ref, n2_ref, trig, act, slope, near, far, ctx, o_ref,
    parts, turned, qa, ka, va, acc, send, recv, out_sems, last_sems,
):
    me = lax.axis_index("sp")
    core, pair = lax.rem(me, 2), me // 2
    frames, width = tok.shape
    half = trig.shape[0] // 2
    dim = 2 * half
    count = frames // chunk
    peers = [peer_at(mask, 0) for mask in (1, 2, 3)]
    greet(peers)
    turned[...] = w_qkv[...].T
    ends = ends_of(len_ref, items)
    scale = dim**-0.5

    def copies(c):
        cols = rows_at(c, chunk)
        ways = (
            (parts.at[1 - core, :, cols], near.at[core, :, cols]),
            (parts.at[core, 2 * dim :, cols], far.at[core, :, cols]),
            (parts.at[1 - core, 2 * dim :, cols], far.at[core, :, cols]),
        )
        return [
            pltpu.make_async_remote_copy(
                src_ref=source, dst_ref=target, send_sem=send.at[i, c], recv_sem=recv.at[i, c],
                device_id=peers[i], device_id_type=MESH,
            )
            for i, (source, target) in enumerate(ways)
        ]

    def results(c):
        rows = rows_at(c, chunk)
        pairs = [(ref.at[rows, :], hbm.at[rows, :]) for ref, hbm in (
            (x1_ref, x1_hbm), (n2_ref, n2_hbm), (act, act_hbm), (slope, slope_hbm)
        )]
        return [pltpu.make_async_copy(source, target, out_sems.at[i, c]) for i, (source, target) in enumerate(pairs)]

    def step(c, carry):
        rows = rows_at(c, chunk)
        x = tok[rows, :].astype(F32)
        hat, _ = norm_parts(x)
        n1 = (hat * row_of(gain1)).astype(BF16)
        a = dg(n1, w_in[...], 1, 0)
        sig = sigmoid(a)
        s = (a * sig).astype(BF16)
        act[rows, :] = s
        slope[rows, :] = (sig * (1.0 + a * (1.0 - sig))).astype(BF16)
        x1 = x + 0.5 * dg(s, w_out[...], 1, 0)
        x1_ref[rows, :] = x1
        hat, _ = norm_parts(x1)
        n2 = (hat * row_of(gain2)).astype(BF16)
        n2_ref[rows, :] = n2
        joined = dg(turned[...], n2, 1, 1)
        sine, cosine = sine_cosine(
            position_row(me * frames + c * chunk, chunk, ends), freq[:, 0:1], freq[:, 1:2]
        )
        trig[0:half, rows] = sine
        trig[half:, rows] = cosine
        for p in range(2):
            for j in range(2):
                for part, factor in ((0, scale), (1, 1.0)):
                    low = part * width + (2 * p + j) * dim
                    first, second = joined[low : low + half], joined[low + half : low + dim]
                    low = (2 * part + j) * dim
                    parts[p, low : low + half, rows] = ((first * cosine - second * sine) * factor).astype(BF16)
                    parts[p, low + half : low + dim, rows] = (
                        (first * sine + second * cosine) * factor
                    ).astype(BF16)
                low = 2 * width + (2 * p + j) * dim
                parts[p, (4 + j) * dim : (5 + j) * dim, rows] = joined[low : low + dim].astype(BF16)

        @pl.when(c == 0)
        def _():
            await_greetings(peers)

        for copy in copies(c):
            copy.start()
        near[core, :, rows] = parts[core, :, rows]
        for copy in results(c):
            copy.start()
        return carry

    lax.fori_loop(0, count, step, 0)

    def near_arrives(c, carry):
        copies(c)[0].wait()
        return carry

    lax.fori_loop(0, count, near_arrives, 0)
    leaving = start_copies([(near, near_hbm), (trig, trig_hbm)], last_sems)
    reach = 2 * frames
    for slot in range(2):
        first = (2 * pair + slot) * frames
        lay_queries(near, slot, frames, first, ends, items, dim, qa, lse)
        for h in range(2):
            lay_keys(
                near[slot, (2 + h) * dim : (3 + h) * dim, :], near[slot, (4 + h) * dim : (5 + h) * dim, :],
                slice(slot * frames, (slot + 1) * frames), first, ends, items, h, ka, va,
            )

    def near_step(i, carry):
        h, cols = i // (reach // block), rows_at(lax.rem(i, reach // block), block)
        powers = jnp.exp(dg(ka[h, 0:reach, :], qa[h, :, cols], 1, 0)).astype(BF16)
        acc[h, :, cols] = dg(va[h, :, 0:reach], powers, 1, 0)
        return carry

    lax.fori_loop(0, 2 * reach // block, near_step, 0)
    wide = min(1024, reach)

    def far_step(c, carry):
        for copy in copies(c)[1:]:
            copy.wait()
        cols = rows_at(c, chunk)
        for slot in range(2):
            first = (2 * (1 - pair) + slot) * frames + c * chunk
            rows = pl.ds(pl.multiple_of(reach + (2 * c + slot) * chunk, chunk), chunk)
            for h in range(2):
                lay_keys(
                    far[slot, h * dim : (h + 1) * dim, cols], far[slot, (2 + h) * dim : (3 + h) * dim, cols],
                    rows, first, ends, items, h, ka, va,
                )
        rows = pl.ds(pl.multiple_of(reach + 2 * c * chunk, 2 * chunk), 2 * chunk)

        def inner(i, carry):
            h, cols = i // (reach // wide), rows_at(lax.rem(i, reach // wide), wide)
            powers = jnp.exp(dg(ka[h, rows, :], qa[h, :, cols], 1, 0)).astype(BF16)
            acc[h, :, cols] += dg(va[h, :, rows], powers, 1, 0)
            return carry

        return lax.fori_loop(0, 2 * reach // wide, inner, carry)

    lax.fori_loop(0, count, far_step, 0)
    leaving += start_copies([(far, far_hbm)], last_sems.at[pl.ds(2, 1)])
    bad = jnp.zeros((1, reach), F32)
    for h in range(2):
        total = acc[h, dim : dim + 1, :]
        value = acc[h, 0:dim, :] / total
        ctx[h] = value.astype(BF16)
        o_ref[h] = value
        leaving += start_copies([(ctx.at[h], ctx_hbm.at[h]), (o_ref.at[h], o_hbm.at[h])], last_sems.at[pl.ds(3 + 2 * h, 2)])
        lse[h : h + 1, :] = lse[h : h + 1, :] + jnp.log(total)
        bad = jnp.maximum(bad, jnp.where(total < 2.0**60, 0.0, 1.0))
    flag[...] = jnp.broadcast_to(jnp.max(bad, axis=1, keepdims=True), flag.shape)
    for c in range(count):
        wait_all(results(c))
    wait_all(leaving)


def front(lengths, tok, gain1, w_in, w_out, gain2, w_qkv, freq):
    frames, width = tok.shape
    wide = w_in.shape[1]
    chunk = min(256, frames)
    count = frames // chunk
    dim = width // HEADS
    reach = 2 * frames
    return pl.pallas_call(
        functools.partial(front_kernel, lengths.shape[1], chunk, min(512, reach)),
        out_shape=[
            jax.ShapeDtypeStruct((frames, width), F32),
            jax.ShapeDtypeStruct((frames, width), BF16),
            jax.ShapeDtypeStruct((dim, frames), F32),
            jax.ShapeDtypeStruct((frames, wide), BF16),
            jax.ShapeDtypeStruct((frames, wide), BF16),
            jax.ShapeDtypeStruct((2, 6 * dim, frames), BF16),
            jax.ShapeDtypeStruct((2, 4 * dim, frames), BF16),
            jax.ShapeDtypeStruct((2, dim, reach), BF16),
            jax.ShapeDtypeStruct((2, dim, reach), F32),
            jax.ShapeDtypeStruct((2, reach), F32),
            jax.ShapeDtypeStruct((8, 128), F32),
        ],
        in_specs=[SMEM] + [VMEM] * 7,
        out_specs=[pl.BlockSpec(memory_space=pl.ANY)] * 9 + [VMEM] * 2,
        scratch_shapes=[
            pltpu.VMEM((frames, width), F32),
            pltpu.VMEM((frames, width), BF16),
            pltpu.VMEM((dim, frames), F32),
            pltpu.VMEM((frames, wide), BF16),
            pltpu.VMEM((frames, wide), BF16),
            pltpu.VMEM((2, 6 * dim, frames), BF16),
            pltpu.VMEM((2, 4 * dim, frames), BF16),
            pltpu.VMEM((2, dim, reach), BF16),
            pltpu.VMEM((2, dim, reach), F32),
            pltpu.VMEM((2, 6 * dim, frames), BF16),
            pltpu.VMEM((3 * width, width), BF16),
            pltpu.VMEM((2, 2 * dim, reach), BF16),
            pltpu.VMEM((2, 2 * reach, 2 * dim), BF16),
            pltpu.VMEM((2, dim + 16, 2 * reach), BF16),
            pltpu.VMEM((2, dim + 16, reach), F32),
            DMA((3, count)),
            DMA((3, count)),
            DMA((4, count)),
            DMA((7,)),
        ],
        compiler_params=pltpu.CompilerParams(
            collective_id=0, has_side_effects=True, vmem_limit_bytes=VMEM_LIMIT
        ),
        name="front",
    )(lengths, tok, gain1, w_in, w_out, gain2, w_qkv, freq)


def repair_kernel(
    items, block, len_ref, flag, near_hbm, far_hbm, ctx_in, o_in, lse_in, ctx_hbm, o_hbm, lse_hbm,
    near, far, ctx, o_ref, lse, qa, ka, va, sems,
):
    @pl.when(jnp.max(flag[...]) > 0.5)
    def _():
        pair = lax.axis_index("sp") // 2
        frames, dim = near.shape[2], near.shape[1] // 6
        reach = 2 * frames
        ends = ends_of(len_ref, items)
        loads = [
            pltpu.make_async_copy(near_hbm, near, sems.at[0]),
            pltpu.make_async_copy(far_hbm, far, sems.at[1]),
        ]
        for copy in loads:
            copy.start()
        for copy in loads:
            copy.wait()
        for slot in range(2):
            first, other = (2 * pair + slot) * frames, (2 * (1 - pair) + slot) * frames
            lay_queries(near, slot, frames, first, ends, items, dim, qa, lse)
            for h in range(2):
                lay_keys(
                    near[slot, (2 + h) * dim : (3 + h) * dim, :], near[slot, (4 + h) * dim : (5 + h) * dim, :],
                    slice(slot * frames, (slot + 1) * frames), first, ends, items, h, ka, va,
                )
                lay_keys(
                    far[slot, h * dim : (h + 1) * dim, :], far[slot, (2 + h) * dim : (3 + h) * dim, :],
                    slice(reach + slot * frames, reach + (slot + 1) * frames), other, ends, items, h, ka, va,
                )

        def step(i, carry):
            h, cols = i // (reach // block), rows_at(lax.rem(i, reach // block), block)
            query = qa[h, :, cols]

            def highest(j, top):
                scores = dg(ka[h, rows_at(j, block), :], query, 1, 0)
                return jnp.maximum(top, jnp.max(scores, axis=0, keepdims=True))

            top = lax.fori_loop(0, 2 * reach // block, highest, jnp.zeros((1, block), F32))

            def add(j, total):
                rows = rows_at(j, block)
                powers = jnp.exp(dg(ka[h, rows, :], query, 1, 0) - top).astype(BF16)
                return total + dg(va[h, :, rows], powers, 1, 0)

            total = lax.fori_loop(0, 2 * reach // block, add, jnp.zeros((dim + 16, block), F32))
            value = total[0:dim, :] / total[dim : dim + 1, :]
            ctx[h, :, cols] = value.astype(BF16)
            o_ref[h, :, cols] = value
            change = top + jnp.log(total[dim : dim + 1, :])
            row = lax.broadcasted_iota(I32, (2, block), 0)
            lse[:, cols] = lse[:, cols] + jnp.where(row == h, change, 0.0)
            return carry

        lax.fori_loop(0, 2 * reach // block, step, 0)
        stores = [
            pltpu.make_async_copy(ctx, ctx_hbm, sems.at[2]),
            pltpu.make_async_copy(o_ref, o_hbm, sems.at[3]),
            pltpu.make_async_copy(lse, lse_hbm, sems.at[4]),
        ]
        for copy in stores:
            copy.start()
        for copy in stores:
            copy.wait()


def repair(lengths, flag, near, far, ctx, o, lse):
    dim, reach = ctx.shape[1:]
    anywhere = pl.BlockSpec(memory_space=pl.ANY)
    return pl.pallas_call(
        functools.partial(repair_kernel, lengths.shape[1], min(512, reach)),
        out_shape=[jax.ShapeDtypeStruct(x.shape, x.dtype) for x in (ctx, o, lse)],
        in_specs=[SMEM, VMEM] + [anywhere] * 5,
        out_specs=[anywhere] * 3,
        input_output_aliases={4: 0, 5: 1, 6: 2},
        scratch_shapes=[
            pltpu.VMEM(near.shape, BF16),
            pltpu.VMEM(far.shape, BF16),
            pltpu.VMEM(ctx.shape, BF16),
            pltpu.VMEM(o.shape, F32),
            pltpu.VMEM(lse.shape, F32),
            pltpu.VMEM((2, 2 * dim, reach), BF16),
            pltpu.VMEM((2, 2 * reach, 2 * dim), BF16),
            pltpu.VMEM((2, dim + 16, 2 * reach), BF16),
            DMA((5,)),
        ],
        compiler_params=pltpu.CompilerParams(vmem_limit_bytes=VMEM_LIMIT),
        name="repair",
    )(lengths, flag, near, far, ctx, o, lse)


def axis_steps(axis):
    steps, step = [], 1
    while step < lax.axis_size(axis):
        steps.append((axis, step))
        step *= 2
    assert step == lax.axis_size(axis)
    return steps


def stage_plans():
    sp_steps, dp_steps = axis_steps("sp"), axis_steps("dp")
    plane, rest = sp_steps[1:] + dp_steps[:1], dp_steps[1:]

    def groups(steps):
        return [steps[i : i + 2] for i in range(0, len(steps), 2)]

    plans = (
        groups(plane) + groups(rest),
        groups(rest) + groups(plane),
        [dp_steps[:1]] + groups(rest) + groups(sp_steps[1:]),
    )
    return tuple([sp_steps[:1]] + [stage for stage in plan if stage] for plan in plans)


def stage_masks(stage):
    masks = []
    for number in range(1, 1 << len(stage)):
        mask = {"sp": 0, "dp": 0}
        for i, (axis, step) in enumerate(stage):
            if number & (1 << i):
                mask[axis] += step
        masks.append((mask["sp"], mask["dp"]))
    return masks


def place_in(stage, number):
    place = 0
    for i, (axis, step) in enumerate(stage):
        bit = lax.rem(lax.axis_index(axis) // step, 2)
        place = place + (1 << i) * (1 - bit if number & (1 << i) else bit)
    return place


def exchange_plan(rows, stages, offset=0):
    sizes, size = [], rows
    for stage in stages:
        group = 1 << len(stage)
        splits = size % (16 * group) == 0
        size = size // group if splits else size
        sizes.append((splits, size, offset))
        offset += (group - 1) * size
    return sizes, offset, size


class Reduction:
    def __init__(self, base, rows, staged, stages, acc, stage, land, full, send, recv):
        self.stages, self.acc, self.stage, self.land, self.full = stages, acc, stage, land, full
        self.send, self.recv, self.base = send, recv, base
        self.sizes, _, self.own = exchange_plan(rows, stages, staged)
        self.first_sem = [sum((1 << len(s)) - 1 for s in stages[:k]) for k in range(len(stages))]

    def at(self, low, size):
        return pl.ds(pl.multiple_of(low, 16), size)

    def low(self, k):
        return self.base + sum(
            place_in(self.stages[j], 0) * self.sizes[j][1] for j in range(k) if self.sizes[j][0]
        )

    def slot(self, k, i):
        _, size, offset = self.sizes[k]
        return slice(offset + i * size, offset + (i + 1) * size)

    def copies(self, way, k):
        splits, size, _ = self.sizes[k]
        out = []
        for i, masks in enumerate(stage_masks(self.stages[k])):
            if way == 0:
                source = self.stage.at[self.slot(k, i if splits else 0), :]
                target = self.land.at[self.slot(k, i), :]
            else:
                source = target = self.full.at[self.at(self.low(k + 1), size), :]
            out.append(
                pltpu.make_async_remote_copy(
                    src_ref=source,
                    dst_ref=target,
                    send_sem=self.send.at[way, self.first_sem[k] + i],
                    recv_sem=self.recv.at[way, self.first_sem[k] + i],
                    device_id=peer_at(*masks),
                    device_id_type=MESH,
                )
            )
        return out

    def sum_send(self, k):
        splits, size, _ = self.sizes[k]
        copies = self.copies(0, k)
        for i, copy in enumerate(copies):
            if splits:
                away = self.low(k) + place_in(self.stages[k], i + 1) * size
                self.stage[self.slot(k, i), :] = self.acc[self.at(away, size), :].astype(BF16)
            elif i == 0:
                self.stage[self.slot(k, 0), :] = self.acc[self.at(self.low(k), size), :].astype(BF16)
            copy.start()

    def sum_recv(self, k):
        splits, size, _ = self.sizes[k]
        copies = self.copies(0, k)
        for copy in copies:
            copy.wait()
        values = [self.land[self.slot(k, i), :].astype(F32) for i in range(len(copies))]
        if splits:
            values = [self.acc[self.at(self.low(k + 1), size), :]] + values
        else:
            values = [self.stage[self.slot(k, 0), :].astype(F32)] + values
        while len(values) > 1:
            values = [values[i] + values[i + 1] for i in range(0, len(values), 2)]
        self.acc[self.at(self.low(k + 1), size), :] = values[0]

    def close(self):
        where = self.at(self.low(len(self.stages)), self.own)
        self.full[where, :] = self.acc[where, :].astype(BF16)

    def share_send(self, k):
        if self.sizes[k][0]:
            for copy in self.copies(1, k):
                copy.start()

    def share_recv(self, k):
        if self.sizes[k][0]:
            for copy in self.copies(1, k):
                copy.wait()


def advance(streams, position):
    for stream in streams:
        n = len(stream.stages)
        if 0 < position <= n:
            stream.sum_recv(position - 1)
        if position < n:
            stream.sum_send(position)
        else:
            if position == n:
                stream.close()
            else:
                stream.share_recv(2 * n - position)
            if position < 2 * n:
                stream.share_send(2 * n - 1 - position)


def reduction_scratch(rows_list):
    staged = sum(max(exchange_plan(rows, stages)[1] for stages in stage_plans()) for rows in rows_list)
    sems = max(sum((1 << len(stage)) - 1 for stage in plan) for plan in stage_plans())
    return staged, (len(rows_list), 2, sems)


def make_streams(items, acc, stage, land, full, send, recv):
    streams, staged = [], 0
    for i, (base, rows, order) in enumerate(items):
        stages = stage_plans()[order]
        streams.append(
            Reduction(base, rows, staged, stages, acc, stage, land, full, send.at[i], recv.at[i])
        )
        staged += max(exchange_plan(rows, plan)[1] for plan in stage_plans())
    return streams


def all_masks(sp):
    masks = [(mask, 0) for mask in range(1, sp)]
    for plan in stage_plans():
        for stage in plan:
            masks += [m for m in stage_masks(stage) if m not in masks]
    return masks


def halves_of(ref, rows):
    return jnp.concatenate([ref[0, rows, :], ref[1, rows, :]], axis=1)


def combine(entries):
    count = sum(e[2] for e in entries)
    safe = jnp.maximum(count, 1.0)
    mean = sum(e[2] * e[0] for e in entries) / safe
    spread = sum(e[1] + e[2] * (e[0] - mean) * (e[0] - mean) for e in entries)
    return mean, spread, count


def pick(ref):
    return ref[0:1, :], ref[1:2, :], ref[2:3, :]


def total(entries):
    return tuple(sum(e[i] for e in entries) for i in range(3))


def middle_kernel(
    sp, dp, items, taps, chunk, block, len_ref, parts, x1_hbm, cot_hbm, gain3, gain4, gain5, w_out_hbm,
    w_point1_hbm, depthwise, bn_gain, bn_bias, w_point2_hbm, w_in_hbm, w_down_hbm,
    out_hbm, x2_hbm, heads, mid_hbm, point_two_hbm, bn_grads, partial,
    x1_ref, cot, w_out, w_point1, w_point2, w_in, w_down, out_ref, grad_x2, mid, point_two, two, load_sems, out_sems,
    stage, land, sum_send, sum_recv,
    ctx, x2_ref, n3_keep, point, glu, conv, low_lim, high_lim, act, hidden, n4_keep, branch, swish, branch2,
    grad_x3, grad_y, grad_conv, grad_glu, grad_point, branch3, back_parts, tap_sums, edge_out, edge_in,
    send_box, near_box, far_box, sums,
    send, recv, local, back_send, back_recv, back_local, rim_send, rim_recv, box_send, box_recv,
):
    me, me_dp = lax.axis_index("sp"), lax.axis_index("dp")
    frames, width = x1_ref.shape
    lanes = width // 2
    reach = taps // 2
    count = frames // chunk
    peers = sp_peers(sp)
    far_peers = [peer_at(0, mask) for mask in range(1, dp)]
    masks = all_masks(sp)
    masks += [(0, mask) for mask in range(1, dp) if (0, mask) not in masks]
    greeted = [peer_at(*mask) for mask in masks]
    core = lax.rem(me, 2)
    sibling = peer_at(1, 0)
    length = sp * frames
    ends = ends_of(len_ref, items)
    first_frame = me * frames

    def limits(b, carry):
        rows = rows_at(b, chunk)
        frame = first_frame + b * chunk + lax.broadcasted_iota(I32, (chunk, lanes), 0)
        low, high = jnp.zeros_like(frame), jnp.full_like(frame, length)
        for end in ends:
            low = jnp.where(frame >= end, end, low)
        for end in reversed(ends):
            high = jnp.where(frame < end, end, high)
        low_lim[rows, :] = low - frame
        high_lim[rows, :] = high - 1 - frame
        return carry

    for ref in (glu, grad_conv):
        for h in range(2):
            ref[h, 0:reach, :] = jnp.zeros((reach, lanes), F32)
            ref[h, reach + frames :, :] = jnp.zeros((reach, lanes), F32)
    edge_in[...] = jnp.zeros_like(edge_in)
    send_box[...] = jnp.zeros_like(send_box)
    greet(greeted)
    loads = start_copies(
        [
            (w_out_hbm, w_out), (x1_hbm, x1_ref), (w_point1_hbm, w_point1), (w_point2_hbm, w_point2),
            (w_in_hbm, w_in), (w_down_hbm, w_down), (cot_hbm, cot),
        ],
        load_sems,
    )
    lax.fori_loop(0, count, limits, 0)
    tap_sums[...] = jnp.zeros_like(tap_sums)
    sums[...] = jnp.zeros_like(sums)
    await_greetings(greeted)

    def moves(c, source, target, send_sems, recv_sems, local_sems):
        return [
            pltpu.make_async_remote_copy(
                src_ref=source(1 - core, c), dst_ref=target(core, c),
                send_sem=send_sems.at[c], recv_sem=recv_sems.at[c],
                device_id=sibling, device_id_type=MESH,
            ),
            pltpu.make_async_copy(source(core, c), target(core, c), local_sems.at[c]),
        ]

    def by_frames(ref):
        return lambda slot, c: ref.at[:, :, frame_cols(slot, frames, c, chunk)]

    def by_head(ref):
        return lambda slot, c: ref.at[slot, :, :, rows_at(c, chunk)]

    def context_moves(c):
        return moves(c, by_frames(parts), by_head(ctx), send, recv, local)

    def begin(c, carry):
        for copy in context_moves(c):
            copy.start()
        return carry

    lax.fori_loop(0, count, begin, 0)
    wait_all(loads[:3])

    def open_step(c, carry):
        rows = rows_at(c, chunk)
        for copy in context_moves(c):
            copy.wait()
        context = ctx[:, :, :, rows].reshape(width, chunk)
        x2 = x1_ref[rows, :] + dg(context, w_out[...], 0, 0)
        x2_ref[rows, :] = x2
        hat, _ = norm_parts(x2)
        n3 = (hat * row_of(gain3)).astype(BF16)
        n3_keep[rows, :] = n3
        pair = dg(n3, w_point1[...], 1, 0)
        point[rows, :] = pair
        gated = (pair[:, :width] * sigmoid(pair[:, width:])).astype(BF16).astype(F32)
        where = pl.ds(pl.multiple_of(reach + c * chunk, 8), chunk)
        glu[0, where, :] = gated[:, :lanes]
        glu[1, where, :] = gated[:, lanes:]
        return carry

    lax.fori_loop(0, count, open_step, 0)

    def rim_copies(call, side, source, target):
        peer = (me_dp, lax.rem(me + (sp - 1 if side == 0 else 1), sp))
        return pltpu.make_async_remote_copy(
            src_ref=source, dst_ref=target, send_sem=rim_send.at[call, side], recv_sem=rim_recv.at[call, side],
            device_id=peer, device_id_type=MESH,
        )

    def swap_rims(call, sources, targets):
        @pl.when(me > 0)
        def _():
            rim_copies(call, 0, sources[0], targets[1]).start()

        @pl.when(me < sp - 1)
        def _():
            rim_copies(call, 1, sources[1], targets[0]).start()

    def await_rims(call, sources, targets):
        @pl.when(me > 0)
        def _():
            rim_copies(call, 0, sources[0], targets[1]).wait_send()
            rim_copies(call, 1, sources[1], targets[0]).wait_recv()

        @pl.when(me < sp - 1)
        def _():
            rim_copies(call, 1, sources[1], targets[0]).wait_send()
            rim_copies(call, 0, sources[0], targets[1]).wait_recv()

    for side, rows in ((0, slice(reach, 2 * reach)), (1, slice(frames, frames + reach))):
        for h in range(2):
            edge_out[side, 0:reach, h * lanes : (h + 1) * lanes] = glu[h, rows, :]
    glu_rims = (
        [edge_out.at[0, 0:reach, :], edge_out.at[1, 0:reach, :]],
        [edge_in.at[0, 0:reach, :], edge_in.at[1, 0:reach, :]],
    )
    swap_rims(0, *glu_rims)

    zero = jnp.zeros((block, lanes), F32)

    def conv_step(b, carry):
        low, high = low_lim[rows_at(b, block), :], high_lim[rows_at(b, block), :]
        start = pl.multiple_of(b * block, block)
        result = [zero, zero]
        for tap in range(taps):
            shift = tap - reach
            inside = (low <= shift) if shift < 0 else (high >= shift)
            for h in range(2):
                view = glu.at[h, pl.ds(start, block + 2 * reach), :]
                term = jnp.where(inside, view[tap : tap + block, :], 0.0)
                result[h] = result[h] + depthwise[tap : tap + 1, h * lanes : (h + 1) * lanes].astype(F32) * term
        valid = (first_frame + start + lax.broadcasted_iota(I32, (block, lanes), 0)) < ends[-1]
        for h in range(2):
            conv[h, rows_at(b, block), :] = result[h]
            sums[0:1, h * lanes : (h + 1) * lanes] += jnp.sum(jnp.where(valid, result[h], 0.0), axis=0, keepdims=True)
        return carry

    blocks = frames // block
    lax.fori_loop(1, blocks - 1, conv_step, 0)
    await_rims(0, *glu_rims)
    for h in range(2):
        glu[h, 0:reach, :] = edge_in[0, 0:reach, h * lanes : (h + 1) * lanes]
        glu[h, reach + frames :, :] = edge_in[1, 0:reach, h * lanes : (h + 1) * lanes]
    conv_step(0, 0)
    conv_step(blocks - 1, 0)

    own_count = jnp.clip(ends[-1] - first_frame, 0, frames).astype(F32)
    own_mean = sums[0:1, :] / jnp.maximum(own_count, 1.0)
    sums[0:1, :] = jnp.zeros((1, width), F32)

    def spread_step(c, carry):
        rows = rows_at(c, chunk)
        valid = (first_frame + c * chunk + lax.broadcasted_iota(I32, (chunk, width), 0)) < ends[-1]
        apart = jnp.where(valid, halves_of(conv, rows) - own_mean, 0.0)
        sums[1:2, :] += jnp.sum(apart * apart, axis=0, keepdims=True)
        return carry

    lax.fori_loop(0, count, spread_step, 0)

    def box_copies(call, stage):
        group = peers if stage == 0 else far_peers
        target = near_box if stage == 0 else far_box
        base = 0 if stage == 0 else sp - 1
        return [
            pltpu.make_async_remote_copy(
                src_ref=send_box.at[call, stage],
                dst_ref=target.at[call, i],
                send_sem=box_send.at[call, base + i],
                recv_sem=box_recv.at[call, base + i],
                device_id=peer,
                device_id_type=MESH,
            )
            for i, peer in enumerate(group)
        ]

    def box_begin(call, stage, rows):
        for i, row in enumerate(rows):
            send_box[call, stage, i : i + 1, :] = row
        for copy in box_copies(call, stage):
            copy.start()

    def box_end(call, stage, rows, merge):
        target = near_box if stage == 0 else far_box
        copies = box_copies(call, stage)
        for copy in copies:
            copy.wait()
        return merge([rows] + [pick(target[call, i]) for i in range(len(copies))])

    stats = (own_mean, sums[1:2, :], jnp.full((1, width), 1.0, F32) * own_count)
    sums[1:2, :] = jnp.zeros((1, width), F32)
    box_begin(0, 0, stats)
    stats = box_end(0, 0, stats, combine)
    box_begin(0, 1, stats)
    mean, spread, frame_count = box_end(0, 1, stats, combine)
    inv_std = lax.rsqrt(spread / frame_count + EPS)
    norm_gain, norm_bias = row_of(bn_gain), row_of(bn_bias)

    def heart_step(c, carry):
        rows = rows_at(c, chunk)
        normed = (halves_of(conv, rows) - mean) * inv_std
        y = normed * norm_gain + norm_bias
        sig_y = sigmoid(y)
        w = (y * sig_y).astype(BF16)
        swish[rows, :] = w
        x3 = x2_ref[rows, :] + dg(w, w_point2[...], 1, 0)
        hat4, inv4 = norm_parts(x3)
        g4 = row_of(gain4)
        n4 = (hat4 * g4).astype(BF16)
        n4_keep[rows, :] = n4
        a = dg(n4, w_in[...], 1, 0)
        sig = sigmoid(a)
        s = (a * sig).astype(BF16)
        act[rows, :] = s
        x4 = x3 + 0.5 * dg(s, w_down[...], 1, 0)
        hat5, inv5 = norm_parts(x4)
        g5 = row_of(gain5)
        out_ref[rows, :] = (hat5 * g5).astype(BF16)
        top = cot[rows, :].astype(F32)
        mid[3 * width + 4 : 3 * width + 5, :] += jnp.sum(top * hat5, axis=0, keepdims=True)
        grad_x4 = norm_back(top, hat5, inv5, g5)
        low_grad = (0.5 * grad_x4).astype(BF16)
        branch[rows, :] = low_grad
        grad = dg(low_grad, w_down[...], 1, 1)
        low_hidden = (grad * (sig * (1.0 + a * (1.0 - sig)))).astype(BF16)
        hidden[rows, :] = low_hidden
        grad = dg(low_hidden, w_in[...], 1, 1)
        mid[3 * width + 3 : 3 * width + 4, :] += jnp.sum(grad * hat4, axis=0, keepdims=True)
        grad3 = grad_x4 + norm_back(grad, hat4, inv4, g4)
        grad_x3[rows, :] = grad3
        low_grad = grad3.astype(BF16)
        branch2[rows, :] = low_grad
        grad = dg(low_grad, w_point2[...], 1, 1) * (sig_y * (1.0 + y * (1.0 - sig_y)))
        grad_y[0, rows, :] = grad[:, :lanes]
        grad_y[1, rows, :] = grad[:, lanes:]
        sums[2:3, :] += jnp.sum(grad, axis=0, keepdims=True)
        sums[3:4, :] += jnp.sum(grad * normed, axis=0, keepdims=True)
        return carry

    mid[3 * width :, :] = jnp.zeros((width, width), F32)
    wait_all(loads[3:])
    lax.fori_loop(0, count, heart_step, 0)
    leaving = start_copies([(out_ref, out_hbm)], out_sems)

    pair = (sums[2:3, :], sums[3:4, :], jnp.zeros((1, width), F32))
    box_begin(1, 0, pair)
    for side, rows in ((0, slice(0, reach)), (1, slice(frames - reach, frames))):
        for h in range(2):
            cols = slice(h * lanes, (h + 1) * lanes)
            edge_out[side, reach : 2 * reach, cols] = grad_y[h, rows, :]
            edge_out[side, 2 * reach : 3 * reach, cols] = conv[h, rows, :]
    grad_rims = (
        [edge_out.at[0, reach : 3 * reach, :], edge_out.at[1, reach : 3 * reach, :]],
        [edge_in.at[0, reach : 3 * reach, :], edge_in.at[1, reach : 3 * reach, :]],
    )
    swap_rims(1, *grad_rims)
    wide = w_in.shape[1]
    streams = make_streams([(0, wide, 2), (wide, wide, 2)], two, stage, land, None, sum_send, sum_recv)
    early_stages = len(stage_plans()[2]) - 1
    for j in range(0, wide, width):
        two[j : j + width, :] = dg(act[:, j : j + width], branch[...], 0, 0)
    advance(streams[:1], 0)
    pair = box_end(1, 0, pair, total)
    box_begin(1, 1, pair)
    for j in range(0, wide, width):
        two[wide + j : wide + j + width, :] = dg(n4_keep[...], hidden[:, j : j + width], 0, 0)
    advance(streams[1:], 0)
    advance(streams[:1], 1)
    point_two[...] = dg(swish[...], branch2[...], 0, 0)
    leaving += start_copies([(point_two, point_two_hbm)], out_sems.at[pl.ds(1, 1)])
    advance(streams[1:], 1)
    await_rims(1, *grad_rims)
    bias_sum, gain_sum, _ = box_end(1, 1, pair, total)
    bn_grads[0:1, :] = gain_sum
    bn_grads[1:2, :] = bias_sum
    bn_grads[2:8, :] = jnp.zeros((6, width), F32)

    scale = norm_gain * inv_std
    slope = -inv_std * inv_std * norm_gain * gain_sum / frame_count
    shift_all = -inv_std * norm_gain * bias_sum / frame_count

    def conv_grad(grad, value, frame, h):
        cols = slice(h * lanes, (h + 1) * lanes)
        extra = (value - mean[:, cols]) * slope[:, cols] + shift_all[:, cols]
        return grad * scale[:, cols] + jnp.where(frame < ends[-1], extra, 0.0)

    def grad_conv_step(c, carry):
        rows = rows_at(c, chunk)
        frame = first_frame + c * chunk + lax.broadcasted_iota(I32, (chunk, lanes), 0)
        where = pl.ds(pl.multiple_of(reach + c * chunk, 8), chunk)
        for h in range(2):
            grad_conv[h, where, :] = conv_grad(grad_y[h, rows, :], conv[h, rows, :], frame, h)
        return carry

    lax.fori_loop(0, count, grad_conv_step, 0)
    for side, rows, begin_frame in (
        (0, slice(0, reach), first_frame - reach),
        (1, slice(reach + frames, 2 * reach + frames), first_frame + frames),
    ):
        frame = begin_frame + lax.broadcasted_iota(I32, (reach, lanes), 0)
        for h in range(2):
            cols = slice(h * lanes, (h + 1) * lanes)
            grad_conv[h, rows, :] = conv_grad(
                edge_in[side, reach : 2 * reach, cols], edge_in[side, 2 * reach : 3 * reach, cols], frame, h
            )

    def conv_back_step(b, carry):
        low, high = low_lim[rows_at(b, block), :], high_lim[rows_at(b, block), :]
        start = pl.multiple_of(b * block, block)
        result = [zero, zero]
        here = [glu[h, pl.ds(pl.multiple_of(reach + start, 8), block), :] for h in range(2)]
        for tap in range(taps):
            shift = reach - tap
            inside = (low <= shift) if shift < 0 else (high >= shift)
            at = reach + shift
            for h in range(2):
                view = grad_conv.at[h, pl.ds(start, block + 2 * reach), :]
                term = jnp.where(inside, view[at : at + block, :], 0.0)
                result[h] = result[h] + depthwise[tap : tap + 1, h * lanes : (h + 1) * lanes].astype(F32) * term
                tap_sums[tap, h] += jnp.sum((here[h] * term).reshape(block // 8, 8, lanes), axis=0)
        for h in range(2):
            grad_glu[h, rows_at(b, block), :] = result[h]
        return carry

    lax.fori_loop(0, blocks // 2, conv_back_step, 0)
    advance(streams, 2)
    lax.fori_loop(blocks // 2, blocks, conv_back_step, 0)

    def back_moves(c):
        return moves(c, by_head(back_parts), by_frames(heads), back_send, back_recv, back_local)

    def close_step(c, carry):
        rows = rows_at(c, chunk)
        grad = halves_of(grad_glu, rows)
        value, gate = point[rows, :width], sigmoid(point[rows, width:])
        low_grad = jnp.concatenate([grad * gate, grad * value * gate * (1.0 - gate)], axis=1).astype(BF16)
        grad_point[rows, :] = low_grad
        grad = dg(low_grad, w_point1[...], 1, 1)
        hat, inv = norm_parts(x2_ref[rows, :])
        mid[3 * width + 2 : 3 * width + 3, :] += jnp.sum(grad * hat, axis=0, keepdims=True)
        grad2 = grad_x3[rows, :] + norm_back(grad, hat, inv, row_of(gain3))
        grad_x2[rows, :] = grad2
        low_grad = grad2.astype(BF16)
        branch3[rows, :] = low_grad
        back_parts[:, :, :, rows] = dg(w_out[...], low_grad, 1, 1).astype(BF16).reshape(2, 2, width // 4, chunk)
        for copy in back_moves(c):
            copy.start()
        return carry

    lax.fori_loop(0, count, close_step, 0)
    leaving += start_copies([(grad_x2, x2_hbm)], out_sems.at[pl.ds(3, 1)])
    for j in range(2):
        mid[j * width : (j + 1) * width, :] = dg(n3_keep[...], grad_point[:, j * width : (j + 1) * width], 0, 0)
    mid[2 * width : 3 * width, :] = dg(ctx[...].reshape(width, frames), branch3[...], 1, 0)
    for tap in range(taps):
        row = 3 * width + 8 + tap
        for h in range(2):
            mid[row : row + 1, h * lanes : (h + 1) * lanes] = jnp.sum(tap_sums[tap, h], axis=0, keepdims=True)

    leaving += start_copies([(mid, mid_hbm)], out_sems.at[pl.ds(4, 1)])

    def finish(c, carry):
        for copy in back_moves(c):
            copy.wait()
        return carry

    lax.fori_loop(0, count, finish, 0)
    for position in range(3, early_stages):
        advance(streams, position)
    size = streams[0].sizes[early_stages - 1][1]
    for i, stream in enumerate(streams):
        stream.sum_recv(early_stages - 1)
        partial[i * size : (i + 1) * size, :] = two[stream.at(stream.low(early_stages), size), :]
    wait_all(leaving)


def middle(
    lengths, parts, x1, cot, gain3, gain4, gain5, w_out, w_point1, depthwise, bn_gain, bn_bias, w_point2,
    w_in, w_down, dp,
):
    frames, width = x1.shape
    sp = lax.axis_size("sp")
    assert sp == HEADS == 4
    anywhere = pl.BlockSpec(memory_space=pl.ANY)
    paired = pltpu.VMEM((2, 2, width // 4, frames), BF16)
    wide = w_in.shape[1]
    staged, sems = reduction_scratch([wide, wide])
    stages = stage_plans()[2]
    part = exchange_plan(wide, stages[:-1])[2]
    taps = depthwise.shape[0]
    reach = taps // 2
    chunk = min(256, frames)
    count = frames // chunk
    lanes = width // 2
    keep, low_keep = pltpu.VMEM((frames, width), F32), pltpu.VMEM((frames, width), BF16)
    split = pltpu.VMEM((2, frames, lanes), F32)
    rimmed = pltpu.VMEM((2, frames + 2 * reach, lanes), F32)
    rims = pltpu.VMEM((2, 3 * reach, width), F32)
    moves = [DMA((count,)), DMA((count,)), DMA((count,))]
    return pl.pallas_call(
        functools.partial(middle_kernel, sp, dp, lengths.shape[1], taps, chunk, 64),
        out_shape=[
            jax.ShapeDtypeStruct((frames, width), BF16),
            jax.ShapeDtypeStruct((frames, width), F32),
            jax.ShapeDtypeStruct(parts.shape, BF16),
            jax.ShapeDtypeStruct((4 * width, width), F32),
            jax.ShapeDtypeStruct((width, width), F32),
            jax.ShapeDtypeStruct((8, width), F32),
            jax.ShapeDtypeStruct((2 * part, width), F32),
        ],
        in_specs=[
            SMEM, anywhere, anywhere, anywhere, VMEM, VMEM, VMEM, anywhere, anywhere, VMEM, VMEM, VMEM, anywhere,
            anywhere, anywhere,
        ],
        out_specs=[anywhere, anywhere, VMEM, anywhere, anywhere, VMEM, VMEM],
        scratch_shapes=[
            keep,
            low_keep,
            pltpu.VMEM(w_out.shape, BF16),
            pltpu.VMEM(w_point1.shape, BF16),
            pltpu.VMEM(w_point2.shape, BF16),
            pltpu.VMEM(w_in.shape, BF16),
            pltpu.VMEM(w_down.shape, BF16),
            low_keep,
            keep,
            pltpu.VMEM((4 * width, width), F32),
            pltpu.VMEM((width, width), F32),
            pltpu.VMEM((2 * wide, width), F32),
            DMA((7,)),
            DMA((5,)),
            pltpu.VMEM((staged, width), BF16),
            pltpu.VMEM((staged, width), BF16),
            DMA(sems),
            DMA(sems),
            paired,
            keep,
            low_keep,
            pltpu.VMEM((frames, 2 * width), F32),
            rimmed,
            split,
            pltpu.VMEM((frames, lanes), I32),
            pltpu.VMEM((frames, lanes), I32),
            pltpu.VMEM((frames, wide), BF16),
            pltpu.VMEM((frames, wide), BF16),
            low_keep,
            low_keep,
            low_keep,
            low_keep,
            keep,
            split,
            rimmed,
            split,
            pltpu.VMEM((frames, 2 * width), BF16),
            low_keep,
            paired,
            pltpu.VMEM((taps, 2, 8, lanes), F32),
            rims,
            rims,
            pltpu.VMEM((2, 2, 8, width), F32),
            pltpu.VMEM((2, sp - 1, 8, width), F32),
            pltpu.VMEM((2, dp - 1, 8, width), F32),
            pltpu.VMEM((8, width), F32),
        ]
        + moves
        + moves
        + [DMA((2, 2)), DMA((2, 2)), DMA((2, sp + dp - 2)), DMA((2, sp + dp - 2))],
        compiler_params=pltpu.CompilerParams(
            collective_id=1, has_side_effects=True, vmem_limit_bytes=VMEM_LIMIT
        ),
        name="middle",
    )(
        lengths, parts, x1, cot, gain3, gain4, gain5, w_out, w_point1, depthwise, bn_gain, bn_bias, w_point2,
        w_in, w_down,
    )


def back_kernel(
    sp, items, chunk, block, sub, len_ref, lse_ref, gain1, gain2, partial,
    near_hbm, far_hbm, o_hbm, do_hbm, trig_hbm, mid_hbm, point_two_hbm, tok_hbm, x1_hbm, n2_hbm, x2_hbm, act_hbm, slope_hbm, w_in_hbm, w_out_hbm, w_qkv_hbm,
    grad_ref, full,
    near, far, o_ref, do_ref, trig, tok, x1_ref, n2_ref, grad_x2, act, slope, w_in, w_out, w_qkv,
    qa, qt, ka, da, va, dq, turned, far_out, near_out, dq_out, far_kv, near_kv, near_dq,
    joined, branch, hidden, grad_x1, gains, acc, stage, land,
    load_sems, far_send, far_recv, near_send, near_recv, sum_send, sum_recv,
):
    me, dp = lax.axis_index("sp"), lax.axis_index("dp")
    core, pair = lax.rem(me, 2), me // 2
    sibling = peer_at(1, 0)
    frames, width = tok.shape
    wide = w_in.shape[1]
    half = trig.shape[0] // 2
    dim = 2 * half
    count = frames // chunk
    reach = 2 * frames
    greeted = [peer_at(*mask) for mask in all_masks(sp)]
    greet(greeted)
    unit = 4 * width
    last = 6 * unit
    loads = start_copies(
        [
            (near_hbm, near), (do_hbm, do_ref), (o_hbm, o_ref), (far_hbm, far),
            (mid_hbm, acc.at[2 * unit : 3 * unit, :]),
            (point_two_hbm, acc.at[3 * unit + 3 * width : 4 * unit, :]), (trig_hbm, trig),
            (x1_hbm, x1_ref), (x2_hbm, grad_x2), (w_qkv_hbm, w_qkv), (n2_hbm, n2_ref), (act_hbm, act),
            (w_out_hbm, w_out), (slope_hbm, slope), (w_in_hbm, w_in), (tok_hbm, tok),
        ],
        load_sems,
    )
    streams = make_streams(
        [
            (0, unit, 2), (unit, unit, 2), (2 * unit, unit, 2),
            (3 * unit, unit, 1), (4 * unit, unit, 0), (5 * unit, unit, 0), (last, 16, 0),
        ],
        acc, stage, land, full, sum_send, sum_recv,
    )
    early, (qkv, down, up, rest) = streams[:3], ([stream] for stream in streams[3:])
    steps = len(stage_plans()[0])
    acc[last : last + 16, :] = jnp.zeros((16, width), F32)
    gains[...] = jnp.zeros_like(gains)
    for h in range(2):
        dq[h] = jnp.zeros((dim, reach), F32)
    wait_all(loads[:4])
    ends = ends_of(len_ref, items)
    wide_pad = jnp.zeros((dim - 16, frames), BF16)
    for slot in range(2):
        cols = slice(slot * frames, (slot + 1) * frames)
        far_cols = slice(reach + slot * frames, reach + (slot + 1) * frames)
        segment = segment_row((2 * pair + slot) * frames, frames, ends)
        far_segment = segment_row((2 * (1 - pair) + slot) * frames, frames, ends)
        for h in range(2):
            query = near[slot, h * dim : (h + 1) * dim, :]
            qt[h, :, cols] = query
            qa[h, cols, :] = query_rows(query, segment, items, -lse_ref[h : h + 1, cols]).T
            grad = do_ref[h, :, cols]
            row_dot = jnp.sum(grad.astype(F32) * o_ref[h, :, cols], axis=0, keepdims=True)
            da[h, cols, :] = jnp.concatenate([grad, split_rows(-row_dot), wide_pad], axis=0).T
            ka[h, :, cols] = key_rows(near[slot, (2 + h) * dim : (3 + h) * dim, :], segment, items)
            ka[h, :, far_cols] = key_rows(far[slot, h * dim : (h + 1) * dim, :], far_segment, items)
            for where, value in (
                (cols, near[slot, (4 + h) * dim : (5 + h) * dim, :]),
                (far_cols, far[slot, (2 + h) * dim : (3 + h) * dim, :]),
            ):
                va[h, 0:dim, where] = value
                va[h, dim : dim + 16, where] = first_rows(3, frames)
                va[h, dim + 16 :, where] = wide_pad
    wait_all(loads[4:5])

    def attend_block(h, at):
        dk, dv = [], []

        def score(u):
            cols = pl.ds(pl.multiple_of(at + u * sub, sub), sub)
            return dg(qa[h], ka[h, :, cols], 1, 0), dg(da[h], va[h, :, cols], 1, 0)

        ready = score(0)
        for u in range(block // sub):
            scores, grad_probs = ready
            if u + 1 < block // sub:
                ready = score(u + 1)
            probs = jnp.exp(scores)
            grad = (probs * grad_probs).astype(BF16)
            dv.append(dg(do_ref[h], probs.astype(BF16), 1, 0).astype(BF16))
            dk.append(dg(qt[h], grad, 1, 0).astype(BF16))
            turned[u * sub : (u + 1) * sub, :] = grad.T
        dq[h] += dg(ka[h, 0:dim, pl.ds(pl.multiple_of(at, block), block)], turned[...], 1, 0)
        return jnp.concatenate(dk, axis=1), jnp.concatenate(dv, axis=1)

    per = frames // block

    def keep(ref, slot, h, cols, block_grads):
        for i, value in enumerate(block_grads):
            ref[slot, 2 * i + h, :, cols] = value

    def far_copy(b):
        cols = rows_at(lax.rem(b, per), block)
        return pltpu.make_async_remote_copy(
            src_ref=far_out.at[b // per, :, :, cols], dst_ref=far_kv.at[core, :, :, cols],
            send_sem=far_send.at[b], recv_sem=far_recv.at[core, lax.rem(b, per)],
            device_id=(dp, 2 * (1 - pair) + b // per), device_id_type=MESH,
        )

    done = len(early[0].stages) - 1
    size = early[0].sizes[done - 1][1]
    for i, stream in enumerate(early[:2]):
        acc[stream.at(stream.low(done), size), :] = partial[i * size : (i + 1) * size, :]
    schedule, remaining = {}, []
    for stream, times, first in zip(early, (PARTIAL_TIMES, PARTIAL_TIMES, FRESH_TIMES), (done, done, 0)):
        positions = range(first, 2 * len(stream.stages) + 1)
        for position, time in zip(positions, times):
            schedule.setdefault(time, []).append((stream, position, position == first))
        remaining.append([(stream, position) for position in positions[len(times) :]])

    def early_steps(t):
        for time, moves in schedule.items():
            @pl.when(t == min(time, 8 * per - 1))
            def _():
                for stream, position, opening in moves:
                    if opening:
                        stream.sum_send(position)
                    else:
                        advance([stream], position)

    def late_steps():
        for moves in remaining:
            if moves:
                stream, position = moves.pop(0)
                advance([stream], position)

    def far_step(t, carry):
        b, h = t // 2, lax.rem(t, 2)
        cols = rows_at(lax.rem(b, per), block)
        keep(far_out, b // per, h, cols, attend_block(h, reach + b * block))

        @pl.when(t == 0)
        def _():
            await_greetings(greeted)

        @pl.when(h == 1)
        def _():
            far_copy(b).start()

        early_steps(t)
        return carry

    lax.fori_loop(0, 4 * per, far_step, 0)

    def near_copy(b):
        cols = rows_at(b, block)
        return pltpu.make_async_remote_copy(
            src_ref=near_out.at[:, :, cols], dst_ref=near_kv.at[core, :, :, cols],
            send_sem=near_send.at[b], recv_sem=near_recv.at[b], device_id=sibling, device_id_type=MESH,
        )

    def sibling_step(t, carry):
        b, h = t // 2, lax.rem(t, 2)
        block_grads = attend_block(h, (1 - core) * frames + b * block)
        for i, value in enumerate(block_grads):
            near_out[2 * i + h, :, rows_at(b, block)] = value

        @pl.when(h == 1)
        def _():
            near_copy(b).start()

        early_steps(t + 4 * per)
        return carry

    lax.fori_loop(0, 2 * per, sibling_step, 0)

    def own_step(t, carry):
        b, h = t // 2, lax.rem(t, 2)
        keep(near_kv, core, h, rows_at(b, block), attend_block(h, core * frames + b * block))

        early_steps(t + 6 * per)
        return carry

    lax.fori_loop(0, 2 * per, own_step, 0)
    for h in range(2):
        dq_out[h] = (dq[h, :, pl.ds(pl.multiple_of((1 - core) * frames, frames), frames)] * dim**-0.5).astype(BF16)
    dq_copy = pltpu.make_async_remote_copy(
        src_ref=dq_out, dst_ref=near_dq.at[core], send_sem=near_send.at[per], recv_sem=near_recv.at[per],
        device_id=sibling, device_id_type=MESH,
    )
    dq_copy.start()
    for h in range(2):
        near_dq[core, h] = (dq[h, :, pl.ds(pl.multiple_of(core * frames, frames), frames)] * dim**-0.5).astype(BF16)
    wait_all(loads[5:])
    for b in range(2 * per):
        far_copy(b).wait_send()
    for source in range(2):
        for b in range(per):
            pltpu.make_async_remote_copy(
                src_ref=far_out.at[0, :, :, rows_at(b, block)], dst_ref=far_kv.at[source, :, :, rows_at(b, block)],
                send_sem=far_send.at[b], recv_sem=far_recv.at[source, b], device_id=sibling, device_id_type=MESH,
            ).wait_recv()
    for b in range(per):
        near_copy(b).wait()

    def turn_back(first, second, rows, low):
        sine, cosine = trig[0:half, rows], trig[half:, rows]
        joined[low : low + half, rows] = (first * cosine + second * sine).astype(BF16)
        joined[low + half : low + dim, rows] = (second * cosine - first * sine).astype(BF16)

    def keys_step(c, carry):
        rows = rows_at(c, chunk)
        for p in range(2):
            for h in range(2):
                head = 2 * p + h

                def both(i, low, high):
                    return near_kv[p, i, low:high, rows].astype(F32) + far_kv[p, i, low:high, rows].astype(F32)

                turn_back(both(h, 0, half), both(h, half, dim), rows, width + head * dim)
                low = 2 * width + head * dim
                joined[low : low + dim, rows] = both(2 + h, 0, dim).astype(BF16)
        return carry

    lax.fori_loop(0, count, keys_step, 0)
    dq_copy.wait()

    def arrive(c, carry):
        rows = rows_at(c, chunk)
        for p in range(2):
            for h in range(2):
                turn_back(
                    near_dq[p, h, 0:half, rows].astype(F32), near_dq[p, h, half:dim, rows].astype(F32), rows,
                    (2 * p + h) * dim,
                )
        grad = dg(joined[:, rows], w_qkv[...], 0, 1)
        hat, inv = norm_parts(x1_ref[rows, :])
        gains[1:2, :] += jnp.sum(grad * hat, axis=0, keepdims=True)
        grad = grad_x2[rows, :] + norm_back(grad, hat, inv, row_of(gain2))
        grad_x1[rows, :] = grad
        branch[rows, :] = (0.5 * grad).astype(BF16)
        return carry

    lax.fori_loop(0, count, arrive, 0)
    for j in range(0, wide, width):
        acc[4 * unit + j : 4 * unit + j + width, :] = dg(act[:, j : j + width], branch[...], 0, 0)
    advance(down, 0)
    acc[3 * unit : 3 * unit + 3 * width, :] = dg(joined[...], n2_ref[...], 1, 0)
    advance(qkv, 0)

    def through(c, carry):
        rows = rows_at(c, chunk)
        grad = dg(branch[rows, :], w_out[...], 1, 1)
        hidden[rows, :] = (grad * slope[rows, :].astype(F32)).astype(BF16)
        hat, _ = norm_parts(tok[rows, :].astype(F32))
        n2_ref[rows, :] = (hat * row_of(gain1)).astype(BF16)
        return carry

    lax.fori_loop(0, count, through, 0)
    advance(down + qkv, 1)
    for j in range(0, wide, width):
        acc[5 * unit + j : 5 * unit + j + width, :] = dg(n2_ref[...], hidden[:, j : j + width], 0, 0)
    advance(up, 0)

    def last_step(c, carry):
        rows = rows_at(c, chunk)
        grad = dg(hidden[rows, :], w_in[...], 1, 1)
        hat, inv = norm_parts(tok[rows, :].astype(F32))
        gains[0:1, :] += jnp.sum(grad * hat, axis=0, keepdims=True)
        grad_ref[rows, :] = (grad_x1[rows, :] + norm_back(grad, hat, inv, row_of(gain1))).astype(BF16)
        return carry

    lax.fori_loop(0, count // 2, last_step, 0)
    advance(up, 1)
    lax.fori_loop(count // 2, count, last_step, 0)
    acc[last : last + 8, :] = gains[...]
    advance(rest, 0)
    for position in range(2, 2 * steps + 1):
        advance(down + qkv + up, position)
        advance(rest, position - 1)
        late_steps()
    advance(rest, 2 * steps)
    while any(remaining):
        late_steps()


def back(
    lengths, near, far, o, lse, do, trig, gain1, gain2, partial, mid, point_two,
    tok, x1, n2, grad_x2, act, slope, w_in, w_out, w_qkv,
):
    frames, width = tok.shape
    sp = lax.axis_size("sp")
    chunk = min(256, frames)
    block = min(512, frames)
    count, per = frames // chunk, frames // block
    wide = w_in.shape[1]
    dim = width // HEADS
    reach = 2 * frames
    rows = 24 * width + 16
    staged, sems = reduction_scratch([4 * width] * 6 + [16])
    low_keep, keep = pltpu.VMEM((frames, width), BF16), pltpu.VMEM((frames, width), F32)
    return pl.pallas_call(
        functools.partial(back_kernel, sp, lengths.shape[1], chunk, block, min(128, block)),
        out_shape=[
            jax.ShapeDtypeStruct((frames, width), BF16),
            jax.ShapeDtypeStruct((rows, width), BF16),
        ],
        in_specs=[SMEM] + [VMEM] * 4 + [pl.BlockSpec(memory_space=pl.ANY)] * 16,
        out_specs=[VMEM] * 2,
        scratch_shapes=[
            pltpu.VMEM(near.shape, BF16),
            pltpu.VMEM(far.shape, BF16),
            pltpu.VMEM(o.shape, F32),
            pltpu.VMEM(do.shape, BF16),
            pltpu.VMEM(trig.shape, F32),
            low_keep,
            keep,
            low_keep,
            keep,
            pltpu.VMEM((frames, wide), BF16),
            pltpu.VMEM((frames, wide), BF16),
            pltpu.VMEM(w_in.shape, BF16),
            pltpu.VMEM(w_out.shape, BF16),
            pltpu.VMEM(w_qkv.shape, BF16),
            pltpu.VMEM((2, reach, 2 * dim), BF16),
            pltpu.VMEM((2, dim, reach), BF16),
            pltpu.VMEM((2, 2 * dim, 2 * reach), BF16),
            pltpu.VMEM((2, reach, 2 * dim), BF16),
            pltpu.VMEM((2, 2 * dim, 2 * reach), BF16),
            pltpu.VMEM((2, dim, reach), F32),
            pltpu.VMEM((block, reach), BF16),
            pltpu.VMEM((2, 4, dim, frames), BF16),
            pltpu.VMEM((4, dim, frames), BF16),
            pltpu.VMEM((2, dim, frames), BF16),
            pltpu.VMEM((2, 4, dim, frames), BF16),
            pltpu.VMEM((2, 4, dim, frames), BF16),
            pltpu.VMEM((2, 2, dim, frames), BF16),
            pltpu.VMEM((3 * width, frames), BF16),
            low_keep,
            pltpu.VMEM((frames, wide), BF16),
            keep,
            pltpu.VMEM((8, width), F32),
            pltpu.VMEM((rows, width), F32),
            pltpu.VMEM((staged, width), BF16),
            pltpu.VMEM((staged, width), BF16),
            DMA((16,)),
            DMA((2 * per,)),
            DMA((2, per)),
            DMA((per + 1,)),
            DMA((per + 1,)),
            DMA(sems),
            DMA(sems),
        ],
        compiler_params=pltpu.CompilerParams(
            collective_id=2, has_side_effects=True, vmem_limit_bytes=VMEM_LIMIT
        ),
        name="back",
    )(
        lengths, lse, gain1, gain2, partial, near, far, o, do, trig, mid, point_two,
        tok, x1, n2, grad_x2, act, slope, w_in, w_out, w_qkv,
    )


def unpack_kernel(
    taps, full_hbm, bn_grads, output_hbm, input_hbm,
    output_to, input_to, gain1_to, in_one_to, out_one_to, gain2_to, qkv_to, out_weight_to, gain3_to, point_one_to,
    depthwise_to, bn_gain_to, bn_bias_to, point_two_to, gain4_to, in_two_to, out_two_to, gain5_to,
    full, output, input_grad, in_one, out_one, qkv, point_one, point_two, out_weight, in_two, out_two, depthwise,
    load_sems, sems,
):
    width = full.shape[1]
    unit = 4 * width
    copies = []
    pieces = [pl.ds(i * unit, unit) for i in range(6)] + [pl.ds(6 * unit, 16)]
    loads = start_copies(
        [(full_hbm.at[piece, :], full.at[piece, :]) for piece in pieces]
        + [(output_hbm, output), (input_hbm, input_grad)],
        load_sems,
    )

    def send(source, target):
        copies.append(pltpu.make_async_copy(source, target, sems.at[len(copies)]))
        copies[-1].start()

    def block(base):
        return full[base : base + width, :].astype(F32)

    loads[0].wait()
    for j in range(0, unit, width):
        out_two[j : j + width, :] = block(j)
    send(out_two, out_two_to)
    loads[1].wait()
    for j in range(0, unit, width):
        in_two[:, j : j + width] = block(unit + j)
    send(in_two, in_two_to)
    loads[2].wait()
    for j in range(0, 2 * width, width):
        point_one[:, j : j + width] = block(2 * unit + j)
    send(point_one, point_one_to)
    out_weight[...] = block(2 * unit + 2 * width)
    send(out_weight, out_weight_to)
    small = full[2 * unit + 3 * width : 2 * unit + 3 * width + 64, :].astype(F32)
    depthwise[...] = small[8 : 8 + taps]
    send(depthwise, depthwise_to)
    loads[3].wait()
    point_two[...] = block(3 * unit + 3 * width)
    send(point_two, point_two_to)
    for j in range(0, 3 * width, width):
        qkv[:, j : j + width] = block(3 * unit + j).T
    send(qkv, qkv_to)
    loads[4].wait()
    for j in range(0, unit, width):
        out_one[j : j + width, :] = block(4 * unit + j)
    send(out_one, out_one_to)
    loads[5].wait()
    for j in range(0, unit, width):
        in_one[:, j : j + width] = block(5 * unit + j)
    send(in_one, in_one_to)
    wait_all(loads[6:])
    send(output, output_to)
    send(input_grad, input_to)
    rest = full[6 * unit : 6 * unit + 16, :].astype(F32)
    for ref, row in (
        (gain1_to, rest[0]), (gain2_to, rest[1]), (gain3_to, small[2]), (gain4_to, small[3]), (gain5_to, small[4]),
        (bn_gain_to, bn_grads[0, :]), (bn_bias_to, bn_grads[1, :]),
    ):
        ref[...] = row
    wait_all(copies)


def unpack(full, bn_grads, output, input_grad, taps):
    width = full.shape[1]
    row, square, tall, flat = (width,), (width, width), (4 * width, width), (width, 4 * width)
    thrice, twice = (width, 3 * width), (width, 2 * width)
    anywhere = pl.BlockSpec(memory_space=pl.ANY)
    shapes = [
        output.shape, input_grad.shape, row, flat, tall, row, thrice, square, row, twice, (taps, width), row, row,
        square, row, flat, tall, row,
    ]
    return pl.pallas_call(
        functools.partial(unpack_kernel, taps),
        out_shape=[jax.ShapeDtypeStruct(shape, F32 if i > 1 else BF16) for i, shape in enumerate(shapes)],
        in_specs=[anywhere, VMEM, anywhere, anywhere],
        out_specs=[VMEM if shape == row else anywhere for shape in shapes],
        scratch_shapes=[
            pltpu.VMEM(full.shape, BF16),
            pltpu.VMEM(output.shape, BF16),
            pltpu.VMEM(input_grad.shape, BF16),
        ]
        + [
            pltpu.VMEM(shape, F32)
            for shape in (flat, tall, thrice, twice, square, square, flat, tall, (taps, width))
        ]
        + [DMA((9,)), DMA((11,))],
        compiler_params=pltpu.CompilerParams(vmem_limit_bytes=VMEM_LIMIT),
        name="unpack",
    )(full, bn_grads, output, input_grad)


def on_device(
    tokens, ln1_gain, ffn1_in, ffn1_out, ln2_gain, w_qkv, w_out, ln3_gain, w_point1, depthwise,
    bn_gain, bn_bias, w_point2, ln4_gain, ffn2_in, ffn2_out, ln5_gain, lengths, cotangent,
):
    width = tokens.shape[2]
    sp, dp = lax.axis_size("sp"), lax.axis_size("dp")
    assert HEADS == sp and ffn1_in.shape[1] == ffn2_in.shape[1] == 4 * width
    half = width // HEADS // 2
    turns = 10000.0 ** (-np.arange(half, dtype=np.float64) / half) / (2 * np.pi)
    high = np.round(turns * 4096.0) / 4096.0
    freq = jnp.asarray(np.stack([high, turns - high], axis=1), F32)
    x1, n2, trig, act, slope, near, far, context, raw_context, log_sums, flag = front(
        lengths, tokens[0], ln1_gain, ffn1_in, ffn1_out, ln2_gain, w_qkv, freq
    )
    context, raw_context, log_sums = repair(lengths, flag, near, far, context, raw_context, log_sums)
    output, grad_x2, grad_context, mid, point_two, bn_grads, partial = middle(
        lengths, context, x1, cotangent[0], ln3_gain, ln4_gain, ln5_gain, w_out, w_point1, depthwise,
        bn_gain, bn_bias, w_point2, ffn2_in, ffn2_out, dp,
    )
    input_grad, full = back(
        lengths, near, far, raw_context, log_sums, grad_context, trig, ln1_gain, ln2_gain, partial, mid, point_two,
        tokens[0], x1, n2, grad_x2, act, slope, ffn1_in, ffn1_out, w_qkv,
    )
    results = unpack(full, bn_grads, output, input_grad, depthwise.shape[0])
    return (results[0][None], results[1][None]) + tuple(results[2:])


def solution(mesh):
    split = P("dp", "sp", None)
    return jax.shard_map(
        on_device,
        mesh=mesh,
        in_specs=(split,) + (P(),) * 16 + (P("dp", None), split),
        out_specs=(split, split) + (P(),) * 16,
        check_vma=False,
    )
```
